32 devices in a mesh: gz: 16 (over z, y, x), gy: 2 (over core).
Axes of the slice: x: 2, y: 2, z: 4, core: 2. Of those that a mesh axis runs over, the one named last changes fastest.
Arguments:
- scalar: float32 [32, 128, 1024], P('gz', 'gy'), as said below
- bin_index: int32 [32, 128, 1024], P('gz', 'gy'), may hold values from 0 to 255, as said below
- color_table: bfloat16 [3, 257], replicated, may hold values from 0.099609375 to 1
- opacity_table: bfloat16 [257], replicated, may hold values from 0.00049972534 to 0.019897461
- light_dir: float32 [3], replicated, may hold values from -4 to 4
- view_order: int32 [16], replicated, may hold values from 0 to 15, each once
Outputs:
- image_rgba: float32 [4, 2, 64, 1024], P(None, 'gy', 'gz')
The draws below stay inside these ranges and needn't reach their ends.
Inputs may be any that keep to these rules, and one draw needn't show every extreme that they name: bin_index is the floor of 256 scalar in every cell, except that fraction may reach 1. scalar lies between bin_index / 256 and (bin_index + 1) / 256. `view_order`: each brick position appears once.
All inputs are finite; a program needn't handle non-finite values.
Results may differ from the reference program's by a relative error of at most 0.0003.
Values sent between devices are 32-bit elements; how exact they have to be, the bound alone decides.
No kernel may reach another device: no remote copies, remote signals or barrier semaphores. Data moves between devices by JAX's collectives and lax.ppermute only.
A program may use at most 64 MiB of HBM per device.

```python
import math
import jax
import jax.numpy as jnp
from jax import lax

W = 1024
NBINS = 256
DZ = 2
RY = 64
NZ = 32
NY = 128
N_GZ = 16
N_GY = 2


def draw_codes(key):
    return jax.random.randint(jax.random.fold_in(key, 7), (NZ, NY, W), 0, NBINS, dtype=jnp.int32)


def draw_bin_index(key, part):
    return draw_codes(key)


def draw_scalar(key, part):
    bin_codes = draw_codes(key)
    inside = jax.random.uniform(jax.random.fold_in(key, 11), (NZ, NY, W), jnp.float32)
    return (bin_codes.astype(jnp.float32) + inside) / NBINS


def bell_draw(key, dims, deviation, limit, kind=jnp.bfloat16):
    array = deviation * jax.random.normal(key, dims, jnp.float32)
    return jnp.clip(array, min=-limit, max=limit).astype(kind)


def setup_inputs(seed: int = 0) -> dict:
    seeds = jax.random.split(jax.random.key(seed), 7)
    return {
        "scalar": draw_scalar(jax.random.fold_in(seeds[6], 71), 0),
        "bin_index": draw_bin_index(jax.random.fold_in(seeds[6], 71), 0),
        "color_table": jnp.clip(jax.random.uniform(seeds[2], (3, NBINS + 1), jnp.float32, 0.099609375, 1.0), 0.099609375, 1.0).astype(jnp.bfloat16),
        "opacity_table": jnp.clip(jnp.exp(jax.random.uniform(seeds[3], (NBINS + 1,), jnp.float32, math.log(0.00049972534), math.log(0.019897461))), 0.00049972534, 0.019897461).astype(jnp.bfloat16),
        "light_dir": bell_draw(seeds[4], (3,), 1.5, 4.0, jnp.float32),
        "view_order": jax.random.permutation(seeds[5], N_GZ).astype(jnp.int32),
    }


def shading_from(field, row_padded, light_dir):
    next_slice = jnp.concatenate([field[1:], field[-1:]], axis=0)
    behind = jnp.concatenate([field[:1], field[:-1]], axis=0)
    grad_depth = next_slice - behind
    grad_rows = row_padded[:, 2:] - row_padded[:, :-2]
    col_padded = jnp.pad(field, ((0, 0), (0, 0), (1, 1)))
    grad_cols = col_padded[:, :, 2:] - col_padded[:, :, :-2]
    facing = grad_depth * light_dir[0] + grad_rows * light_dir[1] + grad_cols * light_dir[2]
    squared = grad_depth * grad_depth + grad_rows * grad_rows + grad_cols * grad_cols
    return 0.25 + 0.75 * facing * facing / (squared + 1.0)


def blend_emission(lower, upper, fraction, shading):
    blended = (1.0 - fraction) * lower + fraction * upper
    opacity = blended[3]
    emitted = (opacity * shading) * blended[:3]
    return emitted, jnp.log1p(-opacity)


def reference(scalar, bin_index, color_table, opacity_table, light_dir, view_order):
    brick_order = jnp.argsort(view_order).astype(jnp.int32)

    def advance(running, position):
        color_sum, keep_sum = running
        brick_id = brick_order[position]
        start = (brick_id * DZ).astype(jnp.int32)
        field = lax.dynamic_slice_in_dim(scalar, start, DZ, 0)
        bin_codes = lax.dynamic_slice_in_dim(bin_index, start, DZ, 0)
        row_padded = jnp.pad(field, ((0, 0), (1, 1), (0, 0)))
        shading = shading_from(field, row_padded, light_dir)
        fraction = field * NBINS - bin_codes.astype(field.dtype)
        lower = jnp.concatenate([color_table[:, bin_codes], opacity_table[bin_codes][None]], axis=0).astype(field.dtype)
        upper_codes = bin_codes + 1
        upper = jnp.concatenate([color_table[:, upper_codes], opacity_table[upper_codes][None]], axis=0).astype(field.dtype)
        emitted, log_keep = blend_emission(lower, upper, fraction, shading)
        passed = jnp.cumsum(log_keep, axis=0) - log_keep
        brick_color = jnp.sum(emitted * jnp.exp(passed)[None], axis=1)
        brick_keep = jnp.sum(log_keep, axis=0)
        return (color_sum + brick_color * jnp.exp(keep_sum)[None], keep_sum + brick_keep), None

    initial = (jnp.zeros((3, NY, W), scalar.dtype), jnp.zeros((NY, W), scalar.dtype))
    finished, unused = lax.scan(advance, initial, jnp.arange(N_GZ, dtype=jnp.int32))
    color_sum, keep_sum = finished
    coverage = 1.0 - jnp.exp(keep_sum)
    image_rgba = jnp.concatenate([color_sum, coverage[None]], axis=0)
    return image_rgba.reshape(4, N_GY, RY, W)
```

```python
import jax
import jax.numpy as jnp
from jax import lax
from jax.experimental import pallas as pl
from jax.experimental.pallas import tpu as pltpu
from jax.sharding import PartitionSpec as P

SUB, LANES = 8, 128


def pack_kernel(field_ref, out_ref):
    depth, rows, cols = field_ref.shape
    chunks = cols // LANES
    for k in range(depth):
        for j in range(rows // SUB):
            for c in range(chunks):
                tile = field_ref[k, j * SUB:(j + 1) * SUB, c * LANES:(c + 1) * LANES]
                base = (j * SUB * depth + k) * chunks + c
                out_ref[pl.ds(base, SUB, stride=depth * chunks), :] = tile


def packed(field):
    depth, rows, cols = field.shape
    shape = (rows * depth * (cols // LANES), LANES)
    return pl.pallas_call(
        pack_kernel,
        out_shape=jax.ShapeDtypeStruct(shape, field.dtype),
        in_specs=[pl.BlockSpec(memory_space=pltpu.VMEM)],
        out_specs=pl.BlockSpec(memory_space=pltpu.VMEM),
        compiler_params=pltpu.CompilerParams(vmem_limit_bytes=16 << 20),
        name="pack_rows",
    )(field)


def shared(x, axis, shift):
    return pltpu.roll(x, shift % x.shape[axis], axis)


def composite_kernel(order_ref, light_ref, color_ref, opacity_ref, tile_ref, up_ref, down_ref,
                     out_ref, brick_at, staged):
    bricks, rows, depth, chunks, _ = tile_ref.shape
    bins = color_ref.shape[1] - 1
    halves = bins // LANES
    shape = (chunks, LANES)

    def place(b, carry):
        brick_at[order_ref[b]] = b
        return carry

    lax.fori_loop(0, bricks, place, 0)

    table = jnp.concatenate(
        [color_ref[...].astype(jnp.float32), opacity_ref[...].astype(jnp.float32)], axis=0)
    lower = table[:, :bins]
    slope = table[:, 1:] - lower

    def spread(values, channel, half):
        row = values[channel:channel + 1, half * LANES:(half + 1) * LANES]
        return jnp.broadcast_to(row, shape)

    lows = [[spread(lower, c, h) for h in range(halves)] for c in range(4)]
    slopes = [[spread(slope, c, h) for h in range(halves)] for c in range(4)]
    light = [light_ref[i] for i in range(3)]
    lane = lax.broadcasted_iota(jnp.int32, shape, 1)
    chunk = lax.broadcasted_iota(jnp.int32, shape, 0)
    at_first, at_last = lane == 0, lane == LANES - 1
    at_left = at_first & (chunk == 0)
    at_right = at_last & (chunk == chunks - 1)

    def pick(tables, low_bits, upper_half):
        found = [jnp.take_along_axis(t, low_bits, axis=1, mode="promise_in_bounds") for t in tables]
        result = found[0]
        for h in range(1, halves):
            result = jnp.where(upper_half[h - 1], found[h], result)
        return result

    def column_gradient(x):
        right = shared(x, 1, -1)
        right = jnp.where(at_last, shared(right, 0, -1), right)
        right = jnp.where(at_right, 0.0, right)
        left = shared(x, 1, 1)
        left = jnp.where(at_first, shared(left, 0, 1), left)
        left = jnp.where(at_left, 0.0, left)
        return right - left

    def step(position, carry):
        colors, keeps = carry
        b = brick_at[position]
        colors, keeps = list(colors), list(keeps)
        for r in range(rows):
            field = [tile_ref[b, r, k] for k in range(depth)]
            depth_gradient = {}
            for k in range(depth):
                ends = (min(k + 1, depth - 1), max(k - 1, 0))
                if ends not in depth_gradient:
                    depth_gradient[ends] = field[ends[0]] - field[ends[1]]
                dz = depth_gradient[ends]
                above = tile_ref[b, r - 1, k] if r > 0 else up_ref[b, k]
                below = tile_ref[b, r + 1, k] if r + 1 < rows else down_ref[b, k]
                dy = below - above
                x = field[k]
                dx = column_gradient(x)
                facing = dz * light[0] + dy * light[1] + dx * light[2]
                squared = dz * dz + dy * dy + dx * dx
                shading = 0.25 + 0.75 * facing * facing / (squared + 1.0)
                scaled = x * float(bins)
                index = jnp.minimum(scaled.astype(jnp.int32), bins - 1)
                fraction = scaled - index.astype(jnp.float32)
                low_bits = index & (LANES - 1)
                upper_half = [index >= h * LANES for h in range(1, halves)]
                blend = [
                    pick(lows[c], low_bits, upper_half)
                    + fraction * pick(slopes[c], low_bits, upper_half)
                    for c in range(4)
                ]
                weight = keeps[r] * blend[3] * shading
                for c in range(3):
                    colors[c * rows + r] = colors[c * rows + r] + weight * blend[c]
                keeps[r] = keeps[r] - keeps[r] * blend[3]
        return tuple(colors), tuple(keeps)

    zero, one = jnp.zeros(shape, jnp.float32), jnp.ones(shape, jnp.float32)
    colors, keeps = lax.fori_loop(0, bricks, step, ((zero,) * (3 * rows), (one,) * rows))
    for i, value in enumerate(list(colors) + [1.0 - k for k in keeps]):
        staged[i * chunks:(i + 1) * chunks, :] = value
    for c in range(4):
        for q in range(chunks):
            out_ref[c, 0, :, q * LANES:(q + 1) * LANES] = staged[
                pl.ds(c * rows * chunks + q, rows, stride=chunks), :]


def composite(view_order, light_dir, color_table, opacity_table, tiles, up, down):
    bricks, rows, depth, chunks, lanes = tiles.shape
    vmem = pl.BlockSpec(memory_space=pltpu.VMEM)
    smem = pl.BlockSpec(memory_space=pltpu.SMEM)
    return pl.pallas_call(
        composite_kernel,
        out_shape=jax.ShapeDtypeStruct((4, 1, rows, chunks * lanes), jnp.float32),
        in_specs=[smem, smem, vmem, vmem, vmem, vmem, vmem],
        out_specs=vmem,
        scratch_shapes=[
            pltpu.SMEM((bricks,), jnp.int32),
            pltpu.VMEM((4 * rows * chunks, lanes), jnp.float32),
        ],
        compiler_params=pltpu.CompilerParams(vmem_limit_bytes=32 << 20),
        name="composite_bricks",
    )(view_order, light_dir, color_table, opacity_table[None, :], tiles, up, down)


def shards(scalar, bin_index, color_table, opacity_table, light_dir, view_order):
    depth, rows, cols = scalar.shape
    bricks, bands = lax.axis_size("gz"), lax.axis_size("gy")
    tile_rows = rows // bricks
    chunks = cols // LANES
    sent = packed(scalar).reshape(bricks, tile_rows, depth, chunks, LANES)
    tiles = lax.all_to_all(sent, "gz", split_axis=0, concat_axis=0, tiled=True)
    along = [t * bands + g for g in range(bands) for t in range(bricks)]
    ahead = list(zip(along[:-1], along[1:]))
    back = [(j, i) for i, j in ahead]
    up = lax.ppermute(tiles[:, -1], ("gz", "gy"), ahead)
    down = lax.ppermute(tiles[:, 0], ("gz", "gy"), back)
    return composite(view_order, light_dir, color_table, opacity_table, tiles, up, down)


def solution(mesh):
    in_specs = (P("gz", "gy", None), P("gz", "gy", None), P(), P(), P(), P())
    out_specs = P(None, "gy", "gz", None)
    return jax.shard_map(shards, mesh=mesh, in_specs=in_specs, out_specs=out_specs, check_vma=False)
```

```python
import functools

import jax
import jax.numpy as jnp
from jax import lax
from jax.experimental import pallas as pl
from jax.experimental.pallas import tpu as pltpu
from jax.sharding import PartitionSpec as P

SUB, LANES = 8, 128


def pack_kernel(row_groups, field_ref, *rest):
    *out_refs, staged = rest
    depth, rows, cols = field_ref.shape
    chunks = cols // LANES
    tile_rows = sum(len(group) for group in row_groups)
    block = depth * chunks
    for k in range(depth):
        for j in range(rows // SUB):
            for c in range(chunks):
                lines = field_ref[k, j * SUB:(j + 1) * SUB, c * LANES:(c + 1) * LANES]
                staged[pl.ds(j * SUB * block + k * chunks + c, SUB, stride=block), :] = lines
    for group, out_ref in zip(row_groups, out_refs):
        for t in range(rows // tile_rows):
            for i, r in enumerate(group):
                source, target = (t * tile_rows + r) * block, (t * len(group) + i) * block
                out_ref[target:target + block, :] = staged[source:source + block, :]


def packed(field, tiles, row_groups):
    depth, rows, cols = field.shape
    chunks = cols // LANES
    shapes = [(tiles * len(group) * depth * chunks, LANES) for group in row_groups]
    vmem = pl.BlockSpec(memory_space=pltpu.VMEM)
    flat = pl.pallas_call(
        functools.partial(pack_kernel, row_groups),
        out_shape=[jax.ShapeDtypeStruct(shape, field.dtype) for shape in shapes],
        in_specs=[vmem],
        out_specs=[vmem] * len(shapes),
        scratch_shapes=[pltpu.VMEM((rows * depth * chunks, LANES), field.dtype)],
        compiler_params=pltpu.CompilerParams(vmem_limit_bytes=16 << 20),
        name="pack_rows",
    )(field)
    return [x.reshape(tiles, len(group), depth, chunks, LANES) for x, group in zip(flat, row_groups)]


def shifted(x, axis, shift):
    return pltpu.roll(x, shift % x.shape[axis], axis)


def brick_positions(order_ref, brick_at):
    def place(b, carry):
        brick_at[order_ref[b]] = b
        return carry

    lax.fori_loop(0, order_ref.shape[0], place, 0)


def table_lookup(color_ref, opacity_ref, shape):
    bins = color_ref.shape[1] - 1
    halves = bins // LANES
    table = jnp.concatenate(
        [color_ref[...].astype(jnp.float32), opacity_ref[...].astype(jnp.float32)], axis=0)
    lower = table[:, :bins]
    slope = table[:, 1:] - lower

    def spread(values, channel, half):
        row = values[channel:channel + 1, half * LANES:(half + 1) * LANES]
        return jnp.broadcast_to(row, shape)

    lows = [[spread(lower, c, h) for h in range(halves)] for c in range(4)]
    slopes = [[spread(slope, c, h) for h in range(halves)] for c in range(4)]

    def pick(tables, low_bits, upper_half):
        found = [jnp.take_along_axis(t, low_bits, axis=1, mode="promise_in_bounds") for t in tables]
        result = found[0]
        for h in range(1, halves):
            result = jnp.where(upper_half[h - 1], found[h], result)
        return result

    def look_up(x):
        scaled = x * float(bins)
        index = jnp.minimum(scaled.astype(jnp.int32), bins - 1)
        fraction = scaled - index.astype(jnp.float32)
        low_bits = index & (LANES - 1)
        upper_half = [index >= h * LANES for h in range(1, halves)]
        blend = [
            pick(lows[c], low_bits, upper_half) + fraction * pick(slopes[c], low_bits, upper_half)
            for c in range(4)
        ]
        return blend[:3], blend[3]

    return look_up


def column_differences(shape):
    lane = lax.broadcasted_iota(jnp.int32, shape, 1)
    chunk = lax.broadcasted_iota(jnp.int32, shape, 0)
    at_first, at_last = lane == 0, lane == shape[1] - 1
    at_left = at_first & (chunk == 0)
    at_right = at_last & (chunk == shape[0] - 1)

    def difference(x):
        right = shifted(x, 1, -1)
        right = jnp.where(at_last, shifted(right, 0, -1), right)
        right = jnp.where(at_right, 0.0, right)
        left = shifted(x, 1, 1)
        left = jnp.where(at_first, shifted(left, 0, 1), left)
        left = jnp.where(at_left, 0.0, left)
        return right - left

    return difference


def depth_differences(field):
    last = len(field) - 1
    made = {}
    for k in range(last + 1):
        ends = (min(k + 1, last), max(k - 1, 0))
        if ends not in made:
            made[ends] = field[ends[0]] - field[ends[1]]
    return [made[(min(k + 1, last), max(k - 1, 0))] for k in range(last + 1)]


def shading_of(facing, squared_plus_one):
    return 0.25 + 0.75 * facing * facing / squared_plus_one


def edge_kernel(order_ref, light_ref, color_ref, opacity_ref, edge_ref, part_ref, keep_ref, brick_at):
    bricks, rows, depth, chunks, lanes = edge_ref.shape
    shape = (chunks, lanes)
    brick_positions(order_ref, brick_at)
    look_up = table_lookup(color_ref, opacity_ref, shape)
    column_difference = column_differences(shape)
    light = [light_ref[i] for i in range(3)]

    def step(position, keeps):
        b = brick_at[position]
        keeps = list(keeps)
        for r in range(rows):
            field = [edge_ref[b, r, k] for k in range(depth)]
            for k, (x, dz) in enumerate(zip(field, depth_differences(field))):
                dx = column_difference(x)
                color, opacity = look_up(x)
                weight = keeps[r] * opacity
                for c in range(3):
                    part_ref[b, r, k, c] = weight * color[c]
                part_ref[b, r, k, 3] = dz * light[0] + dx * light[2]
                part_ref[b, r, k, 4] = dz * dz + dx * dx + 1.0
                keeps[r] = keeps[r] - weight
        return tuple(keeps)

    keeps = lax.fori_loop(0, bricks, step, (jnp.ones(shape, jnp.float32),) * rows)
    for r in range(rows):
        keep_ref[r] = keeps[r]


def finish_kernel(edge_rows, order_ref, light_ref, color_ref, opacity_ref, edge_ref, part_ref, keep_ref,
                  up_ref, down_ref, *rest):
    inner_ref = rest[0] if len(rest) == 4 else None
    out_ref, brick_at, staged = rest[-3:]
    bricks, _, depth, chunks, lanes = edge_ref.shape
    shape = (chunks, lanes)
    rows = out_ref.shape[2]
    inner_rows = [r for r in range(rows) if r not in edge_rows]
    brick_positions(order_ref, brick_at)
    look_up = table_lookup(color_ref, opacity_ref, shape)
    column_difference = column_differences(shape)
    light = [light_ref[i] for i in range(3)]

    def load(b, r, k):
        if r < 0:
            return up_ref[b, k]
        if r >= rows:
            return down_ref[b, k]
        if r in edge_rows:
            return edge_ref[b, edge_rows.index(r), k]
        return inner_ref[b, inner_rows.index(r), k]

    def step(position, carry):
        colors, keeps = carry
        b = brick_at[position]
        colors, keeps = list(colors), list(keeps)
        for r in inner_rows:
            field = [load(b, r, k) for k in range(depth)]
            for k, (x, dz) in enumerate(zip(field, depth_differences(field))):
                dy = load(b, r + 1, k) - load(b, r - 1, k)
                dx = column_difference(x)
                facing = dz * light[0] + dy * light[1] + dx * light[2]
                squared = dz * dz + dy * dy + dx * dx
                color, opacity = look_up(x)
                weight = keeps[inner_rows.index(r)] * opacity
                shaded = weight * shading_of(facing, squared + 1.0)
                for c in range(3):
                    colors[c * rows + r] = colors[c * rows + r] + shaded * color[c]
                keeps[inner_rows.index(r)] = keeps[inner_rows.index(r)] - weight
        for i, r in enumerate(edge_rows):
            for k in range(depth):
                dy = load(b, r + 1, k) - load(b, r - 1, k)
                shading = shading_of(part_ref[b, i, k, 3] + dy * light[1], part_ref[b, i, k, 4] + dy * dy)
                for c in range(3):
                    colors[c * rows + r] = colors[c * rows + r] + shading * part_ref[b, i, k, c]
        return tuple(colors), tuple(keeps)

    zero, one = jnp.zeros(shape, jnp.float32), jnp.ones(shape, jnp.float32)
    colors, keeps = lax.fori_loop(
        0, bricks, step, ((zero,) * (3 * rows), (one,) * len(inner_rows)))
    kept = [keep_ref[edge_rows.index(r)] if r in edge_rows else keeps[inner_rows.index(r)]
            for r in range(rows)]
    for i, value in enumerate(list(colors) + [1.0 - k for k in kept]):
        staged[i * chunks:(i + 1) * chunks, :] = value
    for c in range(4):
        for q in range(chunks):
            source = pl.ds(c * rows * chunks + q, rows, stride=chunks) if rows > 1 else pl.ds(c * chunks + q, 1)
            out_ref[c, 0, :, q * LANES:(q + 1) * LANES] = staged[source, :]


def shards(scalar, bin_index, color_table, opacity_table, light_dir, view_order):
    depth, rows, cols = scalar.shape
    bricks, bands = lax.axis_size("gz"), lax.axis_size("gy")
    tile_rows = rows // bricks
    chunks = cols // LANES
    edge_rows = sorted({0, tile_rows - 1})
    inner_rows = [r for r in range(tile_rows) if r not in edge_rows]
    groups = [edge_rows] + ([inner_rows] if inner_rows else [])
    edges, *inner = [
        lax.all_to_all(x, "gz", split_axis=0, concat_axis=0, tiled=True)
        for x in packed(scalar, bricks, groups)
    ]
    along = [t * bands + g for g in range(bands) for t in range(bricks)]
    ahead = list(zip(along[:-1], along[1:]))
    back = [(j, i) for i, j in ahead]
    up = lax.ppermute(edges[:, -1], ("gz", "gy"), ahead)
    down = lax.ppermute(edges[:, 0], ("gz", "gy"), back)

    vmem = pl.BlockSpec(memory_space=pltpu.VMEM)
    smem = pl.BlockSpec(memory_space=pltpu.SMEM)
    tables = (view_order, light_dir, color_table, opacity_table[None, :])
    table_specs = [smem, smem, vmem, vmem]
    params = pltpu.CompilerParams(vmem_limit_bytes=32 << 20)
    order_scratch = pltpu.SMEM((bricks,), jnp.int32)
    cells = bricks * depth * cols
    parts, keeps = pl.pallas_call(
        edge_kernel,
        out_shape=[
            jax.ShapeDtypeStruct((bricks, len(edge_rows), depth, 5, chunks, LANES), jnp.float32),
            jax.ShapeDtypeStruct((len(edge_rows), chunks, LANES), jnp.float32),
        ],
        in_specs=table_specs + [vmem],
        out_specs=[vmem, vmem],
        scratch_shapes=[order_scratch],
        compiler_params=params,
        cost_estimate=pl.CostEstimate(
            flops=100 * cells * len(edge_rows), bytes_accessed=24 * cells * len(edge_rows), transcendentals=0),
        name="edge_rows",
    )(*tables, edges)
    return pl.pallas_call(
        functools.partial(finish_kernel, edge_rows),
        out_shape=jax.ShapeDtypeStruct((4, 1, tile_rows, cols), jnp.float32),
        in_specs=table_specs + [vmem] * (5 + len(inner)),
        out_specs=vmem,
        scratch_shapes=[order_scratch, pltpu.VMEM((4 * tile_rows * chunks, LANES), jnp.float32)],
        compiler_params=params,
        cost_estimate=pl.CostEstimate(
            flops=100 * cells * tile_rows, bytes_accessed=24 * cells * tile_rows, transcendentals=0),
        name="inner_rows",
    )(*tables, edges, parts, keeps, up, down, *inner)


def solution(mesh):
    in_specs = (P("gz", "gy", None), P("gz", "gy", None), P(), P(), P(), P())
    out_specs = P(None, "gy", "gz", None)
    return jax.shard_map(shards, mesh=mesh, in_specs=in_specs, out_specs=out_specs, check_vma=False)
```

```python
import functools

import jax
import jax.numpy as jnp
from jax import lax
from jax.experimental import pallas as pl
from jax.experimental.pallas import tpu as pltpu
from jax.sharding import PartitionSpec as P

SUB, LANES = 8, 128
COLOR_UNIT, COLOR_SPAN = 2 ** 11, 2 ** 12
OPACITY_UNIT, OPACITY_BITS = 2 ** 18, 16
OPACITY_SPAN = 2 ** OPACITY_BITS


def pack_kernel(field_ref, out_ref, staged):
    depth, rows, cols = field_ref.shape
    tiles, padded_rows, _, chunks, _ = out_ref.shape
    tile_rows = padded_rows - 2
    block = depth * chunks
    for k in range(depth):
        for j in range(rows // SUB):
            for c in range(chunks):
                lines = field_ref[k, j * SUB:(j + 1) * SUB, c * LANES:(c + 1) * LANES]
                staged[pl.ds(j * SUB * block + k * chunks + c, SUB, stride=block), :] = lines
    for t in range(tiles):
        for i in range(padded_rows):
            r = (t * tile_rows + i - 1) % rows
            for k in range(depth):
                start = (r * depth + k) * chunks
                out_ref[t, i, k] = staged[start:start + chunks, :]


def packed(field, tiles):
    depth, rows, cols = field.shape
    chunks = cols // LANES
    vmem = pl.BlockSpec(memory_space=pltpu.VMEM)
    shape = (tiles, rows // tiles + 2, depth, chunks, LANES)
    return pl.pallas_call(
        pack_kernel,
        out_shape=jax.ShapeDtypeStruct(shape, field.dtype),
        in_specs=[vmem],
        out_specs=vmem,
        scratch_shapes=[pltpu.VMEM((rows * depth * chunks, LANES), field.dtype)],
        compiler_params=pltpu.CompilerParams(vmem_limit_bytes=16 << 20),
        name="pack_rows",
    )(field)


def shifted(x, axis, shift):
    return pltpu.roll(x, shift % x.shape[axis], axis)


def brick_positions(order_ref, brick_at):
    def place(b, carry):
        brick_at[order_ref[b]] = b
        return carry

    lax.fori_loop(0, order_ref.shape[0], place, 0)


def table_lookup(color_ref, opacity_ref, shape):
    bins = color_ref.shape[1] - 1
    halves = bins // LANES

    def parts(values, unit):
        scaled = values.astype(jnp.float32) * float(unit)
        return scaled[:, :bins], scaled[:, 1:] - scaled[:, :bins]

    low, slope = parts(color_ref[...], COLOR_UNIT)
    color_words = slope + low * (1.0 / COLOR_SPAN)
    low, slope = parts(opacity_ref[...], OPACITY_UNIT)
    opacity_words = slope.astype(jnp.int32) * OPACITY_SPAN + low.astype(jnp.int32)

    def spread(words):
        return [jnp.broadcast_to(words[:, h * LANES:(h + 1) * LANES], shape) for h in range(halves)]

    tables = [spread(color_words[c:c + 1]) for c in range(3)] + [spread(opacity_words)]

    def look_up(x):
        scaled = x * float(bins)
        index = jnp.minimum(scaled.astype(jnp.int32), bins - 1)
        fraction = scaled - index.astype(jnp.float32)
        low_bits = index & (LANES - 1)
        words = []
        for table in tables:
            word = jnp.take_along_axis(table[0], low_bits, axis=1, mode="promise_in_bounds")
            for h in range(1, halves):
                found = jnp.take_along_axis(table[h], low_bits, axis=1, mode="promise_in_bounds")
                word = jnp.where(index >= h * LANES, found, word)
            words.append(word)
        color = []
        small = fraction * (1.0 / COLOR_SPAN)
        for word in words[:3]:
            rise = jnp.floor(word)
            color.append((word - rise) + small * rise)
        rise = (words[3] >> OPACITY_BITS).astype(jnp.float32)
        start = (words[3] & (OPACITY_SPAN - 1)).astype(jnp.float32)
        return color, (start + fraction * rise) * (1.0 / OPACITY_UNIT)

    return look_up


def column_differences(shape):
    lane = lax.broadcasted_iota(jnp.int32, shape, 1)
    chunk = lax.broadcasted_iota(jnp.int32, shape, 0)
    at_first, at_last = lane == 0, lane == shape[1] - 1
    at_left = at_first & (chunk == 0)
    at_right = at_last & (chunk == shape[0] - 1)

    def difference(x):
        right = shifted(x, 1, -1)
        right = jnp.where(at_last, shifted(right, 0, -1), right)
        right = jnp.where(at_right, 0.0, right)
        left = shifted(x, 1, 1)
        left = jnp.where(at_first, shifted(left, 0, 1), left)
        left = jnp.where(at_left, 0.0, left)
        return right - left

    return difference


def depth_differences(field):
    last = len(field) - 1
    made = {}
    for k in range(last + 1):
        ends = (min(k + 1, last), max(k - 1, 0))
        if ends not in made:
            made[ends] = field[ends[0]] - field[ends[1]]
    return [made[(min(k + 1, last), max(k - 1, 0))] for k in range(last + 1)]


def shading_of(facing, squared_plus_one):
    return 0.25 + 0.75 * facing * facing / squared_plus_one


def main_kernel(edge_rows, order_ref, light_ref, color_ref, opacity_ref, tile_ref,
                part_ref, color_sum_ref, keep_ref, brick_at):
    bricks, padded_rows, depth, chunks, lanes = tile_ref.shape
    rows = padded_rows - 2
    inner_rows = [r for r in range(rows) if r not in edge_rows]
    shape = (chunks, lanes)
    brick_positions(order_ref, brick_at)
    look_up = table_lookup(color_ref, opacity_ref, shape)
    column_difference = column_differences(shape)
    light = [light_ref[i] for i in range(3)]

    def step(position, carry):
        b = brick_at[position]
        colors, keeps = list(carry[0]), list(carry[1])
        for r in range(rows):
            field = [tile_ref[b, r + 1, k] for k in range(depth)]
            for k, (x, dz) in enumerate(zip(field, depth_differences(field))):
                dx = column_difference(x)
                color, opacity = look_up(x)
                weight = keeps[r] * opacity
                facing = dz * light[0] + dx * light[2]
                squared = dz * dz + dx * dx + 1.0
                if r in edge_rows:
                    i = edge_rows.index(r)
                    for c in range(3):
                        part_ref[b, i, k, c] = weight * color[c]
                    part_ref[b, i, k, 3] = facing
                    part_ref[b, i, k, 4] = squared
                else:
                    i = inner_rows.index(r)
                    dy = tile_ref[b, r + 2, k] - tile_ref[b, r, k]
                    shaded = weight * shading_of(facing + dy * light[1], squared + dy * dy)
                    for c in range(3):
                        at = c * len(inner_rows) + i
                        colors[at] = colors[at] + shaded * color[c]
                keeps[r] = keeps[r] - weight
        return tuple(colors), tuple(keeps)

    zero, one = jnp.zeros(shape, jnp.float32), jnp.ones(shape, jnp.float32)
    colors, keeps = lax.fori_loop(0, bricks, step, ((zero,) * (3 * len(inner_rows)), (one,) * rows))
    for i, value in enumerate(colors):
        color_sum_ref[i] = value
    for r, value in enumerate(keeps):
        keep_ref[r] = value


def finish_kernel(edge_rows, ends_ref, light_ref, tile_ref, other_ref, part_ref, color_sum_ref, keep_ref,
                  out_ref, staged):
    bricks, padded_rows, depth, chunks, lanes = tile_ref.shape
    rows = padded_rows - 2
    inner_rows = [r for r in range(rows) if r not in edge_rows]
    shape = (chunks, lanes)
    light_rows = light_ref[1]
    is_first = jnp.full(shape, ends_ref[0], jnp.int32) == 1
    is_last = jnp.full(shape, ends_ref[1], jnp.int32) == 1

    def step(b, colors):
        colors = list(colors)
        for i, r in enumerate(edge_rows):
            for k in range(depth):
                above, below = tile_ref[b, r, k], tile_ref[b, r + 2, k]
                if r == 0:
                    above = jnp.where(is_first, other_ref[b, k], above)
                if r == rows - 1:
                    below = jnp.where(is_last, other_ref[b, k], below)
                dy = below - above
                shading = shading_of(part_ref[b, i, k, 3] + dy * light_rows, part_ref[b, i, k, 4] + dy * dy)
                for c in range(3):
                    at = c * len(edge_rows) + i
                    colors[at] = colors[at] + shading * part_ref[b, i, k, c]
        return tuple(colors)

    zero = jnp.zeros(shape, jnp.float32)
    edge_colors = lax.fori_loop(0, bricks, step, (zero,) * (3 * len(edge_rows)))
    for r in range(rows):
        for c in range(3):
            if r in edge_rows:
                value = edge_colors[c * len(edge_rows) + edge_rows.index(r)]
            else:
                value = color_sum_ref[c * len(inner_rows) + inner_rows.index(r)]
            at = (c * rows + r) * chunks
            staged[at:at + chunks, :] = value * (COLOR_SPAN / COLOR_UNIT)
        at = (3 * rows + r) * chunks
        staged[at:at + chunks, :] = 1.0 - keep_ref[r]
    for c in range(4):
        for q in range(chunks):
            source = pl.ds(c * rows * chunks + q, rows, stride=chunks) if rows > 1 else pl.ds(c * chunks + q, 1)
            out_ref[c, 0, :, q * LANES:(q + 1) * LANES] = staged[source, :]


def shards(scalar, bin_index, color_table, opacity_table, light_dir, view_order):
    depth, rows, cols = scalar.shape
    bricks, bands = lax.axis_size("gz"), lax.axis_size("gy")
    tile_rows = rows // bricks
    chunks = cols // LANES
    edge_rows = sorted({0, tile_rows - 1})
    inner_count = tile_rows - len(edge_rows)
    tiles = lax.all_to_all(packed(scalar, bricks), "gz", split_axis=0, concat_axis=0, tiled=True)

    here = lax.axis_index("gz")
    ends = jnp.stack([here == 0, here == bricks - 1]).astype(jnp.int32)
    last = bricks - 1
    pairs = [(g, g + 1) for g in range(bands - 1)]
    pairs += [(last * bands + g + 1, last * bands + g) for g in range(bands - 1)]
    wrapped = jnp.where(here == 0, tiles[:, 0], tiles[:, -1])
    other = lax.ppermute(wrapped, ("gz", "gy"), pairs)

    vmem = pl.BlockSpec(memory_space=pltpu.VMEM)
    smem = pl.BlockSpec(memory_space=pltpu.SMEM)
    params = pltpu.CompilerParams(vmem_limit_bytes=32 << 20)
    cells = bricks * depth * cols
    parts, color_sums, keeps = pl.pallas_call(
        functools.partial(main_kernel, edge_rows),
        out_shape=[
            jax.ShapeDtypeStruct((bricks, len(edge_rows), depth, 5, chunks, LANES), jnp.float32),
            jax.ShapeDtypeStruct((max(3 * inner_count, 1), chunks, LANES), jnp.float32),
            jax.ShapeDtypeStruct((tile_rows, chunks, LANES), jnp.float32),
        ],
        in_specs=[smem, smem, vmem, vmem, vmem],
        out_specs=[vmem, vmem, vmem],
        scratch_shapes=[pltpu.SMEM((bricks,), jnp.int32)],
        compiler_params=params,
        cost_estimate=pl.CostEstimate(
            flops=100 * cells * tile_rows, bytes_accessed=24 * cells * tile_rows, transcendentals=0),
        name="main_rows",
    )(view_order, light_dir, color_table, opacity_table[None, :], tiles)
    return pl.pallas_call(
        functools.partial(finish_kernel, edge_rows),
        out_shape=jax.ShapeDtypeStruct((4, 1, tile_rows, cols), jnp.float32),
        in_specs=[smem, smem, vmem, vmem, vmem, vmem, vmem],
        out_specs=vmem,
        scratch_shapes=[pltpu.VMEM((4 * tile_rows * chunks, LANES), jnp.float32)],
        compiler_params=params,
        cost_estimate=pl.CostEstimate(
            flops=10 * cells * tile_rows, bytes_accessed=24 * cells * tile_rows, transcendentals=0),
        name="edge_rows",
    )(ends, light_dir, tiles, other, parts, color_sums, keeps)


def solution(mesh):
    in_specs = (P("gz", "gy", None), P("gz", "gy", None), P(), P(), P(), P())
    out_specs = P(None, "gy", "gz", None)
    return jax.shard_map(shards, mesh=mesh, in_specs=in_specs, out_specs=out_specs, check_vma=False)
```

```python
import functools

import jax
import jax.numpy as jnp
from jax import lax
from jax.experimental import pallas as pl
from jax.experimental.pallas import tpu as pltpu
from jax.sharding import PartitionSpec as P

SUB, LANES = 8, 128
COLOR_UNIT, COLOR_SPAN = 2 ** 11, 2 ** 12
OPACITY_UNIT, OPACITY_BITS = 2 ** 18, 16
OPACITY_SPAN = 2 ** OPACITY_BITS


def pack_kernel(field_ref, out_ref, staged):
    depth, rows, cols = field_ref.shape
    tiles, padded_rows, _, chunks, _ = out_ref.shape
    tile_rows = padded_rows - 2
    block = depth * chunks
    for k in range(depth):
        for j in range(rows // SUB):
            lines = [field_ref[k, j * SUB:(j + 1) * SUB, c * LANES:(c + 1) * LANES] for c in range(chunks)]
            for c, value in enumerate(lines):
                staged[pl.ds(j * SUB * block + k * chunks + c, SUB, stride=block), :] = value
    for t in range(tiles):
        starts = [((t * tile_rows + i - 1) % rows) * block for i in range(padded_rows)]
        blocks = [staged[start:start + block, :] for start in starts]
        for i, value in enumerate(blocks):
            for k in range(depth):
                out_ref[t, i, k] = value[k * chunks:(k + 1) * chunks]


def packed(field, tiles):
    depth, rows, cols = field.shape
    chunks = cols // LANES
    vmem = pl.BlockSpec(memory_space=pltpu.VMEM)
    shape = (tiles, rows // tiles + 2, depth, chunks, LANES)
    return pl.pallas_call(
        pack_kernel,
        out_shape=jax.ShapeDtypeStruct(shape, field.dtype),
        in_specs=[vmem],
        out_specs=vmem,
        scratch_shapes=[pltpu.VMEM((rows * depth * chunks, LANES), field.dtype)],
        compiler_params=pltpu.CompilerParams(vmem_limit_bytes=16 << 20),
        name="pack_rows",
    )(field)


def shifted(x, axis, shift):
    return pltpu.roll(x, shift % x.shape[axis], axis)


def brick_positions(order_ref, brick_at):
    def place(b, carry):
        brick_at[order_ref[b]] = b
        return carry

    lax.fori_loop(0, order_ref.shape[0], place, 0)


def table_lookup(color_ref, opacity_ref, shape):
    bins = color_ref.shape[1] - 1
    halves = bins // LANES

    def parts(values, unit):
        scaled = values.astype(jnp.float32) * float(unit)
        return scaled[:, :bins], scaled[:, 1:] - scaled[:, :bins]

    low, slope = parts(color_ref[...], COLOR_UNIT)
    color_words = slope + low * (1.0 / COLOR_SPAN)
    low, slope = parts(opacity_ref[...], OPACITY_UNIT)
    opacity_words = slope.astype(jnp.int32) * OPACITY_SPAN + low.astype(jnp.int32)

    def spread(words):
        return [jnp.broadcast_to(words[:, h * LANES:(h + 1) * LANES], shape) for h in range(halves)]

    tables = [spread(color_words[c:c + 1]) for c in range(3)] + [spread(opacity_words)]

    def look_up(x):
        scaled = x * float(bins)
        index = jnp.minimum(scaled.astype(jnp.int32), bins - 1)
        fraction = scaled - index.astype(jnp.float32)
        low_bits = index & (LANES - 1)
        words = []
        for table in tables:
            word = jnp.take_along_axis(table[0], low_bits, axis=1, mode="promise_in_bounds")
            for h in range(1, halves):
                found = jnp.take_along_axis(table[h], low_bits, axis=1, mode="promise_in_bounds")
                word = jnp.where(index >= h * LANES, found, word)
            words.append(word)
        color = []
        small = fraction * (1.0 / COLOR_SPAN)
        for word in words[:3]:
            rise = jnp.floor(word)
            color.append((word - rise) + small * rise)
        rise = (words[3] >> OPACITY_BITS).astype(jnp.float32)
        start = (words[3] & (OPACITY_SPAN - 1)).astype(jnp.float32)
        return color, (start + fraction * rise) * (1.0 / OPACITY_UNIT)

    return look_up


def column_differences(shape):
    lane = lax.broadcasted_iota(jnp.int32, shape, 1)
    chunk = lax.broadcasted_iota(jnp.int32, shape, 0)
    at_first, at_last = lane == 0, lane == shape[1] - 1
    at_left = at_first & (chunk == 0)
    at_right = at_last & (chunk == shape[0] - 1)

    def difference(x):
        right = shifted(x, 1, -1)
        right = jnp.where(at_last, shifted(right, 0, -1), right)
        right = jnp.where(at_right, 0.0, right)
        left = shifted(x, 1, 1)
        left = jnp.where(at_first, shifted(left, 0, 1), left)
        left = jnp.where(at_left, 0.0, left)
        return right - left

    return difference


def depth_differences(field):
    last = len(field) - 1
    made = {}
    for k in range(last + 1):
        ends = (min(k + 1, last), max(k - 1, 0))
        if ends not in made:
            made[ends] = field[ends[0]] - field[ends[1]]
    return [made[(min(k + 1, last), max(k - 1, 0))] for k in range(last + 1)]


def shading_of(facing, squared_plus_one):
    near = pltpu.reciprocal(squared_plus_one, approx=True)
    inverse = near * (2.0 - squared_plus_one * near)
    return 0.25 + (0.75 * facing) * (facing * inverse)


def main_kernel(edge_rows, order_ref, light_ref, color_ref, opacity_ref, tile_ref,
                part_ref, color_sum_ref, keep_ref, brick_at):
    bricks, padded_rows, depth, chunks, lanes = tile_ref.shape
    rows = padded_rows - 2
    inner_rows = [r for r in range(rows) if r not in edge_rows]
    shape = (chunks, lanes)
    brick_positions(order_ref, brick_at)
    look_up = table_lookup(color_ref, opacity_ref, shape)
    column_difference = column_differences(shape)
    light = [light_ref[i] for i in range(3)]
    together = 2 if bricks % 2 == 0 else 1

    def step(trip, carry):
        colors, keeps = list(carry[0]), list(carry[1])
        at = [brick_at[trip * together + u] for u in range(together)]
        fields = [[[tile_ref[b, r, k] for k in range(depth)] for r in range(padded_rows)] for b in at]
        kept = []
        for b, field in zip(at, fields):
            for r in range(rows):
                for k, dz in enumerate(depth_differences(field[r + 1])):
                    x = field[r + 1][k]
                    dx = column_difference(x)
                    color, opacity = look_up(x)
                    weight = keeps[r] * opacity
                    facing = dz * light[0] + dx * light[2]
                    squared = dz * dz + dx * dx + 1.0
                    if r in edge_rows:
                        values = [weight * color[c] for c in range(3)] + [facing, squared]
                        kept.append((b, edge_rows.index(r), k, values))
                    else:
                        i = inner_rows.index(r)
                        dy = field[r + 2][k] - field[r][k]
                        shaded = weight * shading_of(facing + dy * light[1], squared + dy * dy)
                        for c in range(3):
                            slot = c * len(inner_rows) + i
                            colors[slot] = colors[slot] + shaded * color[c]
                    keeps[r] = keeps[r] - weight
        for b, i, k, values in kept:
            for v, value in enumerate(values):
                part_ref[b, i, k, v] = value
        return tuple(colors), tuple(keeps)

    zero, one = jnp.zeros(shape, jnp.float32), jnp.ones(shape, jnp.float32)
    colors, keeps = lax.fori_loop(
        0, bricks // together, step, ((zero,) * (3 * len(inner_rows)), (one,) * rows))
    for i, value in enumerate(colors):
        color_sum_ref[i] = value
    for r, value in enumerate(keeps):
        keep_ref[r] = value


def finish_kernel(edge_rows, ends_ref, light_ref, tile_ref, other_ref, part_ref, color_sum_ref, keep_ref,
                  out_ref, staged):
    bricks, padded_rows, depth, chunks, lanes = tile_ref.shape
    rows = padded_rows - 2
    inner_rows = [r for r in range(rows) if r not in edge_rows]
    shape = (chunks, lanes)
    light_rows = light_ref[1]
    is_first = jnp.full(shape, ends_ref[0], jnp.int32) == 1
    is_last = jnp.full(shape, ends_ref[1], jnp.int32) == 1

    together = 4 if bricks % 4 == 0 else 1

    def step(trip, colors):
        colors = list(colors)
        for u in range(together):
            b = trip * together + u
            for i, r in enumerate(edge_rows):
                for k in range(depth):
                    above, below = tile_ref[b, r, k], tile_ref[b, r + 2, k]
                    if r == 0:
                        above = jnp.where(is_first, other_ref[b, k], above)
                    if r == rows - 1:
                        below = jnp.where(is_last, other_ref[b, k], below)
                    dy = below - above
                    facing = part_ref[b, i, k, 3] + dy * light_rows
                    shading = shading_of(facing, part_ref[b, i, k, 4] + dy * dy)
                    for c in range(3):
                        slot = c * len(edge_rows) + i
                        colors[slot] = colors[slot] + shading * part_ref[b, i, k, c]
        return tuple(colors)

    zero = jnp.zeros(shape, jnp.float32)
    edge_colors = lax.fori_loop(0, bricks // together, step, (zero,) * (3 * len(edge_rows)))
    for r in range(rows):
        for c in range(3):
            if r in edge_rows:
                value = edge_colors[c * len(edge_rows) + edge_rows.index(r)]
            else:
                value = color_sum_ref[c * len(inner_rows) + inner_rows.index(r)]
            at = (c * rows + r) * chunks
            staged[at:at + chunks, :] = value * (COLOR_SPAN / COLOR_UNIT)
        at = (3 * rows + r) * chunks
        staged[at:at + chunks, :] = 1.0 - keep_ref[r]
    for c in range(4):
        for q in range(chunks):
            source = pl.ds(c * rows * chunks + q, rows, stride=chunks) if rows > 1 else pl.ds(c * chunks + q, 1)
            out_ref[c, 0, :, q * LANES:(q + 1) * LANES] = staged[source, :]


def shards(scalar, bin_index, color_table, opacity_table, light_dir, view_order):
    depth, rows, cols = scalar.shape
    bricks, bands = lax.axis_size("gz"), lax.axis_size("gy")
    tile_rows = rows // bricks
    chunks = cols // LANES
    edge_rows = sorted({0, tile_rows - 1})
    inner_count = tile_rows - len(edge_rows)
    tiles = lax.all_to_all(packed(scalar, bricks), "gz", split_axis=0, concat_axis=0, tiled=True)

    here = lax.axis_index("gz")
    ends = jnp.stack([here == 0, here == bricks - 1]).astype(jnp.int32)
    last = bricks - 1
    pairs = [(g, g + 1) for g in range(bands - 1)]
    pairs += [(last * bands + g + 1, last * bands + g) for g in range(bands - 1)]
    wrapped = jnp.where(here == 0, tiles[:, 0], tiles[:, -1])
    other = lax.ppermute(wrapped, ("gz", "gy"), pairs)

    vmem = pl.BlockSpec(memory_space=pltpu.VMEM)
    smem = pl.BlockSpec(memory_space=pltpu.SMEM)
    params = pltpu.CompilerParams(vmem_limit_bytes=32 << 20)
    cells = bricks * depth * cols
    parts, color_sums, keeps = pl.pallas_call(
        functools.partial(main_kernel, edge_rows),
        out_shape=[
            jax.ShapeDtypeStruct((bricks, len(edge_rows), depth, 5, chunks, LANES), jnp.float32),
            jax.ShapeDtypeStruct((max(3 * inner_count, 1), chunks, LANES), jnp.float32),
            jax.ShapeDtypeStruct((tile_rows, chunks, LANES), jnp.float32),
        ],
        in_specs=[smem, smem, vmem, vmem, vmem],
        out_specs=[vmem, vmem, vmem],
        scratch_shapes=[pltpu.SMEM((bricks,), jnp.int32)],
        compiler_params=params,
        cost_estimate=pl.CostEstimate(
            flops=100 * cells * tile_rows, bytes_accessed=24 * cells * tile_rows, transcendentals=0),
        name="main_rows",
    )(view_order, light_dir, color_table, opacity_table[None, :], tiles)
    return pl.pallas_call(
        functools.partial(finish_kernel, edge_rows),
        out_shape=jax.ShapeDtypeStruct((4, 1, tile_rows, cols), jnp.float32),
        in_specs=[smem, smem, vmem, vmem, vmem, vmem, vmem],
        out_specs=vmem,
        scratch_shapes=[pltpu.VMEM((4 * tile_rows * chunks, LANES), jnp.float32)],
        compiler_params=params,
        cost_estimate=pl.CostEstimate(
            flops=10 * cells * tile_rows, bytes_accessed=24 * cells * tile_rows, transcendentals=0),
        name="edge_rows",
    )(ends, light_dir, tiles, other, parts, color_sums, keeps)


def solution(mesh):
    in_specs = (P("gz", "gy", None), P("gz", "gy", None), P(), P(), P(), P())
    out_specs = P(None, "gy", "gz", None)
    return jax.shard_map(shards, mesh=mesh, in_specs=in_specs, out_specs=out_specs, check_vma=False)
```

```python
import functools

import jax
import jax.numpy as jnp
from jax import lax
from jax.experimental import pallas as pl
from jax.experimental.pallas import tpu as pltpu
from jax.sharding import PartitionSpec as P

SUB, LANES = 8, 128
COLOR_UNIT, COLOR_SPAN = 2 ** 11, 2 ** 12
OPACITY_UNIT, OPACITY_BITS = 2 ** 18, 16
OPACITY_SPAN = 2 ** OPACITY_BITS


def pack_kernel(field_ref, out_ref):
    depth, rows, cols = field_ref.shape
    chunks = cols // LANES
    block = depth * chunks
    tiles = out_ref.shape[0] // block - rows
    tiles //= 2
    tile_rows = rows // tiles
    padded_rows = tile_rows + 2
    piece = min(SUB, tile_rows)
    for k in range(depth):
        for c in range(chunks):
            lines = [field_ref[k, r:r + piece, c * LANES:(c + 1) * LANES] for r in range(0, rows, piece)]
            for i, value in enumerate(lines):
                t, r = divmod(i * piece, tile_rows)
                at = (t * padded_rows + r + 1) * block + k * chunks + c
                out_ref[pl.ds(at, piece, stride=block), :] = value
    for t in range(tiles):
        before, after = (t - 1) % tiles, (t + 1) % tiles
        copies = [((before * padded_rows + tile_rows) * block, t * padded_rows * block),
                  ((after * padded_rows + 1) * block, (t * padded_rows + tile_rows + 1) * block)]
        values = [out_ref[source:source + block, :] for source, _ in copies]
        for value, (_, target) in zip(values, copies):
            out_ref[target:target + block, :] = value


def packed(field, tiles):
    depth, rows, cols = field.shape
    chunks = cols // LANES
    padded_rows = rows // tiles + 2
    vmem = pl.BlockSpec(memory_space=pltpu.VMEM)
    flat = pl.pallas_call(
        pack_kernel,
        out_shape=jax.ShapeDtypeStruct((tiles * padded_rows * depth * chunks, LANES), field.dtype),
        in_specs=[vmem],
        out_specs=vmem,
        compiler_params=pltpu.CompilerParams(vmem_limit_bytes=16 << 20),
        name="pack_rows",
    )(field)
    return flat.reshape(tiles, padded_rows, depth, chunks, LANES)


def shifted(x, axis, shift):
    return pltpu.roll(x, shift % x.shape[axis], axis)


def prepare_kernel(bands_end_ref, light_ref, color_ref, opacity_ref,
                   color_word_ref, opacity_word_ref, light_rows_ref, end_ref):
    bins = color_ref.shape[1] - 1
    _, halves, chunks, lanes = color_word_ref.shape
    shape = (chunks, lanes)

    def parts(values, unit):
        scaled = values.astype(jnp.float32) * float(unit)
        return scaled[:, :bins], scaled[:, 1:] - scaled[:, :bins]

    low, slope = parts(color_ref[...], COLOR_UNIT)
    color_words = slope + low * (1.0 / COLOR_SPAN)
    low, slope = parts(opacity_ref[...], OPACITY_UNIT)
    opacity_words = slope.astype(jnp.int32) * OPACITY_SPAN + low.astype(jnp.int32)
    for h in range(halves):
        span = slice(h * lanes, (h + 1) * lanes)
        for c in range(3):
            color_word_ref[c, h] = jnp.broadcast_to(color_words[c:c + 1, span], shape)
        opacity_word_ref[h] = jnp.broadcast_to(opacity_words[:, span], shape)
    for i in range(3):
        light_rows_ref[i] = jnp.full(shape, light_ref[i], jnp.float32)
    for i in range(2):
        end_ref[i] = jnp.full(shape, bands_end_ref[i], jnp.int32)


def table_lookup(color_word_ref, opacity_word_ref):
    _, halves, _, lanes = color_word_ref.shape
    bins = halves * lanes

    def look_up(x):
        scaled = x * float(bins)
        index = jnp.minimum(scaled.astype(jnp.int32), bins - 1)
        fraction = scaled - index.astype(jnp.float32)
        low_bits = index & (lanes - 1)

        def gathered(table):
            found = [jnp.take_along_axis(t, low_bits, axis=1, mode="promise_in_bounds") for t in table]
            word = found[0]
            for h in range(1, halves):
                word = jnp.where(index >= h * lanes, found[h], word)
            return word

        color = []
        small = fraction * (1.0 / COLOR_SPAN)
        for c in range(3):
            word = gathered([color_word_ref[c, h] for h in range(halves)])
            rise = jnp.floor(word)
            color.append((word - rise) + small * rise)
        word = gathered([opacity_word_ref[h] for h in range(halves)])
        rise = (word >> OPACITY_BITS).astype(jnp.float32)
        start = (word & (OPACITY_SPAN - 1)).astype(jnp.float32)
        return color, (start + fraction * rise) * (1.0 / OPACITY_UNIT)

    return look_up


def column_differences(shape):
    lane = lax.broadcasted_iota(jnp.int32, shape, 1)
    chunk = lax.broadcasted_iota(jnp.int32, shape, 0)
    at_first, at_last = lane == 0, lane == shape[1] - 1
    at_left = at_first & (chunk == 0)
    at_right = at_last & (chunk == shape[0] - 1)

    def difference(x):
        right = shifted(x, 1, -1)
        right = jnp.where(at_last, shifted(right, 0, -1), right)
        right = jnp.where(at_right, 0.0, right)
        left = shifted(x, 1, 1)
        left = jnp.where(at_first, shifted(left, 0, 1), left)
        left = jnp.where(at_left, 0.0, left)
        return right - left

    return difference


def depth_differences(field):
    last = len(field) - 1
    made = {}
    for k in range(last + 1):
        ends = (min(k + 1, last), max(k - 1, 0))
        if ends not in made:
            made[ends] = field[ends[0]] - field[ends[1]]
    return [made[(min(k + 1, last), max(k - 1, 0))] for k in range(last + 1)]


def shading_of(facing, squared_plus_one):
    near = pltpu.reciprocal(squared_plus_one, approx=True)
    inverse = near * (2.0 - squared_plus_one * near)
    return 0.25 + (0.75 * facing) * (facing * inverse)


def main_kernel(edge_rows, brick_at, light_ref, color_word_ref, opacity_word_ref, tile_ref,
                part_ref, color_sum_ref, keep_ref):
    bricks, padded_rows, depth, chunks, lanes = tile_ref.shape
    rows = padded_rows - 2
    inner_rows = [r for r in range(rows) if r not in edge_rows]
    shape = (chunks, lanes)
    look_up = table_lookup(color_word_ref, opacity_word_ref)
    column_difference = column_differences(shape)
    light = [light_ref[i] for i in range(3)]
    together = 2 if bricks % 2 == 0 else 1

    def step(trip, carry):
        colors, keeps = list(carry[0]), list(carry[1])
        at = [brick_at[trip * together + u] for u in range(together)]
        fields = [[[tile_ref[b, r, k] for k in range(depth)] for r in range(padded_rows)] for b in at]
        kept = []
        for b, field in zip(at, fields):
            for r in range(rows):
                for k, dz in enumerate(depth_differences(field[r + 1])):
                    x = field[r + 1][k]
                    dx = column_difference(x)
                    color, opacity = look_up(x)
                    weight = keeps[r] * opacity
                    facing = dz * light[0] + dx * light[2]
                    squared = dz * dz + dx * dx + 1.0
                    if r in edge_rows:
                        values = [weight * color[c] for c in range(3)] + [facing, squared]
                        kept.append((b, edge_rows.index(r), k, values))
                    else:
                        i = inner_rows.index(r)
                        dy = field[r + 2][k] - field[r][k]
                        shaded = weight * shading_of(facing + dy * light[1], squared + dy * dy)
                        for c in range(3):
                            slot = c * len(inner_rows) + i
                            colors[slot] = colors[slot] + shaded * color[c]
                    keeps[r] = keeps[r] - weight
        for b, i, k, values in kept:
            for v, value in enumerate(values):
                part_ref[b, i, k, v] = value
        return tuple(colors), tuple(keeps)

    zero, one = jnp.zeros(shape, jnp.float32), jnp.ones(shape, jnp.float32)
    colors, keeps = lax.fori_loop(
        0, bricks // together, step, ((zero,) * (3 * len(inner_rows)), (one,) * rows))
    for i, value in enumerate(colors):
        color_sum_ref[i] = value
    for r, value in enumerate(keeps):
        keep_ref[r] = value


def finish_kernel(edge_rows, end_ref, light_ref, tile_ref, other_ref, part_ref, color_sum_ref, keep_ref,
                  out_ref, staged):
    bricks, padded_rows, depth, chunks, lanes = tile_ref.shape
    rows = padded_rows - 2
    inner_rows = [r for r in range(rows) if r not in edge_rows]
    shape = (chunks, lanes)
    light_rows = light_ref[1]
    is_first, is_last = end_ref[0] == 1, end_ref[1] == 1

    together = 4 if bricks % 4 == 0 else 1

    def step(trip, colors):
        colors = list(colors)
        for u in range(together):
            b = trip * together + u
            for i, r in enumerate(edge_rows):
                for k in range(depth):
                    above, below = tile_ref[b, r, k], tile_ref[b, r + 2, k]
                    if r == 0:
                        above = jnp.where(is_first, other_ref[b, k], above)
                    if r == rows - 1:
                        below = jnp.where(is_last, other_ref[b, k], below)
                    dy = below - above
                    facing = part_ref[b, i, k, 3] + dy * light_rows
                    shading = shading_of(facing, part_ref[b, i, k, 4] + dy * dy)
                    for c in range(3):
                        slot = c * len(edge_rows) + i
                        colors[slot] = colors[slot] + shading * part_ref[b, i, k, c]
        return tuple(colors)

    zero = jnp.zeros(shape, jnp.float32)
    edge_colors = lax.fori_loop(0, bricks // together, step, (zero,) * (3 * len(edge_rows)))
    for r in range(rows):
        for c in range(3):
            if r in edge_rows:
                value = edge_colors[c * len(edge_rows) + edge_rows.index(r)]
            else:
                value = color_sum_ref[c * len(inner_rows) + inner_rows.index(r)]
            at = (c * rows + r) * chunks
            staged[at:at + chunks, :] = value * (COLOR_SPAN / COLOR_UNIT)
        at = (3 * rows + r) * chunks
        staged[at:at + chunks, :] = 1.0 - keep_ref[r]
    for c in range(4):
        for q in range(chunks):
            source = pl.ds(c * rows * chunks + q, rows, stride=chunks) if rows > 1 else pl.ds(c * chunks + q, 1)
            out_ref[c, 0, :, q * LANES:(q + 1) * LANES] = staged[source, :]


def shards(scalar, bin_index, color_table, opacity_table, light_dir, view_order):
    depth, rows, cols = scalar.shape
    bricks, bands = lax.axis_size("gz"), lax.axis_size("gy")
    tile_rows = rows // bricks
    chunks = cols // LANES
    edge_rows = sorted({0, tile_rows - 1})
    inner_count = tile_rows - len(edge_rows)
    tiles = lax.all_to_all(packed(scalar, bricks), "gz", split_axis=0, concat_axis=0, tiled=True)

    here = lax.axis_index("gz")
    ends = jnp.stack([here == 0, here == bricks - 1]).astype(jnp.int32)
    last = bricks - 1
    pairs = [(g, g + 1) for g in range(bands - 1)]
    pairs += [(last * bands + g + 1, last * bands + g) for g in range(bands - 1)]
    wrapped = jnp.where(here == 0, tiles[:, 0], tiles[:, -1])
    other = lax.ppermute(wrapped, ("gz", "gy"), pairs)

    vmem = pl.BlockSpec(memory_space=pltpu.VMEM)
    smem = pl.BlockSpec(memory_space=pltpu.SMEM)
    params = pltpu.CompilerParams(vmem_limit_bytes=32 << 20)
    cells = bricks * depth * cols
    lines = (chunks, LANES)
    halves = (color_table.shape[1] - 1) // LANES
    color_words, opacity_words, light_rows, end_rows = pl.pallas_call(
        prepare_kernel,
        out_shape=[
            jax.ShapeDtypeStruct((3, halves) + lines, jnp.float32),
            jax.ShapeDtypeStruct((halves,) + lines, jnp.int32),
            jax.ShapeDtypeStruct((3,) + lines, jnp.float32),
            jax.ShapeDtypeStruct((2,) + lines, jnp.int32),
        ],
        in_specs=[smem, smem, vmem, vmem],
        out_specs=[vmem] * 4,
        compiler_params=params,
        name="prepare_tables",
    )(ends, light_dir, color_table, opacity_table[None, :])
    positions = jnp.arange(bricks, dtype=jnp.int32)
    at_position = view_order[None, :] == positions[:, None]
    brick_at = jnp.sum(jnp.where(at_position, positions[None, :], 0), axis=1)
    parts, color_sums, keeps = pl.pallas_call(
        functools.partial(main_kernel, edge_rows),
        out_shape=[
            jax.ShapeDtypeStruct((bricks, len(edge_rows), depth, 5, chunks, LANES), jnp.float32),
            jax.ShapeDtypeStruct((max(3 * inner_count, 1), chunks, LANES), jnp.float32),
            jax.ShapeDtypeStruct((tile_rows, chunks, LANES), jnp.float32),
        ],
        in_specs=[smem] + [vmem] * 4,
        out_specs=[vmem, vmem, vmem],
        compiler_params=params,
        cost_estimate=pl.CostEstimate(
            flops=100 * cells * tile_rows, bytes_accessed=24 * cells * tile_rows, transcendentals=0),
        name="main_rows",
    )(brick_at, light_rows, color_words, opacity_words, tiles)
    return pl.pallas_call(
        functools.partial(finish_kernel, edge_rows),
        out_shape=jax.ShapeDtypeStruct((4, 1, tile_rows, cols), jnp.float32),
        in_specs=[vmem] * 7,
        out_specs=vmem,
        scratch_shapes=[pltpu.VMEM((4 * tile_rows * chunks, LANES), jnp.float32)],
        compiler_params=params,
        cost_estimate=pl.CostEstimate(
            flops=10 * cells * tile_rows, bytes_accessed=24 * cells * tile_rows, transcendentals=0),
        name="edge_rows",
    )(end_rows, light_rows, tiles, other, parts, color_sums, keeps)


def solution(mesh):
    in_specs = (P("gz", "gy", None), P("gz", "gy", None), P(), P(), P(), P())
    out_specs = P(None, "gy", "gz", None)
    return jax.shard_map(shards, mesh=mesh, in_specs=in_specs, out_specs=out_specs, check_vma=False)
```

```python
import functools

import jax
import jax.numpy as jnp
from jax import lax
from jax.experimental import pallas as pl
from jax.experimental.pallas import tpu as pltpu
from jax.sharding import PartitionSpec as P

SUB, LANES = 8, 128
COLOR_UNIT, COLOR_SPAN = 2 ** 11, 2 ** 12
OPACITY_UNIT, OPACITY_BITS = 2 ** 18, 16
OPACITY_SPAN = 2 ** OPACITY_BITS


def pack_kernel(field_ref, out_ref, staged):
    depth, rows, cols = field_ref.shape
    tiles, padded_rows, _, chunks, _ = out_ref.shape
    tile_rows = padded_rows - 2
    block = depth * chunks

    def spread(j, carry):
        start = pl.multiple_of(j * SUB, SUB)
        for k in range(depth):
            lines = [field_ref[k, pl.ds(start, SUB), c * LANES:(c + 1) * LANES] for c in range(chunks)]
            for c, value in enumerate(lines):
                staged[pl.ds(start * block + k * chunks + c, SUB, stride=block), :] = value
        return carry

    def place(t, carry):
        values = []
        for i in range(padded_rows):
            start = lax.rem(t * tile_rows + i - 1 + rows, rows) * block
            values.append(staged[pl.ds(pl.multiple_of(start, block), block), :])
        for i, value in enumerate(values):
            for k in range(depth):
                out_ref[t, i, k] = value[k * chunks:(k + 1) * chunks]
        return carry

    lax.fori_loop(0, rows // SUB, spread, 0)
    lax.fori_loop(0, tiles, place, 0)


def packed(field, tiles):
    depth, rows, cols = field.shape
    chunks = cols // LANES
    vmem = pl.BlockSpec(memory_space=pltpu.VMEM)
    shape = (tiles, rows // tiles + 2, depth, chunks, LANES)
    return pl.pallas_call(
        pack_kernel,
        out_shape=jax.ShapeDtypeStruct(shape, field.dtype),
        in_specs=[vmem],
        out_specs=vmem,
        scratch_shapes=[pltpu.VMEM((rows * depth * chunks, LANES), field.dtype)],
        compiler_params=pltpu.CompilerParams(vmem_limit_bytes=16 << 20),
        name="pack_rows",
    )(field)


def shifted(x, axis, shift):
    return pltpu.roll(x, shift % x.shape[axis], axis)


def prepare_kernel(bands_end_ref, order_ref, light_ref, color_ref, opacity_ref,
                   brick_at_ref, color_word_ref, opacity_word_ref, light_rows_ref, end_ref):
    bins = color_ref.shape[1] - 1
    _, halves, chunks, lanes = color_word_ref.shape
    shape = (chunks, lanes)

    def parts(values, unit):
        scaled = values.astype(jnp.float32) * float(unit)
        return scaled[:, :bins], scaled[:, 1:] - scaled[:, :bins]

    low, slope = parts(color_ref[...], COLOR_UNIT)
    color_words = slope + low * (1.0 / COLOR_SPAN)
    low, slope = parts(opacity_ref[...], OPACITY_UNIT)
    opacity_words = slope.astype(jnp.int32) * OPACITY_SPAN + low.astype(jnp.int32)
    for h in range(halves):
        span = slice(h * lanes, (h + 1) * lanes)
        for c in range(3):
            color_word_ref[c, h] = jnp.broadcast_to(color_words[c:c + 1, span], shape)
        opacity_word_ref[h] = jnp.broadcast_to(opacity_words[:, span], shape)
    for i in range(3):
        light_rows_ref[i] = jnp.full(shape, light_ref[i], jnp.float32)
    for i in range(2):
        end_ref[i] = jnp.full(shape, bands_end_ref[i], jnp.int32)
    for b in range(order_ref.shape[0]):
        brick_at_ref[order_ref[b]] = b


def table_lookup(color_word_ref, opacity_word_ref):
    _, halves, _, lanes = color_word_ref.shape
    bins = halves * lanes

    def look_up(x):
        scaled = x * float(bins)
        index = jnp.minimum(scaled.astype(jnp.int32), bins - 1)
        fraction = scaled - index.astype(jnp.float32)
        low_bits = index & (lanes - 1)

        def gathered(table):
            found = [jnp.take_along_axis(t, low_bits, axis=1, mode="promise_in_bounds") for t in table]
            word = found[0]
            for h in range(1, halves):
                word = jnp.where(index >= h * lanes, found[h], word)
            return word

        color = []
        small = fraction * (1.0 / COLOR_SPAN)
        for c in range(3):
            word = gathered([color_word_ref[c, h] for h in range(halves)])
            rise = jnp.floor(word)
            color.append((word - rise) + small * rise)
        word = gathered([opacity_word_ref[h] for h in range(halves)])
        rise = (word >> OPACITY_BITS).astype(jnp.float32)
        start = (word & (OPACITY_SPAN - 1)).astype(jnp.float32)
        return color, (start + fraction * rise) * (1.0 / OPACITY_UNIT)

    return look_up


def column_differences(shape):
    lane = lax.broadcasted_iota(jnp.int32, shape, 1)
    chunk = lax.broadcasted_iota(jnp.int32, shape, 0)
    at_first, at_last = lane == 0, lane == shape[1] - 1
    at_left = at_first & (chunk == 0)
    at_right = at_last & (chunk == shape[0] - 1)

    def difference(x):
        right = shifted(x, 1, -1)
        right = jnp.where(at_last, shifted(right, 0, -1), right)
        right = jnp.where(at_right, 0.0, right)
        left = shifted(x, 1, 1)
        left = jnp.where(at_first, shifted(left, 0, 1), left)
        left = jnp.where(at_left, 0.0, left)
        return right - left

    return difference


def depth_differences(field):
    last = len(field) - 1
    made = {}
    for k in range(last + 1):
        ends = (min(k + 1, last), max(k - 1, 0))
        if ends not in made:
            made[ends] = field[ends[0]] - field[ends[1]]
    return [made[(min(k + 1, last), max(k - 1, 0))] for k in range(last + 1)]


def shading_of(facing, squared_plus_one):
    near = pltpu.reciprocal(squared_plus_one, approx=True)
    inverse = near * (2.0 - squared_plus_one * near)
    return 0.25 + (0.75 * facing) * (facing * inverse)


def main_kernel(edge_rows, brick_at, light_ref, color_word_ref, opacity_word_ref, tile_ref,
                part_ref, color_sum_ref, keep_ref):
    bricks, padded_rows, depth, chunks, lanes = tile_ref.shape
    rows = padded_rows - 2
    inner_rows = [r for r in range(rows) if r not in edge_rows]
    shape = (chunks, lanes)
    look_up = table_lookup(color_word_ref, opacity_word_ref)
    column_difference = column_differences(shape)
    light = [light_ref[i] for i in range(3)]
    together = 1

    def step(trip, carry):
        colors, keeps = list(carry[0]), list(carry[1])
        at = [brick_at[trip * together + u] for u in range(together)]
        fields = [[[tile_ref[b, r, k] for k in range(depth)] for r in range(padded_rows)] for b in at]
        kept = []
        for b, field in zip(at, fields):
            for r in range(rows):
                for k, dz in enumerate(depth_differences(field[r + 1])):
                    x = field[r + 1][k]
                    dx = column_difference(x)
                    color, opacity = look_up(x)
                    weight = keeps[r] * opacity
                    facing = dz * light[0] + dx * light[2]
                    squared = dz * dz + dx * dx + 1.0
                    if r in edge_rows:
                        values = [weight * color[c] for c in range(3)] + [facing, squared]
                        kept.append((b, edge_rows.index(r), k, values))
                    else:
                        i = inner_rows.index(r)
                        dy = field[r + 2][k] - field[r][k]
                        shaded = weight * shading_of(facing + dy * light[1], squared + dy * dy)
                        for c in range(3):
                            slot = c * len(inner_rows) + i
                            colors[slot] = colors[slot] + shaded * color[c]
                    keeps[r] = keeps[r] - weight
        for b, i, k, values in kept:
            for v, value in enumerate(values):
                part_ref[b, i, k, v] = value
        return tuple(colors), tuple(keeps)

    zero, one = jnp.zeros(shape, jnp.float32), jnp.ones(shape, jnp.float32)
    colors, keeps = lax.fori_loop(
        0, bricks // together, step, ((zero,) * (3 * len(inner_rows)), (one,) * rows))
    for i, value in enumerate(colors):
        color_sum_ref[i] = value
    for r, value in enumerate(keeps):
        keep_ref[r] = value


def finish_kernel(edge_rows, end_ref, light_ref, tile_ref, other_ref, part_ref, color_sum_ref, keep_ref,
                  out_ref, staged):
    bricks, padded_rows, depth, chunks, lanes = tile_ref.shape
    rows = padded_rows - 2
    inner_rows = [r for r in range(rows) if r not in edge_rows]
    shape = (chunks, lanes)
    light_rows = light_ref[1]
    is_first, is_last = end_ref[0] == 1, end_ref[1] == 1

    together = 4 if bricks % 4 == 0 else 1

    def step(trip, colors):
        colors = list(colors)
        for u in range(together):
            b = trip * together + u
            for i, r in enumerate(edge_rows):
                for k in range(depth):
                    above, below = tile_ref[b, r, k], tile_ref[b, r + 2, k]
                    if r == 0:
                        above = jnp.where(is_first, other_ref[b, k], above)
                    if r == rows - 1:
                        below = jnp.where(is_last, other_ref[b, k], below)
                    dy = below - above
                    facing = part_ref[b, i, k, 3] + dy * light_rows
                    shading = shading_of(facing, part_ref[b, i, k, 4] + dy * dy)
                    for c in range(3):
                        slot = c * len(edge_rows) + i
                        colors[slot] = colors[slot] + shading * part_ref[b, i, k, c]
        return tuple(colors)

    zero = jnp.zeros(shape, jnp.float32)
    edge_colors = lax.fori_loop(0, bricks // together, step, (zero,) * (3 * len(edge_rows)))
    for r in range(rows):
        for c in range(3):
            if r in edge_rows:
                value = edge_colors[c * len(edge_rows) + edge_rows.index(r)]
            else:
                value = color_sum_ref[c * len(inner_rows) + inner_rows.index(r)]
            at = (c * rows + r) * chunks
            staged[at:at + chunks, :] = value * (COLOR_SPAN / COLOR_UNIT)
        at = (3 * rows + r) * chunks
        staged[at:at + chunks, :] = 1.0 - keep_ref[r]
    for c in range(4):
        for q in range(chunks):
            source = pl.ds(c * rows * chunks + q, rows, stride=chunks) if rows > 1 else pl.ds(c * chunks + q, 1)
            out_ref[c, 0, :, q * LANES:(q + 1) * LANES] = staged[source, :]


def shards(scalar, bin_index, color_table, opacity_table, light_dir, view_order):
    depth, rows, cols = scalar.shape
    bricks, bands = lax.axis_size("gz"), lax.axis_size("gy")
    tile_rows = rows // bricks
    chunks = cols // LANES
    edge_rows = sorted({0, tile_rows - 1})
    inner_count = tile_rows - len(edge_rows)
    tiles = lax.all_to_all(packed(scalar, bricks), "gz", split_axis=0, concat_axis=0, tiled=True)

    here = lax.axis_index("gz")
    ends = jnp.stack([here == 0, here == bricks - 1]).astype(jnp.int32)
    last = bricks - 1
    pairs = [(g, g + 1) for g in range(bands - 1)]
    pairs += [(last * bands + g + 1, last * bands + g) for g in range(bands - 1)]

    vmem = pl.BlockSpec(memory_space=pltpu.VMEM)
    smem = pl.BlockSpec(memory_space=pltpu.SMEM)
    params = pltpu.CompilerParams(vmem_limit_bytes=32 << 20)
    cells = bricks * depth * cols
    lines = (chunks, LANES)
    halves = (color_table.shape[1] - 1) // LANES
    brick_at, color_words, opacity_words, light_rows, end_rows = pl.pallas_call(
        prepare_kernel,
        out_shape=[
            jax.ShapeDtypeStruct((bricks,), jnp.int32),
            jax.ShapeDtypeStruct((3, halves) + lines, jnp.float32),
            jax.ShapeDtypeStruct((halves,) + lines, jnp.int32),
            jax.ShapeDtypeStruct((3,) + lines, jnp.float32),
            jax.ShapeDtypeStruct((2,) + lines, jnp.int32),
        ],
        in_specs=[smem, smem, smem, vmem, vmem],
        out_specs=[smem] + [vmem] * 4,
        compiler_params=params,
        name="prepare_tables",
    )(ends, view_order, light_dir, color_table, opacity_table[None, :])
    wrapped = jnp.where(end_rows[0] == 1, tiles[:, 0], tiles[:, -1])
    other = lax.ppermute(wrapped, ("gz", "gy"), pairs)
    parts, color_sums, keeps = pl.pallas_call(
        functools.partial(main_kernel, edge_rows),
        out_shape=[
            jax.ShapeDtypeStruct((bricks, len(edge_rows), depth, 5, chunks, LANES), jnp.float32),
            jax.ShapeDtypeStruct((max(3 * inner_count, 1), chunks, LANES), jnp.float32),
            jax.ShapeDtypeStruct((tile_rows, chunks, LANES), jnp.float32),
        ],
        in_specs=[smem] + [vmem] * 4,
        out_specs=[vmem, vmem, vmem],
        compiler_params=params,
        cost_estimate=pl.CostEstimate(
            flops=100 * cells * tile_rows, bytes_accessed=24 * cells * tile_rows, transcendentals=0),
        name="main_rows",
    )(brick_at, light_rows, color_words, opacity_words, tiles)
    return pl.pallas_call(
        functools.partial(finish_kernel, edge_rows),
        out_shape=jax.ShapeDtypeStruct((4, 1, tile_rows, cols), jnp.float32),
        in_specs=[vmem] * 7,
        out_specs=vmem,
        scratch_shapes=[pltpu.VMEM((4 * tile_rows * chunks, LANES), jnp.float32)],
        compiler_params=params,
        cost_estimate=pl.CostEstimate(
            flops=10 * cells * tile_rows, bytes_accessed=24 * cells * tile_rows, transcendentals=0),
        name="edge_rows",
    )(end_rows, light_rows, tiles, other, parts, color_sums, keeps)


def solution(mesh):
    in_specs = (P("gz", "gy", None), P("gz", "gy", None), P(), P(), P(), P())
    out_specs = P(None, "gy", "gz", None)
    return jax.shard_map(shards, mesh=mesh, in_specs=in_specs, out_specs=out_specs, check_vma=False)
```

```python
import functools

import jax
import jax.numpy as jnp
from jax import lax
from jax.experimental import pallas as pl
from jax.experimental.pallas import tpu as pltpu
from jax.sharding import PartitionSpec as P

SUB, LANES = 8, 128
COLOR_UNIT, COLOR_SPAN = 2 ** 11, 2 ** 12
OPACITY_UNIT, OPACITY_BITS = 2 ** 18, 16
OPACITY_SPAN = 2 ** OPACITY_BITS


def pack_kernel(field_ref, *rest):
    *out_refs, staged = rest
    depth, rows, cols = field_ref.shape
    padded_rows, _, chunks, _ = out_refs[0].shape
    tile_rows = padded_rows - 2
    block = depth * chunks
    here = lax.axis_index("gz")
    for k in range(depth):
        for j in range(rows // SUB):
            lines = [field_ref[k, j * SUB:(j + 1) * SUB, c * LANES:(c + 1) * LANES] for c in range(chunks)]
            for c, value in enumerate(lines):
                staged[pl.ds(j * SUB * block + k * chunks + c, SUB, stride=block), :] = value
    for step, out_ref in enumerate(out_refs):
        tile = here ^ step
        values = []
        for i in range(padded_rows):
            start = lax.rem(tile * tile_rows + i - 1 + rows, rows) * block
            values.append(staged[pl.ds(pl.multiple_of(start, block), block), :])
        for i, value in enumerate(values):
            for k in range(depth):
                out_ref[i, k] = value[k * chunks:(k + 1) * chunks]


def packed(field, tiles):
    depth, rows, cols = field.shape
    chunks = cols // LANES
    vmem = pl.BlockSpec(memory_space=pltpu.VMEM)
    shape = (rows // tiles + 2, depth, chunks, LANES)
    return pl.pallas_call(
        pack_kernel,
        out_shape=[jax.ShapeDtypeStruct(shape, field.dtype)] * tiles,
        in_specs=[vmem],
        out_specs=[vmem] * tiles,
        scratch_shapes=[pltpu.VMEM((rows * depth * chunks, LANES), field.dtype)],
        compiler_params=pltpu.CompilerParams(vmem_limit_bytes=16 << 20),
        name="pack_rows",
    )(field)


def collect_kernel(slot_ref, end_ref, *rest):
    *tile_refs, tiles_ref, wrapped_ref = rest
    padded_rows, depth, chunks, lanes = tile_refs[0].shape
    is_first = end_ref[0] == 1
    for step, tile_ref in enumerate(tile_refs):
        slot = slot_ref[step]
        values = [[tile_ref[i, k] for k in range(depth)] for i in range(padded_rows)]
        for i in range(padded_rows):
            for k in range(depth):
                tiles_ref[slot, i, k] = values[i][k]
        for k in range(depth):
            wrapped_ref[slot, k] = jnp.where(is_first, values[0][k], values[-1][k])


def shifted(x, axis, shift):
    return pltpu.roll(x, shift % x.shape[axis], axis)


def prepare_kernel(bands_end_ref, order_ref, light_ref, color_ref, opacity_ref,
                   slot_ref, color_word_ref, opacity_word_ref, light_rows_ref, end_ref):
    bins = color_ref.shape[1] - 1
    _, halves, chunks, lanes = color_word_ref.shape
    shape = (chunks, lanes)

    def parts(values, unit):
        scaled = values.astype(jnp.float32) * float(unit)
        return scaled[:, :bins], scaled[:, 1:] - scaled[:, :bins]

    low, slope = parts(color_ref[...], COLOR_UNIT)
    color_words = slope + low * (1.0 / COLOR_SPAN)
    low, slope = parts(opacity_ref[...], OPACITY_UNIT)
    opacity_words = slope.astype(jnp.int32) * OPACITY_SPAN + low.astype(jnp.int32)
    for h in range(halves):
        span = slice(h * lanes, (h + 1) * lanes)
        for c in range(3):
            color_word_ref[c, h] = jnp.broadcast_to(color_words[c:c + 1, span], shape)
        opacity_word_ref[h] = jnp.broadcast_to(opacity_words[:, span], shape)
    for i in range(3):
        light_rows_ref[i] = jnp.full(shape, light_ref[i], jnp.float32)
    for i in range(2):
        end_ref[i] = jnp.full(shape, bands_end_ref[i], jnp.int32)
    here = lax.axis_index("gz")
    bricks = order_ref.shape[0]
    for step in range(bricks):
        slot_ref[step] = order_ref[here ^ step]


def table_lookup(color_word_ref, opacity_word_ref):
    _, halves, _, lanes = color_word_ref.shape
    bins = halves * lanes

    def look_up(x):
        scaled = x * float(bins)
        index = jnp.minimum(scaled.astype(jnp.int32), bins - 1)
        fraction = scaled - index.astype(jnp.float32)
        low_bits = index & (lanes - 1)

        def gathered(table):
            found = [jnp.take_along_axis(t, low_bits, axis=1, mode="promise_in_bounds") for t in table]
            word = found[0]
            for h in range(1, halves):
                word = jnp.where(index >= h * lanes, found[h], word)
            return word

        color = []
        small = fraction * (1.0 / COLOR_SPAN)
        for c in range(3):
            word = gathered([color_word_ref[c, h] for h in range(halves)])
            rise = jnp.floor(word)
            color.append((word - rise) + small * rise)
        word = gathered([opacity_word_ref[h] for h in range(halves)])
        rise = (word >> OPACITY_BITS).astype(jnp.float32)
        start = (word & (OPACITY_SPAN - 1)).astype(jnp.float32)
        return color, (start + fraction * rise) * (1.0 / OPACITY_UNIT)

    return look_up


def column_differences(shape):
    lane = lax.broadcasted_iota(jnp.int32, shape, 1)
    chunk = lax.broadcasted_iota(jnp.int32, shape, 0)
    at_first, at_last = lane == 0, lane == shape[1] - 1
    at_left = at_first & (chunk == 0)
    at_right = at_last & (chunk == shape[0] - 1)

    def difference(x):
        right = shifted(x, 1, -1)
        right = jnp.where(at_last, shifted(right, 0, -1), right)
        right = jnp.where(at_right, 0.0, right)
        left = shifted(x, 1, 1)
        left = jnp.where(at_first, shifted(left, 0, 1), left)
        left = jnp.where(at_left, 0.0, left)
        return right - left

    return difference


def depth_differences(field):
    last = len(field) - 1
    made = {}
    for k in range(last + 1):
        ends = (min(k + 1, last), max(k - 1, 0))
        if ends not in made:
            made[ends] = field[ends[0]] - field[ends[1]]
    return [made[(min(k + 1, last), max(k - 1, 0))] for k in range(last + 1)]


def shading_of(facing, squared_plus_one):
    near = pltpu.reciprocal(squared_plus_one, approx=True)
    inverse = near * (2.0 - squared_plus_one * near)
    return 0.25 + (0.75 * facing) * (facing * inverse)


def main_kernel(edge_rows, light_ref, color_word_ref, opacity_word_ref, tile_ref,
                part_ref, color_sum_ref, keep_ref):
    bricks, padded_rows, depth, chunks, lanes = tile_ref.shape
    rows = padded_rows - 2
    inner_rows = [r for r in range(rows) if r not in edge_rows]
    shape = (chunks, lanes)
    look_up = table_lookup(color_word_ref, opacity_word_ref)
    column_difference = column_differences(shape)
    light = [light_ref[i] for i in range(3)]
    together = 2 if bricks % 2 == 0 else 1

    def step(trip, carry):
        colors, keeps = list(carry[0]), list(carry[1])
        at = [trip * together + u for u in range(together)]
        fields = [[[tile_ref[b, r, k] for k in range(depth)] for r in range(padded_rows)] for b in at]
        kept = []
        for b, field in zip(at, fields):
            for r in range(rows):
                for k, dz in enumerate(depth_differences(field[r + 1])):
                    x = field[r + 1][k]
                    dx = column_difference(x)
                    color, opacity = look_up(x)
                    weight = keeps[r] * opacity
                    facing = dz * light[0] + dx * light[2]
                    squared = dz * dz + dx * dx + 1.0
                    if r in edge_rows:
                        values = [weight * color[c] for c in range(3)] + [facing, squared]
                        kept.append((b, edge_rows.index(r), k, values))
                    else:
                        i = inner_rows.index(r)
                        dy = field[r + 2][k] - field[r][k]
                        shaded = weight * shading_of(facing + dy * light[1], squared + dy * dy)
                        for c in range(3):
                            slot = c * len(inner_rows) + i
                            colors[slot] = colors[slot] + shaded * color[c]
                    keeps[r] = keeps[r] - weight
        for b, i, k, values in kept:
            for v, value in enumerate(values):
                part_ref[b, i, k, v] = value
        return tuple(colors), tuple(keeps)

    zero, one = jnp.zeros(shape, jnp.float32), jnp.ones(shape, jnp.float32)
    colors, keeps = lax.fori_loop(
        0, bricks // together, step, ((zero,) * (3 * len(inner_rows)), (one,) * rows))
    for i, value in enumerate(colors):
        color_sum_ref[i] = value
    for r, value in enumerate(keeps):
        keep_ref[r] = value


def finish_kernel(edge_rows, end_ref, light_ref, tile_ref, other_ref, part_ref, color_sum_ref, keep_ref,
                  out_ref, staged):
    bricks, padded_rows, depth, chunks, lanes = tile_ref.shape
    rows = padded_rows - 2
    inner_rows = [r for r in range(rows) if r not in edge_rows]
    shape = (chunks, lanes)
    light_rows = light_ref[1]
    is_first, is_last = end_ref[0] == 1, end_ref[1] == 1

    together = 4 if bricks % 4 == 0 else 1

    def step(trip, colors):
        colors = list(colors)
        for u in range(together):
            b = trip * together + u
            for i, r in enumerate(edge_rows):
                for k in range(depth):
                    above, below = tile_ref[b, r, k], tile_ref[b, r + 2, k]
                    if r == 0:
                        above = jnp.where(is_first, other_ref[b, k], above)
                    if r == rows - 1:
                        below = jnp.where(is_last, other_ref[b, k], below)
                    dy = below - above
                    facing = part_ref[b, i, k, 3] + dy * light_rows
                    shading = shading_of(facing, part_ref[b, i, k, 4] + dy * dy)
                    for c in range(3):
                        slot = c * len(edge_rows) + i
                        colors[slot] = colors[slot] + shading * part_ref[b, i, k, c]
        return tuple(colors)

    zero = jnp.zeros(shape, jnp.float32)
    edge_colors = lax.fori_loop(0, bricks // together, step, (zero,) * (3 * len(edge_rows)))
    for r in range(rows):
        for c in range(3):
            if r in edge_rows:
                value = edge_colors[c * len(edge_rows) + edge_rows.index(r)]
            else:
                value = color_sum_ref[c * len(inner_rows) + inner_rows.index(r)]
            at = (c * rows + r) * chunks
            staged[at:at + chunks, :] = value * (COLOR_SPAN / COLOR_UNIT)
        at = (3 * rows + r) * chunks
        staged[at:at + chunks, :] = 1.0 - keep_ref[r]
    for c in range(4):
        for q in range(chunks):
            source = pl.ds(c * rows * chunks + q, rows, stride=chunks) if rows > 1 else pl.ds(c * chunks + q, 1)
            out_ref[c, 0, :, q * LANES:(q + 1) * LANES] = staged[source, :]


def shards(scalar, bin_index, color_table, opacity_table, light_dir, view_order):
    depth, rows, cols = scalar.shape
    bricks, bands = lax.axis_size("gz"), lax.axis_size("gy")
    tile_rows = rows // bricks
    chunks = cols // LANES
    edge_rows = sorted({0, tile_rows - 1})
    inner_count = tile_rows - len(edge_rows)
    arrived = list(packed(scalar, bricks))
    half = bricks // 2
    for step in [s for s in range(1, bricks) if s & half] + [s for s in range(1, bricks) if not s & half]:
        to = [t ^ step for t in range(bricks)]
        steps = [(t * bands + g, to[t] * bands + g) for t in range(bricks) for g in range(bands)]
        arrived[step] = lax.ppermute(arrived[step], ("gz", "gy"), steps)

    here = lax.axis_index("gz")
    ends = jnp.stack([here == 0, here == bricks - 1]).astype(jnp.int32)
    last = bricks - 1
    pairs = [(g, g + 1) for g in range(bands - 1)]
    pairs += [(last * bands + g + 1, last * bands + g) for g in range(bands - 1)]

    vmem = pl.BlockSpec(memory_space=pltpu.VMEM)
    smem = pl.BlockSpec(memory_space=pltpu.SMEM)
    params = pltpu.CompilerParams(vmem_limit_bytes=32 << 20)
    cells = bricks * depth * cols
    lines = (chunks, LANES)
    halves = (color_table.shape[1] - 1) // LANES
    slots, color_words, opacity_words, light_rows, end_rows = pl.pallas_call(
        prepare_kernel,
        out_shape=[
            jax.ShapeDtypeStruct((bricks,), jnp.int32),
            jax.ShapeDtypeStruct((3, halves) + lines, jnp.float32),
            jax.ShapeDtypeStruct((halves,) + lines, jnp.int32),
            jax.ShapeDtypeStruct((3,) + lines, jnp.float32),
            jax.ShapeDtypeStruct((2,) + lines, jnp.int32),
        ],
        in_specs=[smem, smem, smem, vmem, vmem],
        out_specs=[smem] + [vmem] * 4,
        compiler_params=params,
        name="prepare_tables",
    )(ends, view_order, light_dir, color_table, opacity_table[None, :])
    tiles, wrapped = pl.pallas_call(
        collect_kernel,
        out_shape=[
            jax.ShapeDtypeStruct((bricks, tile_rows + 2, depth) + lines, jnp.float32),
            jax.ShapeDtypeStruct((bricks, depth) + lines, jnp.float32),
        ],
        in_specs=[smem] + [vmem] * (bricks + 1),
        out_specs=[vmem, vmem],
        compiler_params=params,
        name="collect_tiles",
    )(slots, end_rows, *arrived)
    other = lax.ppermute(wrapped, ("gz", "gy"), pairs)
    parts, color_sums, keeps = pl.pallas_call(
        functools.partial(main_kernel, edge_rows),
        out_shape=[
            jax.ShapeDtypeStruct((bricks, len(edge_rows), depth, 5, chunks, LANES), jnp.float32),
            jax.ShapeDtypeStruct((max(3 * inner_count, 1), chunks, LANES), jnp.float32),
            jax.ShapeDtypeStruct((tile_rows, chunks, LANES), jnp.float32),
        ],
        in_specs=[vmem] * 4,
        out_specs=[vmem, vmem, vmem],
        compiler_params=params,
        cost_estimate=pl.CostEstimate(
            flops=100 * cells * tile_rows, bytes_accessed=24 * cells * tile_rows, transcendentals=0),
        name="main_rows",
    )(light_rows, color_words, opacity_words, tiles)
    return pl.pallas_call(
        functools.partial(finish_kernel, edge_rows),
        out_shape=jax.ShapeDtypeStruct((4, 1, tile_rows, cols), jnp.float32),
        in_specs=[vmem] * 7,
        out_specs=vmem,
        scratch_shapes=[pltpu.VMEM((4 * tile_rows * chunks, LANES), jnp.float32)],
        compiler_params=params,
        cost_estimate=pl.CostEstimate(
            flops=10 * cells * tile_rows, bytes_accessed=24 * cells * tile_rows, transcendentals=0),
        name="edge_rows",
    )(end_rows, light_rows, tiles, other, parts, color_sums, keeps)


def solution(mesh):
    in_specs = (P("gz", "gy", None), P("gz", "gy", None), P(), P(), P(), P())
    out_specs = P(None, "gy", "gz", None)
    return jax.shard_map(shards, mesh=mesh, in_specs=in_specs, out_specs=out_specs, check_vma=False)
```

```python
import functools

import jax
import jax.numpy as jnp
from jax import lax
from jax.experimental import pallas as pl
from jax.experimental.pallas import tpu as pltpu
from jax.sharding import PartitionSpec as P

SUB, LANES = 8, 128
COLOR_UNIT, COLOR_SPAN = 2 ** 11, 2 ** 12
OPACITY_UNIT, OPACITY_BITS = 2 ** 18, 16
OPACITY_SPAN = 2 ** OPACITY_BITS


def pack_kernel(field_ref, out_ref, staged):
    depth, rows, cols = field_ref.shape
    tiles, padded_rows, _, chunks, _ = out_ref.shape
    tile_rows = padded_rows - 2
    block = depth * chunks

    for k in range(depth):
        for j in range(rows // SUB):
            lines = [field_ref[k, j * SUB:(j + 1) * SUB, c * LANES:(c + 1) * LANES] for c in range(chunks)]
            for c, value in enumerate(lines):
                staged[pl.ds(j * SUB * block + k * chunks + c, SUB, stride=block), :] = value
    for t in range(tiles):
        starts = [((t * tile_rows + i - 1) % rows) * block for i in range(padded_rows)]
        blocks = [staged[start:start + block, :] for start in starts]
        for i, value in enumerate(blocks):
            for k in range(depth):
                out_ref[t, i, k] = value[k * chunks:(k + 1) * chunks]


def packed(field, tiles):
    depth, rows, cols = field.shape
    chunks = cols // LANES
    vmem = pl.BlockSpec(memory_space=pltpu.VMEM)
    shape = (tiles, rows // tiles + 2, depth, chunks, LANES)
    return pl.pallas_call(
        pack_kernel,
        out_shape=pltpu.VMEM(shape, field.dtype),
        in_specs=[vmem],
        out_specs=vmem,
        scratch_shapes=[pltpu.VMEM((rows * depth * chunks, LANES), field.dtype)],
        compiler_params=pltpu.CompilerParams(vmem_limit_bytes=16 << 20),
        name="pack_rows",
    )(field)


def shifted(x, axis, shift):
    return pltpu.roll(x, shift % x.shape[axis], axis)


def prepare_kernel(bands_end_ref, order_ref, light_ref, color_ref, opacity_ref,
                   brick_at_ref, color_word_ref, opacity_word_ref, light_rows_ref, end_ref):
    bins = color_ref.shape[1] - 1
    _, halves, chunks, lanes = color_word_ref.shape
    shape = (chunks, lanes)

    def parts(values, unit):
        scaled = values.astype(jnp.float32) * float(unit)
        return scaled[:, :bins], scaled[:, 1:] - scaled[:, :bins]

    low, slope = parts(color_ref[...], COLOR_UNIT)
    color_words = slope + low * (1.0 / COLOR_SPAN)
    low, slope = parts(opacity_ref[...], OPACITY_UNIT)
    opacity_words = slope.astype(jnp.int32) * OPACITY_SPAN + low.astype(jnp.int32)
    for h in range(halves):
        span = slice(h * lanes, (h + 1) * lanes)
        for c in range(3):
            color_word_ref[c, h] = jnp.broadcast_to(color_words[c:c + 1, span], shape)
        opacity_word_ref[h] = jnp.broadcast_to(opacity_words[:, span], shape)
    for i in range(3):
        light_rows_ref[i] = jnp.full(shape, light_ref[i], jnp.float32)
    for i in range(2):
        end_ref[i] = jnp.full(shape, bands_end_ref[i], jnp.int32)
    for b in range(order_ref.shape[0]):
        brick_at_ref[order_ref[b]] = b


def table_lookup(color_word_ref, opacity_word_ref):
    _, halves, _, lanes = color_word_ref.shape
    bins = halves * lanes

    def look_up(x):
        scaled = x * float(bins)
        index = jnp.minimum(scaled.astype(jnp.int32), bins - 1)
        fraction = scaled - index.astype(jnp.float32)
        low_bits = index & (lanes - 1)

        def gathered(table):
            found = [jnp.take_along_axis(t, low_bits, axis=1, mode="promise_in_bounds") for t in table]
            word = found[0]
            for h in range(1, halves):
                word = jnp.where(index >= h * lanes, found[h], word)
            return word

        color = []
        small = fraction * (1.0 / COLOR_SPAN)
        for c in range(3):
            word = gathered([color_word_ref[c, h] for h in range(halves)])
            rise = jnp.floor(word)
            color.append((word - rise) + small * rise)
        word = gathered([opacity_word_ref[h] for h in range(halves)])
        rise = (word >> OPACITY_BITS).astype(jnp.float32)
        start = (word & (OPACITY_SPAN - 1)).astype(jnp.float32)
        return color, (start + fraction * rise) * (1.0 / OPACITY_UNIT)

    return look_up


def column_differences(shape):
    lane = lax.broadcasted_iota(jnp.int32, shape, 1)
    chunk = lax.broadcasted_iota(jnp.int32, shape, 0)
    at_first, at_last = lane == 0, lane == shape[1] - 1
    at_left = at_first & (chunk == 0)
    at_right = at_last & (chunk == shape[0] - 1)

    def difference(x):
        right = shifted(x, 1, -1)
        right = jnp.where(at_last, shifted(right, 0, -1), right)
        right = jnp.where(at_right, 0.0, right)
        left = shifted(x, 1, 1)
        left = jnp.where(at_first, shifted(left, 0, 1), left)
        left = jnp.where(at_left, 0.0, left)
        return right - left

    return difference


def depth_differences(field):
    last = len(field) - 1
    made = {}
    for k in range(last + 1):
        ends = (min(k + 1, last), max(k - 1, 0))
        if ends not in made:
            made[ends] = field[ends[0]] - field[ends[1]]
    return [made[(min(k + 1, last), max(k - 1, 0))] for k in range(last + 1)]


def shading_of(facing, squared_plus_one):
    near = pltpu.reciprocal(squared_plus_one, approx=True)
    inverse = near * (2.0 - squared_plus_one * near)
    return 0.25 + (0.75 * facing) * (facing * inverse)


def main_kernel(edge_rows, brick_at, light_ref, color_word_ref, opacity_word_ref, tile_ref,
                part_ref, color_sum_ref, keep_ref):
    bricks, padded_rows, depth, chunks, lanes = tile_ref.shape
    rows = padded_rows - 2
    inner_rows = [r for r in range(rows) if r not in edge_rows]
    shape = (chunks, lanes)
    look_up = table_lookup(color_word_ref, opacity_word_ref)
    column_difference = column_differences(shape)
    light = [light_ref[i] for i in range(3)]
    together = 2 if bricks % 2 == 0 else 1

    def step(trip, carry):
        colors, keeps = list(carry[0]), list(carry[1])
        at = [brick_at[trip * together + u] for u in range(together)]
        fields = [[[tile_ref[b, r, k] for k in range(depth)] for r in range(padded_rows)] for b in at]
        kept = []
        for b, field in zip(at, fields):
            for r in range(rows):
                for k, dz in enumerate(depth_differences(field[r + 1])):
                    x = field[r + 1][k]
                    dx = column_difference(x)
                    color, opacity = look_up(x)
                    weight = keeps[r] * opacity
                    facing = dz * light[0] + dx * light[2]
                    squared = dz * dz + dx * dx + 1.0
                    if r in edge_rows:
                        values = [weight * color[c] for c in range(3)] + [facing, squared]
                        kept.append((b, edge_rows.index(r), k, values))
                    else:
                        i = inner_rows.index(r)
                        dy = field[r + 2][k] - field[r][k]
                        shaded = weight * shading_of(facing + dy * light[1], squared + dy * dy)
                        for c in range(3):
                            slot = c * len(inner_rows) + i
                            colors[slot] = colors[slot] + shaded * color[c]
                    keeps[r] = keeps[r] - weight
        for b, i, k, values in kept:
            for v, value in enumerate(values):
                part_ref[b, i, k, v] = value
        return tuple(colors), tuple(keeps)

    zero, one = jnp.zeros(shape, jnp.float32), jnp.ones(shape, jnp.float32)
    colors, keeps = lax.fori_loop(
        0, bricks // together, step, ((zero,) * (3 * len(inner_rows)), (one,) * rows))
    for i, value in enumerate(colors):
        color_sum_ref[i] = value
    for r, value in enumerate(keeps):
        keep_ref[r] = value


def finish_kernel(edge_rows, end_ref, light_ref, tile_ref, other_ref, part_ref, color_sum_ref, keep_ref,
                  out_ref, staged):
    bricks, padded_rows, depth, chunks, lanes = tile_ref.shape
    rows = padded_rows - 2
    inner_rows = [r for r in range(rows) if r not in edge_rows]
    shape = (chunks, lanes)
    light_rows = light_ref[1]
    is_first, is_last = end_ref[0] == 1, end_ref[1] == 1

    together = 4 if bricks % 4 == 0 else 1

    def step(trip, colors):
        colors = list(colors)
        for u in range(together):
            b = trip * together + u
            for i, r in enumerate(edge_rows):
                for k in range(depth):
                    above, below = tile_ref[b, r, k], tile_ref[b, r + 2, k]
                    if r == 0:
                        above = jnp.where(is_first, other_ref[b, k], above)
                    if r == rows - 1:
                        below = jnp.where(is_last, other_ref[b, k], below)
                    dy = below - above
                    facing = part_ref[b, i, k, 3] + dy * light_rows
                    shading = shading_of(facing, part_ref[b, i, k, 4] + dy * dy)
                    for c in range(3):
                        slot = c * len(edge_rows) + i
                        colors[slot] = colors[slot] + shading * part_ref[b, i, k, c]
        return tuple(colors)

    zero = jnp.zeros(shape, jnp.float32)
    edge_colors = lax.fori_loop(0, bricks // together, step, (zero,) * (3 * len(edge_rows)))
    for r in range(rows):
        for c in range(3):
            if r in edge_rows:
                value = edge_colors[c * len(edge_rows) + edge_rows.index(r)]
            else:
                value = color_sum_ref[c * len(inner_rows) + inner_rows.index(r)]
            at = (c * rows + r) * chunks
            staged[at:at + chunks, :] = value * (COLOR_SPAN / COLOR_UNIT)
        at = (3 * rows + r) * chunks
        staged[at:at + chunks, :] = 1.0 - keep_ref[r]
    for c in range(4):
        for q in range(chunks):
            source = pl.ds(c * rows * chunks + q, rows, stride=chunks) if rows > 1 else pl.ds(c * chunks + q, 1)
            out_ref[c, 0, :, q * LANES:(q + 1) * LANES] = staged[source, :]


def shards(scalar, bin_index, color_table, opacity_table, light_dir, view_order):
    depth, rows, cols = scalar.shape
    bricks, bands = lax.axis_size("gz"), lax.axis_size("gy")
    tile_rows = rows // bricks
    chunks = cols // LANES
    edge_rows = sorted({0, tile_rows - 1})
    inner_count = tile_rows - len(edge_rows)
    tiles = lax.all_to_all(packed(scalar, bricks), "gz", split_axis=0, concat_axis=0, tiled=True)

    here = lax.axis_index("gz")
    ends = jnp.stack([here == 0, here == bricks - 1]).astype(jnp.int32)
    last = bricks - 1
    pairs = [(g, g + 1) for g in range(bands - 1)]
    pairs += [(last * bands + g + 1, last * bands + g) for g in range(bands - 1)]

    vmem = pl.BlockSpec(memory_space=pltpu.VMEM)
    smem = pl.BlockSpec(memory_space=pltpu.SMEM)
    params = pltpu.CompilerParams(vmem_limit_bytes=32 << 20)
    cells = bricks * depth * cols
    lines = (chunks, LANES)
    halves = (color_table.shape[1] - 1) // LANES
    brick_at, color_words, opacity_words, light_rows, end_rows = pl.pallas_call(
        prepare_kernel,
        out_shape=[
            pltpu.SMEM((bricks,), jnp.int32),
            jax.ShapeDtypeStruct((3, halves) + lines, jnp.float32),
            jax.ShapeDtypeStruct((halves,) + lines, jnp.int32),
            jax.ShapeDtypeStruct((3,) + lines, jnp.float32),
            jax.ShapeDtypeStruct((2,) + lines, jnp.int32),
        ],
        in_specs=[smem, smem, smem, vmem, vmem],
        out_specs=[smem] + [vmem] * 4,
        compiler_params=params,
        name="prepare_tables",
    )(ends, view_order, light_dir, color_table, opacity_table[None, :])
    wrapped = jnp.where(end_rows[0] == 1, tiles[:, 0], tiles[:, -1])
    other = lax.ppermute(wrapped, ("gz", "gy"), pairs)
    parts, color_sums, keeps = pl.pallas_call(
        functools.partial(main_kernel, edge_rows),
        out_shape=[
            jax.ShapeDtypeStruct((bricks, len(edge_rows), depth, 5, chunks, LANES), jnp.float32),
            jax.ShapeDtypeStruct((max(3 * inner_count, 1), chunks, LANES), jnp.float32),
            jax.ShapeDtypeStruct((tile_rows, chunks, LANES), jnp.float32),
        ],
        in_specs=[smem] + [vmem] * 4,
        out_specs=[vmem, vmem, vmem],
        compiler_params=params,
        cost_estimate=pl.CostEstimate(
            flops=100 * cells * tile_rows, bytes_accessed=24 * cells * tile_rows, transcendentals=0),
        name="main_rows",
    )(brick_at, light_rows, color_words, opacity_words, tiles)
    return pl.pallas_call(
        functools.partial(finish_kernel, edge_rows),
        out_shape=jax.ShapeDtypeStruct((4, 1, tile_rows, cols), jnp.float32),
        in_specs=[vmem] * 7,
        out_specs=vmem,
        scratch_shapes=[pltpu.VMEM((4 * tile_rows * chunks, LANES), jnp.float32)],
        compiler_params=params,
        cost_estimate=pl.CostEstimate(
            flops=10 * cells * tile_rows, bytes_accessed=24 * cells * tile_rows, transcendentals=0),
        name="edge_rows",
    )(end_rows, light_rows, tiles, other, parts, color_sums, keeps)


def solution(mesh):
    in_specs = (P("gz", "gy", None), P("gz", "gy", None), P(), P(), P(), P())
    out_specs = P(None, "gy", "gz", None)
    return jax.shard_map(shards, mesh=mesh, in_specs=in_specs, out_specs=out_specs, check_vma=False)
```

```python
import functools

import jax
import jax.numpy as jnp
from jax import lax
from jax.experimental import pallas as pl
from jax.experimental.pallas import tpu as pltpu
from jax.sharding import PartitionSpec as P

SUB, LANES = 8, 128
COLOR_UNIT, COLOR_SPAN = 2 ** 11, 2 ** 12
OPACITY_UNIT, OPACITY_BITS = 2 ** 18, 16
OPACITY_SPAN = 2 ** OPACITY_BITS


def exchange_order(tiles):
    parts = 4 if tiles % 4 == 0 else 1
    return [(i % parts) * (tiles // parts) + i // parts for i in range(tiles)]


def pack_kernel(field_ref, out_ref, staged):
    depth, rows, cols = field_ref.shape
    tiles, padded_rows, _, chunks, _ = out_ref.shape
    tile_rows = padded_rows - 2
    block = depth * chunks

    for k in range(depth):
        for j in range(rows // SUB):
            lines = [field_ref[k, j * SUB:(j + 1) * SUB, c * LANES:(c + 1) * LANES] for c in range(chunks)]
            for c, value in enumerate(lines):
                staged[pl.ds(j * SUB * block + k * chunks + c, SUB, stride=block), :] = value
    for place, t in enumerate(exchange_order(tiles)):
        starts = [((t * tile_rows + i - 1) % rows) * block for i in range(padded_rows)]
        blocks = [staged[start:start + block, :] for start in starts]
        for i, value in enumerate(blocks):
            for k in range(depth):
                out_ref[place, i, k] = value[k * chunks:(k + 1) * chunks]


def packed(field, tiles):
    depth, rows, cols = field.shape
    chunks = cols // LANES
    vmem = pl.BlockSpec(memory_space=pltpu.VMEM)
    shape = (tiles, rows // tiles + 2, depth, chunks, LANES)
    return pl.pallas_call(
        pack_kernel,
        out_shape=pltpu.VMEM(shape, field.dtype),
        in_specs=[vmem],
        out_specs=vmem,
        scratch_shapes=[pltpu.VMEM((rows * depth * chunks, LANES), field.dtype)],
        compiler_params=pltpu.CompilerParams(vmem_limit_bytes=16 << 20),
        name="pack_rows",
    )(field)


def shifted(x, axis, shift):
    return pltpu.roll(x, shift % x.shape[axis], axis)


def prepare_kernel(bands_end_ref, order_ref, light_ref, color_ref, opacity_ref,
                   brick_at_ref, color_word_ref, opacity_word_ref, light_rows_ref, end_ref):
    bins = color_ref.shape[1] - 1
    _, halves, chunks, lanes = color_word_ref.shape
    shape = (chunks, lanes)

    def parts(values, unit):
        scaled = values.astype(jnp.float32) * float(unit)
        return scaled[:, :bins], scaled[:, 1:] - scaled[:, :bins]

    low, slope = parts(color_ref[...], COLOR_UNIT)
    color_words = slope + low * (1.0 / COLOR_SPAN)
    low, slope = parts(opacity_ref[...], OPACITY_UNIT)
    opacity_words = slope.astype(jnp.int32) * OPACITY_SPAN + low.astype(jnp.int32)
    for h in range(halves):
        span = slice(h * lanes, (h + 1) * lanes)
        for c in range(3):
            color_word_ref[c, h] = jnp.broadcast_to(color_words[c:c + 1, span], shape)
        opacity_word_ref[h] = jnp.broadcast_to(opacity_words[:, span], shape)
    for i in range(3):
        light_rows_ref[i] = jnp.full(shape, light_ref[i], jnp.float32)
    for i in range(2):
        end_ref[i] = jnp.full(shape, bands_end_ref[i], jnp.int32)
    for place, b in enumerate(exchange_order(order_ref.shape[0])):
        brick_at_ref[order_ref[b]] = place


def table_lookup(color_word_ref, opacity_word_ref):
    _, halves, _, lanes = color_word_ref.shape
    bins = halves * lanes

    def look_up(x):
        scaled = x * float(bins)
        index = jnp.minimum(scaled.astype(jnp.int32), bins - 1)
        fraction = scaled - index.astype(jnp.float32)
        low_bits = index & (lanes - 1)

        def gathered(table):
            found = [jnp.take_along_axis(t, low_bits, axis=1, mode="promise_in_bounds") for t in table]
            word = found[0]
            for h in range(1, halves):
                word = jnp.where(index >= h * lanes, found[h], word)
            return word

        color = []
        small = fraction * (1.0 / COLOR_SPAN)
        for c in range(3):
            word = gathered([color_word_ref[c, h] for h in range(halves)])
            rise = jnp.floor(word)
            color.append((word - rise) + small * rise)
        word = gathered([opacity_word_ref[h] for h in range(halves)])
        rise = (word >> OPACITY_BITS).astype(jnp.float32)
        start = (word & (OPACITY_SPAN - 1)).astype(jnp.float32)
        return color, (start + fraction * rise) * (1.0 / OPACITY_UNIT)

    return look_up


def column_differences(shape):
    lane = lax.broadcasted_iota(jnp.int32, shape, 1)
    chunk = lax.broadcasted_iota(jnp.int32, shape, 0)
    at_first, at_last = lane == 0, lane == shape[1] - 1
    at_left = at_first & (chunk == 0)
    at_right = at_last & (chunk == shape[0] - 1)

    def difference(x):
        right = shifted(x, 1, -1)
        right = jnp.where(at_last, shifted(right, 0, -1), right)
        right = jnp.where(at_right, 0.0, right)
        left = shifted(x, 1, 1)
        left = jnp.where(at_first, shifted(left, 0, 1), left)
        left = jnp.where(at_left, 0.0, left)
        return right - left

    return difference


def depth_differences(field):
    last = len(field) - 1
    made = {}
    for k in range(last + 1):
        ends = (min(k + 1, last), max(k - 1, 0))
        if ends not in made:
            made[ends] = field[ends[0]] - field[ends[1]]
    return [made[(min(k + 1, last), max(k - 1, 0))] for k in range(last + 1)]


def shading_of(facing, squared_plus_one):
    near = pltpu.reciprocal(squared_plus_one, approx=True)
    inverse = near * (2.0 - squared_plus_one * near)
    return 0.25 + (0.75 * facing) * (facing * inverse)


def main_kernel(edge_rows, brick_at, light_ref, color_word_ref, opacity_word_ref, tile_ref,
                part_ref, color_sum_ref, keep_ref):
    bricks, padded_rows, depth, chunks, lanes = tile_ref.shape
    rows = padded_rows - 2
    inner_rows = [r for r in range(rows) if r not in edge_rows]
    shape = (chunks, lanes)
    look_up = table_lookup(color_word_ref, opacity_word_ref)
    column_difference = column_differences(shape)
    light = [light_ref[i] for i in range(3)]
    together = 2 if bricks % 2 == 0 else 1

    def step(trip, carry):
        colors, keeps = list(carry[0]), list(carry[1])
        at = [brick_at[trip * together + u] for u in range(together)]
        fields = [[[tile_ref[b, r, k] for k in range(depth)] for r in range(padded_rows)] for b in at]
        kept = []
        for b, field in zip(at, fields):
            for r in range(rows):
                for k, dz in enumerate(depth_differences(field[r + 1])):
                    x = field[r + 1][k]
                    dx = column_difference(x)
                    color, opacity = look_up(x)
                    weight = keeps[r] * opacity
                    facing = dz * light[0] + dx * light[2]
                    squared = dz * dz + dx * dx + 1.0
                    if r in edge_rows:
                        values = [weight * color[c] for c in range(3)] + [facing, squared]
                        kept.append((b, edge_rows.index(r), k, values))
                    else:
                        i = inner_rows.index(r)
                        dy = field[r + 2][k] - field[r][k]
                        shaded = weight * shading_of(facing + dy * light[1], squared + dy * dy)
                        for c in range(3):
                            slot = c * len(inner_rows) + i
                            colors[slot] = colors[slot] + shaded * color[c]
                    keeps[r] = keeps[r] - weight
        for b, i, k, values in kept:
            for v, value in enumerate(values):
                part_ref[b, i, k, v] = value
        return tuple(colors), tuple(keeps)

    zero, one = jnp.zeros(shape, jnp.float32), jnp.ones(shape, jnp.float32)
    colors, keeps = lax.fori_loop(
        0, bricks // together, step, ((zero,) * (3 * len(inner_rows)), (one,) * rows))
    for i, value in enumerate(colors):
        color_sum_ref[i] = value
    for r, value in enumerate(keeps):
        keep_ref[r] = value


def finish_kernel(edge_rows, end_ref, light_ref, tile_ref, other_ref, part_ref, color_sum_ref, keep_ref,
                  out_ref, staged):
    bricks, padded_rows, depth, chunks, lanes = tile_ref.shape
    rows = padded_rows - 2
    inner_rows = [r for r in range(rows) if r not in edge_rows]
    shape = (chunks, lanes)
    light_rows = light_ref[1]
    is_first, is_last = end_ref[0] == 1, end_ref[1] == 1

    together = 4 if bricks % 4 == 0 else 1

    def step(trip, colors):
        colors = list(colors)
        for u in range(together):
            b = trip * together + u
            for i, r in enumerate(edge_rows):
                for k in range(depth):
                    above, below = tile_ref[b, r, k], tile_ref[b, r + 2, k]
                    if r == 0:
                        above = jnp.where(is_first, other_ref[b, k], above)
                    if r == rows - 1:
                        below = jnp.where(is_last, other_ref[b, k], below)
                    dy = below - above
                    facing = part_ref[b, i, k, 3] + dy * light_rows
                    shading = shading_of(facing, part_ref[b, i, k, 4] + dy * dy)
                    for c in range(3):
                        slot = c * len(edge_rows) + i
                        colors[slot] = colors[slot] + shading * part_ref[b, i, k, c]
        return tuple(colors)

    zero = jnp.zeros(shape, jnp.float32)
    edge_colors = lax.fori_loop(0, bricks // together, step, (zero,) * (3 * len(edge_rows)))
    for r in range(rows):
        for c in range(3):
            if r in edge_rows:
                value = edge_colors[c * len(edge_rows) + edge_rows.index(r)]
            else:
                value = color_sum_ref[c * len(inner_rows) + inner_rows.index(r)]
            at = (c * rows + r) * chunks
            staged[at:at + chunks, :] = value * (COLOR_SPAN / COLOR_UNIT)
        at = (3 * rows + r) * chunks
        staged[at:at + chunks, :] = 1.0 - keep_ref[r]
    for c in range(4):
        for q in range(chunks):
            source = pl.ds(c * rows * chunks + q, rows, stride=chunks) if rows > 1 else pl.ds(c * chunks + q, 1)
            out_ref[c, 0, :, q * LANES:(q + 1) * LANES] = staged[source, :]


def shards(scalar, bin_index, color_table, opacity_table, light_dir, view_order):
    depth, rows, cols = scalar.shape
    bricks, bands = lax.axis_size("gz"), lax.axis_size("gy")
    tile_rows = rows // bricks
    chunks = cols // LANES
    edge_rows = sorted({0, tile_rows - 1})
    inner_count = tile_rows - len(edge_rows)
    tiles = lax.all_to_all(
        packed(scalar, bricks), "gz", split_axis=0, concat_axis=0, tiled=True,
        axis_index_groups=[exchange_order(bricks)])

    here = lax.axis_index("gz")
    ends = jnp.stack([here == 0, here == bricks - 1]).astype(jnp.int32)
    last = bricks - 1
    pairs = [(g, g + 1) for g in range(bands - 1)]
    pairs += [(last * bands + g + 1, last * bands + g) for g in range(bands - 1)]

    vmem = pl.BlockSpec(memory_space=pltpu.VMEM)
    smem = pl.BlockSpec(memory_space=pltpu.SMEM)
    params = pltpu.CompilerParams(vmem_limit_bytes=32 << 20)
    cells = bricks * depth * cols
    lines = (chunks, LANES)
    halves = (color_table.shape[1] - 1) // LANES
    brick_at, color_words, opacity_words, light_rows, end_rows = pl.pallas_call(
        prepare_kernel,
        out_shape=[
            pltpu.SMEM((bricks,), jnp.int32),
            jax.ShapeDtypeStruct((3, halves) + lines, jnp.float32),
            jax.ShapeDtypeStruct((halves,) + lines, jnp.int32),
            jax.ShapeDtypeStruct((3,) + lines, jnp.float32),
            jax.ShapeDtypeStruct((2,) + lines, jnp.int32),
        ],
        in_specs=[smem, smem, smem, vmem, vmem],
        out_specs=[smem] + [vmem] * 4,
        compiler_params=params,
        name="prepare_tables",
    )(ends, view_order, light_dir, color_table, opacity_table[None, :])
    wrapped = jnp.where(end_rows[0] == 1, tiles[:, 0], tiles[:, -1])
    other = lax.ppermute(wrapped, ("gz", "gy"), pairs)
    parts, color_sums, keeps = pl.pallas_call(
        functools.partial(main_kernel, edge_rows),
        out_shape=[
            jax.ShapeDtypeStruct((bricks, len(edge_rows), depth, 5, chunks, LANES), jnp.float32),
            jax.ShapeDtypeStruct((max(3 * inner_count, 1), chunks, LANES), jnp.float32),
            jax.ShapeDtypeStruct((tile_rows, chunks, LANES), jnp.float32),
        ],
        in_specs=[smem] + [vmem] * 4,
        out_specs=[vmem, vmem, vmem],
        compiler_params=params,
        cost_estimate=pl.CostEstimate(
            flops=100 * cells * tile_rows, bytes_accessed=24 * cells * tile_rows, transcendentals=0),
        name="main_rows",
    )(brick_at, light_rows, color_words, opacity_words, tiles)
    return pl.pallas_call(
        functools.partial(finish_kernel, edge_rows),
        out_shape=jax.ShapeDtypeStruct((4, 1, tile_rows, cols), jnp.float32),
        in_specs=[vmem] * 7,
        out_specs=vmem,
        scratch_shapes=[pltpu.VMEM((4 * tile_rows * chunks, LANES), jnp.float32)],
        compiler_params=params,
        cost_estimate=pl.CostEstimate(
            flops=10 * cells * tile_rows, bytes_accessed=24 * cells * tile_rows, transcendentals=0),
        name="edge_rows",
    )(end_rows, light_rows, tiles, other, parts, color_sums, keeps)


def solution(mesh):
    in_specs = (P("gz", "gy", None), P("gz", "gy", None), P(), P(), P(), P())
    out_specs = P(None, "gy", "gz", None)
    return jax.shard_map(shards, mesh=mesh, in_specs=in_specs, out_specs=out_specs, check_vma=False)
```

```python
import functools

import jax
import jax.numpy as jnp
from jax import lax
from jax.experimental import pallas as pl
from jax.experimental.pallas import tpu as pltpu
from jax.sharding import PartitionSpec as P

SUB, LANES = 8, 128
COLOR_UNIT, COLOR_SPAN = 2 ** 11, 2 ** 12
OPACITY_UNIT, OPACITY_BITS = 2 ** 18, 16
OPACITY_SPAN = 2 ** OPACITY_BITS


def exchange_order(tiles):
    return list(range(tiles))[::-1]


def pack_kernel(field_ref, out_ref, staged):
    depth, rows, cols = field_ref.shape
    tiles, padded_rows, _, chunks, _ = out_ref.shape
    tile_rows = padded_rows - 2
    block = depth * chunks

    for k in range(depth):
        for j in range(rows // SUB):
            lines = [field_ref[k, j * SUB:(j + 1) * SUB, c * LANES:(c + 1) * LANES] for c in range(chunks)]
            for c, value in enumerate(lines):
                staged[pl.ds(j * SUB * block + k * chunks + c, SUB, stride=block), :] = value
    for place, t in enumerate(exchange_order(tiles)):
        starts = [((t * tile_rows + i - 1) % rows) * block for i in range(padded_rows)]
        blocks = [staged[start:start + block, :] for start in starts]
        for i, value in enumerate(blocks):
            for k in range(depth):
                out_ref[place, i, k] = value[k * chunks:(k + 1) * chunks]


def packed(field, tiles):
    depth, rows, cols = field.shape
    chunks = cols // LANES
    vmem = pl.BlockSpec(memory_space=pltpu.VMEM)
    shape = (tiles, rows // tiles + 2, depth, chunks, LANES)
    return pl.pallas_call(
        pack_kernel,
        out_shape=pltpu.VMEM(shape, field.dtype),
        in_specs=[vmem],
        out_specs=vmem,
        scratch_shapes=[pltpu.VMEM((rows * depth * chunks, LANES), field.dtype)],
        compiler_params=pltpu.CompilerParams(vmem_limit_bytes=16 << 20),
        name="pack_rows",
    )(field)


def shifted(x, axis, shift):
    return pltpu.roll(x, shift % x.shape[axis], axis)


def prepare_kernel(bands_end_ref, order_ref, light_ref, color_ref, opacity_ref,
                   brick_at_ref, color_word_ref, opacity_word_ref, light_rows_ref, end_ref):
    bins = color_ref.shape[1] - 1
    _, halves, chunks, lanes = color_word_ref.shape
    shape = (chunks, lanes)

    def parts(values, unit):
        scaled = values.astype(jnp.float32) * float(unit)
        return scaled[:, :bins], scaled[:, 1:] - scaled[:, :bins]

    low, slope = parts(color_ref[...], COLOR_UNIT)
    color_words = slope + low * (1.0 / COLOR_SPAN)
    low, slope = parts(opacity_ref[...], OPACITY_UNIT)
    opacity_words = slope.astype(jnp.int32) * OPACITY_SPAN + low.astype(jnp.int32)
    for h in range(halves):
        span = slice(h * lanes, (h + 1) * lanes)
        for c in range(3):
            color_word_ref[c, h] = jnp.broadcast_to(color_words[c:c + 1, span], shape)
        opacity_word_ref[h] = jnp.broadcast_to(opacity_words[:, span], shape)
    for i in range(3):
        light_rows_ref[i] = jnp.full(shape, light_ref[i], jnp.float32)
    for i in range(2):
        end_ref[i] = jnp.full(shape, bands_end_ref[i], jnp.int32)
    for place, b in enumerate(exchange_order(order_ref.shape[0])):
        brick_at_ref[order_ref[b]] = place


def table_lookup(color_word_ref, opacity_word_ref):
    _, halves, _, lanes = color_word_ref.shape
    bins = halves * lanes

    def look_up(x):
        scaled = x * float(bins)
        index = jnp.minimum(scaled.astype(jnp.int32), bins - 1)
        fraction = scaled - index.astype(jnp.float32)
        low_bits = index & (lanes - 1)

        def gathered(table):
            found = [jnp.take_along_axis(t, low_bits, axis=1, mode="promise_in_bounds") for t in table]
            word = found[0]
            for h in range(1, halves):
                word = jnp.where(index >= h * lanes, found[h], word)
            return word

        color = []
        small = fraction * (1.0 / COLOR_SPAN)
        for c in range(3):
            word = gathered([color_word_ref[c, h] for h in range(halves)])
            rise = jnp.floor(word)
            color.append((word - rise) + small * rise)
        word = gathered([opacity_word_ref[h] for h in range(halves)])
        rise = (word >> OPACITY_BITS).astype(jnp.float32)
        start = (word & (OPACITY_SPAN - 1)).astype(jnp.float32)
        return color, (start + fraction * rise) * (1.0 / OPACITY_UNIT)

    return look_up


def column_differences(shape):
    lane = lax.broadcasted_iota(jnp.int32, shape, 1)
    chunk = lax.broadcasted_iota(jnp.int32, shape, 0)
    at_first, at_last = lane == 0, lane == shape[1] - 1
    at_left = at_first & (chunk == 0)
    at_right = at_last & (chunk == shape[0] - 1)

    def difference(x):
        right = shifted(x, 1, -1)
        right = jnp.where(at_last, shifted(right, 0, -1), right)
        right = jnp.where(at_right, 0.0, right)
        left = shifted(x, 1, 1)
        left = jnp.where(at_first, shifted(left, 0, 1), left)
        left = jnp.where(at_left, 0.0, left)
        return right - left

    return difference


def depth_differences(field):
    last = len(field) - 1
    made = {}
    for k in range(last + 1):
        ends = (min(k + 1, last), max(k - 1, 0))
        if ends not in made:
            made[ends] = field[ends[0]] - field[ends[1]]
    return [made[(min(k + 1, last), max(k - 1, 0))] for k in range(last + 1)]


def shading_of(facing, squared_plus_one):
    near = pltpu.reciprocal(squared_plus_one, approx=True)
    inverse = near * (2.0 - squared_plus_one * near)
    return 0.25 + (0.75 * facing) * (facing * inverse)


def main_kernel(edge_rows, brick_at, light_ref, color_word_ref, opacity_word_ref, tile_ref,
                part_ref, color_sum_ref, keep_ref):
    bricks, padded_rows, depth, chunks, lanes = tile_ref.shape
    rows = padded_rows - 2
    inner_rows = [r for r in range(rows) if r not in edge_rows]
    shape = (chunks, lanes)
    look_up = table_lookup(color_word_ref, opacity_word_ref)
    column_difference = column_differences(shape)
    light = [light_ref[i] for i in range(3)]
    together = 2 if bricks % 2 == 0 else 1

    def step(trip, carry):
        colors, keeps = list(carry[0]), list(carry[1])
        at = [brick_at[trip * together + u] for u in range(together)]
        fields = [[[tile_ref[b, r, k] for k in range(depth)] for r in range(padded_rows)] for b in at]
        kept = []
        for b, field in zip(at, fields):
            for r in range(rows):
                for k, dz in enumerate(depth_differences(field[r + 1])):
                    x = field[r + 1][k]
                    dx = column_difference(x)
                    color, opacity = look_up(x)
                    weight = keeps[r] * opacity
                    facing = dz * light[0] + dx * light[2]
                    squared = dz * dz + dx * dx + 1.0
                    if r in edge_rows:
                        values = [weight * color[c] for c in range(3)] + [facing, squared]
                        kept.append((b, edge_rows.index(r), k, values))
                    else:
                        i = inner_rows.index(r)
                        dy = field[r + 2][k] - field[r][k]
                        shaded = weight * shading_of(facing + dy * light[1], squared + dy * dy)
                        for c in range(3):
                            slot = c * len(inner_rows) + i
                            colors[slot] = colors[slot] + shaded * color[c]
                    keeps[r] = keeps[r] - weight
        for b, i, k, values in kept:
            for v, value in enumerate(values):
                part_ref[b, i, k, v] = value
        return tuple(colors), tuple(keeps)

    zero, one = jnp.zeros(shape, jnp.float32), jnp.ones(shape, jnp.float32)
    colors, keeps = lax.fori_loop(
        0, bricks // together, step, ((zero,) * (3 * len(inner_rows)), (one,) * rows))
    for i, value in enumerate(colors):
        color_sum_ref[i] = value
    for r, value in enumerate(keeps):
        keep_ref[r] = value


def finish_kernel(edge_rows, end_ref, light_ref, tile_ref, other_ref, part_ref, color_sum_ref, keep_ref,
                  out_ref, staged):
    bricks, padded_rows, depth, chunks, lanes = tile_ref.shape
    rows = padded_rows - 2
    inner_rows = [r for r in range(rows) if r not in edge_rows]
    shape = (chunks, lanes)
    light_rows = light_ref[1]
    is_first, is_last = end_ref[0] == 1, end_ref[1] == 1

    together = 4 if bricks % 4 == 0 else 1

    def step(trip, colors):
        colors = list(colors)
        for u in range(together):
            b = trip * together + u
            for i, r in enumerate(edge_rows):
                for k in range(depth):
                    above, below = tile_ref[b, r, k], tile_ref[b, r + 2, k]
                    if r == 0:
                        above = jnp.where(is_first, other_ref[b, k], above)
                    if r == rows - 1:
                        below = jnp.where(is_last, other_ref[b, k], below)
                    dy = below - above
                    facing = part_ref[b, i, k, 3] + dy * light_rows
                    shading = shading_of(facing, part_ref[b, i, k, 4] + dy * dy)
                    for c in range(3):
                        slot = c * len(edge_rows) + i
                        colors[slot] = colors[slot] + shading * part_ref[b, i, k, c]
        return tuple(colors)

    zero = jnp.zeros(shape, jnp.float32)
    edge_colors = lax.fori_loop(0, bricks // together, step, (zero,) * (3 * len(edge_rows)))
    for r in range(rows):
        for c in range(3):
            if r in edge_rows:
                value = edge_colors[c * len(edge_rows) + edge_rows.index(r)]
            else:
                value = color_sum_ref[c * len(inner_rows) + inner_rows.index(r)]
            at = (c * rows + r) * chunks
            staged[at:at + chunks, :] = value * (COLOR_SPAN / COLOR_UNIT)
        at = (3 * rows + r) * chunks
        staged[at:at + chunks, :] = 1.0 - keep_ref[r]
    for c in range(4):
        for q in range(chunks):
            source = pl.ds(c * rows * chunks + q, rows, stride=chunks) if rows > 1 else pl.ds(c * chunks + q, 1)
            out_ref[c, 0, :, q * LANES:(q + 1) * LANES] = staged[source, :]


def shards(scalar, bin_index, color_table, opacity_table, light_dir, view_order):
    depth, rows, cols = scalar.shape
    bricks, bands = lax.axis_size("gz"), lax.axis_size("gy")
    tile_rows = rows // bricks
    chunks = cols // LANES
    edge_rows = sorted({0, tile_rows - 1})
    inner_count = tile_rows - len(edge_rows)
    tiles = lax.all_to_all(
        packed(scalar, bricks), "gz", split_axis=0, concat_axis=0, tiled=True,
        axis_index_groups=[exchange_order(bricks)])

    here = lax.axis_index("gz")
    ends = jnp.stack([here == 0, here == bricks - 1]).astype(jnp.int32)
    last = bricks - 1
    pairs = [(g, g + 1) for g in range(bands - 1)]
    pairs += [(last * bands + g + 1, last * bands + g) for g in range(bands - 1)]

    vmem = pl.BlockSpec(memory_space=pltpu.VMEM)
    smem = pl.BlockSpec(memory_space=pltpu.SMEM)
    params = pltpu.CompilerParams(vmem_limit_bytes=32 << 20)
    cells = bricks * depth * cols
    lines = (chunks, LANES)
    halves = (color_table.shape[1] - 1) // LANES
    brick_at, color_words, opacity_words, light_rows, end_rows = pl.pallas_call(
        prepare_kernel,
        out_shape=[
            pltpu.SMEM((bricks,), jnp.int32),
            jax.ShapeDtypeStruct((3, halves) + lines, jnp.float32),
            jax.ShapeDtypeStruct((halves,) + lines, jnp.int32),
            jax.ShapeDtypeStruct((3,) + lines, jnp.float32),
            jax.ShapeDtypeStruct((2,) + lines, jnp.int32),
        ],
        in_specs=[smem, smem, smem, vmem, vmem],
        out_specs=[smem] + [vmem] * 4,
        compiler_params=params,
        name="prepare_tables",
    )(ends, view_order, light_dir, color_table, opacity_table[None, :])
    wrapped = jnp.where(end_rows[0] == 1, tiles[:, 0], tiles[:, -1])
    other = lax.ppermute(wrapped, ("gz", "gy"), pairs)
    parts, color_sums, keeps = pl.pallas_call(
        functools.partial(main_kernel, edge_rows),
        out_shape=[
            jax.ShapeDtypeStruct((bricks, len(edge_rows), depth, 5, chunks, LANES), jnp.float32),
            jax.ShapeDtypeStruct((max(3 * inner_count, 1), chunks, LANES), jnp.float32),
            jax.ShapeDtypeStruct((tile_rows, chunks, LANES), jnp.float32),
        ],
        in_specs=[smem] + [vmem] * 4,
        out_specs=[vmem, vmem, vmem],
        compiler_params=params,
        cost_estimate=pl.CostEstimate(
            flops=100 * cells * tile_rows, bytes_accessed=24 * cells * tile_rows, transcendentals=0),
        name="main_rows",
    )(brick_at, light_rows, color_words, opacity_words, tiles)
    return pl.pallas_call(
        functools.partial(finish_kernel, edge_rows),
        out_shape=jax.ShapeDtypeStruct((4, 1, tile_rows, cols), jnp.float32),
        in_specs=[vmem] * 7,
        out_specs=vmem,
        scratch_shapes=[pltpu.VMEM((4 * tile_rows * chunks, LANES), jnp.float32)],
        compiler_params=params,
        cost_estimate=pl.CostEstimate(
            flops=10 * cells * tile_rows, bytes_accessed=24 * cells * tile_rows, transcendentals=0),
        name="edge_rows",
    )(end_rows, light_rows, tiles, other, parts, color_sums, keeps)


def solution(mesh):
    in_specs = (P("gz", "gy", None), P("gz", "gy", None), P(), P(), P(), P())
    out_specs = P(None, "gy", "gz", None)
    return jax.shard_map(shards, mesh=mesh, in_specs=in_specs, out_specs=out_specs, check_vma=False)
```

```python
import functools

import jax
import jax.numpy as jnp
from jax import lax
from jax.experimental import pallas as pl
from jax.experimental.pallas import tpu as pltpu
from jax.sharding import PartitionSpec as P

SUB, LANES = 8, 128
COLOR_UNIT, COLOR_SPAN = 2 ** 11, 2 ** 12
OPACITY_UNIT, OPACITY_BITS = 2 ** 18, 16
OPACITY_SPAN = 2 ** OPACITY_BITS


def exchange_order(tiles):
    flip = tiles - tiles // 4 if tiles & (tiles - 1) == 0 else 0
    return [t ^ flip for t in range(tiles)]


def pack_kernel(field_ref, out_ref, staged):
    depth, rows, cols = field_ref.shape
    tiles, padded_rows, _, chunks, _ = out_ref.shape
    tile_rows = padded_rows - 2
    block = depth * chunks

    for k in range(depth):
        for j in range(rows // SUB):
            lines = [field_ref[k, j * SUB:(j + 1) * SUB, c * LANES:(c + 1) * LANES] for c in range(chunks)]
            for c, value in enumerate(lines):
                staged[pl.ds(j * SUB * block + k * chunks + c, SUB, stride=block), :] = value
    for place, t in enumerate(exchange_order(tiles)):
        starts = [((t * tile_rows + i - 1) % rows) * block for i in range(padded_rows)]
        blocks = [staged[start:start + block, :] for start in starts]
        for i, value in enumerate(blocks):
            for k in range(depth):
                out_ref[place, i, k] = value[k * chunks:(k + 1) * chunks]


def packed(field, tiles):
    depth, rows, cols = field.shape
    chunks = cols // LANES
    vmem = pl.BlockSpec(memory_space=pltpu.VMEM)
    shape = (tiles, rows // tiles + 2, depth, chunks, LANES)
    return pl.pallas_call(
        pack_kernel,
        out_shape=pltpu.VMEM(shape, field.dtype),
        in_specs=[vmem],
        out_specs=vmem,
        scratch_shapes=[pltpu.VMEM((rows * depth * chunks, LANES), field.dtype)],
        compiler_params=pltpu.CompilerParams(vmem_limit_bytes=16 << 20),
        name="pack_rows",
    )(field)


def shifted(x, axis, shift):
    return pltpu.roll(x, shift % x.shape[axis], axis)


def prepare_kernel(bands_end_ref, order_ref, light_ref, color_ref, opacity_ref,
                   brick_at_ref, color_word_ref, opacity_word_ref, light_rows_ref, end_ref):
    bins = color_ref.shape[1] - 1
    _, halves, chunks, lanes = color_word_ref.shape
    shape = (chunks, lanes)

    def parts(values, unit):
        scaled = values.astype(jnp.float32) * float(unit)
        return scaled[:, :bins], scaled[:, 1:] - scaled[:, :bins]

    low, slope = parts(color_ref[...], COLOR_UNIT)
    color_words = slope + low * (1.0 / COLOR_SPAN)
    low, slope = parts(opacity_ref[...], OPACITY_UNIT)
    opacity_words = slope.astype(jnp.int32) * OPACITY_SPAN + low.astype(jnp.int32)
    for h in range(halves):
        span = slice(h * lanes, (h + 1) * lanes)
        for c in range(3):
            color_word_ref[c, h] = jnp.broadcast_to(color_words[c:c + 1, span], shape)
        opacity_word_ref[h] = jnp.broadcast_to(opacity_words[:, span], shape)
    for i in range(3):
        light_rows_ref[i] = jnp.full(shape, light_ref[i], jnp.float32)
    for i in range(2):
        end_ref[i] = jnp.full(shape, bands_end_ref[i], jnp.int32)
    for place, b in enumerate(exchange_order(order_ref.shape[0])):
        brick_at_ref[order_ref[b]] = place


def table_lookup(color_word_ref, opacity_word_ref):
    _, halves, _, lanes = color_word_ref.shape
    bins = halves * lanes

    def look_up(x):
        scaled = x * float(bins)
        index = jnp.minimum(scaled.astype(jnp.int32), bins - 1)
        fraction = scaled - index.astype(jnp.float32)
        low_bits = index & (lanes - 1)

        def gathered(table):
            found = [jnp.take_along_axis(t, low_bits, axis=1, mode="promise_in_bounds") for t in table]
            word = found[0]
            for h in range(1, halves):
                word = jnp.where(index >= h * lanes, found[h], word)
            return word

        color = []
        small = fraction * (1.0 / COLOR_SPAN)
        for c in range(3):
            word = gathered([color_word_ref[c, h] for h in range(halves)])
            rise = jnp.floor(word)
            color.append((word - rise) + small * rise)
        word = gathered([opacity_word_ref[h] for h in range(halves)])
        rise = (word >> OPACITY_BITS).astype(jnp.float32)
        start = (word & (OPACITY_SPAN - 1)).astype(jnp.float32)
        return color, (start + fraction * rise) * (1.0 / OPACITY_UNIT)

    return look_up


def column_differences(shape):
    lane = lax.broadcasted_iota(jnp.int32, shape, 1)
    chunk = lax.broadcasted_iota(jnp.int32, shape, 0)
    at_first, at_last = lane == 0, lane == shape[1] - 1
    at_left = at_first & (chunk == 0)
    at_right = at_last & (chunk == shape[0] - 1)

    def difference(x):
        right = shifted(x, 1, -1)
        right = jnp.where(at_last, shifted(right, 0, -1), right)
        right = jnp.where(at_right, 0.0, right)
        left = shifted(x, 1, 1)
        left = jnp.where(at_first, shifted(left, 0, 1), left)
        left = jnp.where(at_left, 0.0, left)
        return right - left

    return difference


def depth_differences(field):
    last = len(field) - 1
    made = {}
    for k in range(last + 1):
        ends = (min(k + 1, last), max(k - 1, 0))
        if ends not in made:
            made[ends] = field[ends[0]] - field[ends[1]]
    return [made[(min(k + 1, last), max(k - 1, 0))] for k in range(last + 1)]


def shading_of(facing, squared_plus_one):
    near = pltpu.reciprocal(squared_plus_one, approx=True)
    inverse = near * (2.0 - squared_plus_one * near)
    return 0.25 + (0.75 * facing) * (facing * inverse)


def main_kernel(edge_rows, brick_at, light_ref, color_word_ref, opacity_word_ref, tile_ref,
                part_ref, color_sum_ref, keep_ref):
    bricks, padded_rows, depth, chunks, lanes = tile_ref.shape
    rows = padded_rows - 2
    inner_rows = [r for r in range(rows) if r not in edge_rows]
    shape = (chunks, lanes)
    look_up = table_lookup(color_word_ref, opacity_word_ref)
    column_difference = column_differences(shape)
    light = [light_ref[i] for i in range(3)]
    together = 2 if bricks % 2 == 0 else 1

    def step(trip, carry):
        colors, keeps = list(carry[0]), list(carry[1])
        at = [brick_at[trip * together + u] for u in range(together)]
        fields = [[[tile_ref[b, r, k] for k in range(depth)] for r in range(padded_rows)] for b in at]
        kept = []
        for b, field in zip(at, fields):
            for r in range(rows):
                for k, dz in enumerate(depth_differences(field[r + 1])):
                    x = field[r + 1][k]
                    dx = column_difference(x)
                    color, opacity = look_up(x)
                    weight = keeps[r] * opacity
                    facing = dz * light[0] + dx * light[2]
                    squared = dz * dz + dx * dx + 1.0
                    if r in edge_rows:
                        values = [weight * color[c] for c in range(3)] + [facing, squared]
                        kept.append((b, edge_rows.index(r), k, values))
                    else:
                        i = inner_rows.index(r)
                        dy = field[r + 2][k] - field[r][k]
                        shaded = weight * shading_of(facing + dy * light[1], squared + dy * dy)
                        for c in range(3):
                            slot = c * len(inner_rows) + i
                            colors[slot] = colors[slot] + shaded * color[c]
                    keeps[r] = keeps[r] - weight
        for b, i, k, values in kept:
            for v, value in enumerate(values):
                part_ref[b, i, k, v] = value
        return tuple(colors), tuple(keeps)

    zero, one = jnp.zeros(shape, jnp.float32), jnp.ones(shape, jnp.float32)
    colors, keeps = lax.fori_loop(
        0, bricks // together, step, ((zero,) * (3 * len(inner_rows)), (one,) * rows))
    for i, value in enumerate(colors):
        color_sum_ref[i] = value
    for r, value in enumerate(keeps):
        keep_ref[r] = value


def finish_kernel(edge_rows, end_ref, light_ref, tile_ref, other_ref, part_ref, color_sum_ref, keep_ref,
                  out_ref, staged):
    bricks, padded_rows, depth, chunks, lanes = tile_ref.shape
    rows = padded_rows - 2
    inner_rows = [r for r in range(rows) if r not in edge_rows]
    shape = (chunks, lanes)
    light_rows = light_ref[1]
    is_first, is_last = end_ref[0] == 1, end_ref[1] == 1

    together = 4 if bricks % 4 == 0 else 1

    def step(trip, colors):
        colors = list(colors)
        for u in range(together):
            b = trip * together + u
            for i, r in enumerate(edge_rows):
                for k in range(depth):
                    above, below = tile_ref[b, r, k], tile_ref[b, r + 2, k]
                    if r == 0:
                        above = jnp.where(is_first, other_ref[b, k], above)
                    if r == rows - 1:
                        below = jnp.where(is_last, other_ref[b, k], below)
                    dy = below - above
                    facing = part_ref[b, i, k, 3] + dy * light_rows
                    shading = shading_of(facing, part_ref[b, i, k, 4] + dy * dy)
                    for c in range(3):
                        slot = c * len(edge_rows) + i
                        colors[slot] = colors[slot] + shading * part_ref[b, i, k, c]
        return tuple(colors)

    zero = jnp.zeros(shape, jnp.float32)
    edge_colors = lax.fori_loop(0, bricks // together, step, (zero,) * (3 * len(edge_rows)))
    for r in range(rows):
        for c in range(3):
            if r in edge_rows:
                value = edge_colors[c * len(edge_rows) + edge_rows.index(r)]
            else:
                value = color_sum_ref[c * len(inner_rows) + inner_rows.index(r)]
            at = (c * rows + r) * chunks
            staged[at:at + chunks, :] = value * (COLOR_SPAN / COLOR_UNIT)
        at = (3 * rows + r) * chunks
        staged[at:at + chunks, :] = 1.0 - keep_ref[r]
    for c in range(4):
        for q in range(chunks):
            source = pl.ds(c * rows * chunks + q, rows, stride=chunks) if rows > 1 else pl.ds(c * chunks + q, 1)
            out_ref[c, 0, :, q * LANES:(q + 1) * LANES] = staged[source, :]


def shards(scalar, bin_index, color_table, opacity_table, light_dir, view_order):
    depth, rows, cols = scalar.shape
    bricks, bands = lax.axis_size("gz"), lax.axis_size("gy")
    tile_rows = rows // bricks
    chunks = cols // LANES
    edge_rows = sorted({0, tile_rows - 1})
    inner_count = tile_rows - len(edge_rows)
    tiles = lax.all_to_all(
        packed(scalar, bricks), "gz", split_axis=0, concat_axis=0, tiled=True,
        axis_index_groups=[exchange_order(bricks)])

    here = lax.axis_index("gz")
    ends = jnp.stack([here == 0, here == bricks - 1]).astype(jnp.int32)
    last = bricks - 1
    pairs = [(g, g + 1) for g in range(bands - 1)]
    pairs += [(last * bands + g + 1, last * bands + g) for g in range(bands - 1)]

    vmem = pl.BlockSpec(memory_space=pltpu.VMEM)
    smem = pl.BlockSpec(memory_space=pltpu.SMEM)
    params = pltpu.CompilerParams(vmem_limit_bytes=32 << 20)
    cells = bricks * depth * cols
    lines = (chunks, LANES)
    halves = (color_table.shape[1] - 1) // LANES
    brick_at, color_words, opacity_words, light_rows, end_rows = pl.pallas_call(
        prepare_kernel,
        out_shape=[
            pltpu.SMEM((bricks,), jnp.int32),
            jax.ShapeDtypeStruct((3, halves) + lines, jnp.float32),
            jax.ShapeDtypeStruct((halves,) + lines, jnp.int32),
            jax.ShapeDtypeStruct((3,) + lines, jnp.float32),
            jax.ShapeDtypeStruct((2,) + lines, jnp.int32),
        ],
        in_specs=[smem, smem, smem, vmem, vmem],
        out_specs=[smem] + [vmem] * 4,
        compiler_params=params,
        name="prepare_tables",
    )(ends, view_order, light_dir, color_table, opacity_table[None, :])
    wrapped = jnp.where(end_rows[0] == 1, tiles[:, 0], tiles[:, -1])
    other = lax.ppermute(wrapped, ("gz", "gy"), pairs)
    parts, color_sums, keeps = pl.pallas_call(
        functools.partial(main_kernel, edge_rows),
        out_shape=[
            jax.ShapeDtypeStruct((bricks, len(edge_rows), depth, 5, chunks, LANES), jnp.float32),
            jax.ShapeDtypeStruct((max(3 * inner_count, 1), chunks, LANES), jnp.float32),
            jax.ShapeDtypeStruct((tile_rows, chunks, LANES), jnp.float32),
        ],
        in_specs=[smem] + [vmem] * 4,
        out_specs=[vmem, vmem, vmem],
        compiler_params=params,
        cost_estimate=pl.CostEstimate(
            flops=100 * cells * tile_rows, bytes_accessed=24 * cells * tile_rows, transcendentals=0),
        name="main_rows",
    )(brick_at, light_rows, color_words, opacity_words, tiles)
    return pl.pallas_call(
        functools.partial(finish_kernel, edge_rows),
        out_shape=jax.ShapeDtypeStruct((4, 1, tile_rows, cols), jnp.float32),
        in_specs=[vmem] * 7,
        out_specs=vmem,
        scratch_shapes=[pltpu.VMEM((4 * tile_rows * chunks, LANES), jnp.float32)],
        compiler_params=params,
        cost_estimate=pl.CostEstimate(
            flops=10 * cells * tile_rows, bytes_accessed=24 * cells * tile_rows, transcendentals=0),
        name="edge_rows",
    )(end_rows, light_rows, tiles, other, parts, color_sums, keeps)


def solution(mesh):
    in_specs = (P("gz", "gy", None), P("gz", "gy", None), P(), P(), P(), P())
    out_specs = P(None, "gy", "gz", None)
    return jax.shard_map(shards, mesh=mesh, in_specs=in_specs, out_specs=out_specs, check_vma=False)
```

```python
import functools
import math

import jax
import jax.numpy as jnp
from jax import lax
from jax.experimental import pallas as pl
from jax.experimental.pallas import tpu as pltpu
from jax.sharding import PartitionSpec as P

SUB, LANES = 8, 128
COLOR_UNIT, COLOR_SPAN = 2 ** 11, 2 ** 12
OPACITY_UNIT, OPACITY_BITS = 2 ** 18, 16
OPACITY_SPAN = 2 ** OPACITY_BITS


def exchange_order(tiles):
    flip = tiles - tiles // 4 if tiles & (tiles - 1) == 0 else 0
    return [t ^ flip for t in range(tiles)]


def pack_kernel(tiles, field_ref, out_ref, field, spread, in_sems, out_sems):
    depth, rows, cols = field_ref.shape
    chunks = cols // LANES
    block = depth * chunks
    tile_rows = rows // tiles
    pieces = in_sems.shape[0]
    piece_rows = rows // pieces
    order = exchange_order(tiles)

    def copy_in(p):
        part = pl.ds(p * piece_rows, piece_rows)
        return pltpu.make_async_copy(field_ref.at[:, part], field.at[:, part], in_sems.at[p])

    def copy_out(t):
        part = spread.at[pl.ds(t * tile_rows * block, (tile_rows + 2) * block)]
        return pltpu.make_async_copy(part, out_ref.at[order.index(t)], out_sems.at[t])

    for p in range(pieces):
        copy_in(p).start()
    started = 0
    for p in range(pieces):
        copy_in(p).wait()
        for k in range(depth):
            for row in range(p * piece_rows, (p + 1) * piece_rows, SUB):
                lines = [field[k, row:row + SUB, c * LANES:(c + 1) * LANES] for c in range(chunks)]
                for c, value in enumerate(lines):
                    spread[pl.ds((row + 1) * block + k * chunks + c, SUB, stride=block), :] = value
        if p == 0:
            spread[(rows + 1) * block:, :] = spread[block:2 * block, :]
        if p == pieces - 1:
            spread[:block, :] = spread[rows * block:(rows + 1) * block, :]
        ready = [t for t in range(1, tiles) if (t + 1) * tile_rows < (p + 1) * piece_rows]
        if p == pieces - 1:
            ready = list(range(1, tiles)) + [0]
        for t in ready[started:]:
            copy_out(t).start()
        started = len(ready)
    for t in range(tiles):
        copy_out(t).wait()


def packed(field, tiles):
    depth, rows, cols = field.shape
    chunks = cols // LANES
    padded_rows = rows // tiles + 2
    pieces = 4 if rows % (4 * SUB) == 0 else 1
    hbm = pl.BlockSpec(memory_space=pltpu.HBM)
    flat = pl.pallas_call(
        functools.partial(pack_kernel, tiles),
        out_shape=jax.ShapeDtypeStruct((tiles, padded_rows * depth * chunks, LANES), field.dtype),
        in_specs=[hbm],
        out_specs=hbm,
        scratch_shapes=[
            pltpu.VMEM((depth, rows, cols), field.dtype),
            pltpu.VMEM(((rows + 2) * depth * chunks, LANES), field.dtype),
            pltpu.SemaphoreType.DMA((pieces,)),
            pltpu.SemaphoreType.DMA((tiles,)),
        ],
        compiler_params=pltpu.CompilerParams(vmem_limit_bytes=16 << 20),
        name="pack_rows",
    )(field)
    return flat.reshape(tiles, padded_rows, depth, chunks, LANES)


def shifted(x, axis, shift):
    return pltpu.roll(x, shift % x.shape[axis], axis)


def prepare_kernel(bands_end_ref, order_ref, light_ref, color_ref, opacity_ref,
                   brick_at_ref, color_word_ref, opacity_word_ref, light_rows_ref, end_ref):
    bins = color_ref.shape[1] - 1
    _, halves, chunks, lanes = color_word_ref.shape
    shape = (chunks, lanes)

    def parts(values, unit):
        scaled = values.astype(jnp.float32) * float(unit)
        return scaled[:, :bins], scaled[:, 1:] - scaled[:, :bins]

    low, slope = parts(color_ref[...], COLOR_UNIT)
    color_words = slope + low * (1.0 / COLOR_SPAN)
    low, slope = parts(opacity_ref[...], OPACITY_UNIT)
    opacity_words = slope.astype(jnp.int32) * OPACITY_SPAN + low.astype(jnp.int32)
    for h in range(halves):
        span = slice(h * lanes, (h + 1) * lanes)
        for c in range(3):
            color_word_ref[c, h] = jnp.broadcast_to(color_words[c:c + 1, span], shape)
        opacity_word_ref[h] = jnp.broadcast_to(opacity_words[:, span], shape)
    for i in range(3):
        light_rows_ref[i] = jnp.full(shape, light_ref[i], jnp.float32) * math.sqrt(0.75)
    for i in range(2):
        end_ref[i] = jnp.full(shape, bands_end_ref[i], jnp.int32)
    for place, b in enumerate(exchange_order(order_ref.shape[0])):
        brick_at_ref[order_ref[b]] = place


def table_lookup(color_word_ref, opacity_word_ref):
    _, halves, _, lanes = color_word_ref.shape
    bins = halves * lanes

    def look_up(x):
        scaled = x * float(bins)
        index = jnp.minimum(scaled.astype(jnp.int32), bins - 1)
        fraction = scaled - index.astype(jnp.float32)
        low_bits = index & (lanes - 1)

        def gathered(table):
            found = [jnp.take_along_axis(t, low_bits, axis=1, mode="promise_in_bounds") for t in table]
            word = found[0]
            for h in range(1, halves):
                word = jnp.where(index >= h * lanes, found[h], word)
            return word

        color = []
        small = fraction * (1.0 / COLOR_SPAN)
        for c in range(3):
            word = gathered([color_word_ref[c, h] for h in range(halves)])
            rise = jnp.floor(word)
            color.append((word - rise) + small * rise)
        word = gathered([opacity_word_ref[h] for h in range(halves)])
        rise = (word >> OPACITY_BITS).astype(jnp.float32)
        start = (word & (OPACITY_SPAN - 1)).astype(jnp.float32)
        return color, (start + fraction * rise) * (1.0 / OPACITY_UNIT)

    return look_up


def column_differences(shape):
    lane = lax.broadcasted_iota(jnp.int32, shape, 1)
    chunk = lax.broadcasted_iota(jnp.int32, shape, 0)
    at_first, at_last = lane == 0, lane == shape[1] - 1
    at_left = at_first & (chunk == 0)
    at_right = at_last & (chunk == shape[0] - 1)

    def difference(x):
        right = shifted(x, 1, -1)
        right = jnp.where(at_last, shifted(right, 0, -1), right)
        right = jnp.where(at_right, 0.0, right)
        left = shifted(x, 1, 1)
        left = jnp.where(at_first, shifted(left, 0, 1), left)
        left = jnp.where(at_left, 0.0, left)
        return right - left

    return difference


def depth_differences(field):
    last = len(field) - 1
    made = {}
    for k in range(last + 1):
        ends = (min(k + 1, last), max(k - 1, 0))
        if ends not in made:
            made[ends] = field[ends[0]] - field[ends[1]]
    return [made[(min(k + 1, last), max(k - 1, 0))] for k in range(last + 1)]


def shading_of(facing, squared_plus_one):
    near = pltpu.reciprocal(squared_plus_one, approx=True)
    inverse = near * (2.0 - squared_plus_one * near)
    return 0.25 + (facing * facing) * inverse


def main_kernel(edge_rows, brick_at, light_ref, color_word_ref, opacity_word_ref, tile_ref,
                part_ref, color_sum_ref, keep_ref):
    bricks, padded_rows, depth, chunks, lanes = tile_ref.shape
    rows = padded_rows - 2
    inner_rows = [r for r in range(rows) if r not in edge_rows]
    shape = (chunks, lanes)
    look_up = table_lookup(color_word_ref, opacity_word_ref)
    column_difference = column_differences(shape)
    light = [light_ref[i] for i in range(3)]
    together = 4 if bricks % 4 == 0 else 1

    def step(trip, carry):
        colors, keeps = list(carry[0]), list(carry[1])
        at = [brick_at[trip * together + u] for u in range(together)]
        fields = [[[tile_ref[b, r, k] for k in range(depth)] for r in range(padded_rows)] for b in at]
        kept = []
        for b, field in zip(at, fields):
            for r in range(rows):
                for k, dz in enumerate(depth_differences(field[r + 1])):
                    x = field[r + 1][k]
                    dx = column_difference(x)
                    color, opacity = look_up(x)
                    weight = keeps[r] * opacity
                    facing = dz * light[0] + dx * light[2]
                    squared = dz * dz + dx * dx + 1.0
                    if r in edge_rows:
                        values = [weight * color[c] for c in range(3)] + [facing, squared]
                        kept.append((b, edge_rows.index(r), k, values))
                    else:
                        i = inner_rows.index(r)
                        dy = field[r + 2][k] - field[r][k]
                        shaded = weight * shading_of(facing + dy * light[1], squared + dy * dy)
                        for c in range(3):
                            slot = c * len(inner_rows) + i
                            colors[slot] = colors[slot] + shaded * color[c]
                    keeps[r] = keeps[r] - weight
        for b, i, k, values in kept:
            for v, value in enumerate(values):
                part_ref[b, i, k, v] = value
        return tuple(colors), tuple(keeps)

    zero, one = jnp.zeros(shape, jnp.float32), jnp.ones(shape, jnp.float32)
    colors, keeps = lax.fori_loop(
        0, bricks // together, step, ((zero,) * (3 * len(inner_rows)), (one,) * rows))
    for i, value in enumerate(colors):
        color_sum_ref[i] = value
    for r, value in enumerate(keeps):
        keep_ref[r] = value


def finish_kernel(edge_rows, end_ref, light_ref, tile_ref, other_ref, part_ref, color_sum_ref, keep_ref,
                  out_ref, staged):
    bricks, padded_rows, depth, chunks, lanes = tile_ref.shape
    rows = padded_rows - 2
    inner_rows = [r for r in range(rows) if r not in edge_rows]
    shape = (chunks, lanes)
    light_rows = light_ref[1]
    is_first, is_last = end_ref[0] == 1, end_ref[1] == 1

    together = 8 if bricks % 8 == 0 else 1

    def step(trip, colors):
        colors = list(colors)
        for u in range(together):
            b = trip * together + u
            for i, r in enumerate(edge_rows):
                for k in range(depth):
                    above, below = tile_ref[b, r, k], tile_ref[b, r + 2, k]
                    if r == 0:
                        above = jnp.where(is_first, other_ref[b, k], above)
                    if r == rows - 1:
                        below = jnp.where(is_last, other_ref[b, k], below)
                    dy = below - above
                    facing = part_ref[b, i, k, 3] + dy * light_rows
                    shading = shading_of(facing, part_ref[b, i, k, 4] + dy * dy)
                    for c in range(3):
                        slot = c * len(edge_rows) + i
                        colors[slot] = colors[slot] + shading * part_ref[b, i, k, c]
        return tuple(colors)

    zero = jnp.zeros(shape, jnp.float32)
    edge_colors = lax.fori_loop(0, bricks // together, step, (zero,) * (3 * len(edge_rows)))
    for r in range(rows):
        for c in range(3):
            if r in edge_rows:
                value = edge_colors[c * len(edge_rows) + edge_rows.index(r)]
            else:
                value = color_sum_ref[c * len(inner_rows) + inner_rows.index(r)]
            at = (c * rows + r) * chunks
            staged[at:at + chunks, :] = value * (COLOR_SPAN / COLOR_UNIT)
        at = (3 * rows + r) * chunks
        staged[at:at + chunks, :] = 1.0 - keep_ref[r]
    for c in range(4):
        for q in range(chunks):
            source = pl.ds(c * rows * chunks + q, rows, stride=chunks) if rows > 1 else pl.ds(c * chunks + q, 1)
            out_ref[c, 0, :, q * LANES:(q + 1) * LANES] = staged[source, :]


def shards(scalar, bin_index, color_table, opacity_table, light_dir, view_order):
    depth, rows, cols = scalar.shape
    bricks, bands = lax.axis_size("gz"), lax.axis_size("gy")
    tile_rows = rows // bricks
    chunks = cols // LANES
    edge_rows = sorted({0, tile_rows - 1})
    inner_count = tile_rows - len(edge_rows)
    tiles = lax.all_to_all(
        packed(scalar, bricks), "gz", split_axis=0, concat_axis=0, tiled=True,
        axis_index_groups=[exchange_order(bricks)])

    here = lax.axis_index("gz")
    ends = jnp.stack([here == 0, here == bricks - 1]).astype(jnp.int32)
    last = bricks - 1
    pairs = [(g, g + 1) for g in range(bands - 1)]
    pairs += [(last * bands + g + 1, last * bands + g) for g in range(bands - 1)]

    vmem = pl.BlockSpec(memory_space=pltpu.VMEM)
    smem = pl.BlockSpec(memory_space=pltpu.SMEM)
    params = pltpu.CompilerParams(vmem_limit_bytes=32 << 20)
    cells = bricks * depth * cols
    lines = (chunks, LANES)
    halves = (color_table.shape[1] - 1) // LANES
    brick_at, color_words, opacity_words, light_rows, end_rows = pl.pallas_call(
        prepare_kernel,
        out_shape=[
            pltpu.SMEM((bricks,), jnp.int32),
            jax.ShapeDtypeStruct((3, halves) + lines, jnp.float32),
            jax.ShapeDtypeStruct((halves,) + lines, jnp.int32),
            jax.ShapeDtypeStruct((3,) + lines, jnp.float32),
            jax.ShapeDtypeStruct((2,) + lines, jnp.int32),
        ],
        in_specs=[smem, smem, smem, vmem, vmem],
        out_specs=[smem] + [vmem] * 4,
        compiler_params=params,
        name="prepare_tables",
    )(ends, view_order, light_dir, color_table, opacity_table[None, :])
    wrapped = jnp.where(end_rows[0] == 1, tiles[:, 0], tiles[:, -1])
    other = lax.ppermute(wrapped, ("gz", "gy"), pairs)
    parts, color_sums, keeps = pl.pallas_call(
        functools.partial(main_kernel, edge_rows),
        out_shape=[
            jax.ShapeDtypeStruct((bricks, len(edge_rows), depth, 5, chunks, LANES), jnp.float32),
            jax.ShapeDtypeStruct((max(3 * inner_count, 1), chunks, LANES), jnp.float32),
            jax.ShapeDtypeStruct((tile_rows, chunks, LANES), jnp.float32),
        ],
        in_specs=[smem] + [vmem] * 4,
        out_specs=[vmem, vmem, vmem],
        compiler_params=params,
        cost_estimate=pl.CostEstimate(
            flops=100 * cells * tile_rows, bytes_accessed=24 * cells * tile_rows, transcendentals=0),
        name="main_rows",
    )(brick_at, light_rows, color_words, opacity_words, tiles)
    return pl.pallas_call(
        functools.partial(finish_kernel, edge_rows),
        out_shape=jax.ShapeDtypeStruct((4, 1, tile_rows, cols), jnp.float32),
        in_specs=[vmem] * 7,
        out_specs=vmem,
        scratch_shapes=[pltpu.VMEM((4 * tile_rows * chunks, LANES), jnp.float32)],
        compiler_params=params,
        cost_estimate=pl.CostEstimate(
            flops=10 * cells * tile_rows, bytes_accessed=24 * cells * tile_rows, transcendentals=0),
        name="edge_rows",
    )(end_rows, light_rows, tiles, other, parts, color_sums, keeps)


def solution(mesh):
    in_specs = (P("gz", "gy", None), P("gz", "gy", None), P(), P(), P(), P())
    out_specs = P(None, "gy", "gz", None)
    return jax.shard_map(shards, mesh=mesh, in_specs=in_specs, out_specs=out_specs, check_vma=False)
```

```python
import functools
import math

import jax
import jax.numpy as jnp
from jax import lax
from jax.experimental import pallas as pl
from jax.experimental.pallas import tpu as pltpu
from jax.sharding import PartitionSpec as P

SUB, LANES = 8, 128
COLOR_UNIT, COLOR_SPAN = 2 ** 11, 2 ** 12
OPACITY_UNIT, OPACITY_BITS = 2 ** 18, 16
OPACITY_SPAN = 2 ** OPACITY_BITS


def exchange_order(tiles):
    flip = tiles - tiles // 4 if tiles & (tiles - 1) == 0 else 0
    return [t ^ flip for t in range(tiles)]


def pack_kernel(tiles, field_ref, out_ref, field, spread, in_sems, out_sems):
    depth, rows, cols = field_ref.shape
    chunks = cols // LANES
    block = depth * chunks
    tile_rows = rows // tiles
    pieces = in_sems.shape[0]
    piece_rows = rows // pieces
    order = exchange_order(tiles)

    def copy_in(p):
        part = pl.ds(p * piece_rows, piece_rows)
        return pltpu.make_async_copy(field_ref.at[:, part], field.at[:, part], in_sems.at[p])

    def copy_out(t):
        part = spread.at[pl.ds(t * tile_rows * block, (tile_rows + 2) * block)]
        return pltpu.make_async_copy(part, out_ref.at[order.index(t)], out_sems.at[t])

    for p in range(pieces):
        copy_in(p).start()
    started = 0
    for p in range(pieces):
        copy_in(p).wait()
        for k in range(depth):
            for row in range(p * piece_rows, (p + 1) * piece_rows, SUB):
                lines = [field[k, row:row + SUB, c * LANES:(c + 1) * LANES] for c in range(chunks)]
                for c, value in enumerate(lines):
                    spread[pl.ds((row + 1) * block + k * chunks + c, SUB, stride=block), :] = value
        if p == 0:
            spread[(rows + 1) * block:, :] = spread[block:2 * block, :]
        if p == pieces - 1:
            spread[:block, :] = spread[rows * block:(rows + 1) * block, :]
        ready = [t for t in range(1, tiles) if (t + 1) * tile_rows < (p + 1) * piece_rows]
        if p == pieces - 1:
            ready = list(range(1, tiles)) + [0]
        for t in ready[started:]:
            copy_out(t).start()
        started = len(ready)
    for t in range(tiles):
        copy_out(t).wait()


def packed(field, tiles):
    depth, rows, cols = field.shape
    chunks = cols // LANES
    padded_rows = rows // tiles + 2
    pieces = 4 if rows % (4 * SUB) == 0 else 1
    hbm = pl.BlockSpec(memory_space=pltpu.HBM)
    flat = pl.pallas_call(
        functools.partial(pack_kernel, tiles),
        out_shape=jax.ShapeDtypeStruct((tiles, padded_rows * depth * chunks, LANES), field.dtype),
        in_specs=[hbm],
        out_specs=hbm,
        scratch_shapes=[
            pltpu.VMEM((depth, rows, cols), field.dtype),
            pltpu.VMEM(((rows + 2) * depth * chunks, LANES), field.dtype),
            pltpu.SemaphoreType.DMA((pieces,)),
            pltpu.SemaphoreType.DMA((tiles,)),
        ],
        compiler_params=pltpu.CompilerParams(vmem_limit_bytes=16 << 20),
        name="pack_rows",
    )(pltpu.with_memory_space_constraint(field, pltpu.HBM))
    return flat.reshape(tiles, padded_rows, depth, chunks, LANES)


def shifted(x, axis, shift):
    return pltpu.roll(x, shift % x.shape[axis], axis)


def prepare_kernel(bands_end_ref, order_ref, light_ref, color_ref, opacity_ref,
                   brick_at_ref, color_word_ref, opacity_word_ref, light_rows_ref, end_ref):
    bins = color_ref.shape[1] - 1
    _, halves, chunks, lanes = color_word_ref.shape
    shape = (chunks, lanes)

    def parts(values, unit):
        scaled = values.astype(jnp.float32) * float(unit)
        return scaled[:, :bins], scaled[:, 1:] - scaled[:, :bins]

    low, slope = parts(color_ref[...], COLOR_UNIT)
    color_words = slope + low * (1.0 / COLOR_SPAN)
    low, slope = parts(opacity_ref[...], OPACITY_UNIT)
    opacity_words = slope.astype(jnp.int32) * OPACITY_SPAN + low.astype(jnp.int32)
    for h in range(halves):
        span = slice(h * lanes, (h + 1) * lanes)
        for c in range(3):
            color_word_ref[c, h] = jnp.broadcast_to(color_words[c:c + 1, span], shape)
        opacity_word_ref[h] = jnp.broadcast_to(opacity_words[:, span], shape)
    for i in range(3):
        light_rows_ref[i] = jnp.full(shape, light_ref[i], jnp.float32) * math.sqrt(0.75)
    for i in range(2):
        end_ref[i] = jnp.full(shape, bands_end_ref[i], jnp.int32)
    for place, b in enumerate(exchange_order(order_ref.shape[0])):
        brick_at_ref[order_ref[b]] = place


def table_lookup(color_word_ref, opacity_word_ref):
    _, halves, _, lanes = color_word_ref.shape
    bins = halves * lanes

    def look_up(x):
        scaled = x * float(bins)
        index = jnp.minimum(scaled.astype(jnp.int32), bins - 1)
        fraction = scaled - index.astype(jnp.float32)
        low_bits = index & (lanes - 1)

        def gathered(table):
            found = [jnp.take_along_axis(t, low_bits, axis=1, mode="promise_in_bounds") for t in table]
            word = found[0]
            for h in range(1, halves):
                word = jnp.where(index >= h * lanes, found[h], word)
            return word

        color = []
        small = fraction * (1.0 / COLOR_SPAN)
        for c in range(3):
            word = gathered([color_word_ref[c, h] for h in range(halves)])
            rise = jnp.floor(word)
            color.append((word - rise) + small * rise)
        word = gathered([opacity_word_ref[h] for h in range(halves)])
        rise = (word >> OPACITY_BITS).astype(jnp.float32)
        start = (word & (OPACITY_SPAN - 1)).astype(jnp.float32)
        return color, (start + fraction * rise) * (1.0 / OPACITY_UNIT)

    return look_up


def column_differences(shape):
    lane = lax.broadcasted_iota(jnp.int32, shape, 1)
    chunk = lax.broadcasted_iota(jnp.int32, shape, 0)
    at_first, at_last = lane == 0, lane == shape[1] - 1
    at_left = at_first & (chunk == 0)
    at_right = at_last & (chunk == shape[0] - 1)

    def difference(x):
        right = shifted(x, 1, -1)
        right = jnp.where(at_last, shifted(right, 0, -1), right)
        right = jnp.where(at_right, 0.0, right)
        left = shifted(x, 1, 1)
        left = jnp.where(at_first, shifted(left, 0, 1), left)
        left = jnp.where(at_left, 0.0, left)
        return right - left

    return difference


def depth_differences(field):
    last = len(field) - 1
    made = {}
    for k in range(last + 1):
        ends = (min(k + 1, last), max(k - 1, 0))
        if ends not in made:
            made[ends] = field[ends[0]] - field[ends[1]]
    return [made[(min(k + 1, last), max(k - 1, 0))] for k in range(last + 1)]


def shading_of(facing, squared_plus_one):
    near = pltpu.reciprocal(squared_plus_one, approx=True)
    inverse = near * (2.0 - squared_plus_one * near)
    return 0.25 + (facing * facing) * inverse


def main_kernel(edge_rows, brick_at, light_ref, color_word_ref, opacity_word_ref, tile_ref,
                part_ref, color_sum_ref, keep_ref):
    bricks, padded_rows, depth, chunks, lanes = tile_ref.shape
    rows = padded_rows - 2
    inner_rows = [r for r in range(rows) if r not in edge_rows]
    shape = (chunks, lanes)
    look_up = table_lookup(color_word_ref, opacity_word_ref)
    column_difference = column_differences(shape)
    light = [light_ref[i] for i in range(3)]
    together = 4 if bricks % 4 == 0 else 1

    def step(trip, carry):
        colors, keeps = list(carry[0]), list(carry[1])
        at = [brick_at[trip * together + u] for u in range(together)]
        fields = [[[tile_ref[b, r, k] for k in range(depth)] for r in range(padded_rows)] for b in at]
        kept = []
        for b, field in zip(at, fields):
            for r in range(rows):
                for k, dz in enumerate(depth_differences(field[r + 1])):
                    x = field[r + 1][k]
                    dx = column_difference(x)
                    color, opacity = look_up(x)
                    weight = keeps[r] * opacity
                    facing = dz * light[0] + dx * light[2]
                    squared = dz * dz + dx * dx + 1.0
                    if r in edge_rows:
                        values = [weight * color[c] for c in range(3)] + [facing, squared]
                        kept.append((b, edge_rows.index(r), k, values))
                    else:
                        i = inner_rows.index(r)
                        dy = field[r + 2][k] - field[r][k]
                        shaded = weight * shading_of(facing + dy * light[1], squared + dy * dy)
                        for c in range(3):
                            slot = c * len(inner_rows) + i
                            colors[slot] = colors[slot] + shaded * color[c]
                    keeps[r] = keeps[r] - weight
        for b, i, k, values in kept:
            for v, value in enumerate(values):
                part_ref[b, i, k, v] = value
        return tuple(colors), tuple(keeps)

    zero, one = jnp.zeros(shape, jnp.float32), jnp.ones(shape, jnp.float32)
    colors, keeps = lax.fori_loop(
        0, bricks // together, step, ((zero,) * (3 * len(inner_rows)), (one,) * rows))
    for i, value in enumerate(colors):
        color_sum_ref[i] = value
    for r, value in enumerate(keeps):
        keep_ref[r] = value


def finish_kernel(edge_rows, end_ref, light_ref, tile_ref, other_ref, part_ref, color_sum_ref, keep_ref,
                  out_ref, staged):
    bricks, padded_rows, depth, chunks, lanes = tile_ref.shape
    rows = padded_rows - 2
    inner_rows = [r for r in range(rows) if r not in edge_rows]
    shape = (chunks, lanes)
    light_rows = light_ref[1]
    is_first, is_last = end_ref[0] == 1, end_ref[1] == 1

    together = 8 if bricks % 8 == 0 else 1

    def step(trip, colors):
        colors = list(colors)
        for u in range(together):
            b = trip * together + u
            for i, r in enumerate(edge_rows):
                for k in range(depth):
                    above, below = tile_ref[b, r, k], tile_ref[b, r + 2, k]
                    if r == 0:
                        above = jnp.where(is_first, other_ref[b, k], above)
                    if r == rows - 1:
                        below = jnp.where(is_last, other_ref[b, k], below)
                    dy = below - above
                    facing = part_ref[b, i, k, 3] + dy * light_rows
                    shading = shading_of(facing, part_ref[b, i, k, 4] + dy * dy)
                    for c in range(3):
                        slot = c * len(edge_rows) + i
                        colors[slot] = colors[slot] + shading * part_ref[b, i, k, c]
        return tuple(colors)

    zero = jnp.zeros(shape, jnp.float32)
    edge_colors = lax.fori_loop(0, bricks // together, step, (zero,) * (3 * len(edge_rows)))
    for r in range(rows):
        for c in range(3):
            if r in edge_rows:
                value = edge_colors[c * len(edge_rows) + edge_rows.index(r)]
            else:
                value = color_sum_ref[c * len(inner_rows) + inner_rows.index(r)]
            at = (c * rows + r) * chunks
            staged[at:at + chunks, :] = value * (COLOR_SPAN / COLOR_UNIT)
        at = (3 * rows + r) * chunks
        staged[at:at + chunks, :] = 1.0 - keep_ref[r]
    for c in range(4):
        for q in range(chunks):
            source = pl.ds(c * rows * chunks + q, rows, stride=chunks) if rows > 1 else pl.ds(c * chunks + q, 1)
            out_ref[c, 0, :, q * LANES:(q + 1) * LANES] = staged[source, :]


def shards(scalar, bin_index, color_table, opacity_table, light_dir, view_order):
    depth, rows, cols = scalar.shape
    bricks, bands = lax.axis_size("gz"), lax.axis_size("gy")
    tile_rows = rows // bricks
    chunks = cols // LANES
    edge_rows = sorted({0, tile_rows - 1})
    inner_count = tile_rows - len(edge_rows)
    tiles = lax.all_to_all(
        packed(scalar, bricks), "gz", split_axis=0, concat_axis=0, tiled=True,
        axis_index_groups=[exchange_order(bricks)])

    here = lax.axis_index("gz")
    ends = jnp.stack([here == 0, here == bricks - 1]).astype(jnp.int32)
    last = bricks - 1
    pairs = [(g, g + 1) for g in range(bands - 1)]
    pairs += [(last * bands + g + 1, last * bands + g) for g in range(bands - 1)]

    vmem = pl.BlockSpec(memory_space=pltpu.VMEM)
    smem = pl.BlockSpec(memory_space=pltpu.SMEM)
    params = pltpu.CompilerParams(vmem_limit_bytes=32 << 20)
    cells = bricks * depth * cols
    lines = (chunks, LANES)
    halves = (color_table.shape[1] - 1) // LANES
    brick_at, color_words, opacity_words, light_rows, end_rows = pl.pallas_call(
        prepare_kernel,
        out_shape=[
            pltpu.SMEM((bricks,), jnp.int32),
            jax.ShapeDtypeStruct((3, halves) + lines, jnp.float32),
            jax.ShapeDtypeStruct((halves,) + lines, jnp.int32),
            jax.ShapeDtypeStruct((3,) + lines, jnp.float32),
            jax.ShapeDtypeStruct((2,) + lines, jnp.int32),
        ],
        in_specs=[smem, smem, smem, vmem, vmem],
        out_specs=[smem] + [vmem] * 4,
        compiler_params=params,
        name="prepare_tables",
    )(ends, view_order, light_dir, color_table, opacity_table[None, :])
    wrapped = jnp.where(end_rows[0] == 1, tiles[:, 0], tiles[:, -1])
    other = lax.ppermute(wrapped, ("gz", "gy"), pairs)
    parts, color_sums, keeps = pl.pallas_call(
        functools.partial(main_kernel, edge_rows),
        out_shape=[
            jax.ShapeDtypeStruct((bricks, len(edge_rows), depth, 5, chunks, LANES), jnp.float32),
            jax.ShapeDtypeStruct((max(3 * inner_count, 1), chunks, LANES), jnp.float32),
            jax.ShapeDtypeStruct((tile_rows, chunks, LANES), jnp.float32),
        ],
        in_specs=[smem] + [vmem] * 4,
        out_specs=[vmem, vmem, vmem],
        compiler_params=params,
        cost_estimate=pl.CostEstimate(
            flops=100 * cells * tile_rows, bytes_accessed=24 * cells * tile_rows, transcendentals=0),
        name="main_rows",
    )(brick_at, light_rows, color_words, opacity_words, tiles)
    return pl.pallas_call(
        functools.partial(finish_kernel, edge_rows),
        out_shape=jax.ShapeDtypeStruct((4, 1, tile_rows, cols), jnp.float32),
        in_specs=[vmem] * 7,
        out_specs=vmem,
        scratch_shapes=[pltpu.VMEM((4 * tile_rows * chunks, LANES), jnp.float32)],
        compiler_params=params,
        cost_estimate=pl.CostEstimate(
            flops=10 * cells * tile_rows, bytes_accessed=24 * cells * tile_rows, transcendentals=0),
        name="edge_rows",
    )(end_rows, light_rows, tiles, other, parts, color_sums, keeps)


def solution(mesh):
    in_specs = (P("gz", "gy", None), P("gz", "gy", None), P(), P(), P(), P())
    out_specs = P(None, "gy", "gz", None)
    return jax.shard_map(shards, mesh=mesh, in_specs=in_specs, out_specs=out_specs, check_vma=False)
```

```python
import functools
import math

import jax
import jax.numpy as jnp
from jax import lax
from jax.experimental import pallas as pl
from jax.experimental.pallas import tpu as pltpu
from jax.sharding import PartitionSpec as P

SUB, LANES = 8, 128
COLOR_UNIT, COLOR_SPAN = 2 ** 11, 2 ** 12
OPACITY_UNIT, OPACITY_BITS = 2 ** 18, 16
OPACITY_SPAN = 2 ** OPACITY_BITS


def exchange_order(tiles):
    flip = tiles - tiles // 8 if tiles & (tiles - 1) == 0 else 0
    return [t ^ flip for t in range(tiles)]


def pack_kernel(tiles, field_ref, out_ref, field, spread, in_sems, out_sems):
    depth, rows, cols = field_ref.shape
    chunks = cols // LANES
    block = depth * chunks
    tile_rows = rows // tiles
    pieces = in_sems.shape[0]
    piece_rows = rows // pieces
    order = exchange_order(tiles)

    def copy_in(p):
        part = pl.ds(p * piece_rows, piece_rows)
        return pltpu.make_async_copy(field_ref.at[:, part], field.at[:, part], in_sems.at[p])

    def copy_out(t):
        part = spread.at[pl.ds(t * tile_rows * block, (tile_rows + 2) * block)]
        return pltpu.make_async_copy(part, out_ref.at[order.index(t)], out_sems.at[t])

    for p in range(pieces):
        copy_in(p).start()
    started = 0
    for p in range(pieces):
        copy_in(p).wait()
        for k in range(depth):
            for row in range(p * piece_rows, (p + 1) * piece_rows, SUB):
                lines = [field[k, row:row + SUB, c * LANES:(c + 1) * LANES] for c in range(chunks)]
                for c, value in enumerate(lines):
                    spread[pl.ds((row + 1) * block + k * chunks + c, SUB, stride=block), :] = value
        if p == 0:
            spread[(rows + 1) * block:, :] = spread[block:2 * block, :]
        if p == pieces - 1:
            spread[:block, :] = spread[rows * block:(rows + 1) * block, :]
        ready = [t for t in range(1, tiles) if (t + 1) * tile_rows < (p + 1) * piece_rows]
        if p == pieces - 1:
            ready = list(range(1, tiles)) + [0]
        for t in ready[started:]:
            copy_out(t).start()
        started = len(ready)
    for t in range(tiles):
        copy_out(t).wait()


def packed(field, tiles):
    depth, rows, cols = field.shape
    chunks = cols // LANES
    padded_rows = rows // tiles + 2
    pieces = 4 if rows % (4 * SUB) == 0 else 1
    hbm = pl.BlockSpec(memory_space=pltpu.HBM)
    flat = pl.pallas_call(
        functools.partial(pack_kernel, tiles),
        out_shape=jax.ShapeDtypeStruct((tiles, padded_rows * depth * chunks, LANES), field.dtype),
        in_specs=[hbm],
        out_specs=hbm,
        scratch_shapes=[
            pltpu.VMEM((depth, rows, cols), field.dtype),
            pltpu.VMEM(((rows + 2) * depth * chunks, LANES), field.dtype),
            pltpu.SemaphoreType.DMA((pieces,)),
            pltpu.SemaphoreType.DMA((tiles,)),
        ],
        compiler_params=pltpu.CompilerParams(vmem_limit_bytes=16 << 20),
        name="pack_rows",
    )(pltpu.with_memory_space_constraint(field, pltpu.HBM))
    return flat.reshape(tiles, padded_rows, depth, chunks, LANES)


def shifted(x, axis, shift):
    return pltpu.roll(x, shift % x.shape[axis], axis)


def prepare_kernel(bands_end_ref, order_ref, light_ref, color_ref, opacity_ref,
                   brick_at_ref, color_word_ref, opacity_word_ref, light_rows_ref, end_ref):
    bins = color_ref.shape[1] - 1
    _, halves, chunks, lanes = color_word_ref.shape
    shape = (chunks, lanes)

    def parts(values, unit):
        scaled = values.astype(jnp.float32) * float(unit)
        return scaled[:, :bins], scaled[:, 1:] - scaled[:, :bins]

    low, slope = parts(color_ref[...], COLOR_UNIT)
    color_words = slope + low * (1.0 / COLOR_SPAN)
    low, slope = parts(opacity_ref[...], OPACITY_UNIT)
    opacity_words = slope.astype(jnp.int32) * OPACITY_SPAN + low.astype(jnp.int32)
    for h in range(halves):
        span = slice(h * lanes, (h + 1) * lanes)
        for c in range(3):
            color_word_ref[c, h] = jnp.broadcast_to(color_words[c:c + 1, span], shape)
        opacity_word_ref[h] = jnp.broadcast_to(opacity_words[:, span], shape)
    for i in range(3):
        light_rows_ref[i] = jnp.full(shape, light_ref[i], jnp.float32) * math.sqrt(0.75)
    for i in range(2):
        end_ref[i] = jnp.full(shape, bands_end_ref[i], jnp.int32)
    for place, b in enumerate(exchange_order(order_ref.shape[0])):
        brick_at_ref[order_ref[b]] = place


def table_lookup(color_word_ref, opacity_word_ref):
    _, halves, _, lanes = color_word_ref.shape
    bins = halves * lanes

    def look_up(x):
        scaled = x * float(bins)
        index = jnp.minimum(scaled.astype(jnp.int32), bins - 1)
        fraction = scaled - index.astype(jnp.float32)
        low_bits = index & (lanes - 1)

        def gathered(table):
            found = [jnp.take_along_axis(t, low_bits, axis=1, mode="promise_in_bounds") for t in table]
            word = found[0]
            for h in range(1, halves):
                word = jnp.where(index >= h * lanes, found[h], word)
            return word

        color = []
        small = fraction * (1.0 / COLOR_SPAN)
        for c in range(3):
            word = gathered([color_word_ref[c, h] for h in range(halves)])
            rise = jnp.floor(word)
            color.append((word - rise) + small * rise)
        word = gathered([opacity_word_ref[h] for h in range(halves)])
        rise = (word >> OPACITY_BITS).astype(jnp.float32)
        start = (word & (OPACITY_SPAN - 1)).astype(jnp.float32)
        return color, (start + fraction * rise) * (1.0 / OPACITY_UNIT)

    return look_up


def column_differences(shape):
    lane = lax.broadcasted_iota(jnp.int32, shape, 1)
    chunk = lax.broadcasted_iota(jnp.int32, shape, 0)
    at_first, at_last = lane == 0, lane == shape[1] - 1
    at_left = at_first & (chunk == 0)
    at_right = at_last & (chunk == shape[0] - 1)

    def difference(x):
        right = shifted(x, 1, -1)
        right = jnp.where(at_last, shifted(right, 0, -1), right)
        right = jnp.where(at_right, 0.0, right)
        left = shifted(x, 1, 1)
        left = jnp.where(at_first, shifted(left, 0, 1), left)
        left = jnp.where(at_left, 0.0, left)
        return right - left

    return difference


def depth_differences(field):
    last = len(field) - 1
    made = {}
    for k in range(last + 1):
        ends = (min(k + 1, last), max(k - 1, 0))
        if ends not in made:
            made[ends] = field[ends[0]] - field[ends[1]]
    return [made[(min(k + 1, last), max(k - 1, 0))] for k in range(last + 1)]


def shading_of(facing, squared_plus_one):
    near = pltpu.reciprocal(squared_plus_one, approx=True)
    inverse = near * (2.0 - squared_plus_one * near)
    return 0.25 + (facing * facing) * inverse


def main_kernel(edge_rows, brick_at, light_ref, color_word_ref, opacity_word_ref, tile_ref,
                part_ref, color_sum_ref, keep_ref):
    bricks, padded_rows, depth, chunks, lanes = tile_ref.shape
    rows = padded_rows - 2
    inner_rows = [r for r in range(rows) if r not in edge_rows]
    shape = (chunks, lanes)
    look_up = table_lookup(color_word_ref, opacity_word_ref)
    column_difference = column_differences(shape)
    light = [light_ref[i] for i in range(3)]
    together = 4 if bricks % 4 == 0 else 1

    def step(trip, carry):
        colors, keeps = list(carry[0]), list(carry[1])
        at = [brick_at[trip * together + u] for u in range(together)]
        fields = [[[tile_ref[b, r, k] for k in range(depth)] for r in range(padded_rows)] for b in at]
        kept = []
        for b, field in zip(at, fields):
            for r in range(rows):
                for k, dz in enumerate(depth_differences(field[r + 1])):
                    x = field[r + 1][k]
                    dx = column_difference(x)
                    color, opacity = look_up(x)
                    weight = keeps[r] * opacity
                    facing = dz * light[0] + dx * light[2]
                    squared = dz * dz + dx * dx + 1.0
                    if r in edge_rows:
                        values = [weight * color[c] for c in range(3)] + [facing, squared]
                        kept.append((b, edge_rows.index(r), k, values))
                    else:
                        i = inner_rows.index(r)
                        dy = field[r + 2][k] - field[r][k]
                        shaded = weight * shading_of(facing + dy * light[1], squared + dy * dy)
                        for c in range(3):
                            slot = c * len(inner_rows) + i
                            colors[slot] = colors[slot] + shaded * color[c]
                    keeps[r] = keeps[r] - weight
        for b, i, k, values in kept:
            for v, value in enumerate(values):
                part_ref[b, i, k, v] = value
        return tuple(colors), tuple(keeps)

    zero, one = jnp.zeros(shape, jnp.float32), jnp.ones(shape, jnp.float32)
    colors, keeps = lax.fori_loop(
        0, bricks // together, step, ((zero,) * (3 * len(inner_rows)), (one,) * rows))
    for i, value in enumerate(colors):
        color_sum_ref[i] = value
    for r, value in enumerate(keeps):
        keep_ref[r] = value


def finish_kernel(edge_rows, end_ref, light_ref, tile_ref, other_ref, part_ref, color_sum_ref, keep_ref,
                  out_ref, staged):
    bricks, padded_rows, depth, chunks, lanes = tile_ref.shape
    rows = padded_rows - 2
    inner_rows = [r for r in range(rows) if r not in edge_rows]
    shape = (chunks, lanes)
    light_rows = light_ref[1]
    is_first, is_last = end_ref[0] == 1, end_ref[1] == 1

    together = 8 if bricks % 8 == 0 else 1

    def step(trip, colors):
        colors = list(colors)
        for u in range(together):
            b = trip * together + u
            for i, r in enumerate(edge_rows):
                for k in range(depth):
                    above, below = tile_ref[b, r, k], tile_ref[b, r + 2, k]
                    if r == 0:
                        above = jnp.where(is_first, other_ref[b, k], above)
                    if r == rows - 1:
                        below = jnp.where(is_last, other_ref[b, k], below)
                    dy = below - above
                    facing = part_ref[b, i, k, 3] + dy * light_rows
                    shading = shading_of(facing, part_ref[b, i, k, 4] + dy * dy)
                    for c in range(3):
                        slot = c * len(edge_rows) + i
                        colors[slot] = colors[slot] + shading * part_ref[b, i, k, c]
        return tuple(colors)

    zero = jnp.zeros(shape, jnp.float32)
    edge_colors = lax.fori_loop(0, bricks // together, step, (zero,) * (3 * len(edge_rows)))
    for r in range(rows):
        for c in range(3):
            if r in edge_rows:
                value = edge_colors[c * len(edge_rows) + edge_rows.index(r)]
            else:
                value = color_sum_ref[c * len(inner_rows) + inner_rows.index(r)]
            at = (c * rows + r) * chunks
            staged[at:at + chunks, :] = value * (COLOR_SPAN / COLOR_UNIT)
        at = (3 * rows + r) * chunks
        staged[at:at + chunks, :] = 1.0 - keep_ref[r]
    for c in range(4):
        for q in range(chunks):
            source = pl.ds(c * rows * chunks + q, rows, stride=chunks) if rows > 1 else pl.ds(c * chunks + q, 1)
            out_ref[c, 0, :, q * LANES:(q + 1) * LANES] = staged[source, :]


def shards(scalar, bin_index, color_table, opacity_table, light_dir, view_order):
    depth, rows, cols = scalar.shape
    bricks, bands = lax.axis_size("gz"), lax.axis_size("gy")
    tile_rows = rows // bricks
    chunks = cols // LANES
    edge_rows = sorted({0, tile_rows - 1})
    inner_count = tile_rows - len(edge_rows)
    tiles = lax.all_to_all(
        packed(scalar, bricks), "gz", split_axis=0, concat_axis=0, tiled=True,
        axis_index_groups=[exchange_order(bricks)])

    here = lax.axis_index("gz")
    ends = jnp.stack([here == 0, here == bricks - 1]).astype(jnp.int32)
    last = bricks - 1
    pairs = [(g, g + 1) for g in range(bands - 1)]
    pairs += [(last * bands + g + 1, last * bands + g) for g in range(bands - 1)]

    vmem = pl.BlockSpec(memory_space=pltpu.VMEM)
    smem = pl.BlockSpec(memory_space=pltpu.SMEM)
    params = pltpu.CompilerParams(vmem_limit_bytes=32 << 20)
    cells = bricks * depth * cols
    lines = (chunks, LANES)
    halves = (color_table.shape[1] - 1) // LANES
    brick_at, color_words, opacity_words, light_rows, end_rows = pl.pallas_call(
        prepare_kernel,
        out_shape=[
            pltpu.SMEM((bricks,), jnp.int32),
            jax.ShapeDtypeStruct((3, halves) + lines, jnp.float32),
            jax.ShapeDtypeStruct((halves,) + lines, jnp.int32),
            jax.ShapeDtypeStruct((3,) + lines, jnp.float32),
            jax.ShapeDtypeStruct((2,) + lines, jnp.int32),
        ],
        in_specs=[smem, smem, smem, vmem, vmem],
        out_specs=[smem] + [vmem] * 4,
        compiler_params=params,
        name="prepare_tables",
    )(ends, view_order, light_dir, color_table, opacity_table[None, :])
    wrapped = jnp.where(end_rows[0] == 1, tiles[:, 0], tiles[:, -1])
    other = lax.ppermute(wrapped, ("gz", "gy"), pairs)
    parts, color_sums, keeps = pl.pallas_call(
        functools.partial(main_kernel, edge_rows),
        out_shape=[
            jax.ShapeDtypeStruct((bricks, len(edge_rows), depth, 5, chunks, LANES), jnp.float32),
            jax.ShapeDtypeStruct((max(3 * inner_count, 1), chunks, LANES), jnp.float32),
            jax.ShapeDtypeStruct((tile_rows, chunks, LANES), jnp.float32),
        ],
        in_specs=[smem] + [vmem] * 4,
        out_specs=[vmem, vmem, vmem],
        compiler_params=params,
        cost_estimate=pl.CostEstimate(
            flops=100 * cells * tile_rows, bytes_accessed=24 * cells * tile_rows, transcendentals=0),
        name="main_rows",
    )(brick_at, light_rows, color_words, opacity_words, tiles)
    return pl.pallas_call(
        functools.partial(finish_kernel, edge_rows),
        out_shape=jax.ShapeDtypeStruct((4, 1, tile_rows, cols), jnp.float32),
        in_specs=[vmem] * 7,
        out_specs=vmem,
        scratch_shapes=[pltpu.VMEM((4 * tile_rows * chunks, LANES), jnp.float32)],
        compiler_params=params,
        cost_estimate=pl.CostEstimate(
            flops=10 * cells * tile_rows, bytes_accessed=24 * cells * tile_rows, transcendentals=0),
        name="edge_rows",
    )(end_rows, light_rows, tiles, other, parts, color_sums, keeps)


def solution(mesh):
    in_specs = (P("gz", "gy", None), P("gz", "gy", None), P(), P(), P(), P())
    out_specs = P(None, "gy", "gz", None)
    return jax.shard_map(shards, mesh=mesh, in_specs=in_specs, out_specs=out_specs, check_vma=False)
```

```python
import functools
import math

import jax
import jax.numpy as jnp
from jax import lax
from jax.experimental import pallas as pl
from jax.experimental.pallas import tpu as pltpu
from jax.sharding import PartitionSpec as P

SUB, LANES = 8, 128
COLOR_UNIT, COLOR_SPAN = 2 ** 11, 2 ** 12
OPACITY_UNIT, OPACITY_BITS = 2 ** 18, 16
OPACITY_SPAN = 2 ** OPACITY_BITS


def exchange_order(tiles):
    ranks = sorted(range(tiles), key=lambda rank: (rank.bit_count(), rank))
    chips = [0] + sorted(range(1, tiles), key=lambda chip: (-chip.bit_count(), -chip))
    placed = dict(zip(ranks, chips))
    return [placed[rank] for rank in range(tiles)]


def pack_kernel(tiles, field_ref, out_ref, field, spread, in_sems, out_sems):
    depth, rows, cols = field_ref.shape
    chunks = cols // LANES
    block = depth * chunks
    tile_rows = rows // tiles
    pieces = in_sems.shape[0]
    piece_rows = rows // pieces
    order = exchange_order(tiles)

    def copy_in(p):
        part = pl.ds(p * piece_rows, piece_rows)
        return pltpu.make_async_copy(field_ref.at[:, part], field.at[:, part], in_sems.at[p])

    def copy_out(t):
        part = spread.at[pl.ds(t * tile_rows * block, (tile_rows + 2) * block)]
        return pltpu.make_async_copy(part, out_ref.at[order.index(t)], out_sems.at[t])

    for p in range(pieces):
        copy_in(p).start()
    started = 0
    for p in range(pieces):
        copy_in(p).wait()
        for k in range(depth):
            for row in range(p * piece_rows, (p + 1) * piece_rows, SUB):
                lines = [field[k, row:row + SUB, c * LANES:(c + 1) * LANES] for c in range(chunks)]
                for c, value in enumerate(lines):
                    spread[pl.ds((row + 1) * block + k * chunks + c, SUB, stride=block), :] = value
        if p == 0:
            spread[(rows + 1) * block:, :] = spread[block:2 * block, :]
        if p == pieces - 1:
            spread[:block, :] = spread[rows * block:(rows + 1) * block, :]
        ready = [t for t in range(1, tiles) if (t + 1) * tile_rows < (p + 1) * piece_rows]
        if p == pieces - 1:
            ready = list(range(1, tiles)) + [0]
        for t in ready[started:]:
            copy_out(t).start()
        started = len(ready)
    for t in range(tiles):
        copy_out(t).wait()


def packed(field, tiles):
    depth, rows, cols = field.shape
    chunks = cols // LANES
    padded_rows = rows // tiles + 2
    pieces = 4 if rows % (4 * SUB) == 0 else 1
    hbm = pl.BlockSpec(memory_space=pltpu.HBM)
    flat = pl.pallas_call(
        functools.partial(pack_kernel, tiles),
        out_shape=jax.ShapeDtypeStruct((tiles, padded_rows * depth * chunks, LANES), field.dtype),
        in_specs=[hbm],
        out_specs=hbm,
        scratch_shapes=[
            pltpu.VMEM((depth, rows, cols), field.dtype),
            pltpu.VMEM(((rows + 2) * depth * chunks, LANES), field.dtype),
            pltpu.SemaphoreType.DMA((pieces,)),
            pltpu.SemaphoreType.DMA((tiles,)),
        ],
        compiler_params=pltpu.CompilerParams(vmem_limit_bytes=16 << 20),
        name="pack_rows",
    )(pltpu.with_memory_space_constraint(field, pltpu.HBM))
    return flat.reshape(tiles, padded_rows, depth, chunks, LANES)


def shifted(x, axis, shift):
    return pltpu.roll(x, shift % x.shape[axis], axis)


def prepare_kernel(bands_end_ref, order_ref, light_ref, color_ref, opacity_ref,
                   brick_at_ref, color_word_ref, opacity_word_ref, light_rows_ref, end_ref):
    bins = color_ref.shape[1] - 1
    _, halves, chunks, lanes = color_word_ref.shape
    shape = (chunks, lanes)

    def parts(values, unit):
        scaled = values.astype(jnp.float32) * float(unit)
        return scaled[:, :bins], scaled[:, 1:] - scaled[:, :bins]

    low, slope = parts(color_ref[...], COLOR_UNIT)
    color_words = slope + low * (1.0 / COLOR_SPAN)
    low, slope = parts(opacity_ref[...], OPACITY_UNIT)
    opacity_words = slope.astype(jnp.int32) * OPACITY_SPAN + low.astype(jnp.int32)
    for h in range(halves):
        span = slice(h * lanes, (h + 1) * lanes)
        for c in range(3):
            color_word_ref[c, h] = jnp.broadcast_to(color_words[c:c + 1, span], shape)
        opacity_word_ref[h] = jnp.broadcast_to(opacity_words[:, span], shape)
    for i in range(3):
        light_rows_ref[i] = jnp.full(shape, light_ref[i], jnp.float32) * math.sqrt(0.75)
    for i in range(2):
        end_ref[i] = jnp.full(shape, bands_end_ref[i], jnp.int32)
    for place, b in enumerate(exchange_order(order_ref.shape[0])):
        brick_at_ref[order_ref[b]] = place


def table_lookup(color_word_ref, opacity_word_ref):
    _, halves, _, lanes = color_word_ref.shape
    bins = halves * lanes

    def look_up(x):
        scaled = x * float(bins)
        index = jnp.minimum(scaled.astype(jnp.int32), bins - 1)
        fraction = scaled - index.astype(jnp.float32)
        low_bits = index & (lanes - 1)

        def gathered(table):
            found = [jnp.take_along_axis(t, low_bits, axis=1, mode="promise_in_bounds") for t in table]
            word = found[0]
            for h in range(1, halves):
                word = jnp.where(index >= h * lanes, found[h], word)
            return word

        color = []
        small = fraction * (1.0 / COLOR_SPAN)
        for c in range(3):
            word = gathered([color_word_ref[c, h] for h in range(halves)])
            rise = jnp.floor(word)
            color.append((word - rise) + small * rise)
        word = gathered([opacity_word_ref[h] for h in range(halves)])
        rise = (word >> OPACITY_BITS).astype(jnp.float32)
        start = (word & (OPACITY_SPAN - 1)).astype(jnp.float32)
        return color, (start + fraction * rise) * (1.0 / OPACITY_UNIT)

    return look_up


def column_differences(shape):
    lane = lax.broadcasted_iota(jnp.int32, shape, 1)
    chunk = lax.broadcasted_iota(jnp.int32, shape, 0)
    at_first, at_last = lane == 0, lane == shape[1] - 1
    at_left = at_first & (chunk == 0)
    at_right = at_last & (chunk == shape[0] - 1)

    def difference(x):
        right = shifted(x, 1, -1)
        right = jnp.where(at_last, shifted(right, 0, -1), right)
        right = jnp.where(at_right, 0.0, right)
        left = shifted(x, 1, 1)
        left = jnp.where(at_first, shifted(left, 0, 1), left)
        left = jnp.where(at_left, 0.0, left)
        return right - left

    return difference


def depth_differences(field):
    last = len(field) - 1
    made = {}
    for k in range(last + 1):
        ends = (min(k + 1, last), max(k - 1, 0))
        if ends not in made:
            made[ends] = field[ends[0]] - field[ends[1]]
    return [made[(min(k + 1, last), max(k - 1, 0))] for k in range(last + 1)]


def shading_of(facing, squared_plus_one):
    near = pltpu.reciprocal(squared_plus_one, approx=True)
    inverse = near * (2.0 - squared_plus_one * near)
    return 0.25 + (facing * facing) * inverse


def main_kernel(edge_rows, brick_at, light_ref, color_word_ref, opacity_word_ref, tile_ref,
                part_ref, color_sum_ref, keep_ref):
    bricks, padded_rows, depth, chunks, lanes = tile_ref.shape
    rows = padded_rows - 2
    inner_rows = [r for r in range(rows) if r not in edge_rows]
    shape = (chunks, lanes)
    look_up = table_lookup(color_word_ref, opacity_word_ref)
    column_difference = column_differences(shape)
    light = [light_ref[i] for i in range(3)]
    together = 4 if bricks % 4 == 0 else 1

    def step(trip, carry):
        colors, keeps = list(carry[0]), list(carry[1])
        at = [brick_at[trip * together + u] for u in range(together)]
        fields = [[[tile_ref[b, r, k] for k in range(depth)] for r in range(padded_rows)] for b in at]
        kept = []
        for b, field in zip(at, fields):
            for r in range(rows):
                for k, dz in enumerate(depth_differences(field[r + 1])):
                    x = field[r + 1][k]
                    dx = column_difference(x)
                    color, opacity = look_up(x)
                    weight = keeps[r] * opacity
                    facing = dz * light[0] + dx * light[2]
                    squared = dz * dz + dx * dx + 1.0
                    if r in edge_rows:
                        values = [weight * color[c] for c in range(3)] + [facing, squared]
                        kept.append((b, edge_rows.index(r), k, values))
                    else:
                        i = inner_rows.index(r)
                        dy = field[r + 2][k] - field[r][k]
                        shaded = weight * shading_of(facing + dy * light[1], squared + dy * dy)
                        for c in range(3):
                            slot = c * len(inner_rows) + i
                            colors[slot] = colors[slot] + shaded * color[c]
                    keeps[r] = keeps[r] - weight
        for b, i, k, values in kept:
            for v, value in enumerate(values):
                part_ref[b, i, k, v] = value
        return tuple(colors), tuple(keeps)

    zero, one = jnp.zeros(shape, jnp.float32), jnp.ones(shape, jnp.float32)
    colors, keeps = lax.fori_loop(
        0, bricks // together, step, ((zero,) * (3 * len(inner_rows)), (one,) * rows))
    for i, value in enumerate(colors):
        color_sum_ref[i] = value
    for r, value in enumerate(keeps):
        keep_ref[r] = value


def finish_kernel(edge_rows, end_ref, light_ref, tile_ref, other_ref, part_ref, color_sum_ref, keep_ref,
                  out_ref, staged):
    bricks, padded_rows, depth, chunks, lanes = tile_ref.shape
    rows = padded_rows - 2
    inner_rows = [r for r in range(rows) if r not in edge_rows]
    shape = (chunks, lanes)
    light_rows = light_ref[1]
    is_first, is_last = end_ref[0] == 1, end_ref[1] == 1

    together = 8 if bricks % 8 == 0 else 1

    def step(trip, colors):
        colors = list(colors)
        for u in range(together):
            b = trip * together + u
            for i, r in enumerate(edge_rows):
                for k in range(depth):
                    above, below = tile_ref[b, r, k], tile_ref[b, r + 2, k]
                    if r == 0:
                        above = jnp.where(is_first, other_ref[b, k], above)
                    if r == rows - 1:
                        below = jnp.where(is_last, other_ref[b, k], below)
                    dy = below - above
                    facing = part_ref[b, i, k, 3] + dy * light_rows
                    shading = shading_of(facing, part_ref[b, i, k, 4] + dy * dy)
                    for c in range(3):
                        slot = c * len(edge_rows) + i
                        colors[slot] = colors[slot] + shading * part_ref[b, i, k, c]
        return tuple(colors)

    zero = jnp.zeros(shape, jnp.float32)
    edge_colors = lax.fori_loop(0, bricks // together, step, (zero,) * (3 * len(edge_rows)))
    for r in range(rows):
        for c in range(3):
            if r in edge_rows:
                value = edge_colors[c * len(edge_rows) + edge_rows.index(r)]
            else:
                value = color_sum_ref[c * len(inner_rows) + inner_rows.index(r)]
            at = (c * rows + r) * chunks
            staged[at:at + chunks, :] = value * (COLOR_SPAN / COLOR_UNIT)
        at = (3 * rows + r) * chunks
        staged[at:at + chunks, :] = 1.0 - keep_ref[r]
    for c in range(4):
        for q in range(chunks):
            source = pl.ds(c * rows * chunks + q, rows, stride=chunks) if rows > 1 else pl.ds(c * chunks + q, 1)
            out_ref[c, 0, :, q * LANES:(q + 1) * LANES] = staged[source, :]


def shards(scalar, bin_index, color_table, opacity_table, light_dir, view_order):
    depth, rows, cols = scalar.shape
    bricks, bands = lax.axis_size("gz"), lax.axis_size("gy")
    tile_rows = rows // bricks
    chunks = cols // LANES
    edge_rows = sorted({0, tile_rows - 1})
    inner_count = tile_rows - len(edge_rows)
    tiles = lax.all_to_all(
        packed(scalar, bricks), "gz", split_axis=0, concat_axis=0, tiled=True,
        axis_index_groups=[exchange_order(bricks)])

    here = lax.axis_index("gz")
    ends = jnp.stack([here == 0, here == bricks - 1]).astype(jnp.int32)
    last = bricks - 1
    pairs = [(g, g + 1) for g in range(bands - 1)]
    pairs += [(last * bands + g + 1, last * bands + g) for g in range(bands - 1)]

    vmem = pl.BlockSpec(memory_space=pltpu.VMEM)
    smem = pl.BlockSpec(memory_space=pltpu.SMEM)
    params = pltpu.CompilerParams(vmem_limit_bytes=32 << 20)
    cells = bricks * depth * cols
    lines = (chunks, LANES)
    halves = (color_table.shape[1] - 1) // LANES
    brick_at, color_words, opacity_words, light_rows, end_rows = pl.pallas_call(
        prepare_kernel,
        out_shape=[
            pltpu.SMEM((bricks,), jnp.int32),
            jax.ShapeDtypeStruct((3, halves) + lines, jnp.float32),
            jax.ShapeDtypeStruct((halves,) + lines, jnp.int32),
            jax.ShapeDtypeStruct((3,) + lines, jnp.float32),
            jax.ShapeDtypeStruct((2,) + lines, jnp.int32),
        ],
        in_specs=[smem, smem, smem, vmem, vmem],
        out_specs=[smem] + [vmem] * 4,
        compiler_params=params,
        name="prepare_tables",
    )(ends, view_order, light_dir, color_table, opacity_table[None, :])
    wrapped = jnp.where(end_rows[0] == 1, tiles[:, 0], tiles[:, -1])
    other = lax.ppermute(wrapped, ("gz", "gy"), pairs)
    parts, color_sums, keeps = pl.pallas_call(
        functools.partial(main_kernel, edge_rows),
        out_shape=[
            jax.ShapeDtypeStruct((bricks, len(edge_rows), depth, 5, chunks, LANES), jnp.float32),
            jax.ShapeDtypeStruct((max(3 * inner_count, 1), chunks, LANES), jnp.float32),
            jax.ShapeDtypeStruct((tile_rows, chunks, LANES), jnp.float32),
        ],
        in_specs=[smem] + [vmem] * 4,
        out_specs=[vmem, vmem, vmem],
        compiler_params=params,
        cost_estimate=pl.CostEstimate(
            flops=100 * cells * tile_rows, bytes_accessed=24 * cells * tile_rows, transcendentals=0),
        name="main_rows",
    )(brick_at, light_rows, color_words, opacity_words, tiles)
    return pl.pallas_call(
        functools.partial(finish_kernel, edge_rows),
        out_shape=jax.ShapeDtypeStruct((4, 1, tile_rows, cols), jnp.float32),
        in_specs=[vmem] * 7,
        out_specs=vmem,
        scratch_shapes=[pltpu.VMEM((4 * tile_rows * chunks, LANES), jnp.float32)],
        compiler_params=params,
        cost_estimate=pl.CostEstimate(
            flops=10 * cells * tile_rows, bytes_accessed=24 * cells * tile_rows, transcendentals=0),
        name="edge_rows",
    )(end_rows, light_rows, tiles, other, parts, color_sums, keeps)


def solution(mesh):
    in_specs = (P("gz", "gy", None), P("gz", "gy", None), P(), P(), P(), P())
    out_specs = P(None, "gy", "gz", None)
    return jax.shard_map(shards, mesh=mesh, in_specs=in_specs, out_specs=out_specs, check_vma=False)
```

```python
import functools
import math

import jax
import jax.numpy as jnp
from jax import lax
from jax.experimental import pallas as pl
from jax.experimental.pallas import tpu as pltpu
from jax.sharding import PartitionSpec as P

SUB, LANES = 8, 128
COLOR_UNIT, COLOR_SPAN = 2 ** 11, 2 ** 12
OPACITY_UNIT, OPACITY_BITS = 2 ** 18, 16
OPACITY_SPAN = 2 ** OPACITY_BITS


def exchange_order(tiles):
    flip = tiles - tiles // 4 if tiles & (tiles - 1) == 0 else 0
    return [t ^ flip for t in range(tiles)]


def pack_kernel(tiles, field_ref, order_ref, light_ref, color_ref, opacity_ref,
                out_ref, brick_at_ref, color_word_ref, opacity_word_ref, light_rows_ref, end_ref,
                field, spread, order, light, color, opacity, sems, table_sems):
    depth, rows, cols = field_ref.shape
    chunks = cols // LANES
    block = depth * chunks
    tile_rows = rows // tiles
    pieces = sems.shape[0]
    piece_rows = rows // pieces

    def copy_in(p):
        part = pl.ds(p * piece_rows, piece_rows)
        return pltpu.make_async_copy(field_ref.at[:, part], field.at[:, part], sems.at[p])

    table_copies = [
        pltpu.make_async_copy(source, target, table_sems.at[i])
        for i, (source, target) in enumerate(
            [(color_ref, color), (opacity_ref, opacity), (order_ref, order), (light_ref, light)])
    ]
    for copy in table_copies:
        copy.start()
    for p in range(pieces):
        copy_in(p).start()
    for copy in table_copies:
        copy.wait()
    prepare(order, light, color, opacity, brick_at_ref, color_word_ref, opacity_word_ref, light_rows_ref, end_ref)
    for p in range(pieces):
        copy_in(p).wait()
        for k in range(depth):
            for row in range(p * piece_rows, (p + 1) * piece_rows, SUB):
                lines = [field[k, row:row + SUB, c * LANES:(c + 1) * LANES] for c in range(chunks)]
                for c, value in enumerate(lines):
                    spread[pl.ds((row + 1) * block + k * chunks + c, SUB, stride=block), :] = value
    spread[(rows + 1) * block:, :] = spread[block:2 * block, :]
    spread[:block, :] = spread[rows * block:(rows + 1) * block, :]
    size = (tile_rows + 2) * block
    for place, t in enumerate(exchange_order(tiles)):
        start = t * tile_rows * block
        out_ref[place] = spread[start:start + size, :]


def prepare(order_ref, light_ref, color_ref, opacity_ref,
            brick_at_ref, color_word_ref, opacity_word_ref, light_rows_ref, end_ref):
    bins = color_ref.shape[1] - 1
    _, halves, chunks, lanes = color_word_ref.shape
    shape = (chunks, lanes)

    def parts(values, unit):
        scaled = values.astype(jnp.float32) * float(unit)
        return scaled[:, :bins], scaled[:, 1:] - scaled[:, :bins]

    low, slope = parts(color_ref[...], COLOR_UNIT)
    color_words = slope + low * (1.0 / COLOR_SPAN)
    low, slope = parts(opacity_ref[...].reshape(1, bins + 1), OPACITY_UNIT)
    opacity_words = slope.astype(jnp.int32) * OPACITY_SPAN + low.astype(jnp.int32)
    for h in range(halves):
        span = slice(h * lanes, (h + 1) * lanes)
        for c in range(3):
            color_word_ref[c, h] = jnp.broadcast_to(color_words[c:c + 1, span], shape)
        opacity_word_ref[h] = jnp.broadcast_to(opacity_words[:, span], shape)
    for i in range(3):
        light_rows_ref[i] = jnp.full(shape, light_ref[i], jnp.float32) * math.sqrt(0.75)
    here, last = lax.axis_index("gz"), order_ref.shape[0] - 1
    for i, place in enumerate([here == 0, here == last, here != 0]):
        end_ref[i] = jnp.full(shape, place.astype(jnp.float32), jnp.float32)
    for place, b in enumerate(exchange_order(order_ref.shape[0])):
        brick_at_ref[order_ref[b]] = place


def shifted(x, axis, shift):
    return pltpu.roll(x, shift % x.shape[axis], axis)


def table_lookup(color_word_ref, opacity_word_ref):
    _, halves, _, lanes = color_word_ref.shape
    bins = halves * lanes

    def look_up(x):
        scaled = x * float(bins)
        index = jnp.minimum(scaled.astype(jnp.int32), bins - 1)
        fraction = scaled - index.astype(jnp.float32)
        low_bits = index & (lanes - 1)

        def gathered(table):
            found = [jnp.take_along_axis(t, low_bits, axis=1, mode="promise_in_bounds") for t in table]
            word = found[0]
            for h in range(1, halves):
                word = jnp.where(index >= h * lanes, found[h], word)
            return word

        color = []
        small = fraction * (1.0 / COLOR_SPAN)
        for c in range(3):
            word = gathered([color_word_ref[c, h] for h in range(halves)])
            rise = jnp.floor(word)
            color.append((word - rise) + small * rise)
        word = gathered([opacity_word_ref[h] for h in range(halves)])
        rise = (word >> OPACITY_BITS).astype(jnp.float32)
        start = (word & (OPACITY_SPAN - 1)).astype(jnp.float32)
        return color, (start + fraction * rise) * (1.0 / OPACITY_UNIT)

    return look_up


def column_differences(shape):
    lane = lax.broadcasted_iota(jnp.int32, shape, 1)
    chunk = lax.broadcasted_iota(jnp.int32, shape, 0)
    at_first, at_last = lane == 0, lane == shape[1] - 1
    at_left = at_first & (chunk == 0)
    at_right = at_last & (chunk == shape[0] - 1)

    def difference(x):
        right = shifted(x, 1, -1)
        right = jnp.where(at_last, shifted(right, 0, -1), right)
        right = jnp.where(at_right, 0.0, right)
        left = shifted(x, 1, 1)
        left = jnp.where(at_first, shifted(left, 0, 1), left)
        left = jnp.where(at_left, 0.0, left)
        return right - left

    return difference


def depth_differences(field):
    last = len(field) - 1
    made = {}
    for k in range(last + 1):
        ends = (min(k + 1, last), max(k - 1, 0))
        if ends not in made:
            made[ends] = field[ends[0]] - field[ends[1]]
    return [made[(min(k + 1, last), max(k - 1, 0))] for k in range(last + 1)]


def shading_of(facing, squared_plus_one):
    near = pltpu.reciprocal(squared_plus_one, approx=True)
    inverse = near * (2.0 - squared_plus_one * near)
    return 0.25 + (facing * facing) * inverse


def main_kernel(edge_rows, brick_at, light_ref, color_word_ref, opacity_word_ref, tile_ref,
                part_ref, color_sum_ref, keep_ref):
    bricks, padded_rows, depth, chunks, lanes = tile_ref.shape
    rows = padded_rows - 2
    inner_rows = [r for r in range(rows) if r not in edge_rows]
    shape = (chunks, lanes)
    look_up = table_lookup(color_word_ref, opacity_word_ref)
    column_difference = column_differences(shape)
    light = [light_ref[i] for i in range(3)]
    together = 4 if bricks % 4 == 0 else 1

    def step(trip, carry):
        colors, keeps = list(carry[0]), list(carry[1])
        at = [brick_at[trip * together + u] for u in range(together)]
        fields = [[[tile_ref[b, r, k] for k in range(depth)] for r in range(padded_rows)] for b in at]
        kept = []
        for b, field in zip(at, fields):
            for r in range(rows):
                for k, dz in enumerate(depth_differences(field[r + 1])):
                    x = field[r + 1][k]
                    dx = column_difference(x)
                    color, opacity = look_up(x)
                    weight = keeps[r] * opacity
                    facing = dz * light[0] + dx * light[2]
                    squared = dz * dz + dx * dx + 1.0
                    if r in edge_rows:
                        values = [weight * color[c] for c in range(3)] + [facing, squared]
                        kept.append((b, edge_rows.index(r), k, values))
                    else:
                        i = inner_rows.index(r)
                        dy = field[r + 2][k] - field[r][k]
                        shaded = weight * shading_of(facing + dy * light[1], squared + dy * dy)
                        for c in range(3):
                            slot = c * len(inner_rows) + i
                            colors[slot] = colors[slot] + shaded * color[c]
                    keeps[r] = keeps[r] - weight
        for b, i, k, values in kept:
            for v, value in enumerate(values):
                part_ref[b, i, k, v] = value
        return tuple(colors), tuple(keeps)

    zero, one = jnp.zeros(shape, jnp.float32), jnp.ones(shape, jnp.float32)
    colors, keeps = lax.fori_loop(
        0, bricks // together, step, ((zero,) * (3 * len(inner_rows)), (one,) * rows))
    for i, value in enumerate(colors):
        color_sum_ref[i] = value
    for r, value in enumerate(keeps):
        keep_ref[r] = value


def finish_kernel(edge_rows, end_ref, light_ref, tile_ref, other_ref, part_ref, color_sum_ref, keep_ref,
                  out_ref, staged):
    bricks, padded_rows, depth, chunks, lanes = tile_ref.shape
    rows = padded_rows - 2
    inner_rows = [r for r in range(rows) if r not in edge_rows]
    shape = (chunks, lanes)
    light_rows = light_ref[1]
    is_first, is_last = end_ref[0] == 1.0, end_ref[1] == 1.0

    together = 8 if bricks % 8 == 0 else 1

    def step(trip, colors):
        colors = list(colors)
        for u in range(together):
            b = trip * together + u
            for i, r in enumerate(edge_rows):
                for k in range(depth):
                    above, below = tile_ref[b, r, k], tile_ref[b, r + 2, k]
                    if r == 0:
                        above = jnp.where(is_first, other_ref[b, k], above)
                    if r == rows - 1:
                        below = jnp.where(is_last, other_ref[b, k], below)
                    dy = below - above
                    facing = part_ref[b, i, k, 3] + dy * light_rows
                    shading = shading_of(facing, part_ref[b, i, k, 4] + dy * dy)
                    for c in range(3):
                        slot = c * len(edge_rows) + i
                        colors[slot] = colors[slot] + shading * part_ref[b, i, k, c]
        return tuple(colors)

    zero = jnp.zeros(shape, jnp.float32)
    edge_colors = lax.fori_loop(0, bricks // together, step, (zero,) * (3 * len(edge_rows)))
    for r in range(rows):
        for c in range(3):
            if r in edge_rows:
                value = edge_colors[c * len(edge_rows) + edge_rows.index(r)]
            else:
                value = color_sum_ref[c * len(inner_rows) + inner_rows.index(r)]
            at = (c * rows + r) * chunks
            staged[at:at + chunks, :] = value * (COLOR_SPAN / COLOR_UNIT)
        at = (3 * rows + r) * chunks
        staged[at:at + chunks, :] = 1.0 - keep_ref[r]
    for c in range(4):
        for q in range(chunks):
            source = pl.ds(c * rows * chunks + q, rows, stride=chunks) if rows > 1 else pl.ds(c * chunks + q, 1)
            out_ref[c, 0, :, q * LANES:(q + 1) * LANES] = staged[source, :]


def shards(scalar, bin_index, color_table, opacity_table, light_dir, view_order):
    depth, rows, cols = scalar.shape
    bricks, bands = lax.axis_size("gz"), lax.axis_size("gy")
    tile_rows = rows // bricks
    chunks = cols // LANES
    edge_rows = sorted({0, tile_rows - 1})
    inner_count = tile_rows - len(edge_rows)
    vmem = pl.BlockSpec(memory_space=pltpu.VMEM)
    smem = pl.BlockSpec(memory_space=pltpu.SMEM)
    params = pltpu.CompilerParams(vmem_limit_bytes=32 << 20)
    cells = bricks * depth * cols
    lines = (chunks, LANES)
    halves = (color_table.shape[1] - 1) // LANES
    pieces = 4 if rows % (4 * SUB) == 0 else 1
    hbm = pl.BlockSpec(memory_space=pltpu.HBM)
    given = [scalar, view_order, light_dir, color_table, opacity_table]
    sent, brick_at, color_words, opacity_words, light_rows, end_rows = pl.pallas_call(
        functools.partial(pack_kernel, bricks),
        out_shape=[
            pltpu.VMEM((bricks, (tile_rows + 2) * depth * chunks, LANES), jnp.float32),
            pltpu.SMEM((bricks,), jnp.int32),
            jax.ShapeDtypeStruct((3, halves) + lines, jnp.float32),
            jax.ShapeDtypeStruct((halves,) + lines, jnp.int32),
            jax.ShapeDtypeStruct((3,) + lines, jnp.float32),
            jax.ShapeDtypeStruct((3,) + lines, jnp.float32),
        ],
        in_specs=[hbm] * 5,
        out_specs=[vmem, smem] + [vmem] * 4,
        scratch_shapes=[
            pltpu.VMEM(scalar.shape, scalar.dtype),
            pltpu.VMEM(((rows + 2) * depth * chunks, LANES), scalar.dtype),
            pltpu.SMEM(view_order.shape, view_order.dtype),
            pltpu.SMEM(light_dir.shape, light_dir.dtype),
            pltpu.VMEM(color_table.shape, color_table.dtype),
            pltpu.VMEM(opacity_table.shape, opacity_table.dtype),
            pltpu.SemaphoreType.DMA((pieces,)),
            pltpu.SemaphoreType.DMA((4,)),
        ],
        compiler_params=params,
        name="pack_rows",
    )(*[pltpu.with_memory_space_constraint(x, pltpu.HBM) for x in given])
    arrived = lax.all_to_all(
        sent, "gz", split_axis=0, concat_axis=0, tiled=True, axis_index_groups=[exchange_order(bricks)])
    tiles = arrived.reshape(bricks, tile_rows + 2, depth, chunks, LANES)

    last = bricks - 1
    pairs = [(g, g + 1) for g in range(bands - 1)]
    pairs += [(last * bands + g + 1, last * bands + g) for g in range(bands - 1)]
    wrapped = tiles[:, 0] * end_rows[0] + tiles[:, -1] * end_rows[2]
    other = lax.ppermute(wrapped, ("gz", "gy"), pairs)
    parts, color_sums, keeps = pl.pallas_call(
        functools.partial(main_kernel, edge_rows),
        out_shape=[
            jax.ShapeDtypeStruct((bricks, len(edge_rows), depth, 5, chunks, LANES), jnp.float32),
            jax.ShapeDtypeStruct((max(3 * inner_count, 1), chunks, LANES), jnp.float32),
            jax.ShapeDtypeStruct((tile_rows, chunks, LANES), jnp.float32),
        ],
        in_specs=[smem] + [vmem] * 4,
        out_specs=[vmem, vmem, vmem],
        compiler_params=params,
        cost_estimate=pl.CostEstimate(
            flops=100 * cells * tile_rows, bytes_accessed=24 * cells * tile_rows, transcendentals=0),
        name="main_rows",
    )(brick_at, light_rows, color_words, opacity_words, tiles)
    return pl.pallas_call(
        functools.partial(finish_kernel, edge_rows),
        out_shape=jax.ShapeDtypeStruct((4, 1, tile_rows, cols), jnp.float32),
        in_specs=[vmem] * 7,
        out_specs=vmem,
        scratch_shapes=[pltpu.VMEM((4 * tile_rows * chunks, LANES), jnp.float32)],
        compiler_params=params,
        cost_estimate=pl.CostEstimate(
            flops=10 * cells * tile_rows, bytes_accessed=24 * cells * tile_rows, transcendentals=0),
        name="edge_rows",
    )(end_rows, light_rows, tiles, other, parts, color_sums, keeps)


def solution(mesh):
    in_specs = (P("gz", "gy", None), P("gz", "gy", None), P(), P(), P(), P())
    out_specs = P(None, "gy", "gz", None)
    return jax.shard_map(shards, mesh=mesh, in_specs=in_specs, out_specs=out_specs, check_vma=False)
```

```python
import functools
import math

import jax
import jax.numpy as jnp
from jax import lax
from jax.experimental import pallas as pl
from jax.experimental.pallas import tpu as pltpu
from jax.sharding import PartitionSpec as P

SUB, LANES = 8, 128
COLOR_UNIT, COLOR_SPAN = 2 ** 11, 2 ** 12
OPACITY_UNIT, OPACITY_BITS = 2 ** 18, 16
OPACITY_SPAN = 2 ** OPACITY_BITS


def exchange_order(tiles):
    flip = tiles - tiles // 4 if tiles & (tiles - 1) == 0 else 0
    return [t ^ flip for t in range(tiles)]


def pack_kernel(tiles, field_ref, order_ref, light_ref, color_ref, opacity_ref,
                out_ref, brick_at_ref, color_word_ref, opacity_word_ref, light_rows_ref, first_ref, last_ref, later_ref,
                field, spread, order, light, color, opacity, sems, table_sems):
    depth, rows, cols = field_ref.shape
    chunks = cols // LANES
    block = depth * chunks
    tile_rows = rows // tiles
    pieces = sems.shape[0]
    piece_rows = rows // pieces

    def copy_in(p):
        part = pl.ds(p * piece_rows, piece_rows)
        return pltpu.make_async_copy(field_ref.at[:, part], field.at[:, part], sems.at[p])

    table_copies = [
        pltpu.make_async_copy(source, target, table_sems.at[i])
        for i, (source, target) in enumerate(
            [(color_ref, color), (opacity_ref, opacity), (order_ref, order), (light_ref, light)])
    ]
    for copy in table_copies:
        copy.start()
    for p in range(pieces):
        copy_in(p).start()
    for copy in table_copies:
        copy.wait()
    prepare(order, light, color, opacity, brick_at_ref, color_word_ref, opacity_word_ref, light_rows_ref, first_ref, last_ref, later_ref)
    for p in range(pieces):
        copy_in(p).wait()
        for k in range(depth):
            for row in range(p * piece_rows, (p + 1) * piece_rows, SUB):
                lines = [field[k, row:row + SUB, c * LANES:(c + 1) * LANES] for c in range(chunks)]
                for c, value in enumerate(lines):
                    spread[pl.ds((row + 1) * block + k * chunks + c, SUB, stride=block), :] = value
    spread[(rows + 1) * block:, :] = spread[block:2 * block, :]
    spread[:block, :] = spread[rows * block:(rows + 1) * block, :]
    size = (tile_rows + 2) * block
    for place, t in enumerate(exchange_order(tiles)):
        start = t * tile_rows * block
        out_ref[place] = spread[start:start + size, :]


def prepare(order_ref, light_ref, color_ref, opacity_ref,
            brick_at_ref, color_word_ref, opacity_word_ref, light_rows_ref, first_ref, last_ref, later_ref):
    bins = color_ref.shape[1] - 1
    _, halves, chunks, lanes = color_word_ref.shape
    shape = (chunks, lanes)

    def parts(values, unit):
        scaled = values.astype(jnp.float32) * float(unit)
        return scaled[:, :bins], scaled[:, 1:] - scaled[:, :bins]

    low, slope = parts(color_ref[...], COLOR_UNIT)
    color_words = slope + low * (1.0 / COLOR_SPAN)
    low, slope = parts(opacity_ref[...].reshape(1, bins + 1), OPACITY_UNIT)
    opacity_words = slope.astype(jnp.int32) * OPACITY_SPAN + low.astype(jnp.int32)
    for h in range(halves):
        span = slice(h * lanes, (h + 1) * lanes)
        for c in range(3):
            color_word_ref[c, h] = jnp.broadcast_to(color_words[c:c + 1, span], shape)
        opacity_word_ref[h] = jnp.broadcast_to(opacity_words[:, span], shape)
    for i in range(3):
        light_rows_ref[i] = jnp.full(shape, light_ref[i], jnp.float32) * math.sqrt(0.75)
    here, last = lax.axis_index("gz"), order_ref.shape[0] - 1
    for ref, place in [(first_ref, here == 0), (last_ref, here == last), (later_ref, here != 0)]:
        ref[...] = jnp.full(shape, place.astype(jnp.float32), jnp.float32)
    for place, b in enumerate(exchange_order(order_ref.shape[0])):
        brick_at_ref[order_ref[b]] = place


def shifted(x, axis, shift):
    return pltpu.roll(x, shift % x.shape[axis], axis)


def table_lookup(color_word_ref, opacity_word_ref):
    _, halves, _, lanes = color_word_ref.shape
    bins = halves * lanes

    def look_up(x):
        scaled = x * float(bins)
        index = jnp.minimum(scaled.astype(jnp.int32), bins - 1)
        fraction = scaled - index.astype(jnp.float32)
        low_bits = index & (lanes - 1)

        def gathered(table):
            found = [jnp.take_along_axis(t, low_bits, axis=1, mode="promise_in_bounds") for t in table]
            word = found[0]
            for h in range(1, halves):
                word = jnp.where(index >= h * lanes, found[h], word)
            return word

        color = []
        small = fraction * (1.0 / COLOR_SPAN)
        for c in range(3):
            word = gathered([color_word_ref[c, h] for h in range(halves)])
            rise = jnp.floor(word)
            color.append((word - rise) + small * rise)
        word = gathered([opacity_word_ref[h] for h in range(halves)])
        rise = (word >> OPACITY_BITS).astype(jnp.float32)
        start = (word & (OPACITY_SPAN - 1)).astype(jnp.float32)
        return color, (start + fraction * rise) * (1.0 / OPACITY_UNIT)

    return look_up


def column_differences(shape):
    lane = lax.broadcasted_iota(jnp.int32, shape, 1)
    chunk = lax.broadcasted_iota(jnp.int32, shape, 0)
    at_first, at_last = lane == 0, lane == shape[1] - 1
    at_left = at_first & (chunk == 0)
    at_right = at_last & (chunk == shape[0] - 1)

    def difference(x):
        right = shifted(x, 1, -1)
        right = jnp.where(at_last, shifted(right, 0, -1), right)
        right = jnp.where(at_right, 0.0, right)
        left = shifted(x, 1, 1)
        left = jnp.where(at_first, shifted(left, 0, 1), left)
        left = jnp.where(at_left, 0.0, left)
        return right - left

    return difference


def depth_differences(field):
    last = len(field) - 1
    made = {}
    for k in range(last + 1):
        ends = (min(k + 1, last), max(k - 1, 0))
        if ends not in made:
            made[ends] = field[ends[0]] - field[ends[1]]
    return [made[(min(k + 1, last), max(k - 1, 0))] for k in range(last + 1)]


def shading_of(facing, squared_plus_one):
    near = pltpu.reciprocal(squared_plus_one, approx=True)
    inverse = near * (2.0 - squared_plus_one * near)
    return 0.25 + (facing * facing) * inverse


def main_kernel(edge_rows, brick_at, light_ref, color_word_ref, opacity_word_ref, tile_ref,
                part_ref, color_sum_ref, keep_ref):
    bricks, padded_rows, depth, chunks, lanes = tile_ref.shape
    rows = padded_rows - 2
    inner_rows = [r for r in range(rows) if r not in edge_rows]
    shape = (chunks, lanes)
    look_up = table_lookup(color_word_ref, opacity_word_ref)
    column_difference = column_differences(shape)
    light = [light_ref[i] for i in range(3)]
    together = 4 if bricks % 4 == 0 else 1

    def step(trip, carry):
        colors, keeps = list(carry[0]), list(carry[1])
        at = [brick_at[trip * together + u] for u in range(together)]
        fields = [[[tile_ref[b, r, k] for k in range(depth)] for r in range(padded_rows)] for b in at]
        kept = []
        for b, field in zip(at, fields):
            for r in range(rows):
                for k, dz in enumerate(depth_differences(field[r + 1])):
                    x = field[r + 1][k]
                    dx = column_difference(x)
                    color, opacity = look_up(x)
                    weight = keeps[r] * opacity
                    facing = dz * light[0] + dx * light[2]
                    squared = dz * dz + dx * dx + 1.0
                    if r in edge_rows:
                        values = [weight * color[c] for c in range(3)] + [facing, squared]
                        kept.append((b, edge_rows.index(r), k, values))
                    else:
                        i = inner_rows.index(r)
                        dy = field[r + 2][k] - field[r][k]
                        shaded = weight * shading_of(facing + dy * light[1], squared + dy * dy)
                        for c in range(3):
                            slot = c * len(inner_rows) + i
                            colors[slot] = colors[slot] + shaded * color[c]
                    keeps[r] = keeps[r] - weight
        for b, i, k, values in kept:
            for v, value in enumerate(values):
                part_ref[b, i, k, v] = value
        return tuple(colors), tuple(keeps)

    zero, one = jnp.zeros(shape, jnp.float32), jnp.ones(shape, jnp.float32)
    colors, keeps = lax.fori_loop(
        0, bricks // together, step, ((zero,) * (3 * len(inner_rows)), (one,) * rows))
    for i, value in enumerate(colors):
        color_sum_ref[i] = value
    for r, value in enumerate(keeps):
        keep_ref[r] = value


def finish_kernel(edge_rows, first_ref, last_ref, light_ref, tile_ref, other_ref, part_ref, color_sum_ref, keep_ref,
                  out_ref, staged):
    bricks, padded_rows, depth, chunks, lanes = tile_ref.shape
    rows = padded_rows - 2
    inner_rows = [r for r in range(rows) if r not in edge_rows]
    shape = (chunks, lanes)
    light_rows = light_ref[1]
    is_first, is_last = first_ref[...] == 1.0, last_ref[...] == 1.0

    together = 8 if bricks % 8 == 0 else 1

    def step(trip, colors):
        colors = list(colors)
        for u in range(together):
            b = trip * together + u
            for i, r in enumerate(edge_rows):
                for k in range(depth):
                    above, below = tile_ref[b, r, k], tile_ref[b, r + 2, k]
                    if r == 0:
                        above = jnp.where(is_first, other_ref[b, k], above)
                    if r == rows - 1:
                        below = jnp.where(is_last, other_ref[b, k], below)
                    dy = below - above
                    facing = part_ref[b, i, k, 3] + dy * light_rows
                    shading = shading_of(facing, part_ref[b, i, k, 4] + dy * dy)
                    for c in range(3):
                        slot = c * len(edge_rows) + i
                        colors[slot] = colors[slot] + shading * part_ref[b, i, k, c]
        return tuple(colors)

    zero = jnp.zeros(shape, jnp.float32)
    edge_colors = lax.fori_loop(0, bricks // together, step, (zero,) * (3 * len(edge_rows)))
    for r in range(rows):
        for c in range(3):
            if r in edge_rows:
                value = edge_colors[c * len(edge_rows) + edge_rows.index(r)]
            else:
                value = color_sum_ref[c * len(inner_rows) + inner_rows.index(r)]
            at = (c * rows + r) * chunks
            staged[at:at + chunks, :] = value * (COLOR_SPAN / COLOR_UNIT)
        at = (3 * rows + r) * chunks
        staged[at:at + chunks, :] = 1.0 - keep_ref[r]
    for c in range(4):
        for q in range(chunks):
            source = pl.ds(c * rows * chunks + q, rows, stride=chunks) if rows > 1 else pl.ds(c * chunks + q, 1)
            out_ref[c, 0, :, q * LANES:(q + 1) * LANES] = staged[source, :]


def shards(scalar, bin_index, color_table, opacity_table, light_dir, view_order):
    depth, rows, cols = scalar.shape
    bricks, bands = lax.axis_size("gz"), lax.axis_size("gy")
    tile_rows = rows // bricks
    chunks = cols // LANES
    edge_rows = sorted({0, tile_rows - 1})
    inner_count = tile_rows - len(edge_rows)
    vmem = pl.BlockSpec(memory_space=pltpu.VMEM)
    smem = pl.BlockSpec(memory_space=pltpu.SMEM)
    params = pltpu.CompilerParams(vmem_limit_bytes=32 << 20)
    cells = bricks * depth * cols
    lines = (chunks, LANES)
    halves = (color_table.shape[1] - 1) // LANES
    pieces = 4 if rows % (4 * SUB) == 0 else 1
    hbm = pl.BlockSpec(memory_space=pltpu.HBM)
    given = [scalar, view_order, light_dir, color_table, opacity_table]
    sent, brick_at, color_words, opacity_words, light_rows, first, final, later = pl.pallas_call(
        functools.partial(pack_kernel, bricks),
        out_shape=[
            pltpu.VMEM((bricks, (tile_rows + 2) * depth * chunks, LANES), jnp.float32),
            pltpu.SMEM((bricks,), jnp.int32),
            jax.ShapeDtypeStruct((3, halves) + lines, jnp.float32),
            jax.ShapeDtypeStruct((halves,) + lines, jnp.int32),
            jax.ShapeDtypeStruct((3,) + lines, jnp.float32),
        ] + [jax.ShapeDtypeStruct(lines, jnp.float32)] * 3,
        in_specs=[hbm] * 5,
        out_specs=[vmem, smem] + [vmem] * 6,
        scratch_shapes=[
            pltpu.VMEM(scalar.shape, scalar.dtype),
            pltpu.VMEM(((rows + 2) * depth * chunks, LANES), scalar.dtype),
            pltpu.SMEM(view_order.shape, view_order.dtype),
            pltpu.SMEM(light_dir.shape, light_dir.dtype),
            pltpu.VMEM(color_table.shape, color_table.dtype),
            pltpu.VMEM(opacity_table.shape, opacity_table.dtype),
            pltpu.SemaphoreType.DMA((pieces,)),
            pltpu.SemaphoreType.DMA((4,)),
        ],
        compiler_params=params,
        name="pack_rows",
    )(*[pltpu.with_memory_space_constraint(x, pltpu.HBM) for x in given])
    arrived = lax.all_to_all(
        sent, "gz", split_axis=0, concat_axis=0, tiled=True, axis_index_groups=[exchange_order(bricks)])
    tiles = arrived.reshape(bricks, tile_rows + 2, depth, chunks, LANES)

    last = bricks - 1
    pairs = [(g, g + 1) for g in range(bands - 1)]
    pairs += [(last * bands + g + 1, last * bands + g) for g in range(bands - 1)]
    wrapped = tiles[:, 0] * first + tiles[:, -1] * later
    other = lax.ppermute(wrapped, ("gz", "gy"), pairs)
    parts, color_sums, keeps = pl.pallas_call(
        functools.partial(main_kernel, edge_rows),
        out_shape=[
            jax.ShapeDtypeStruct((bricks, len(edge_rows), depth, 5, chunks, LANES), jnp.float32),
            jax.ShapeDtypeStruct((max(3 * inner_count, 1), chunks, LANES), jnp.float32),
            jax.ShapeDtypeStruct((tile_rows, chunks, LANES), jnp.float32),
        ],
        in_specs=[smem] + [vmem] * 4,
        out_specs=[vmem, vmem, vmem],
        compiler_params=params,
        cost_estimate=pl.CostEstimate(
            flops=100 * cells * tile_rows, bytes_accessed=24 * cells * tile_rows, transcendentals=0),
        name="main_rows",
    )(brick_at, light_rows, color_words, opacity_words, tiles)
    return pl.pallas_call(
        functools.partial(finish_kernel, edge_rows),
        out_shape=jax.ShapeDtypeStruct((4, 1, tile_rows, cols), jnp.float32),
        in_specs=[vmem] * 8,
        out_specs=vmem,
        scratch_shapes=[pltpu.VMEM((4 * tile_rows * chunks, LANES), jnp.float32)],
        compiler_params=params,
        cost_estimate=pl.CostEstimate(
            flops=10 * cells * tile_rows, bytes_accessed=24 * cells * tile_rows, transcendentals=0),
        name="edge_rows",
    )(first, final, light_rows, tiles, other, parts, color_sums, keeps)


def solution(mesh):
    in_specs = (P("gz", "gy", None), P("gz", "gy", None), P(), P(), P(), P())
    out_specs = P(None, "gy", "gz", None)
    return jax.shard_map(shards, mesh=mesh, in_specs=in_specs, out_specs=out_specs, check_vma=False)
```

```python
import functools
import math

import jax
import jax.numpy as jnp
from jax import lax
from jax.experimental import pallas as pl
from jax.experimental.pallas import tpu as pltpu
from jax.sharding import PartitionSpec as P

SUB, LANES = 8, 128
COLOR_UNIT, COLOR_SPAN = 2 ** 11, 2 ** 12
OPACITY_UNIT, OPACITY_BITS = 2 ** 18, 16
OPACITY_SPAN = 2 ** OPACITY_BITS


def exchange_order(tiles):
    parts = 4 if tiles % 4 == 0 else 1
    return [(parts - 1 - i % parts) * (tiles // parts) + i // parts for i in range(tiles)]


def pack_kernel(tiles, field_ref, order_ref, light_ref, color_ref, opacity_ref,
                out_ref, brick_at_ref, color_word_ref, opacity_word_ref, light_rows_ref, first_ref, last_ref, later_ref,
                field, spread, order, light, color, opacity, sems, table_sems):
    depth, rows, cols = field_ref.shape
    chunks = cols // LANES
    block = depth * chunks
    tile_rows = rows // tiles
    pieces = sems.shape[0]
    piece_rows = rows // pieces

    def copy_in(p):
        part = pl.ds(p * piece_rows, piece_rows)
        return pltpu.make_async_copy(field_ref.at[:, part], field.at[:, part], sems.at[p])

    table_copies = [
        pltpu.make_async_copy(source, target, table_sems.at[i])
        for i, (source, target) in enumerate(
            [(color_ref, color), (opacity_ref, opacity), (order_ref, order), (light_ref, light)])
    ]
    for copy in table_copies:
        copy.start()
    for p in range(pieces):
        copy_in(p).start()
    for copy in table_copies:
        copy.wait()
    prepare(order, light, color, opacity, brick_at_ref, color_word_ref, opacity_word_ref, light_rows_ref, first_ref, last_ref, later_ref)
    for p in range(pieces):
        copy_in(p).wait()
        for k in range(depth):
            for row in range(p * piece_rows, (p + 1) * piece_rows, SUB):
                lines = [field[k, row:row + SUB, c * LANES:(c + 1) * LANES] for c in range(chunks)]
                for c, value in enumerate(lines):
                    spread[pl.ds((row + 1) * block + k * chunks + c, SUB, stride=block), :] = value
    spread[(rows + 1) * block:, :] = spread[block:2 * block, :]
    spread[:block, :] = spread[rows * block:(rows + 1) * block, :]
    size = (tile_rows + 2) * block
    for place, t in enumerate(exchange_order(tiles)):
        start = t * tile_rows * block
        out_ref[place] = spread[start:start + size, :]


def prepare(order_ref, light_ref, color_ref, opacity_ref,
            brick_at_ref, color_word_ref, opacity_word_ref, light_rows_ref, first_ref, last_ref, later_ref):
    bins = color_ref.shape[1] - 1
    _, halves, chunks, lanes = color_word_ref.shape
    shape = (chunks, lanes)

    def parts(values, unit):
        scaled = values.astype(jnp.float32) * float(unit)
        return scaled[:, :bins], scaled[:, 1:] - scaled[:, :bins]

    low, slope = parts(color_ref[...], COLOR_UNIT)
    color_words = slope + low * (1.0 / COLOR_SPAN)
    low, slope = parts(opacity_ref[...].reshape(1, bins + 1), OPACITY_UNIT)
    opacity_words = slope.astype(jnp.int32) * OPACITY_SPAN + low.astype(jnp.int32)
    for h in range(halves):
        span = slice(h * lanes, (h + 1) * lanes)
        for c in range(3):
            color_word_ref[c, h] = jnp.broadcast_to(color_words[c:c + 1, span], shape)
        opacity_word_ref[h] = jnp.broadcast_to(opacity_words[:, span], shape)
    for i in range(3):
        light_rows_ref[i] = jnp.full(shape, light_ref[i], jnp.float32) * math.sqrt(0.75)
    here, last = lax.axis_index("gz"), order_ref.shape[0] - 1
    for ref, place in [(first_ref, here == 0), (last_ref, here == last), (later_ref, here != 0)]:
        ref[...] = jnp.full(shape, place.astype(jnp.float32), jnp.float32)
    for place, b in enumerate(exchange_order(order_ref.shape[0])):
        brick_at_ref[order_ref[b]] = place


def shifted(x, axis, shift):
    return pltpu.roll(x, shift % x.shape[axis], axis)


def table_lookup(color_word_ref, opacity_word_ref):
    _, halves, _, lanes = color_word_ref.shape
    bins = halves * lanes

    def look_up(x):
        scaled = x * float(bins)
        index = jnp.minimum(scaled.astype(jnp.int32), bins - 1)
        fraction = scaled - index.astype(jnp.float32)
        low_bits = index & (lanes - 1)

        def gathered(table):
            found = [jnp.take_along_axis(t, low_bits, axis=1, mode="promise_in_bounds") for t in table]
            word = found[0]
            for h in range(1, halves):
                word = jnp.where(index >= h * lanes, found[h], word)
            return word

        color = []
        small = fraction * (1.0 / COLOR_SPAN)
        for c in range(3):
            word = gathered([color_word_ref[c, h] for h in range(halves)])
            rise = jnp.floor(word)
            color.append((word - rise) + small * rise)
        word = gathered([opacity_word_ref[h] for h in range(halves)])
        rise = (word >> OPACITY_BITS).astype(jnp.float32)
        start = (word & (OPACITY_SPAN - 1)).astype(jnp.float32)
        return color, (start + fraction * rise) * (1.0 / OPACITY_UNIT)

    return look_up


def column_differences(shape):
    lane = lax.broadcasted_iota(jnp.int32, shape, 1)
    chunk = lax.broadcasted_iota(jnp.int32, shape, 0)
    at_first, at_last = lane == 0, lane == shape[1] - 1
    at_left = at_first & (chunk == 0)
    at_right = at_last & (chunk == shape[0] - 1)

    def difference(x):
        right = shifted(x, 1, -1)
        right = jnp.where(at_last, shifted(right, 0, -1), right)
        right = jnp.where(at_right, 0.0, right)
        left = shifted(x, 1, 1)
        left = jnp.where(at_first, shifted(left, 0, 1), left)
        left = jnp.where(at_left, 0.0, left)
        return right - left

    return difference


def depth_differences(field):
    last = len(field) - 1
    made = {}
    for k in range(last + 1):
        ends = (min(k + 1, last), max(k - 1, 0))
        if ends not in made:
            made[ends] = field[ends[0]] - field[ends[1]]
    return [made[(min(k + 1, last), max(k - 1, 0))] for k in range(last + 1)]


def shading_of(facing, squared_plus_one):
    near = pltpu.reciprocal(squared_plus_one, approx=True)
    inverse = near * (2.0 - squared_plus_one * near)
    return 0.25 + (facing * facing) * inverse


def main_kernel(edge_rows, brick_at, light_ref, color_word_ref, opacity_word_ref, tile_ref,
                part_ref, color_sum_ref, keep_ref):
    bricks, padded_rows, depth, chunks, lanes = tile_ref.shape
    rows = padded_rows - 2
    inner_rows = [r for r in range(rows) if r not in edge_rows]
    shape = (chunks, lanes)
    look_up = table_lookup(color_word_ref, opacity_word_ref)
    column_difference = column_differences(shape)
    light = [light_ref[i] for i in range(3)]
    together = 4 if bricks % 4 == 0 else 1

    def step(trip, carry):
        colors, keeps = list(carry[0]), list(carry[1])
        at = [brick_at[trip * together + u] for u in range(together)]
        fields = [[[tile_ref[b, r, k] for k in range(depth)] for r in range(padded_rows)] for b in at]
        kept = []
        for b, field in zip(at, fields):
            for r in range(rows):
                for k, dz in enumerate(depth_differences(field[r + 1])):
                    x = field[r + 1][k]
                    dx = column_difference(x)
                    color, opacity = look_up(x)
                    weight = keeps[r] * opacity
                    facing = dz * light[0] + dx * light[2]
                    squared = dz * dz + dx * dx + 1.0
                    if r in edge_rows:
                        values = [weight * color[c] for c in range(3)] + [facing, squared]
                        kept.append((b, edge_rows.index(r), k, values))
                    else:
                        i = inner_rows.index(r)
                        dy = field[r + 2][k] - field[r][k]
                        shaded = weight * shading_of(facing + dy * light[1], squared + dy * dy)
                        for c in range(3):
                            slot = c * len(inner_rows) + i
                            colors[slot] = colors[slot] + shaded * color[c]
                    keeps[r] = keeps[r] - weight
        for b, i, k, values in kept:
            for v, value in enumerate(values):
                part_ref[b, i, k, v] = value
        return tuple(colors), tuple(keeps)

    zero, one = jnp.zeros(shape, jnp.float32), jnp.ones(shape, jnp.float32)
    colors, keeps = lax.fori_loop(
        0, bricks // together, step, ((zero,) * (3 * len(inner_rows)), (one,) * rows))
    for i, value in enumerate(colors):
        color_sum_ref[i] = value
    for r, value in enumerate(keeps):
        keep_ref[r] = value


def finish_kernel(edge_rows, first_ref, last_ref, light_ref, tile_ref, other_ref, part_ref, color_sum_ref, keep_ref,
                  out_ref, staged):
    bricks, padded_rows, depth, chunks, lanes = tile_ref.shape
    rows = padded_rows - 2
    inner_rows = [r for r in range(rows) if r not in edge_rows]
    shape = (chunks, lanes)
    light_rows = light_ref[1]
    is_first, is_last = first_ref[...] == 1.0, last_ref[...] == 1.0

    together = 8 if bricks % 8 == 0 else 1

    def step(trip, colors):
        colors = list(colors)
        for u in range(together):
            b = trip * together + u
            for i, r in enumerate(edge_rows):
                for k in range(depth):
                    above, below = tile_ref[b, r, k], tile_ref[b, r + 2, k]
                    if r == 0:
                        above = jnp.where(is_first, other_ref[b, k], above)
                    if r == rows - 1:
                        below = jnp.where(is_last, other_ref[b, k], below)
                    dy = below - above
                    facing = part_ref[b, i, k, 3] + dy * light_rows
                    shading = shading_of(facing, part_ref[b, i, k, 4] + dy * dy)
                    for c in range(3):
                        slot = c * len(edge_rows) + i
                        colors[slot] = colors[slot] + shading * part_ref[b, i, k, c]
        return tuple(colors)

    zero = jnp.zeros(shape, jnp.float32)
    edge_colors = lax.fori_loop(0, bricks // together, step, (zero,) * (3 * len(edge_rows)))
    for r in range(rows):
        for c in range(3):
            if r in edge_rows:
                value = edge_colors[c * len(edge_rows) + edge_rows.index(r)]
            else:
                value = color_sum_ref[c * len(inner_rows) + inner_rows.index(r)]
            at = (c * rows + r) * chunks
            staged[at:at + chunks, :] = value * (COLOR_SPAN / COLOR_UNIT)
        at = (3 * rows + r) * chunks
        staged[at:at + chunks, :] = 1.0 - keep_ref[r]
    for c in range(4):
        for q in range(chunks):
            source = pl.ds(c * rows * chunks + q, rows, stride=chunks) if rows > 1 else pl.ds(c * chunks + q, 1)
            out_ref[c, 0, :, q * LANES:(q + 1) * LANES] = staged[source, :]


def shards(scalar, bin_index, color_table, opacity_table, light_dir, view_order):
    depth, rows, cols = scalar.shape
    bricks, bands = lax.axis_size("gz"), lax.axis_size("gy")
    tile_rows = rows // bricks
    chunks = cols // LANES
    edge_rows = sorted({0, tile_rows - 1})
    inner_count = tile_rows - len(edge_rows)
    vmem = pl.BlockSpec(memory_space=pltpu.VMEM)
    smem = pl.BlockSpec(memory_space=pltpu.SMEM)
    params = pltpu.CompilerParams(vmem_limit_bytes=32 << 20)
    cells = bricks * depth * cols
    lines = (chunks, LANES)
    halves = (color_table.shape[1] - 1) // LANES
    pieces = 4 if rows % (4 * SUB) == 0 else 1
    hbm = pl.BlockSpec(memory_space=pltpu.HBM)
    given = [scalar, view_order, light_dir, color_table, opacity_table]
    sent, brick_at, color_words, opacity_words, light_rows, first, final, later = pl.pallas_call(
        functools.partial(pack_kernel, bricks),
        out_shape=[
            pltpu.VMEM((bricks, (tile_rows + 2) * depth * chunks, LANES), jnp.float32),
            pltpu.SMEM((bricks,), jnp.int32),
            jax.ShapeDtypeStruct((3, halves) + lines, jnp.float32),
            jax.ShapeDtypeStruct((halves,) + lines, jnp.int32),
            jax.ShapeDtypeStruct((3,) + lines, jnp.float32),
        ] + [jax.ShapeDtypeStruct(lines, jnp.float32)] * 3,
        in_specs=[hbm] * 5,
        out_specs=[vmem, smem] + [vmem] * 6,
        scratch_shapes=[
            pltpu.VMEM(scalar.shape, scalar.dtype),
            pltpu.VMEM(((rows + 2) * depth * chunks, LANES), scalar.dtype),
            pltpu.SMEM(view_order.shape, view_order.dtype),
            pltpu.SMEM(light_dir.shape, light_dir.dtype),
            pltpu.VMEM(color_table.shape, color_table.dtype),
            pltpu.VMEM(opacity_table.shape, opacity_table.dtype),
            pltpu.SemaphoreType.DMA((pieces,)),
            pltpu.SemaphoreType.DMA((4,)),
        ],
        compiler_params=params,
        name="pack_rows",
    )(*[pltpu.with_memory_space_constraint(x, pltpu.HBM) for x in given])
    arrived = lax.all_to_all(
        sent, "gz", split_axis=0, concat_axis=0, tiled=True, axis_index_groups=[exchange_order(bricks)])
    tiles = arrived.reshape(bricks, tile_rows + 2, depth, chunks, LANES)

    last = bricks - 1
    pairs = [(g, g + 1) for g in range(bands - 1)]
    pairs += [(last * bands + g + 1, last * bands + g) for g in range(bands - 1)]
    wrapped = tiles[:, 0] * first + tiles[:, -1] * later
    other = lax.ppermute(wrapped, ("gz", "gy"), pairs)
    parts, color_sums, keeps = pl.pallas_call(
        functools.partial(main_kernel, edge_rows),
        out_shape=[
            jax.ShapeDtypeStruct((bricks, len(edge_rows), depth, 5, chunks, LANES), jnp.float32),
            jax.ShapeDtypeStruct((max(3 * inner_count, 1), chunks, LANES), jnp.float32),
            jax.ShapeDtypeStruct((tile_rows, chunks, LANES), jnp.float32),
        ],
        in_specs=[smem] + [vmem] * 4,
        out_specs=[vmem, vmem, vmem],
        compiler_params=params,
        cost_estimate=pl.CostEstimate(
            flops=100 * cells * tile_rows, bytes_accessed=24 * cells * tile_rows, transcendentals=0),
        name="main_rows",
    )(brick_at, light_rows, color_words, opacity_words, tiles)
    return pl.pallas_call(
        functools.partial(finish_kernel, edge_rows),
        out_shape=jax.ShapeDtypeStruct((4, 1, tile_rows, cols), jnp.float32),
        in_specs=[vmem] * 8,
        out_specs=vmem,
        scratch_shapes=[pltpu.VMEM((4 * tile_rows * chunks, LANES), jnp.float32)],
        compiler_params=params,
        cost_estimate=pl.CostEstimate(
            flops=10 * cells * tile_rows, bytes_accessed=24 * cells * tile_rows, transcendentals=0),
        name="edge_rows",
    )(first, final, light_rows, tiles, other, parts, color_sums, keeps)


def solution(mesh):
    in_specs = (P("gz", "gy", None), P("gz", "gy", None), P(), P(), P(), P())
    out_specs = P(None, "gy", "gz", None)
    return jax.shard_map(shards, mesh=mesh, in_specs=in_specs, out_specs=out_specs, check_vma=False)
```

```python
import functools
import math

import jax
import jax.numpy as jnp
from jax import lax
from jax.experimental import pallas as pl
from jax.experimental.pallas import tpu as pltpu
from jax.sharding import PartitionSpec as P

SUB, LANES = 8, 128
COLOR_UNIT, COLOR_SPAN = 2 ** 11, 2 ** 12
OPACITY_UNIT, OPACITY_BITS = 2 ** 18, 16
OPACITY_SPAN = 2 ** OPACITY_BITS


def exchange_order(tiles):
    parts = 4 if tiles % 4 == 0 else 1
    size = tiles // parts
    walk = [i ^ (i >> 1) for i in range(size)] if size & (size - 1) == 0 else range(size)
    return [(parts - 1 - p) * size + i for i in walk for p in range(parts)]


def pack_kernel(tiles, field_ref, order_ref, light_ref, color_ref, opacity_ref,
                out_ref, brick_at_ref, color_word_ref, opacity_word_ref, light_rows_ref, first_ref, last_ref, later_ref,
                field, spread, order, light, color, opacity, sems, table_sems):
    depth, rows, cols = field_ref.shape
    chunks = cols // LANES
    block = depth * chunks
    tile_rows = rows // tiles
    pieces = sems.shape[0]
    piece_rows = rows // pieces

    def copy_in(p):
        part = pl.ds(p * piece_rows, piece_rows)
        return pltpu.make_async_copy(field_ref.at[:, part], field.at[:, part], sems.at[p])

    table_copies = [
        pltpu.make_async_copy(source, target, table_sems.at[i])
        for i, (source, target) in enumerate(
            [(color_ref, color), (opacity_ref, opacity), (order_ref, order), (light_ref, light)])
    ]
    for copy in table_copies:
        copy.start()
    for p in range(pieces):
        copy_in(p).start()
    for copy in table_copies:
        copy.wait()
    prepare(order, light, color, opacity, brick_at_ref, color_word_ref, opacity_word_ref, light_rows_ref, first_ref, last_ref, later_ref)
    for p in range(pieces):
        copy_in(p).wait()
        for k in range(depth):
            for row in range(p * piece_rows, (p + 1) * piece_rows, SUB):
                lines = [field[k, row:row + SUB, c * LANES:(c + 1) * LANES] for c in range(chunks)]
                for c, value in enumerate(lines):
                    spread[pl.ds((row + 1) * block + k * chunks + c, SUB, stride=block), :] = value
    spread[(rows + 1) * block:, :] = spread[block:2 * block, :]
    spread[:block, :] = spread[rows * block:(rows + 1) * block, :]
    size = (tile_rows + 2) * block
    for place, t in enumerate(exchange_order(tiles)):
        start = t * tile_rows * block
        out_ref[place] = spread[start:start + size, :]


def prepare(order_ref, light_ref, color_ref, opacity_ref,
            brick_at_ref, color_word_ref, opacity_word_ref, light_rows_ref, first_ref, last_ref, later_ref):
    bins = color_ref.shape[1] - 1
    _, halves, chunks, lanes = color_word_ref.shape
    shape = (chunks, lanes)

    def parts(values, unit):
        scaled = values.astype(jnp.float32) * float(unit)
        return scaled[:, :bins], scaled[:, 1:] - scaled[:, :bins]

    low, slope = parts(color_ref[...], COLOR_UNIT)
    color_words = slope + low * (1.0 / COLOR_SPAN)
    low, slope = parts(opacity_ref[...].reshape(1, bins + 1), OPACITY_UNIT)
    opacity_words = slope.astype(jnp.int32) * OPACITY_SPAN + low.astype(jnp.int32)
    for h in range(halves):
        span = slice(h * lanes, (h + 1) * lanes)
        for c in range(3):
            color_word_ref[c, h] = jnp.broadcast_to(color_words[c:c + 1, span], shape)
        opacity_word_ref[h] = jnp.broadcast_to(opacity_words[:, span], shape)
    for i in range(3):
        light_rows_ref[i] = jnp.full(shape, light_ref[i], jnp.float32) * math.sqrt(0.75)
    here, last = lax.axis_index("gz"), order_ref.shape[0] - 1
    for ref, place in [(first_ref, here == 0), (last_ref, here == last), (later_ref, here != 0)]:
        ref[...] = jnp.full(shape, place.astype(jnp.float32), jnp.float32)
    for place, b in enumerate(exchange_order(order_ref.shape[0])):
        brick_at_ref[order_ref[b]] = place


def shifted(x, axis, shift):
    return pltpu.roll(x, shift % x.shape[axis], axis)


def table_lookup(color_word_ref, opacity_word_ref):
    _, halves, _, lanes = color_word_ref.shape
    bins = halves * lanes

    def look_up(x):
        scaled = x * float(bins)
        index = jnp.minimum(scaled.astype(jnp.int32), bins - 1)
        fraction = scaled - index.astype(jnp.float32)
        low_bits = index & (lanes - 1)

        def gathered(table):
            found = [jnp.take_along_axis(t, low_bits, axis=1, mode="promise_in_bounds") for t in table]
            word = found[0]
            for h in range(1, halves):
                word = jnp.where(index >= h * lanes, found[h], word)
            return word

        color = []
        small = fraction * (1.0 / COLOR_SPAN)
        for c in range(3):
            word = gathered([color_word_ref[c, h] for h in range(halves)])
            rise = jnp.floor(word)
            color.append((word - rise) + small * rise)
        word = gathered([opacity_word_ref[h] for h in range(halves)])
        rise = (word >> OPACITY_BITS).astype(jnp.float32)
        start = (word & (OPACITY_SPAN - 1)).astype(jnp.float32)
        return color, (start + fraction * rise) * (1.0 / OPACITY_UNIT)

    return look_up


def column_differences(shape):
    lane = lax.broadcasted_iota(jnp.int32, shape, 1)
    chunk = lax.broadcasted_iota(jnp.int32, shape, 0)
    at_first, at_last = lane == 0, lane == shape[1] - 1
    at_left = at_first & (chunk == 0)
    at_right = at_last & (chunk == shape[0] - 1)

    def difference(x):
        right = shifted(x, 1, -1)
        right = jnp.where(at_last, shifted(right, 0, -1), right)
        right = jnp.where(at_right, 0.0, right)
        left = shifted(x, 1, 1)
        left = jnp.where(at_first, shifted(left, 0, 1), left)
        left = jnp.where(at_left, 0.0, left)
        return right - left

    return difference


def depth_differences(field):
    last = len(field) - 1
    made = {}
    for k in range(last + 1):
        ends = (min(k + 1, last), max(k - 1, 0))
        if ends not in made:
            made[ends] = field[ends[0]] - field[ends[1]]
    return [made[(min(k + 1, last), max(k - 1, 0))] for k in range(last + 1)]


def shading_of(facing, squared_plus_one):
    near = pltpu.reciprocal(squared_plus_one, approx=True)
    inverse = near * (2.0 - squared_plus_one * near)
    return 0.25 + (facing * facing) * inverse


def main_kernel(edge_rows, brick_at, light_ref, color_word_ref, opacity_word_ref, tile_ref,
                part_ref, color_sum_ref, keep_ref):
    bricks, padded_rows, depth, chunks, lanes = tile_ref.shape
    rows = padded_rows - 2
    inner_rows = [r for r in range(rows) if r not in edge_rows]
    shape = (chunks, lanes)
    look_up = table_lookup(color_word_ref, opacity_word_ref)
    column_difference = column_differences(shape)
    light = [light_ref[i] for i in range(3)]
    together = 4 if bricks % 4 == 0 else 1

    def step(trip, carry):
        colors, keeps = list(carry[0]), list(carry[1])
        at = [brick_at[trip * together + u] for u in range(together)]
        fields = [[[tile_ref[b, r, k] for k in range(depth)] for r in range(padded_rows)] for b in at]
        kept = []
        for b, field in zip(at, fields):
            for r in range(rows):
                for k, dz in enumerate(depth_differences(field[r + 1])):
                    x = field[r + 1][k]
                    dx = column_difference(x)
                    color, opacity = look_up(x)
                    weight = keeps[r] * opacity
                    facing = dz * light[0] + dx * light[2]
                    squared = dz * dz + dx * dx + 1.0
                    if r in edge_rows:
                        values = [weight * color[c] for c in range(3)] + [facing, squared]
                        kept.append((b, edge_rows.index(r), k, values))
                    else:
                        i = inner_rows.index(r)
                        dy = field[r + 2][k] - field[r][k]
                        shaded = weight * shading_of(facing + dy * light[1], squared + dy * dy)
                        for c in range(3):
                            slot = c * len(inner_rows) + i
                            colors[slot] = colors[slot] + shaded * color[c]
                    keeps[r] = keeps[r] - weight
        for b, i, k, values in kept:
            for v, value in enumerate(values):
                part_ref[b, i, k, v] = value
        return tuple(colors), tuple(keeps)

    zero, one = jnp.zeros(shape, jnp.float32), jnp.ones(shape, jnp.float32)
    colors, keeps = lax.fori_loop(
        0, bricks // together, step, ((zero,) * (3 * len(inner_rows)), (one,) * rows))
    for i, value in enumerate(colors):
        color_sum_ref[i] = value
    for r, value in enumerate(keeps):
        keep_ref[r] = value


def finish_kernel(edge_rows, first_ref, last_ref, light_ref, tile_ref, other_ref, part_ref, color_sum_ref, keep_ref,
                  out_ref, staged):
    bricks, padded_rows, depth, chunks, lanes = tile_ref.shape
    rows = padded_rows - 2
    inner_rows = [r for r in range(rows) if r not in edge_rows]
    shape = (chunks, lanes)
    light_rows = light_ref[1]
    is_first, is_last = first_ref[...] == 1.0, last_ref[...] == 1.0

    together = 8 if bricks % 8 == 0 else 1

    def step(trip, colors):
        colors = list(colors)
        for u in range(together):
            b = trip * together + u
            for i, r in enumerate(edge_rows):
                for k in range(depth):
                    above, below = tile_ref[b, r, k], tile_ref[b, r + 2, k]
                    if r == 0:
                        above = jnp.where(is_first, other_ref[b, k], above)
                    if r == rows - 1:
                        below = jnp.where(is_last, other_ref[b, k], below)
                    dy = below - above
                    facing = part_ref[b, i, k, 3] + dy * light_rows
                    shading = shading_of(facing, part_ref[b, i, k, 4] + dy * dy)
                    for c in range(3):
                        slot = c * len(edge_rows) + i
                        colors[slot] = colors[slot] + shading * part_ref[b, i, k, c]
        return tuple(colors)

    zero = jnp.zeros(shape, jnp.float32)
    edge_colors = lax.fori_loop(0, bricks // together, step, (zero,) * (3 * len(edge_rows)))
    for r in range(rows):
        for c in range(3):
            if r in edge_rows:
                value = edge_colors[c * len(edge_rows) + edge_rows.index(r)]
            else:
                value = color_sum_ref[c * len(inner_rows) + inner_rows.index(r)]
            at = (c * rows + r) * chunks
            staged[at:at + chunks, :] = value * (COLOR_SPAN / COLOR_UNIT)
        at = (3 * rows + r) * chunks
        staged[at:at + chunks, :] = 1.0 - keep_ref[r]
    for c in range(4):
        for q in range(chunks):
            source = pl.ds(c * rows * chunks + q, rows, stride=chunks) if rows > 1 else pl.ds(c * chunks + q, 1)
            out_ref[c, 0, :, q * LANES:(q + 1) * LANES] = staged[source, :]


def shards(scalar, bin_index, color_table, opacity_table, light_dir, view_order):
    depth, rows, cols = scalar.shape
    bricks, bands = lax.axis_size("gz"), lax.axis_size("gy")
    tile_rows = rows // bricks
    chunks = cols // LANES
    edge_rows = sorted({0, tile_rows - 1})
    inner_count = tile_rows - len(edge_rows)
    vmem = pl.BlockSpec(memory_space=pltpu.VMEM)
    smem = pl.BlockSpec(memory_space=pltpu.SMEM)
    params = pltpu.CompilerParams(vmem_limit_bytes=32 << 20)
    cells = bricks * depth * cols
    lines = (chunks, LANES)
    halves = (color_table.shape[1] - 1) // LANES
    pieces = 4 if rows % (4 * SUB) == 0 else 1
    hbm = pl.BlockSpec(memory_space=pltpu.HBM)
    given = [scalar, view_order, light_dir, color_table, opacity_table]
    sent, brick_at, color_words, opacity_words, light_rows, first, final, later = pl.pallas_call(
        functools.partial(pack_kernel, bricks),
        out_shape=[
            pltpu.VMEM((bricks, (tile_rows + 2) * depth * chunks, LANES), jnp.float32),
            pltpu.SMEM((bricks,), jnp.int32),
            jax.ShapeDtypeStruct((3, halves) + lines, jnp.float32),
            jax.ShapeDtypeStruct((halves,) + lines, jnp.int32),
            jax.ShapeDtypeStruct((3,) + lines, jnp.float32),
        ] + [jax.ShapeDtypeStruct(lines, jnp.float32)] * 3,
        in_specs=[hbm] * 5,
        out_specs=[vmem, smem] + [vmem] * 6,
        scratch_shapes=[
            pltpu.VMEM(scalar.shape, scalar.dtype),
            pltpu.VMEM(((rows + 2) * depth * chunks, LANES), scalar.dtype),
            pltpu.SMEM(view_order.shape, view_order.dtype),
            pltpu.SMEM(light_dir.shape, light_dir.dtype),
            pltpu.VMEM(color_table.shape, color_table.dtype),
            pltpu.VMEM(opacity_table.shape, opacity_table.dtype),
            pltpu.SemaphoreType.DMA((pieces,)),
            pltpu.SemaphoreType.DMA((4,)),
        ],
        compiler_params=params,
        name="pack_rows",
    )(*[pltpu.with_memory_space_constraint(x, pltpu.HBM) for x in given])
    arrived = lax.all_to_all(
        sent, "gz", split_axis=0, concat_axis=0, tiled=True, axis_index_groups=[exchange_order(bricks)])
    tiles = arrived.reshape(bricks, tile_rows + 2, depth, chunks, LANES)

    last = bricks - 1
    pairs = [(g, g + 1) for g in range(bands - 1)]
    pairs += [(last * bands + g + 1, last * bands + g) for g in range(bands - 1)]
    wrapped = tiles[:, 0] * first + tiles[:, -1] * later
    other = lax.ppermute(wrapped, ("gz", "gy"), pairs)
    parts, color_sums, keeps = pl.pallas_call(
        functools.partial(main_kernel, edge_rows),
        out_shape=[
            jax.ShapeDtypeStruct((bricks, len(edge_rows), depth, 5, chunks, LANES), jnp.float32),
            jax.ShapeDtypeStruct((max(3 * inner_count, 1), chunks, LANES), jnp.float32),
            jax.ShapeDtypeStruct((tile_rows, chunks, LANES), jnp.float32),
        ],
        in_specs=[smem] + [vmem] * 4,
        out_specs=[vmem, vmem, vmem],
        compiler_params=params,
        cost_estimate=pl.CostEstimate(
            flops=100 * cells * tile_rows, bytes_accessed=24 * cells * tile_rows, transcendentals=0),
        name="main_rows",
    )(brick_at, light_rows, color_words, opacity_words, tiles)
    return pl.pallas_call(
        functools.partial(finish_kernel, edge_rows),
        out_shape=jax.ShapeDtypeStruct((4, 1, tile_rows, cols), jnp.float32),
        in_specs=[vmem] * 8,
        out_specs=vmem,
        scratch_shapes=[pltpu.VMEM((4 * tile_rows * chunks, LANES), jnp.float32)],
        compiler_params=params,
        cost_estimate=pl.CostEstimate(
            flops=10 * cells * tile_rows, bytes_accessed=24 * cells * tile_rows, transcendentals=0),
        name="edge_rows",
    )(first, final, light_rows, tiles, other, parts, color_sums, keeps)


def solution(mesh):
    in_specs = (P("gz", "gy", None), P("gz", "gy", None), P(), P(), P(), P())
    out_specs = P(None, "gy", "gz", None)
    return jax.shard_map(shards, mesh=mesh, in_specs=in_specs, out_specs=out_specs, check_vma=False)
```

```python
import functools
import math

import jax
import jax.numpy as jnp
from jax import lax
from jax.experimental import pallas as pl
from jax.experimental.pallas import tpu as pltpu
from jax.sharding import PartitionSpec as P

SUB, LANES = 8, 128
COLOR_UNIT, COLOR_SPAN = 2 ** 11, 2 ** 12
OPACITY_UNIT, OPACITY_BITS = 2 ** 18, 16
OPACITY_SPAN = 2 ** OPACITY_BITS


def exchange_order(tiles):
    parts = 4 if tiles % 4 == 0 else 1
    size = tiles // parts
    walk = [i ^ (i >> 1) for i in range(size)] if size & (size - 1) == 0 else range(size)
    down, up = range(parts)[::-1], range(parts)
    return [p * size + i for turn, i in enumerate(walk) for p in (up if turn % 2 else down)]


def pack_kernel(tiles, field_ref, order_ref, light_ref, color_ref, opacity_ref,
                out_ref, brick_at_ref, color_word_ref, opacity_word_ref, light_rows_ref, first_ref, last_ref, later_ref,
                field, spread, order, light, color, opacity, sems, table_sems):
    depth, rows, cols = field_ref.shape
    chunks = cols // LANES
    block = depth * chunks
    tile_rows = rows // tiles
    pieces = sems.shape[0]
    piece_rows = rows // pieces

    def copy_in(p):
        part = pl.ds(p * piece_rows, piece_rows)
        return pltpu.make_async_copy(field_ref.at[:, part], field.at[:, part], sems.at[p])

    table_copies = [
        pltpu.make_async_copy(source, target, table_sems.at[i])
        for i, (source, target) in enumerate(
            [(color_ref, color), (opacity_ref, opacity), (order_ref, order), (light_ref, light)])
    ]
    for copy in table_copies:
        copy.start()
    for p in range(pieces):
        copy_in(p).start()
    for copy in table_copies:
        copy.wait()
    prepare(order, light, color, opacity, brick_at_ref, color_word_ref, opacity_word_ref, light_rows_ref, first_ref, last_ref, later_ref)
    for p in range(pieces):
        copy_in(p).wait()
        for k in range(depth):
            for row in range(p * piece_rows, (p + 1) * piece_rows, SUB):
                lines = [field[k, row:row + SUB, c * LANES:(c + 1) * LANES] for c in range(chunks)]
                for c, value in enumerate(lines):
                    spread[pl.ds((row + 1) * block + k * chunks + c, SUB, stride=block), :] = value
    spread[(rows + 1) * block:, :] = spread[block:2 * block, :]
    spread[:block, :] = spread[rows * block:(rows + 1) * block, :]
    size = (tile_rows + 2) * block
    for place, t in enumerate(exchange_order(tiles)):
        start = t * tile_rows * block
        out_ref[place] = spread[start:start + size, :]


def prepare(order_ref, light_ref, color_ref, opacity_ref,
            brick_at_ref, color_word_ref, opacity_word_ref, light_rows_ref, first_ref, last_ref, later_ref):
    bins = color_ref.shape[1] - 1
    _, halves, chunks, lanes = color_word_ref.shape
    shape = (chunks, lanes)

    def parts(values, unit):
        scaled = values.astype(jnp.float32) * float(unit)
        return scaled[:, :bins], scaled[:, 1:] - scaled[:, :bins]

    low, slope = parts(color_ref[...], COLOR_UNIT)
    color_words = slope + low * (1.0 / COLOR_SPAN)
    low, slope = parts(opacity_ref[...].reshape(1, bins + 1), OPACITY_UNIT)
    opacity_words = slope.astype(jnp.int32) * OPACITY_SPAN + low.astype(jnp.int32)
    for h in range(halves):
        span = slice(h * lanes, (h + 1) * lanes)
        for c in range(3):
            color_word_ref[c, h] = jnp.broadcast_to(color_words[c:c + 1, span], shape)
        opacity_word_ref[h] = jnp.broadcast_to(opacity_words[:, span], shape)
    for i in range(3):
        light_rows_ref[i] = jnp.full(shape, light_ref[i], jnp.float32) * math.sqrt(0.75)
    here, last = lax.axis_index("gz"), order_ref.shape[0] - 1
    for ref, place in [(first_ref, here == 0), (last_ref, here == last), (later_ref, here != 0)]:
        ref[...] = jnp.full(shape, place.astype(jnp.float32), jnp.float32)
    for place, b in enumerate(exchange_order(order_ref.shape[0])):
        brick_at_ref[order_ref[b]] = place


def shifted(x, axis, shift):
    return pltpu.roll(x, shift % x.shape[axis], axis)


def table_lookup(color_word_ref, opacity_word_ref):
    _, halves, _, lanes = color_word_ref.shape
    bins = halves * lanes

    def look_up(x):
        scaled = x * float(bins)
        index = jnp.minimum(scaled.astype(jnp.int32), bins - 1)
        fraction = scaled - index.astype(jnp.float32)
        low_bits = index & (lanes - 1)

        def gathered(table):
            found = [jnp.take_along_axis(t, low_bits, axis=1, mode="promise_in_bounds") for t in table]
            word = found[0]
            for h in range(1, halves):
                word = jnp.where(index >= h * lanes, found[h], word)
            return word

        color = []
        small = fraction * (1.0 / COLOR_SPAN)
        for c in range(3):
            word = gathered([color_word_ref[c, h] for h in range(halves)])
            rise = jnp.floor(word)
            color.append((word - rise) + small * rise)
        word = gathered([opacity_word_ref[h] for h in range(halves)])
        rise = (word >> OPACITY_BITS).astype(jnp.float32)
        start = (word & (OPACITY_SPAN - 1)).astype(jnp.float32)
        return color, (start + fraction * rise) * (1.0 / OPACITY_UNIT)

    return look_up


def column_differences(shape):
    lane = lax.broadcasted_iota(jnp.int32, shape, 1)
    chunk = lax.broadcasted_iota(jnp.int32, shape, 0)
    at_first, at_last = lane == 0, lane == shape[1] - 1
    at_left = at_first & (chunk == 0)
    at_right = at_last & (chunk == shape[0] - 1)

    def difference(x):
        right = shifted(x, 1, -1)
        right = jnp.where(at_last, shifted(right, 0, -1), right)
        right = jnp.where(at_right, 0.0, right)
        left = shifted(x, 1, 1)
        left = jnp.where(at_first, shifted(left, 0, 1), left)
        left = jnp.where(at_left, 0.0, left)
        return right - left

    return difference


def depth_differences(field):
    last = len(field) - 1
    made = {}
    for k in range(last + 1):
        ends = (min(k + 1, last), max(k - 1, 0))
        if ends not in made:
            made[ends] = field[ends[0]] - field[ends[1]]
    return [made[(min(k + 1, last), max(k - 1, 0))] for k in range(last + 1)]


def shading_of(facing, squared_plus_one):
    near = pltpu.reciprocal(squared_plus_one, approx=True)
    inverse = near * (2.0 - squared_plus_one * near)
    return 0.25 + (facing * facing) * inverse


def main_kernel(edge_rows, brick_at, light_ref, color_word_ref, opacity_word_ref, tile_ref,
                part_ref, color_sum_ref, keep_ref):
    bricks, padded_rows, depth, chunks, lanes = tile_ref.shape
    rows = padded_rows - 2
    inner_rows = [r for r in range(rows) if r not in edge_rows]
    shape = (chunks, lanes)
    look_up = table_lookup(color_word_ref, opacity_word_ref)
    column_difference = column_differences(shape)
    light = [light_ref[i] for i in range(3)]
    together = 4 if bricks % 4 == 0 else 1

    def step(trip, carry):
        colors, keeps = list(carry[0]), list(carry[1])
        at = [brick_at[trip * together + u] for u in range(together)]
        fields = [[[tile_ref[b, r, k] for k in range(depth)] for r in range(padded_rows)] for b in at]
        kept = []
        for b, field in zip(at, fields):
            for r in range(rows):
                for k, dz in enumerate(depth_differences(field[r + 1])):
                    x = field[r + 1][k]
                    dx = column_difference(x)
                    color, opacity = look_up(x)
                    weight = keeps[r] * opacity
                    facing = dz * light[0] + dx * light[2]
                    squared = dz * dz + dx * dx + 1.0
                    if r in edge_rows:
                        values = [weight * color[c] for c in range(3)] + [facing, squared]
                        kept.append((b, edge_rows.index(r), k, values))
                    else:
                        i = inner_rows.index(r)
                        dy = field[r + 2][k] - field[r][k]
                        shaded = weight * shading_of(facing + dy * light[1], squared + dy * dy)
                        for c in range(3):
                            slot = c * len(inner_rows) + i
                            colors[slot] = colors[slot] + shaded * color[c]
                    keeps[r] = keeps[r] - weight
        for b, i, k, values in kept:
            for v, value in enumerate(values):
                part_ref[b, i, k, v] = value
        return tuple(colors), tuple(keeps)

    zero, one = jnp.zeros(shape, jnp.float32), jnp.ones(shape, jnp.float32)
    colors, keeps = lax.fori_loop(
        0, bricks // together, step, ((zero,) * (3 * len(inner_rows)), (one,) * rows))
    for i, value in enumerate(colors):
        color_sum_ref[i] = value
    for r, value in enumerate(keeps):
        keep_ref[r] = value


def finish_kernel(edge_rows, first_ref, last_ref, light_ref, tile_ref, other_ref, part_ref, color_sum_ref, keep_ref,
                  out_ref, staged):
    bricks, padded_rows, depth, chunks, lanes = tile_ref.shape
    rows = padded_rows - 2
    inner_rows = [r for r in range(rows) if r not in edge_rows]
    shape = (chunks, lanes)
    light_rows = light_ref[1]
    is_first, is_last = first_ref[...] == 1.0, last_ref[...] == 1.0

    together = 8 if bricks % 8 == 0 else 1

    def step(trip, colors):
        colors = list(colors)
        for u in range(together):
            b = trip * together + u
            for i, r in enumerate(edge_rows):
                for k in range(depth):
                    above, below = tile_ref[b, r, k], tile_ref[b, r + 2, k]
                    if r == 0:
                        above = jnp.where(is_first, other_ref[b, k], above)
                    if r == rows - 1:
                        below = jnp.where(is_last, other_ref[b, k], below)
                    dy = below - above
                    facing = part_ref[b, i, k, 3] + dy * light_rows
                    shading = shading_of(facing, part_ref[b, i, k, 4] + dy * dy)
                    for c in range(3):
                        slot = c * len(edge_rows) + i
                        colors[slot] = colors[slot] + shading * part_ref[b, i, k, c]
        return tuple(colors)

    zero = jnp.zeros(shape, jnp.float32)
    edge_colors = lax.fori_loop(0, bricks // together, step, (zero,) * (3 * len(edge_rows)))
    for r in range(rows):
        for c in range(3):
            if r in edge_rows:
                value = edge_colors[c * len(edge_rows) + edge_rows.index(r)]
            else:
                value = color_sum_ref[c * len(inner_rows) + inner_rows.index(r)]
            at = (c * rows + r) * chunks
            staged[at:at + chunks, :] = value * (COLOR_SPAN / COLOR_UNIT)
        at = (3 * rows + r) * chunks
        staged[at:at + chunks, :] = 1.0 - keep_ref[r]
    for c in range(4):
        for q in range(chunks):
            source = pl.ds(c * rows * chunks + q, rows, stride=chunks) if rows > 1 else pl.ds(c * chunks + q, 1)
            out_ref[c, 0, :, q * LANES:(q + 1) * LANES] = staged[source, :]


def shards(scalar, bin_index, color_table, opacity_table, light_dir, view_order):
    depth, rows, cols = scalar.shape
    bricks, bands = lax.axis_size("gz"), lax.axis_size("gy")
    tile_rows = rows // bricks
    chunks = cols // LANES
    edge_rows = sorted({0, tile_rows - 1})
    inner_count = tile_rows - len(edge_rows)
    vmem = pl.BlockSpec(memory_space=pltpu.VMEM)
    smem = pl.BlockSpec(memory_space=pltpu.SMEM)
    params = pltpu.CompilerParams(vmem_limit_bytes=32 << 20)
    cells = bricks * depth * cols
    lines = (chunks, LANES)
    halves = (color_table.shape[1] - 1) // LANES
    pieces = 4 if rows % (4 * SUB) == 0 else 1
    hbm = pl.BlockSpec(memory_space=pltpu.HBM)
    given = [scalar, view_order, light_dir, color_table, opacity_table]
    sent, brick_at, color_words, opacity_words, light_rows, first, final, later = pl.pallas_call(
        functools.partial(pack_kernel, bricks),
        out_shape=[
            pltpu.VMEM((bricks, (tile_rows + 2) * depth * chunks, LANES), jnp.float32),
            pltpu.SMEM((bricks,), jnp.int32),
            jax.ShapeDtypeStruct((3, halves) + lines, jnp.float32),
            jax.ShapeDtypeStruct((halves,) + lines, jnp.int32),
            jax.ShapeDtypeStruct((3,) + lines, jnp.float32),
        ] + [jax.ShapeDtypeStruct(lines, jnp.float32)] * 3,
        in_specs=[hbm] * 5,
        out_specs=[vmem, smem] + [vmem] * 6,
        scratch_shapes=[
            pltpu.VMEM(scalar.shape, scalar.dtype),
            pltpu.VMEM(((rows + 2) * depth * chunks, LANES), scalar.dtype),
            pltpu.SMEM(view_order.shape, view_order.dtype),
            pltpu.SMEM(light_dir.shape, light_dir.dtype),
            pltpu.VMEM(color_table.shape, color_table.dtype),
            pltpu.VMEM(opacity_table.shape, opacity_table.dtype),
            pltpu.SemaphoreType.DMA((pieces,)),
            pltpu.SemaphoreType.DMA((4,)),
        ],
        compiler_params=params,
        name="pack_rows",
    )(*[pltpu.with_memory_space_constraint(x, pltpu.HBM) for x in given])
    arrived = lax.all_to_all(
        sent, "gz", split_axis=0, concat_axis=0, tiled=True, axis_index_groups=[exchange_order(bricks)])
    tiles = arrived.reshape(bricks, tile_rows + 2, depth, chunks, LANES)

    last = bricks - 1
    pairs = [(g, g + 1) for g in range(bands - 1)]
    pairs += [(last * bands + g + 1, last * bands + g) for g in range(bands - 1)]
    wrapped = tiles[:, 0] * first + tiles[:, -1] * later
    other = lax.ppermute(wrapped, ("gz", "gy"), pairs)
    parts, color_sums, keeps = pl.pallas_call(
        functools.partial(main_kernel, edge_rows),
        out_shape=[
            jax.ShapeDtypeStruct((bricks, len(edge_rows), depth, 5, chunks, LANES), jnp.float32),
            jax.ShapeDtypeStruct((max(3 * inner_count, 1), chunks, LANES), jnp.float32),
            jax.ShapeDtypeStruct((tile_rows, chunks, LANES), jnp.float32),
        ],
        in_specs=[smem] + [vmem] * 4,
        out_specs=[vmem, vmem, vmem],
        compiler_params=params,
        cost_estimate=pl.CostEstimate(
            flops=100 * cells * tile_rows, bytes_accessed=24 * cells * tile_rows, transcendentals=0),
        name="main_rows",
    )(brick_at, light_rows, color_words, opacity_words, tiles)
    return pl.pallas_call(
        functools.partial(finish_kernel, edge_rows),
        out_shape=jax.ShapeDtypeStruct((4, 1, tile_rows, cols), jnp.float32),
        in_specs=[vmem] * 8,
        out_specs=vmem,
        scratch_shapes=[pltpu.VMEM((4 * tile_rows * chunks, LANES), jnp.float32)],
        compiler_params=params,
        cost_estimate=pl.CostEstimate(
            flops=10 * cells * tile_rows, bytes_accessed=24 * cells * tile_rows, transcendentals=0),
        name="edge_rows",
    )(first, final, light_rows, tiles, other, parts, color_sums, keeps)


def solution(mesh):
    in_specs = (P("gz", "gy", None), P("gz", "gy", None), P(), P(), P(), P())
    out_specs = P(None, "gy", "gz", None)
    return jax.shard_map(shards, mesh=mesh, in_specs=in_specs, out_specs=out_specs, check_vma=False)
```

```python
import functools
import math

import jax
import jax.numpy as jnp
from jax import lax
from jax.experimental import pallas as pl
from jax.experimental.pallas import tpu as pltpu
from jax.sharding import PartitionSpec as P

SUB, LANES = 8, 128
COLOR_UNIT, COLOR_SPAN = 2 ** 11, 2 ** 12
OPACITY_UNIT, OPACITY_BITS = 2 ** 18, 16
OPACITY_SPAN = 2 ** OPACITY_BITS


def exchange_order(tiles):
    parts = 4 if tiles % 4 == 0 else 1
    return [(parts - 1 - i % parts) * (tiles // parts) + i // parts for i in range(tiles)]


def pack_kernel(tiles, field_ref, order_ref, light_ref, color_ref, opacity_ref,
                out_ref, brick_at_ref, color_word_ref, opacity_word_ref, light_rows_ref, first_ref, last_ref, later_ref,
                field, spread, order, light, color, opacity, sems, table_sems):
    depth, rows, cols = field_ref.shape
    chunks = cols // LANES
    block = depth * chunks
    tile_rows = rows // tiles
    pieces = sems.shape[0]
    piece_rows = rows // pieces

    def copy_in(p):
        part = pl.ds(p * piece_rows, piece_rows)
        return pltpu.make_async_copy(field_ref.at[:, part], field.at[:, part], sems.at[p])

    table_copies = [
        pltpu.make_async_copy(source, target, table_sems.at[i])
        for i, (source, target) in enumerate(
            [(color_ref, color), (opacity_ref, opacity), (order_ref, order), (light_ref, light)])
    ]
    for copy in table_copies:
        copy.start()
    for p in range(pieces):
        copy_in(p).start()
    for copy in table_copies:
        copy.wait()
    prepare(order, light, color, opacity, brick_at_ref, color_word_ref, opacity_word_ref, light_rows_ref, first_ref, last_ref, later_ref)
    for p in range(pieces):
        copy_in(p).wait()
        for k in range(depth):
            for row in range(p * piece_rows, (p + 1) * piece_rows, SUB):
                lines = [field[k, row:row + SUB, c * LANES:(c + 1) * LANES] for c in range(chunks)]
                for c, value in enumerate(lines):
                    spread[pl.ds((row + 1) * block + k * chunks + c, SUB, stride=block), :] = value
    spread[(rows + 1) * block:, :] = spread[block:2 * block, :]
    spread[:block, :] = spread[rows * block:(rows + 1) * block, :]
    size = (tile_rows + 2) * block
    for place, t in enumerate(exchange_order(tiles)):
        start = t * tile_rows * block
        out_ref[place] = spread[start:start + size, :]


def prepare(order_ref, light_ref, color_ref, opacity_ref,
            brick_at_ref, color_word_ref, opacity_word_ref, light_rows_ref, first_ref, last_ref, later_ref):
    bins = color_ref.shape[1] - 1
    _, halves, chunks, lanes = color_word_ref.shape
    shape = (chunks, lanes)

    def parts(values, unit):
        scaled = values.astype(jnp.float32) * float(unit)
        return scaled[:, :bins], scaled[:, 1:] - scaled[:, :bins]

    low, slope = parts(color_ref[...], COLOR_UNIT)
    color_words = slope + low * (1.0 / COLOR_SPAN)
    low, slope = parts(opacity_ref[...].reshape(1, bins + 1), OPACITY_UNIT)
    opacity_words = slope.astype(jnp.int32) * OPACITY_SPAN + low.astype(jnp.int32)
    for h in range(halves):
        span = slice(h * lanes, (h + 1) * lanes)
        for c in range(3):
            color_word_ref[c, h] = jnp.broadcast_to(color_words[c:c + 1, span], shape)
        opacity_word_ref[h] = jnp.broadcast_to(opacity_words[:, span], shape)
    for i in range(3):
        light_rows_ref[i] = jnp.full(shape, light_ref[i], jnp.float32) * math.sqrt(0.75)
    here, last = lax.axis_index("gz"), order_ref.shape[0] - 1
    for ref, place in [(first_ref, here == 0), (last_ref, here == last), (later_ref, here != 0)]:
        ref[...] = jnp.full(shape, place.astype(jnp.float32), jnp.float32)
    for place, b in enumerate(exchange_order(order_ref.shape[0])):
        brick_at_ref[order_ref[b]] = place


def shifted(x, axis, shift):
    return pltpu.roll(x, shift % x.shape[axis], axis)


def table_lookup(color_word_ref, opacity_word_ref):
    _, halves, _, lanes = color_word_ref.shape
    bins = halves * lanes

    def look_up(x):
        scaled = x * float(bins)
        index = jnp.minimum(scaled.astype(jnp.int32), bins - 1)
        fraction = scaled - index.astype(jnp.float32)
        low_bits = index & (lanes - 1)

        def gathered(table):
            found = [jnp.take_along_axis(t, low_bits, axis=1, mode="promise_in_bounds") for t in table]
            word = found[0]
            for h in range(1, halves):
                word = jnp.where(index >= h * lanes, found[h], word)
            return word

        color = []
        small = fraction * (1.0 / COLOR_SPAN)
        for c in range(3):
            word = gathered([color_word_ref[c, h] for h in range(halves)])
            rise = jnp.floor(word)
            color.append((word - rise) + small * rise)
        word = gathered([opacity_word_ref[h] for h in range(halves)])
        rise = (word >> OPACITY_BITS).astype(jnp.float32)
        start = (word & (OPACITY_SPAN - 1)).astype(jnp.float32)
        return color, (start + fraction * rise) * (1.0 / OPACITY_UNIT)

    return look_up


def column_differences(shape):
    lane = lax.broadcasted_iota(jnp.int32, shape, 1)
    chunk = lax.broadcasted_iota(jnp.int32, shape, 0)
    at_first, at_last = lane == 0, lane == shape[1] - 1
    at_left = at_first & (chunk == 0)
    at_right = at_last & (chunk == shape[0] - 1)

    def difference(x):
        right = shifted(x, 1, -1)
        right = jnp.where(at_last, shifted(right, 0, -1), right)
        right = jnp.where(at_right, 0.0, right)
        left = shifted(x, 1, 1)
        left = jnp.where(at_first, shifted(left, 0, 1), left)
        left = jnp.where(at_left, 0.0, left)
        return right - left

    return difference


def depth_differences(field):
    last = len(field) - 1
    made = {}
    for k in range(last + 1):
        ends = (min(k + 1, last), max(k - 1, 0))
        if ends not in made:
            made[ends] = field[ends[0]] - field[ends[1]]
    return [made[(min(k + 1, last), max(k - 1, 0))] for k in range(last + 1)]


def shading_of(facing, squared_plus_one):
    near = pltpu.reciprocal(squared_plus_one, approx=True)
    inverse = near * (2.0 - squared_plus_one * near)
    return 0.25 + (facing * facing) * inverse


def main_kernel(edge_rows, brick_at, light_ref, color_word_ref, opacity_word_ref, tile_ref,
                part_ref, color_sum_ref, keep_ref):
    bricks, padded_rows, depth, chunks, lanes = tile_ref.shape
    rows = padded_rows - 2
    inner_rows = [r for r in range(rows) if r not in edge_rows]
    shape = (chunks, lanes)
    look_up = table_lookup(color_word_ref, opacity_word_ref)
    column_difference = column_differences(shape)
    light = [light_ref[i] for i in range(3)]
    together = 8 if bricks % 8 == 0 else 1

    def step(trip, carry):
        colors, keeps = list(carry[0]), list(carry[1])
        at = [brick_at[trip * together + u] for u in range(together)]
        fields = [[[tile_ref[b, r, k] for k in range(depth)] for r in range(padded_rows)] for b in at]
        kept = []
        for b, field in zip(at, fields):
            for r in range(rows):
                for k, dz in enumerate(depth_differences(field[r + 1])):
                    x = field[r + 1][k]
                    dx = column_difference(x)
                    color, opacity = look_up(x)
                    weight = keeps[r] * opacity
                    facing = dz * light[0] + dx * light[2]
                    squared = dz * dz + dx * dx + 1.0
                    if r in edge_rows:
                        values = [weight * color[c] for c in range(3)] + [facing, squared]
                        kept.append((b, edge_rows.index(r), k, values))
                    else:
                        i = inner_rows.index(r)
                        dy = field[r + 2][k] - field[r][k]
                        shaded = weight * shading_of(facing + dy * light[1], squared + dy * dy)
                        for c in range(3):
                            slot = c * len(inner_rows) + i
                            colors[slot] = colors[slot] + shaded * color[c]
                    keeps[r] = keeps[r] - weight
        for b, i, k, values in kept:
            for v, value in enumerate(values):
                part_ref[b, i, k, v] = value
        return tuple(colors), tuple(keeps)

    zero, one = jnp.zeros(shape, jnp.float32), jnp.ones(shape, jnp.float32)
    colors, keeps = lax.fori_loop(
        0, bricks // together, step, ((zero,) * (3 * len(inner_rows)), (one,) * rows))
    for i, value in enumerate(colors):
        color_sum_ref[i] = value
    for r, value in enumerate(keeps):
        keep_ref[r] = value


def finish_kernel(edge_rows, first_ref, last_ref, light_ref, tile_ref, other_ref, part_ref, color_sum_ref, keep_ref,
                  out_ref, staged):
    bricks, padded_rows, depth, chunks, lanes = tile_ref.shape
    rows = padded_rows - 2
    inner_rows = [r for r in range(rows) if r not in edge_rows]
    shape = (chunks, lanes)
    light_rows = light_ref[1]
    is_first, is_last = first_ref[...] == 1.0, last_ref[...] == 1.0

    together = 16 if bricks % 16 == 0 else 1

    def step(trip, colors):
        colors = list(colors)
        for u in range(together):
            b = trip * together + u
            for i, r in enumerate(edge_rows):
                for k in range(depth):
                    above, below = tile_ref[b, r, k], tile_ref[b, r + 2, k]
                    if r == 0:
                        above = jnp.where(is_first, other_ref[b, k], above)
                    if r == rows - 1:
                        below = jnp.where(is_last, other_ref[b, k], below)
                    dy = below - above
                    facing = part_ref[b, i, k, 3] + dy * light_rows
                    shading = shading_of(facing, part_ref[b, i, k, 4] + dy * dy)
                    for c in range(3):
                        slot = c * len(edge_rows) + i
                        colors[slot] = colors[slot] + shading * part_ref[b, i, k, c]
        return tuple(colors)

    zero = jnp.zeros(shape, jnp.float32)
    edge_colors = lax.fori_loop(0, bricks // together, step, (zero,) * (3 * len(edge_rows)))
    for r in range(rows):
        for c in range(3):
            if r in edge_rows:
                value = edge_colors[c * len(edge_rows) + edge_rows.index(r)]
            else:
                value = color_sum_ref[c * len(inner_rows) + inner_rows.index(r)]
            at = (c * rows + r) * chunks
            staged[at:at + chunks, :] = value * (COLOR_SPAN / COLOR_UNIT)
        at = (3 * rows + r) * chunks
        staged[at:at + chunks, :] = 1.0 - keep_ref[r]
    for c in range(4):
        for q in range(chunks):
            source = pl.ds(c * rows * chunks + q, rows, stride=chunks) if rows > 1 else pl.ds(c * chunks + q, 1)
            out_ref[c, 0, :, q * LANES:(q + 1) * LANES] = staged[source, :]


def shards(scalar, bin_index, color_table, opacity_table, light_dir, view_order):
    depth, rows, cols = scalar.shape
    bricks, bands = lax.axis_size("gz"), lax.axis_size("gy")
    tile_rows = rows // bricks
    chunks = cols // LANES
    edge_rows = sorted({0, tile_rows - 1})
    inner_count = tile_rows - len(edge_rows)
    vmem = pl.BlockSpec(memory_space=pltpu.VMEM)
    smem = pl.BlockSpec(memory_space=pltpu.SMEM)
    params = pltpu.CompilerParams(vmem_limit_bytes=32 << 20)
    cells = bricks * depth * cols
    lines = (chunks, LANES)
    halves = (color_table.shape[1] - 1) // LANES
    pieces = 4 if rows % (4 * SUB) == 0 else 1
    hbm = pl.BlockSpec(memory_space=pltpu.HBM)
    given = [scalar, view_order, light_dir, color_table, opacity_table]
    sent, brick_at, color_words, opacity_words, light_rows, first, final, later = pl.pallas_call(
        functools.partial(pack_kernel, bricks),
        out_shape=[
            pltpu.VMEM((bricks, (tile_rows + 2) * depth * chunks, LANES), jnp.float32),
            pltpu.SMEM((bricks,), jnp.int32),
            jax.ShapeDtypeStruct((3, halves) + lines, jnp.float32),
            jax.ShapeDtypeStruct((halves,) + lines, jnp.int32),
            jax.ShapeDtypeStruct((3,) + lines, jnp.float32),
        ] + [jax.ShapeDtypeStruct(lines, jnp.float32)] * 3,
        in_specs=[hbm] * 5,
        out_specs=[vmem, smem] + [vmem] * 6,
        scratch_shapes=[
            pltpu.VMEM(scalar.shape, scalar.dtype),
            pltpu.VMEM(((rows + 2) * depth * chunks, LANES), scalar.dtype),
            pltpu.SMEM(view_order.shape, view_order.dtype),
            pltpu.SMEM(light_dir.shape, light_dir.dtype),
            pltpu.VMEM(color_table.shape, color_table.dtype),
            pltpu.VMEM(opacity_table.shape, opacity_table.dtype),
            pltpu.SemaphoreType.DMA((pieces,)),
            pltpu.SemaphoreType.DMA((4,)),
        ],
        compiler_params=params,
        name="pack_rows",
    )(*[pltpu.with_memory_space_constraint(x, pltpu.HBM) for x in given])
    arrived = lax.all_to_all(
        sent, "gz", split_axis=0, concat_axis=0, tiled=True, axis_index_groups=[exchange_order(bricks)])
    tiles = arrived.reshape(bricks, tile_rows + 2, depth, chunks, LANES)

    last = bricks - 1
    pairs = [(g, g + 1) for g in range(bands - 1)]
    pairs += [(last * bands + g + 1, last * bands + g) for g in range(bands - 1)]
    wrapped = tiles[:, 0] * first + tiles[:, -1] * later
    other = lax.ppermute(wrapped, ("gz", "gy"), pairs)
    parts, color_sums, keeps = pl.pallas_call(
        functools.partial(main_kernel, edge_rows),
        out_shape=[
            jax.ShapeDtypeStruct((bricks, len(edge_rows), depth, 5, chunks, LANES), jnp.float32),
            jax.ShapeDtypeStruct((max(3 * inner_count, 1), chunks, LANES), jnp.float32),
            jax.ShapeDtypeStruct((tile_rows, chunks, LANES), jnp.float32),
        ],
        in_specs=[smem] + [vmem] * 4,
        out_specs=[vmem, vmem, vmem],
        compiler_params=params,
        cost_estimate=pl.CostEstimate(
            flops=100 * cells * tile_rows, bytes_accessed=24 * cells * tile_rows, transcendentals=0),
        name="main_rows",
    )(brick_at, light_rows, color_words, opacity_words, tiles)
    return pl.pallas_call(
        functools.partial(finish_kernel, edge_rows),
        out_shape=jax.ShapeDtypeStruct((4, 1, tile_rows, cols), jnp.float32),
        in_specs=[vmem] * 8,
        out_specs=vmem,
        scratch_shapes=[pltpu.VMEM((4 * tile_rows * chunks, LANES), jnp.float32)],
        compiler_params=params,
        cost_estimate=pl.CostEstimate(
            flops=10 * cells * tile_rows, bytes_accessed=24 * cells * tile_rows, transcendentals=0),
        name="edge_rows",
    )(first, final, light_rows, tiles, other, parts, color_sums, keeps)


def solution(mesh):
    in_specs = (P("gz", "gy", None), P("gz", "gy", None), P(), P(), P(), P())
    out_specs = P(None, "gy", "gz", None)
    return jax.shard_map(shards, mesh=mesh, in_specs=in_specs, out_specs=out_specs, check_vma=False)
```

```python
import functools
import math

import jax
import jax.numpy as jnp
from jax import lax
from jax.experimental import pallas as pl
from jax.experimental.pallas import tpu as pltpu
from jax.sharding import PartitionSpec as P

SUB, LANES = 8, 128
COLOR_UNIT, COLOR_SPAN = 2 ** 11, 2 ** 12
OPACITY_UNIT, OPACITY_BITS = 2 ** 18, 16
OPACITY_SPAN = 2 ** OPACITY_BITS


def exchange_order(tiles):
    parts = 4 if tiles % 4 == 0 else 1
    return [(parts - 1 - i % parts) * (tiles // parts) + i // parts for i in range(tiles)]


def pack_kernel(tiles, field_ref, order_ref, light_ref, color_ref, opacity_ref,
                out_ref, brick_at_ref, color_word_ref, opacity_word_ref, light_rows_ref, first_ref, last_ref, later_ref,
                field, spread, order, light, color, opacity, sems, table_sems):
    depth, rows, cols = field_ref.shape
    chunks = cols // LANES
    block = depth * chunks
    tile_rows = rows // tiles
    pieces = sems.shape[0]
    piece_rows = rows // pieces

    def copy_in(p):
        part = pl.ds(p * piece_rows, piece_rows)
        return pltpu.make_async_copy(field_ref.at[:, part], field.at[:, part], sems.at[p])

    table_copies = [
        pltpu.make_async_copy(source, target, table_sems.at[i])
        for i, (source, target) in enumerate(
            [(color_ref, color), (opacity_ref, opacity), (order_ref, order), (light_ref, light)])
    ]
    for copy in table_copies:
        copy.start()
    for p in range(pieces):
        copy_in(p).start()
    for copy in table_copies:
        copy.wait()
    prepare(order, light, color, opacity, brick_at_ref, color_word_ref, opacity_word_ref, light_rows_ref, first_ref, last_ref, later_ref)
    for p in range(pieces):
        copy_in(p).wait()
        for k in range(depth):
            for row in range(p * piece_rows, (p + 1) * piece_rows, SUB):
                lines = [field[k, row:row + SUB, c * LANES:(c + 1) * LANES] for c in range(chunks)]
                for c, value in enumerate(lines):
                    spread[pl.ds((row + 1) * block + k * chunks + c, SUB, stride=block), :] = value
    spread[(rows + 1) * block:, :] = spread[block:2 * block, :]
    spread[:block, :] = spread[rows * block:(rows + 1) * block, :]
    size = (tile_rows + 2) * block
    for place, t in enumerate(exchange_order(tiles)):
        start = t * tile_rows * block
        out_ref[place] = spread[start:start + size, :]


def prepare(order_ref, light_ref, color_ref, opacity_ref,
            brick_at_ref, color_word_ref, opacity_word_ref, light_rows_ref, first_ref, last_ref, later_ref):
    bins = color_ref.shape[1] - 1
    _, halves, chunks, lanes = color_word_ref.shape
    shape = (chunks, lanes)

    def parts(values, unit):
        scaled = values.astype(jnp.float32) * float(unit)
        return scaled[:, :bins], scaled[:, 1:] - scaled[:, :bins]

    low, slope = parts(color_ref[...], COLOR_UNIT)
    color_words = slope + low * (1.0 / COLOR_SPAN)
    low, slope = parts(opacity_ref[...].reshape(1, bins + 1), OPACITY_UNIT)
    opacity_words = slope.astype(jnp.int32) * OPACITY_SPAN + low.astype(jnp.int32)
    for h in range(halves):
        span = slice(h * lanes, (h + 1) * lanes)
        for c in range(3):
            color_word_ref[c, h] = jnp.broadcast_to(color_words[c:c + 1, span], shape)
        opacity_word_ref[h] = jnp.broadcast_to(opacity_words[:, span], shape)
    for i in range(3):
        light_rows_ref[i] = jnp.full(shape, light_ref[i], jnp.float32) * math.sqrt(0.75)
    here, last = lax.axis_index("gz"), order_ref.shape[0] - 1
    for ref, place in [(first_ref, here == 0), (last_ref, here == last), (later_ref, here != 0)]:
        ref[...] = jnp.full(shape, place.astype(jnp.float32), jnp.float32)
    for place, b in enumerate(exchange_order(order_ref.shape[0])):
        brick_at_ref[order_ref[b]] = place


def shifted(x, axis, shift):
    return pltpu.roll(x, shift % x.shape[axis], axis)


def table_lookup(color_word_ref, opacity_word_ref):
    _, halves, _, lanes = color_word_ref.shape
    bins = halves * lanes

    def look_up(x):
        scaled = x * float(bins)
        index = jnp.minimum(scaled.astype(jnp.int32), bins - 1)
        fraction = scaled - index.astype(jnp.float32)
        low_bits = index & (lanes - 1)

        def gathered(table):
            found = [jnp.take_along_axis(t, low_bits, axis=1, mode="promise_in_bounds") for t in table]
            word = found[0]
            for h in range(1, halves):
                word = jnp.where(index >= h * lanes, found[h], word)
            return word

        color = []
        small = fraction * (1.0 / COLOR_SPAN)
        for c in range(3):
            word = gathered([color_word_ref[c, h] for h in range(halves)])
            rise = jnp.floor(word)
            color.append((word - rise) + small * rise)
        word = gathered([opacity_word_ref[h] for h in range(halves)])
        rise = (word >> OPACITY_BITS).astype(jnp.float32)
        start = (word & (OPACITY_SPAN - 1)).astype(jnp.float32)
        return color, (start + fraction * rise) * (1.0 / OPACITY_UNIT)

    return look_up


def column_differences(shape):
    lane = lax.broadcasted_iota(jnp.int32, shape, 1)
    chunk = lax.broadcasted_iota(jnp.int32, shape, 0)
    at_first, at_last = lane == 0, lane == shape[1] - 1
    at_left = at_first & (chunk == 0)
    at_right = at_last & (chunk == shape[0] - 1)

    def difference(x):
        right = shifted(x, 1, -1)
        right = jnp.where(at_last, shifted(right, 0, -1), right)
        right = jnp.where(at_right, 0.0, right)
        left = shifted(x, 1, 1)
        left = jnp.where(at_first, shifted(left, 0, 1), left)
        left = jnp.where(at_left, 0.0, left)
        return right - left

    return difference


def depth_differences(field):
    last = len(field) - 1
    made = {}
    for k in range(last + 1):
        ends = (min(k + 1, last), max(k - 1, 0))
        if ends not in made:
            made[ends] = field[ends[0]] - field[ends[1]]
    return [made[(min(k + 1, last), max(k - 1, 0))] for k in range(last + 1)]


def shading_of(facing, squared_plus_one):
    return 0.25 + (facing * facing) * pltpu.reciprocal(squared_plus_one, approx=True)


def main_kernel(edge_rows, brick_at, light_ref, color_word_ref, opacity_word_ref, tile_ref,
                part_ref, color_sum_ref, keep_ref):
    bricks, padded_rows, depth, chunks, lanes = tile_ref.shape
    rows = padded_rows - 2
    inner_rows = [r for r in range(rows) if r not in edge_rows]
    shape = (chunks, lanes)
    look_up = table_lookup(color_word_ref, opacity_word_ref)
    column_difference = column_differences(shape)
    light = [light_ref[i] for i in range(3)]
    together = 8 if bricks % 8 == 0 else 1

    def step(trip, carry):
        colors, keeps = list(carry[0]), list(carry[1])
        at = [brick_at[trip * together + u] for u in range(together)]
        fields = [[[tile_ref[b, r, k] for k in range(depth)] for r in range(padded_rows)] for b in at]
        kept = []
        for b, field in zip(at, fields):
            for r in range(rows):
                for k, dz in enumerate(depth_differences(field[r + 1])):
                    x = field[r + 1][k]
                    dx = column_difference(x)
                    color, opacity = look_up(x)
                    weight = keeps[r] * opacity
                    facing = dz * light[0] + dx * light[2]
                    squared = (dz * dz + 1.0) + dx * dx
                    if r in edge_rows:
                        values = [weight * color[c] for c in range(3)] + [facing, squared]
                        kept.append((b, edge_rows.index(r), k, values))
                    else:
                        i = inner_rows.index(r)
                        dy = field[r + 2][k] - field[r][k]
                        shaded = weight * shading_of(facing + dy * light[1], squared + dy * dy)
                        for c in range(3):
                            slot = c * len(inner_rows) + i
                            colors[slot] = colors[slot] + shaded * color[c]
                    keeps[r] = keeps[r] - weight
        for b, i, k, values in kept:
            for v, value in enumerate(values):
                part_ref[b, i, k, v] = value
        return tuple(colors), tuple(keeps)

    zero, one = jnp.zeros(shape, jnp.float32), jnp.ones(shape, jnp.float32)
    colors, keeps = lax.fori_loop(
        0, bricks // together, step, ((zero,) * (3 * len(inner_rows)), (one,) * rows))
    for i, value in enumerate(colors):
        color_sum_ref[i] = value
    for r, value in enumerate(keeps):
        keep_ref[r] = value


def finish_kernel(edge_rows, first_ref, last_ref, light_ref, tile_ref, other_ref, part_ref, color_sum_ref, keep_ref,
                  out_ref, staged):
    bricks, padded_rows, depth, chunks, lanes = tile_ref.shape
    rows = padded_rows - 2
    inner_rows = [r for r in range(rows) if r not in edge_rows]
    shape = (chunks, lanes)
    light_rows = light_ref[1]
    is_first, is_last = first_ref[...] == 1.0, last_ref[...] == 1.0

    together = 16 if bricks % 16 == 0 else 1

    def step(trip, colors):
        colors = list(colors)
        for u in range(together):
            b = trip * together + u
            for i, r in enumerate(edge_rows):
                for k in range(depth):
                    above, below = tile_ref[b, r, k], tile_ref[b, r + 2, k]
                    if r == 0:
                        above = jnp.where(is_first, other_ref[b, k], above)
                    if r == rows - 1:
                        below = jnp.where(is_last, other_ref[b, k], below)
                    dy = below - above
                    facing = part_ref[b, i, k, 3] + dy * light_rows
                    shading = shading_of(facing, part_ref[b, i, k, 4] + dy * dy)
                    for c in range(3):
                        slot = c * len(edge_rows) + i
                        colors[slot] = colors[slot] + shading * part_ref[b, i, k, c]
        return tuple(colors)

    zero = jnp.zeros(shape, jnp.float32)
    edge_colors = lax.fori_loop(0, bricks // together, step, (zero,) * (3 * len(edge_rows)))
    for r in range(rows):
        for c in range(3):
            if r in edge_rows:
                value = edge_colors[c * len(edge_rows) + edge_rows.index(r)]
            else:
                value = color_sum_ref[c * len(inner_rows) + inner_rows.index(r)]
            at = (c * rows + r) * chunks
            staged[at:at + chunks, :] = value * (COLOR_SPAN / COLOR_UNIT)
        at = (3 * rows + r) * chunks
        staged[at:at + chunks, :] = 1.0 - keep_ref[r]
    for c in range(4):
        for q in range(chunks):
            source = pl.ds(c * rows * chunks + q, rows, stride=chunks) if rows > 1 else pl.ds(c * chunks + q, 1)
            out_ref[c, 0, :, q * LANES:(q + 1) * LANES] = staged[source, :]


def shards(scalar, bin_index, color_table, opacity_table, light_dir, view_order):
    depth, rows, cols = scalar.shape
    bricks, bands = lax.axis_size("gz"), lax.axis_size("gy")
    tile_rows = rows // bricks
    chunks = cols // LANES
    edge_rows = sorted({0, tile_rows - 1})
    inner_count = tile_rows - len(edge_rows)
    vmem = pl.BlockSpec(memory_space=pltpu.VMEM)
    smem = pl.BlockSpec(memory_space=pltpu.SMEM)
    params = pltpu.CompilerParams(vmem_limit_bytes=32 << 20)
    cells = bricks * depth * cols
    lines = (chunks, LANES)
    halves = (color_table.shape[1] - 1) // LANES
    pieces = 4 if rows % (4 * SUB) == 0 else 1
    hbm = pl.BlockSpec(memory_space=pltpu.HBM)
    given = [scalar, view_order, light_dir, color_table, opacity_table]
    sent, brick_at, color_words, opacity_words, light_rows, first, final, later = pl.pallas_call(
        functools.partial(pack_kernel, bricks),
        out_shape=[
            pltpu.VMEM((bricks, (tile_rows + 2) * depth * chunks, LANES), jnp.float32),
            pltpu.SMEM((bricks,), jnp.int32),
            jax.ShapeDtypeStruct((3, halves) + lines, jnp.float32),
            jax.ShapeDtypeStruct((halves,) + lines, jnp.int32),
            jax.ShapeDtypeStruct((3,) + lines, jnp.float32),
        ] + [jax.ShapeDtypeStruct(lines, jnp.float32)] * 3,
        in_specs=[hbm] * 5,
        out_specs=[vmem, smem] + [vmem] * 6,
        scratch_shapes=[
            pltpu.VMEM(scalar.shape, scalar.dtype),
            pltpu.VMEM(((rows + 2) * depth * chunks, LANES), scalar.dtype),
            pltpu.SMEM(view_order.shape, view_order.dtype),
            pltpu.SMEM(light_dir.shape, light_dir.dtype),
            pltpu.VMEM(color_table.shape, color_table.dtype),
            pltpu.VMEM(opacity_table.shape, opacity_table.dtype),
            pltpu.SemaphoreType.DMA((pieces,)),
            pltpu.SemaphoreType.DMA((4,)),
        ],
        compiler_params=params,
        name="pack_rows",
    )(*[pltpu.with_memory_space_constraint(x, pltpu.HBM) for x in given])
    arrived = lax.all_to_all(
        sent, "gz", split_axis=0, concat_axis=0, tiled=True, axis_index_groups=[exchange_order(bricks)])
    tiles = arrived.reshape(bricks, tile_rows + 2, depth, chunks, LANES)

    last = bricks - 1
    pairs = [(g, g + 1) for g in range(bands - 1)]
    pairs += [(last * bands + g + 1, last * bands + g) for g in range(bands - 1)]
    wrapped = tiles[:, 0] * first + tiles[:, -1] * later
    other = lax.ppermute(wrapped, ("gz", "gy"), pairs)
    parts, color_sums, keeps = pl.pallas_call(
        functools.partial(main_kernel, edge_rows),
        out_shape=[
            jax.ShapeDtypeStruct((bricks, len(edge_rows), depth, 5, chunks, LANES), jnp.float32),
            jax.ShapeDtypeStruct((max(3 * inner_count, 1), chunks, LANES), jnp.float32),
            jax.ShapeDtypeStruct((tile_rows, chunks, LANES), jnp.float32),
        ],
        in_specs=[smem] + [vmem] * 4,
        out_specs=[vmem, vmem, vmem],
        compiler_params=params,
        cost_estimate=pl.CostEstimate(
            flops=100 * cells * tile_rows, bytes_accessed=24 * cells * tile_rows, transcendentals=0),
        name="main_rows",
    )(brick_at, light_rows, color_words, opacity_words, tiles)
    return pl.pallas_call(
        functools.partial(finish_kernel, edge_rows),
        out_shape=jax.ShapeDtypeStruct((4, 1, tile_rows, cols), jnp.float32),
        in_specs=[vmem] * 8,
        out_specs=vmem,
        scratch_shapes=[pltpu.VMEM((4 * tile_rows * chunks, LANES), jnp.float32)],
        compiler_params=params,
        cost_estimate=pl.CostEstimate(
            flops=10 * cells * tile_rows, bytes_accessed=24 * cells * tile_rows, transcendentals=0),
        name="edge_rows",
    )(first, final, light_rows, tiles, other, parts, color_sums, keeps)


def solution(mesh):
    in_specs = (P("gz", "gy", None), P("gz", "gy", None), P(), P(), P(), P())
    out_specs = P(None, "gy", "gz", None)
    return jax.shard_map(shards, mesh=mesh, in_specs=in_specs, out_specs=out_specs, check_vma=False)
```

```python
import functools
import math

import jax
import jax.numpy as jnp
from jax import lax
from jax.experimental import pallas as pl
from jax.experimental.pallas import tpu as pltpu
from jax.sharding import PartitionSpec as P

SUB, LANES = 8, 128
COLOR_UNIT, COLOR_LEAST, OPACITY_UNIT = 2 ** 11, 204, 2 ** 18


def exchange_order(tiles):
    parts = 4 if tiles % 4 == 0 else 1
    return [(parts - 1 - i % parts) * (tiles // parts) + i // parts for i in range(tiles)]


def pack_kernel(tiles, field_ref, order_ref, light_ref, color_ref, opacity_ref,
                out_ref, brick_at_ref, word_ref, light_rows_ref, first_ref, last_ref, later_ref,
                field, spread, order, light, color, opacity, sems, table_sems):
    depth, rows, cols = field_ref.shape
    chunks = cols // LANES
    block = depth * chunks
    tile_rows = rows // tiles
    pieces = sems.shape[0]
    piece_rows = rows // pieces

    def copy_in(p):
        part = pl.ds(p * piece_rows, piece_rows)
        return pltpu.make_async_copy(field_ref.at[:, part], field.at[:, part], sems.at[p])

    table_copies = [
        pltpu.make_async_copy(source, target, table_sems.at[i])
        for i, (source, target) in enumerate(
            [(color_ref, color), (opacity_ref, opacity), (order_ref, order), (light_ref, light)])
    ]
    for copy in table_copies:
        copy.start()
    for p in range(pieces):
        copy_in(p).start()
    for copy in table_copies:
        copy.wait()
    prepare(order, light, color, opacity, brick_at_ref, word_ref, light_rows_ref, first_ref, last_ref, later_ref)
    for p in range(pieces):
        copy_in(p).wait()
        for k in range(depth):
            for row in range(p * piece_rows, (p + 1) * piece_rows, SUB):
                lines = [field[k, row:row + SUB, c * LANES:(c + 1) * LANES] for c in range(chunks)]
                for c, value in enumerate(lines):
                    spread[pl.ds((row + 1) * block + k * chunks + c, SUB, stride=block), :] = value
    spread[(rows + 1) * block:, :] = spread[block:2 * block, :]
    spread[:block, :] = spread[rows * block:(rows + 1) * block, :]
    size = (tile_rows + 2) * block
    for place, t in enumerate(exchange_order(tiles)):
        start = t * tile_rows * block
        out_ref[place] = spread[start:start + size, :]


def prepare(order_ref, light_ref, color_ref, opacity_ref,
            brick_at_ref, word_ref, light_rows_ref, first_ref, last_ref, later_ref):
    bins = color_ref.shape[1] - 1
    _, halves, chunks, lanes = word_ref.shape
    shape = (chunks, lanes)

    def parts(values, unit):
        scaled = (values.astype(jnp.float32) * float(unit)).astype(jnp.int32)
        return scaled[:, :bins], scaled[:, 1:] - scaled[:, :bins]

    start, slope = parts(opacity_ref[...].reshape(1, bins + 1), OPACITY_UNIT)
    pieces = [start & 511, (start >> 9) + ((slope & 31) << 4), (slope >> 5) & 511]
    start, slope = parts(color_ref[...], COLOR_UNIT)
    upper = (slope << 20) + ((start - COLOR_LEAST) << 9)
    for c in range(3):
        word = upper[c:c + 1] + pieces[c]
        for h in range(halves):
            word_ref[c, h] = jnp.broadcast_to(word[:, h * lanes:(h + 1) * lanes], shape)
    for i in range(3):
        light_rows_ref[i] = jnp.full(shape, light_ref[i], jnp.float32) * math.sqrt(0.75)
    here, last = lax.axis_index("gz"), order_ref.shape[0] - 1
    for ref, place in [(first_ref, here == 0), (last_ref, here == last), (later_ref, here != 0)]:
        ref[...] = jnp.full(shape, place.astype(jnp.float32), jnp.float32)
    for place, b in enumerate(exchange_order(order_ref.shape[0])):
        brick_at_ref[order_ref[b]] = place


def shifted(x, axis, shift):
    return pltpu.roll(x, shift % x.shape[axis], axis)


def table_lookup(word_ref):
    _, halves, _, lanes = word_ref.shape
    bins = halves * lanes

    def look_up(x):
        scaled = x * float(bins)
        index = jnp.minimum(scaled.astype(jnp.int32), bins - 1)
        fraction = scaled - index.astype(jnp.float32)
        low_bits = index & (lanes - 1)
        words = []
        for c in range(3):
            found = [
                jnp.take_along_axis(word_ref[c, h], low_bits, axis=1, mode="promise_in_bounds")
                for h in range(halves)
            ]
            word = found[0]
            for h in range(1, halves):
                word = jnp.where(index >= h * lanes, found[h], word)
            words.append(word)

        def blended(start, slope):
            return start.astype(jnp.float32) + fraction * slope.astype(jnp.float32)

        color = [blended(((w >> 9) & 2047) + COLOR_LEAST, w >> 20) for w in words]
        low, middle, high = words
        start = (low & 511) + ((middle & 15) << 9)
        slope = ((high << 23) >> 18) + ((middle >> 4) & 31)
        return color, blended(start, slope) * (1.0 / OPACITY_UNIT)

    return look_up


def column_differences(shape):
    lane = lax.broadcasted_iota(jnp.int32, shape, 1)
    chunk = lax.broadcasted_iota(jnp.int32, shape, 0)
    at_first, at_last = lane == 0, lane == shape[1] - 1
    at_left = at_first & (chunk == 0)
    at_right = at_last & (chunk == shape[0] - 1)

    def difference(x):
        right = shifted(x, 1, -1)
        right = jnp.where(at_last, shifted(right, 0, -1), right)
        right = jnp.where(at_right, 0.0, right)
        left = shifted(x, 1, 1)
        left = jnp.where(at_first, shifted(left, 0, 1), left)
        left = jnp.where(at_left, 0.0, left)
        return right - left

    return difference


def depth_differences(field):
    last = len(field) - 1
    made = {}
    for k in range(last + 1):
        ends = (min(k + 1, last), max(k - 1, 0))
        if ends not in made:
            made[ends] = field[ends[0]] - field[ends[1]]
    return [made[(min(k + 1, last), max(k - 1, 0))] for k in range(last + 1)]


def shading_of(facing, squared_plus_one):
    return 0.25 + (facing * facing) * pltpu.reciprocal(squared_plus_one, approx=True)


def main_kernel(edge_rows, brick_at, light_ref, word_ref, tile_ref,
                part_ref, color_sum_ref, keep_ref):
    bricks, padded_rows, depth, chunks, lanes = tile_ref.shape
    rows = padded_rows - 2
    inner_rows = [r for r in range(rows) if r not in edge_rows]
    shape = (chunks, lanes)
    look_up = table_lookup(word_ref)
    column_difference = column_differences(shape)
    light = [light_ref[i] for i in range(3)]
    together = 8 if bricks % 8 == 0 else 1

    def step(trip, carry):
        colors, keeps = list(carry[0]), list(carry[1])
        at = [brick_at[trip * together + u] for u in range(together)]
        fields = [[[tile_ref[b, r, k] for k in range(depth)] for r in range(padded_rows)] for b in at]
        kept = []
        for b, field in zip(at, fields):
            for r in range(rows):
                for k, dz in enumerate(depth_differences(field[r + 1])):
                    x = field[r + 1][k]
                    dx = column_difference(x)
                    color, opacity = look_up(x)
                    weight = keeps[r] * opacity
                    facing = dz * light[0] + dx * light[2]
                    squared = (dz * dz + 1.0) + dx * dx
                    if r in edge_rows:
                        values = [weight * color[c] for c in range(3)] + [facing, squared]
                        kept.append((b, edge_rows.index(r), k, values))
                    else:
                        i = inner_rows.index(r)
                        dy = field[r + 2][k] - field[r][k]
                        shaded = weight * shading_of(facing + dy * light[1], squared + dy * dy)
                        for c in range(3):
                            slot = c * len(inner_rows) + i
                            colors[slot] = colors[slot] + shaded * color[c]
                    keeps[r] = keeps[r] - weight
        for b, i, k, values in kept:
            for v, value in enumerate(values):
                part_ref[b, i, k, v] = value
        return tuple(colors), tuple(keeps)

    zero, one = jnp.zeros(shape, jnp.float32), jnp.ones(shape, jnp.float32)
    colors, keeps = lax.fori_loop(
        0, bricks // together, step, ((zero,) * (3 * len(inner_rows)), (one,) * rows))
    for i, value in enumerate(colors):
        color_sum_ref[i] = value
    for r, value in enumerate(keeps):
        keep_ref[r] = value


def finish_kernel(edge_rows, first_ref, last_ref, light_ref, tile_ref, other_ref, part_ref, color_sum_ref, keep_ref,
                  out_ref, staged):
    bricks, padded_rows, depth, chunks, lanes = tile_ref.shape
    rows = padded_rows - 2
    inner_rows = [r for r in range(rows) if r not in edge_rows]
    shape = (chunks, lanes)
    light_rows = light_ref[1]
    is_first, is_last = first_ref[...] == 1.0, last_ref[...] == 1.0

    together = 16 if bricks % 16 == 0 else 1

    def step(trip, colors):
        colors = list(colors)
        for u in range(together):
            b = trip * together + u
            for i, r in enumerate(edge_rows):
                for k in range(depth):
                    above, below = tile_ref[b, r, k], tile_ref[b, r + 2, k]
                    if r == 0:
                        above = jnp.where(is_first, other_ref[b, k], above)
                    if r == rows - 1:
                        below = jnp.where(is_last, other_ref[b, k], below)
                    dy = below - above
                    facing = part_ref[b, i, k, 3] + dy * light_rows
                    shading = shading_of(facing, part_ref[b, i, k, 4] + dy * dy)
                    for c in range(3):
                        slot = c * len(edge_rows) + i
                        colors[slot] = colors[slot] + shading * part_ref[b, i, k, c]
        return tuple(colors)

    zero = jnp.zeros(shape, jnp.float32)
    edge_colors = lax.fori_loop(0, bricks // together, step, (zero,) * (3 * len(edge_rows)))
    for r in range(rows):
        for c in range(3):
            if r in edge_rows:
                value = edge_colors[c * len(edge_rows) + edge_rows.index(r)]
            else:
                value = color_sum_ref[c * len(inner_rows) + inner_rows.index(r)]
            at = (c * rows + r) * chunks
            staged[at:at + chunks, :] = value * (1.0 / COLOR_UNIT)
        at = (3 * rows + r) * chunks
        staged[at:at + chunks, :] = 1.0 - keep_ref[r]
    for c in range(4):
        for q in range(chunks):
            source = pl.ds(c * rows * chunks + q, rows, stride=chunks) if rows > 1 else pl.ds(c * chunks + q, 1)
            out_ref[c, 0, :, q * LANES:(q + 1) * LANES] = staged[source, :]


def shards(scalar, bin_index, color_table, opacity_table, light_dir, view_order):
    depth, rows, cols = scalar.shape
    bricks, bands = lax.axis_size("gz"), lax.axis_size("gy")
    tile_rows = rows // bricks
    chunks = cols // LANES
    edge_rows = sorted({0, tile_rows - 1})
    inner_count = tile_rows - len(edge_rows)
    vmem = pl.BlockSpec(memory_space=pltpu.VMEM)
    smem = pl.BlockSpec(memory_space=pltpu.SMEM)
    params = pltpu.CompilerParams(vmem_limit_bytes=32 << 20)
    cells = bricks * depth * cols
    lines = (chunks, LANES)
    halves = (color_table.shape[1] - 1) // LANES
    pieces = 4 if rows % (4 * SUB) == 0 else 1
    hbm = pl.BlockSpec(memory_space=pltpu.HBM)
    given = [scalar, view_order, light_dir, color_table, opacity_table]
    sent, brick_at, words, light_rows, first, final, later = pl.pallas_call(
        functools.partial(pack_kernel, bricks),
        out_shape=[
            pltpu.VMEM((bricks, (tile_rows + 2) * depth * chunks, LANES), jnp.float32),
            pltpu.SMEM((bricks,), jnp.int32),
            jax.ShapeDtypeStruct((3, halves) + lines, jnp.int32),
            jax.ShapeDtypeStruct((3,) + lines, jnp.float32),
        ] + [jax.ShapeDtypeStruct(lines, jnp.float32)] * 3,
        in_specs=[hbm] * 5,
        out_specs=[vmem, smem] + [vmem] * 5,
        scratch_shapes=[
            pltpu.VMEM(scalar.shape, scalar.dtype),
            pltpu.VMEM(((rows + 2) * depth * chunks, LANES), scalar.dtype),
            pltpu.SMEM(view_order.shape, view_order.dtype),
            pltpu.SMEM(light_dir.shape, light_dir.dtype),
            pltpu.VMEM(color_table.shape, color_table.dtype),
            pltpu.VMEM(opacity_table.shape, opacity_table.dtype),
            pltpu.SemaphoreType.DMA((pieces,)),
            pltpu.SemaphoreType.DMA((4,)),
        ],
        compiler_params=params,
        name="pack_rows",
    )(*[pltpu.with_memory_space_constraint(x, pltpu.HBM) for x in given])
    arrived = lax.all_to_all(
        sent, "gz", split_axis=0, concat_axis=0, tiled=True, axis_index_groups=[exchange_order(bricks)])
    tiles = arrived.reshape(bricks, tile_rows + 2, depth, chunks, LANES)

    last = bricks - 1
    pairs = [(g, g + 1) for g in range(bands - 1)]
    pairs += [(last * bands + g + 1, last * bands + g) for g in range(bands - 1)]
    wrapped = tiles[:, 0] * first + tiles[:, -1] * later
    other = lax.ppermute(wrapped, ("gz", "gy"), pairs)
    parts, color_sums, keeps = pl.pallas_call(
        functools.partial(main_kernel, edge_rows),
        out_shape=[
            jax.ShapeDtypeStruct((bricks, len(edge_rows), depth, 5, chunks, LANES), jnp.float32),
            jax.ShapeDtypeStruct((max(3 * inner_count, 1), chunks, LANES), jnp.float32),
            jax.ShapeDtypeStruct((tile_rows, chunks, LANES), jnp.float32),
        ],
        in_specs=[smem] + [vmem] * 3,
        out_specs=[vmem, vmem, vmem],
        compiler_params=params,
        cost_estimate=pl.CostEstimate(
            flops=100 * cells * tile_rows, bytes_accessed=24 * cells * tile_rows, transcendentals=0),
        name="main_rows",
    )(brick_at, light_rows, words, tiles)
    return pl.pallas_call(
        functools.partial(finish_kernel, edge_rows),
        out_shape=jax.ShapeDtypeStruct((4, 1, tile_rows, cols), jnp.float32),
        in_specs=[vmem] * 8,
        out_specs=vmem,
        scratch_shapes=[pltpu.VMEM((4 * tile_rows * chunks, LANES), jnp.float32)],
        compiler_params=params,
        cost_estimate=pl.CostEstimate(
            flops=10 * cells * tile_rows, bytes_accessed=24 * cells * tile_rows, transcendentals=0),
        name="edge_rows",
    )(first, final, light_rows, tiles, other, parts, color_sums, keeps)


def solution(mesh):
    in_specs = (P("gz", "gy", None), P("gz", "gy", None), P(), P(), P(), P())
    out_specs = P(None, "gy", "gz", None)
    return jax.shard_map(shards, mesh=mesh, in_specs=in_specs, out_specs=out_specs, check_vma=False)
```

```python
import functools
import math

import jax
import jax.numpy as jnp
from jax import lax
from jax.experimental import pallas as pl
from jax.experimental.pallas import tpu as pltpu
from jax.sharding import PartitionSpec as P

SUB, LANES = 8, 128
COLOR_UNIT, COLOR_LEAST, OPACITY_UNIT = 2 ** 11, 204, 2 ** 18


def exchange_order(tiles):
    parts = 4 if tiles % 4 == 0 else 1
    size = tiles // parts
    return [p * size + i for i in range(size)[::-1] for p in range(parts)[::-1]]


def pack_kernel(tiles, field_ref, order_ref, light_ref, color_ref, opacity_ref,
                out_ref, brick_at_ref, word_ref, light_rows_ref, first_ref, last_ref, later_ref,
                field, spread, order, light, color, opacity, sems, table_sems):
    depth, rows, cols = field_ref.shape
    chunks = cols // LANES
    block = depth * chunks
    tile_rows = rows // tiles
    pieces = sems.shape[0]
    piece_rows = rows // pieces

    def copy_in(p):
        part = pl.ds(p * piece_rows, piece_rows)
        return pltpu.make_async_copy(field_ref.at[:, part], field.at[:, part], sems.at[p])

    table_copies = [
        pltpu.make_async_copy(source, target, table_sems.at[i])
        for i, (source, target) in enumerate(
            [(color_ref, color), (opacity_ref, opacity), (order_ref, order), (light_ref, light)])
    ]
    for copy in table_copies:
        copy.start()
    for p in range(pieces):
        copy_in(p).start()
    for copy in table_copies:
        copy.wait()
    for p in range(pieces):
        copy_in(p).wait()
    prepare(order, light, color, opacity, brick_at_ref, word_ref, light_rows_ref, first_ref, last_ref, later_ref)
    for k in range(depth):
        for row in range(0, rows, SUB):
            lines = [field[k, row:row + SUB, c * LANES:(c + 1) * LANES] for c in range(chunks)]
            for c, value in enumerate(lines):
                spread[pl.ds((row + 1) * block + k * chunks + c, SUB, stride=block), :] = value
    spread[(rows + 1) * block:, :] = spread[block:2 * block, :]
    spread[:block, :] = spread[rows * block:(rows + 1) * block, :]
    size = (tile_rows + 2) * block
    for place, t in enumerate(exchange_order(tiles)):
        start = t * tile_rows * block
        out_ref[place] = spread[start:start + size, :]


def prepare(order_ref, light_ref, color_ref, opacity_ref,
            brick_at_ref, word_ref, light_rows_ref, first_ref, last_ref, later_ref):
    bins = color_ref.shape[1] - 1
    _, halves, chunks, lanes = word_ref.shape
    shape = (chunks, lanes)

    def parts(values, unit):
        scaled = (values.astype(jnp.float32) * float(unit)).astype(jnp.int32)
        return scaled[:, :bins], scaled[:, 1:] - scaled[:, :bins]

    start, slope = parts(opacity_ref[...].reshape(1, bins + 1), OPACITY_UNIT)
    pieces = [start & 511, (start >> 9) + ((slope & 31) << 4), (slope >> 5) & 511]
    start, slope = parts(color_ref[...], COLOR_UNIT)
    upper = (slope << 20) + ((start - COLOR_LEAST) << 9)
    for c in range(3):
        word = upper[c:c + 1] + pieces[c]
        for h in range(halves):
            word_ref[c, h] = jnp.broadcast_to(word[:, h * lanes:(h + 1) * lanes], shape)
    for i in range(3):
        light_rows_ref[i] = jnp.full(shape, light_ref[i], jnp.float32) * math.sqrt(0.75)
    here, last = lax.axis_index("gz"), order_ref.shape[0] - 1
    for ref, place in [(first_ref, here == 0), (last_ref, here == last), (later_ref, here != 0)]:
        ref[...] = jnp.full(shape, place.astype(jnp.float32), jnp.float32)
    for place, b in enumerate(exchange_order(order_ref.shape[0])):
        brick_at_ref[order_ref[b]] = place


def shifted(x, axis, shift):
    return pltpu.roll(x, shift % x.shape[axis], axis)


def table_lookup(word_ref):
    _, halves, _, lanes = word_ref.shape
    bins = halves * lanes

    def look_up(x):
        scaled = x * float(bins)
        index = jnp.minimum(scaled.astype(jnp.int32), bins - 1)
        fraction = scaled - index.astype(jnp.float32)
        low_bits = index & (lanes - 1)
        words = []
        for c in range(3):
            found = [
                jnp.take_along_axis(word_ref[c, h], low_bits, axis=1, mode="promise_in_bounds")
                for h in range(halves)
            ]
            word = found[0]
            for h in range(1, halves):
                word = jnp.where(index >= h * lanes, found[h], word)
            words.append(word)

        def blended(start, slope):
            return start.astype(jnp.float32) + fraction * slope.astype(jnp.float32)

        color = [blended(((w >> 9) & 2047) + COLOR_LEAST, w >> 20) for w in words]
        low, middle, high = words
        start = (low & 511) + ((middle & 15) << 9)
        slope = ((high << 23) >> 18) + ((middle >> 4) & 31)
        return color, blended(start, slope) * (1.0 / OPACITY_UNIT)

    return look_up


def column_differences(shape):
    lane = lax.broadcasted_iota(jnp.int32, shape, 1)
    chunk = lax.broadcasted_iota(jnp.int32, shape, 0)
    at_first, at_last = lane == 0, lane == shape[1] - 1
    at_left = at_first & (chunk == 0)
    at_right = at_last & (chunk == shape[0] - 1)

    def difference(x):
        right = shifted(x, 1, -1)
        right = jnp.where(at_last, shifted(right, 0, -1), right)
        right = jnp.where(at_right, 0.0, right)
        left = shifted(x, 1, 1)
        left = jnp.where(at_first, shifted(left, 0, 1), left)
        left = jnp.where(at_left, 0.0, left)
        return right - left

    return difference


def depth_differences(field):
    last = len(field) - 1
    made = {}
    for k in range(last + 1):
        ends = (min(k + 1, last), max(k - 1, 0))
        if ends not in made:
            made[ends] = field[ends[0]] - field[ends[1]]
    return [made[(min(k + 1, last), max(k - 1, 0))] for k in range(last + 1)]


def shading_of(facing, squared_plus_one):
    return 0.25 + (facing * facing) * pltpu.reciprocal(squared_plus_one, approx=True)


def main_kernel(edge_rows, brick_at, light_ref, word_ref, tile_ref,
                part_ref, color_sum_ref, keep_ref):
    bricks, padded_rows, depth, chunks, lanes = tile_ref.shape
    rows = padded_rows - 2
    inner_rows = [r for r in range(rows) if r not in edge_rows]
    shape = (chunks, lanes)
    look_up = table_lookup(word_ref)
    column_difference = column_differences(shape)
    light = [light_ref[i] for i in range(3)]
    together = 8 if bricks % 8 == 0 else 1

    def step(trip, carry):
        colors, keeps = list(carry[0]), list(carry[1])
        at = [brick_at[trip * together + u] for u in range(together)]
        fields = [[[tile_ref[b, r, k] for k in range(depth)] for r in range(padded_rows)] for b in at]
        kept = []
        for b, field in zip(at, fields):
            for r in range(rows):
                for k, dz in enumerate(depth_differences(field[r + 1])):
                    x = field[r + 1][k]
                    dx = column_difference(x)
                    color, opacity = look_up(x)
                    weight = keeps[r] * opacity
                    facing = dz * light[0] + dx * light[2]
                    squared = (dz * dz + 1.0) + dx * dx
                    if r in edge_rows:
                        values = [weight * color[c] for c in range(3)] + [facing, squared]
                        kept.append((b, edge_rows.index(r), k, values))
                    else:
                        i = inner_rows.index(r)
                        dy = field[r + 2][k] - field[r][k]
                        shaded = weight * shading_of(facing + dy * light[1], squared + dy * dy)
                        for c in range(3):
                            slot = c * len(inner_rows) + i
                            colors[slot] = colors[slot] + shaded * color[c]
                    keeps[r] = keeps[r] - weight
        for b, i, k, values in kept:
            for v, value in enumerate(values):
                part_ref[b, i, k, v] = value
        return tuple(colors), tuple(keeps)

    zero, one = jnp.zeros(shape, jnp.float32), jnp.ones(shape, jnp.float32)
    colors, keeps = lax.fori_loop(
        0, bricks // together, step, ((zero,) * (3 * len(inner_rows)), (one,) * rows))
    for i, value in enumerate(colors):
        color_sum_ref[i] = value
    for r, value in enumerate(keeps):
        keep_ref[r] = value


def finish_kernel(edge_rows, first_ref, last_ref, light_ref, tile_ref, other_ref, part_ref, color_sum_ref, keep_ref,
                  out_ref, staged):
    bricks, padded_rows, depth, chunks, lanes = tile_ref.shape
    rows = padded_rows - 2
    inner_rows = [r for r in range(rows) if r not in edge_rows]
    shape = (chunks, lanes)
    light_rows = light_ref[1]
    is_first, is_last = first_ref[...] == 1.0, last_ref[...] == 1.0

    together = 16 if bricks % 16 == 0 else 1

    def step(trip, colors):
        colors = list(colors)
        for u in range(together):
            b = trip * together + u
            for i, r in enumerate(edge_rows):
                for k in range(depth):
                    above, below = tile_ref[b, r, k], tile_ref[b, r + 2, k]
                    if r == 0:
                        above = jnp.where(is_first, other_ref[b, k], above)
                    if r == rows - 1:
                        below = jnp.where(is_last, other_ref[b, k], below)
                    dy = below - above
                    facing = part_ref[b, i, k, 3] + dy * light_rows
                    shading = shading_of(facing, part_ref[b, i, k, 4] + dy * dy)
                    for c in range(3):
                        slot = c * len(edge_rows) + i
                        colors[slot] = colors[slot] + shading * part_ref[b, i, k, c]
        return tuple(colors)

    zero = jnp.zeros(shape, jnp.float32)
    edge_colors = lax.fori_loop(0, bricks // together, step, (zero,) * (3 * len(edge_rows)))
    for r in range(rows):
        for c in range(3):
            if r in edge_rows:
                value = edge_colors[c * len(edge_rows) + edge_rows.index(r)]
            else:
                value = color_sum_ref[c * len(inner_rows) + inner_rows.index(r)]
            at = (c * rows + r) * chunks
            staged[at:at + chunks, :] = value * (1.0 / COLOR_UNIT)
        at = (3 * rows + r) * chunks
        staged[at:at + chunks, :] = 1.0 - keep_ref[r]
    for c in range(4):
        for q in range(chunks):
            source = pl.ds(c * rows * chunks + q, rows, stride=chunks) if rows > 1 else pl.ds(c * chunks + q, 1)
            out_ref[c, 0, :, q * LANES:(q + 1) * LANES] = staged[source, :]


def shards(scalar, bin_index, color_table, opacity_table, light_dir, view_order):
    depth, rows, cols = scalar.shape
    bricks, bands = lax.axis_size("gz"), lax.axis_size("gy")
    tile_rows = rows // bricks
    chunks = cols // LANES
    edge_rows = sorted({0, tile_rows - 1})
    inner_count = tile_rows - len(edge_rows)
    vmem = pl.BlockSpec(memory_space=pltpu.VMEM)
    smem = pl.BlockSpec(memory_space=pltpu.SMEM)
    params = pltpu.CompilerParams(vmem_limit_bytes=32 << 20)
    cells = bricks * depth * cols
    lines = (chunks, LANES)
    halves = (color_table.shape[1] - 1) // LANES
    pieces = 4 if rows % (4 * SUB) == 0 else 1
    hbm = pl.BlockSpec(memory_space=pltpu.HBM)
    given = [scalar, view_order, light_dir, color_table, opacity_table]
    sent, brick_at, words, light_rows, first, final, later = pl.pallas_call(
        functools.partial(pack_kernel, bricks),
        out_shape=[
            pltpu.VMEM((bricks, (tile_rows + 2) * depth * chunks, LANES), jnp.float32),
            pltpu.SMEM((bricks,), jnp.int32),
            jax.ShapeDtypeStruct((3, halves) + lines, jnp.int32),
            jax.ShapeDtypeStruct((3,) + lines, jnp.float32),
        ] + [jax.ShapeDtypeStruct(lines, jnp.float32)] * 3,
        in_specs=[hbm] * 5,
        out_specs=[vmem, smem] + [vmem] * 5,
        scratch_shapes=[
            pltpu.VMEM(scalar.shape, scalar.dtype),
            pltpu.VMEM(((rows + 2) * depth * chunks, LANES), scalar.dtype),
            pltpu.SMEM(view_order.shape, view_order.dtype),
            pltpu.SMEM(light_dir.shape, light_dir.dtype),
            pltpu.VMEM(color_table.shape, color_table.dtype),
            pltpu.VMEM(opacity_table.shape, opacity_table.dtype),
            pltpu.SemaphoreType.DMA((pieces,)),
            pltpu.SemaphoreType.DMA((4,)),
        ],
        compiler_params=params,
        name="pack_rows",
    )(*[pltpu.with_memory_space_constraint(x, pltpu.HBM) for x in given])
    arrived = lax.all_to_all(
        sent, "gz", split_axis=0, concat_axis=0, tiled=True, axis_index_groups=[exchange_order(bricks)])
    tiles = arrived.reshape(bricks, tile_rows + 2, depth, chunks, LANES)

    last = bricks - 1
    pairs = [(g, g + 1) for g in range(bands - 1)]
    pairs += [(last * bands + g + 1, last * bands + g) for g in range(bands - 1)]
    wrapped = tiles[:, 0] * first + tiles[:, -1] * later
    other = lax.ppermute(wrapped, ("gz", "gy"), pairs)
    parts, color_sums, keeps = pl.pallas_call(
        functools.partial(main_kernel, edge_rows),
        out_shape=[
            jax.ShapeDtypeStruct((bricks, len(edge_rows), depth, 5, chunks, LANES), jnp.float32),
            jax.ShapeDtypeStruct((max(3 * inner_count, 1), chunks, LANES), jnp.float32),
            jax.ShapeDtypeStruct((tile_rows, chunks, LANES), jnp.float32),
        ],
        in_specs=[smem] + [vmem] * 3,
        out_specs=[vmem, vmem, vmem],
        compiler_params=params,
        cost_estimate=pl.CostEstimate(
            flops=100 * cells * tile_rows, bytes_accessed=24 * cells * tile_rows, transcendentals=0),
        name="main_rows",
    )(brick_at, light_rows, words, tiles)
    return pl.pallas_call(
        functools.partial(finish_kernel, edge_rows),
        out_shape=jax.ShapeDtypeStruct((4, 1, tile_rows, cols), jnp.float32),
        in_specs=[vmem] * 8,
        out_specs=vmem,
        scratch_shapes=[pltpu.VMEM((4 * tile_rows * chunks, LANES), jnp.float32)],
        compiler_params=params,
        cost_estimate=pl.CostEstimate(
            flops=10 * cells * tile_rows, bytes_accessed=24 * cells * tile_rows, transcendentals=0),
        name="edge_rows",
    )(first, final, light_rows, tiles, other, parts, color_sums, keeps)


def solution(mesh):
    in_specs = (P("gz", "gy", None), P("gz", "gy", None), P(), P(), P(), P())
    out_specs = P(None, "gy", "gz", None)
    return jax.shard_map(shards, mesh=mesh, in_specs=in_specs, out_specs=out_specs, check_vma=False)
```

```python
import functools
import math

import jax
import jax.numpy as jnp
from jax import lax
from jax.experimental import pallas as pl
from jax.experimental.pallas import tpu as pltpu
from jax.sharding import PartitionSpec as P

SUB, LANES = 8, 128
COLOR_UNIT, COLOR_LEAST, OPACITY_UNIT = 2 ** 11, 204, 2 ** 18


def exchange_order(tiles):
    quarters = [3, 1, 2, 0] if tiles % 4 == 0 else [0]
    size = tiles // len(quarters)
    return [quarter * size + i for i in range(size) for quarter in quarters]


def pack_kernel(tiles, field_ref, order_ref, light_ref, color_ref, opacity_ref,
                out_ref, brick_at_ref, word_ref, light_rows_ref, first_ref, last_ref, later_ref,
                field, spread, order, light, color, opacity, sems, table_sems):
    depth, rows, cols = field_ref.shape
    chunks = cols // LANES
    block = depth * chunks
    tile_rows = rows // tiles
    pieces = sems.shape[0]
    piece_rows = rows // pieces

    def copy_in(p):
        part = pl.ds(p * piece_rows, piece_rows)
        return pltpu.make_async_copy(field_ref.at[:, part], field.at[:, part], sems.at[p])

    table_copies = [
        pltpu.make_async_copy(source, target, table_sems.at[i])
        for i, (source, target) in enumerate(
            [(color_ref, color), (opacity_ref, opacity), (order_ref, order), (light_ref, light)])
    ]
    for copy in table_copies:
        copy.start()
    for p in range(pieces):
        copy_in(p).start()
    for copy in table_copies:
        copy.wait()
    prepare(order, light, color, opacity, brick_at_ref, word_ref, light_rows_ref, first_ref, last_ref, later_ref)
    for p in range(pieces):
        copy_in(p).wait()
        for k in range(depth):
            for row in range(p * piece_rows, (p + 1) * piece_rows, SUB):
                lines = [field[k, row:row + SUB, c * LANES:(c + 1) * LANES] for c in range(chunks)]
                for c, value in enumerate(lines):
                    spread[pl.ds((row + 1) * block + k * chunks + c, SUB, stride=block), :] = value
    spread[(rows + 1) * block:, :] = spread[block:2 * block, :]
    spread[:block, :] = spread[rows * block:(rows + 1) * block, :]
    size = (tile_rows + 2) * block
    for place, t in enumerate(exchange_order(tiles)):
        start = t * tile_rows * block
        out_ref[place] = spread[start:start + size, :]


def prepare(order_ref, light_ref, color_ref, opacity_ref,
            brick_at_ref, word_ref, light_rows_ref, first_ref, last_ref, later_ref):
    bins = color_ref.shape[1] - 1
    _, halves, chunks, lanes = word_ref.shape
    shape = (chunks, lanes)

    def parts(values, unit):
        scaled = (values.astype(jnp.float32) * float(unit)).astype(jnp.int32)
        return scaled[:, :bins], scaled[:, 1:] - scaled[:, :bins]

    start, slope = parts(opacity_ref[...].reshape(1, bins + 1), OPACITY_UNIT)
    pieces = [start & 511, (start >> 9) + ((slope & 31) << 4), (slope >> 5) & 511]
    start, slope = parts(color_ref[...], COLOR_UNIT)
    upper = (slope << 20) + ((start - COLOR_LEAST) << 9)
    for c in range(3):
        word = upper[c:c + 1] + pieces[c]
        for h in range(halves):
            word_ref[c, h] = jnp.broadcast_to(word[:, h * lanes:(h + 1) * lanes], shape)
    for i in range(3):
        light_rows_ref[i] = jnp.full(shape, light_ref[i], jnp.float32) * math.sqrt(0.75)
    here, last = lax.axis_index("gz"), order_ref.shape[0] - 1
    for ref, place in [(first_ref, here == 0), (last_ref, here == last), (later_ref, here != 0)]:
        ref[...] = jnp.full(shape, place.astype(jnp.float32), jnp.float32)
    for place, b in enumerate(exchange_order(order_ref.shape[0])):
        brick_at_ref[order_ref[b]] = place


def shifted(x, axis, shift):
    return pltpu.roll(x, shift % x.shape[axis], axis)


def table_lookup(word_ref):
    _, halves, _, lanes = word_ref.shape
    bins = halves * lanes

    def look_up(x):
        scaled = x * float(bins)
        index = jnp.minimum(scaled.astype(jnp.int32), bins - 1)
        fraction = scaled - index.astype(jnp.float32)
        low_bits = index & (lanes - 1)
        words = []
        for c in range(3):
            found = [
                jnp.take_along_axis(word_ref[c, h], low_bits, axis=1, mode="promise_in_bounds")
                for h in range(halves)
            ]
            word = found[0]
            for h in range(1, halves):
                word = jnp.where(index >= h * lanes, found[h], word)
            words.append(word)

        def blended(start, slope):
            return start.astype(jnp.float32) + fraction * slope.astype(jnp.float32)

        color = [blended(((w >> 9) & 2047) + COLOR_LEAST, w >> 20) for w in words]
        low, middle, high = words
        start = (low & 511) + ((middle & 15) << 9)
        slope = ((high << 23) >> 18) + ((middle >> 4) & 31)
        return color, blended(start, slope) * (1.0 / OPACITY_UNIT)

    return look_up


def column_differences(shape):
    lane = lax.broadcasted_iota(jnp.int32, shape, 1)
    chunk = lax.broadcasted_iota(jnp.int32, shape, 0)
    at_first, at_last = lane == 0, lane == shape[1] - 1
    at_left = at_first & (chunk == 0)
    at_right = at_last & (chunk == shape[0] - 1)

    def difference(x):
        right = shifted(x, 1, -1)
        right = jnp.where(at_last, shifted(right, 0, -1), right)
        right = jnp.where(at_right, 0.0, right)
        left = shifted(x, 1, 1)
        left = jnp.where(at_first, shifted(left, 0, 1), left)
        left = jnp.where(at_left, 0.0, left)
        return right - left

    return difference


def depth_differences(field):
    last = len(field) - 1
    made = {}
    for k in range(last + 1):
        ends = (min(k + 1, last), max(k - 1, 0))
        if ends not in made:
            made[ends] = field[ends[0]] - field[ends[1]]
    return [made[(min(k + 1, last), max(k - 1, 0))] for k in range(last + 1)]


def shading_of(facing, squared_plus_one):
    return 0.25 + (facing * facing) * pltpu.reciprocal(squared_plus_one, approx=True)


def main_kernel(edge_rows, brick_at, light_ref, word_ref, tile_ref,
                part_ref, color_sum_ref, keep_ref):
    bricks, padded_rows, depth, chunks, lanes = tile_ref.shape
    rows = padded_rows - 2
    inner_rows = [r for r in range(rows) if r not in edge_rows]
    shape = (chunks, lanes)
    look_up = table_lookup(word_ref)
    column_difference = column_differences(shape)
    light = [light_ref[i] for i in range(3)]
    together = 8 if bricks % 8 == 0 else 1

    def step(trip, carry):
        colors, keeps = list(carry[0]), list(carry[1])
        at = [brick_at[trip * together + u] for u in range(together)]
        fields = [[[tile_ref[b, r, k] for k in range(depth)] for r in range(padded_rows)] for b in at]
        kept = []
        for b, field in zip(at, fields):
            for r in range(rows):
                for k, dz in enumerate(depth_differences(field[r + 1])):
                    x = field[r + 1][k]
                    dx = column_difference(x)
                    color, opacity = look_up(x)
                    weight = keeps[r] * opacity
                    facing = dz * light[0] + dx * light[2]
                    squared = (dz * dz + 1.0) + dx * dx
                    if r in edge_rows:
                        values = [weight * color[c] for c in range(3)] + [facing, squared]
                        kept.append((b, edge_rows.index(r), k, values))
                    else:
                        i = inner_rows.index(r)
                        dy = field[r + 2][k] - field[r][k]
                        shaded = weight * shading_of(facing + dy * light[1], squared + dy * dy)
                        for c in range(3):
                            slot = c * len(inner_rows) + i
                            colors[slot] = colors[slot] + shaded * color[c]
                    keeps[r] = keeps[r] - weight
        for b, i, k, values in kept:
            for v, value in enumerate(values):
                part_ref[b, i, k, v] = value
        return tuple(colors), tuple(keeps)

    zero, one = jnp.zeros(shape, jnp.float32), jnp.ones(shape, jnp.float32)
    colors, keeps = lax.fori_loop(
        0, bricks // together, step, ((zero,) * (3 * len(inner_rows)), (one,) * rows))
    for i, value in enumerate(colors):
        color_sum_ref[i] = value
    for r, value in enumerate(keeps):
        keep_ref[r] = value


def finish_kernel(edge_rows, first_ref, last_ref, light_ref, tile_ref, other_ref, part_ref, color_sum_ref, keep_ref,
                  out_ref, staged):
    bricks, padded_rows, depth, chunks, lanes = tile_ref.shape
    rows = padded_rows - 2
    inner_rows = [r for r in range(rows) if r not in edge_rows]
    shape = (chunks, lanes)
    light_rows = light_ref[1]
    is_first, is_last = first_ref[...] == 1.0, last_ref[...] == 1.0

    together = 16 if bricks % 16 == 0 else 1

    def step(trip, colors):
        colors = list(colors)
        for u in range(together):
            b = trip * together + u
            for i, r in enumerate(edge_rows):
                for k in range(depth):
                    above, below = tile_ref[b, r, k], tile_ref[b, r + 2, k]
                    if r == 0:
                        above = jnp.where(is_first, other_ref[b, k], above)
                    if r == rows - 1:
                        below = jnp.where(is_last, other_ref[b, k], below)
                    dy = below - above
                    facing = part_ref[b, i, k, 3] + dy * light_rows
                    shading = shading_of(facing, part_ref[b, i, k, 4] + dy * dy)
                    for c in range(3):
                        slot = c * len(edge_rows) + i
                        colors[slot] = colors[slot] + shading * part_ref[b, i, k, c]
        return tuple(colors)

    zero = jnp.zeros(shape, jnp.float32)
    edge_colors = lax.fori_loop(0, bricks // together, step, (zero,) * (3 * len(edge_rows)))
    for r in range(rows):
        for c in range(3):
            if r in edge_rows:
                value = edge_colors[c * len(edge_rows) + edge_rows.index(r)]
            else:
                value = color_sum_ref[c * len(inner_rows) + inner_rows.index(r)]
            at = (c * rows + r) * chunks
            staged[at:at + chunks, :] = value * (1.0 / COLOR_UNIT)
        at = (3 * rows + r) * chunks
        staged[at:at + chunks, :] = 1.0 - keep_ref[r]
    for c in range(4):
        for q in range(chunks):
            source = pl.ds(c * rows * chunks + q, rows, stride=chunks) if rows > 1 else pl.ds(c * chunks + q, 1)
            out_ref[c, 0, :, q * LANES:(q + 1) * LANES] = staged[source, :]


def shards(scalar, bin_index, color_table, opacity_table, light_dir, view_order):
    depth, rows, cols = scalar.shape
    bricks, bands = lax.axis_size("gz"), lax.axis_size("gy")
    tile_rows = rows // bricks
    chunks = cols // LANES
    edge_rows = sorted({0, tile_rows - 1})
    inner_count = tile_rows - len(edge_rows)
    vmem = pl.BlockSpec(memory_space=pltpu.VMEM)
    smem = pl.BlockSpec(memory_space=pltpu.SMEM)
    params = pltpu.CompilerParams(vmem_limit_bytes=32 << 20)
    cells = bricks * depth * cols
    lines = (chunks, LANES)
    halves = (color_table.shape[1] - 1) // LANES
    pieces = 4 if rows % (4 * SUB) == 0 else 1
    hbm = pl.BlockSpec(memory_space=pltpu.HBM)
    given = [scalar, view_order, light_dir, color_table, opacity_table]
    sent, brick_at, words, light_rows, first, final, later = pl.pallas_call(
        functools.partial(pack_kernel, bricks),
        out_shape=[
            pltpu.VMEM((bricks, (tile_rows + 2) * depth * chunks, LANES), jnp.float32),
            pltpu.SMEM((bricks,), jnp.int32),
            jax.ShapeDtypeStruct((3, halves) + lines, jnp.int32),
            jax.ShapeDtypeStruct((3,) + lines, jnp.float32),
        ] + [jax.ShapeDtypeStruct(lines, jnp.float32)] * 3,
        in_specs=[hbm] * 5,
        out_specs=[vmem, smem] + [vmem] * 5,
        scratch_shapes=[
            pltpu.VMEM(scalar.shape, scalar.dtype),
            pltpu.VMEM(((rows + 2) * depth * chunks, LANES), scalar.dtype),
            pltpu.SMEM(view_order.shape, view_order.dtype),
            pltpu.SMEM(light_dir.shape, light_dir.dtype),
            pltpu.VMEM(color_table.shape, color_table.dtype),
            pltpu.VMEM(opacity_table.shape, opacity_table.dtype),
            pltpu.SemaphoreType.DMA((pieces,)),
            pltpu.SemaphoreType.DMA((4,)),
        ],
        compiler_params=params,
        name="pack_rows",
    )(*[pltpu.with_memory_space_constraint(x, pltpu.HBM) for x in given])
    arrived = lax.all_to_all(
        sent, "gz", split_axis=0, concat_axis=0, tiled=True, axis_index_groups=[exchange_order(bricks)])
    tiles = arrived.reshape(bricks, tile_rows + 2, depth, chunks, LANES)

    last = bricks - 1
    pairs = [(g, g + 1) for g in range(bands - 1)]
    pairs += [(last * bands + g + 1, last * bands + g) for g in range(bands - 1)]
    wrapped = tiles[:, 0] * first + tiles[:, -1] * later
    other = lax.ppermute(wrapped, ("gz", "gy"), pairs)
    parts, color_sums, keeps = pl.pallas_call(
        functools.partial(main_kernel, edge_rows),
        out_shape=[
            jax.ShapeDtypeStruct((bricks, len(edge_rows), depth, 5, chunks, LANES), jnp.float32),
            jax.ShapeDtypeStruct((max(3 * inner_count, 1), chunks, LANES), jnp.float32),
            jax.ShapeDtypeStruct((tile_rows, chunks, LANES), jnp.float32),
        ],
        in_specs=[smem] + [vmem] * 3,
        out_specs=[vmem, vmem, vmem],
        compiler_params=params,
        cost_estimate=pl.CostEstimate(
            flops=100 * cells * tile_rows, bytes_accessed=24 * cells * tile_rows, transcendentals=0),
        name="main_rows",
    )(brick_at, light_rows, words, tiles)
    return pl.pallas_call(
        functools.partial(finish_kernel, edge_rows),
        out_shape=jax.ShapeDtypeStruct((4, 1, tile_rows, cols), jnp.float32),
        in_specs=[vmem] * 8,
        out_specs=vmem,
        scratch_shapes=[pltpu.VMEM((4 * tile_rows * chunks, LANES), jnp.float32)],
        compiler_params=params,
        cost_estimate=pl.CostEstimate(
            flops=10 * cells * tile_rows, bytes_accessed=24 * cells * tile_rows, transcendentals=0),
        name="edge_rows",
    )(first, final, light_rows, tiles, other, parts, color_sums, keeps)


def solution(mesh):
    in_specs = (P("gz", "gy", None), P("gz", "gy", None), P(), P(), P(), P())
    out_specs = P(None, "gy", "gz", None)
    return jax.shard_map(shards, mesh=mesh, in_specs=in_specs, out_specs=out_specs, check_vma=False)
```

```python
import functools
import math

import jax
import jax.numpy as jnp
from jax import lax
from jax.experimental import pallas as pl
from jax.experimental.pallas import tpu as pltpu
from jax.sharding import PartitionSpec as P

SUB, LANES = 8, 128
COLOR_UNIT, COLOR_LEAST, OPACITY_UNIT = 2 ** 11, 204, 2 ** 18


def exchange_order(tiles):
    parts = 4 if tiles % 4 == 0 else 1
    return [(parts - 1 - i % parts) * (tiles // parts) + i // parts for i in range(tiles)]


def pack_kernel(tiles, field_ref, order_ref, light_ref, color_ref, opacity_ref,
                out_ref, brick_at_ref, word_ref, light_rows_ref, first_ref, last_ref, later_ref,
                field, spread, order, light, color, opacity, sems, table_sems):
    depth, rows, cols = field_ref.shape
    chunks = cols // LANES
    block = depth * chunks
    tile_rows = rows // tiles
    pieces = sems.shape[0]
    piece_rows = rows // pieces

    def copy_in(p):
        part = pl.ds(p * piece_rows, piece_rows)
        return pltpu.make_async_copy(field_ref.at[:, part], field.at[:, part], sems.at[p])

    table_copies = [
        pltpu.make_async_copy(source, target, table_sems.at[i])
        for i, (source, target) in enumerate(
            [(color_ref, color), (opacity_ref, opacity), (order_ref, order), (light_ref, light)])
    ]
    for copy in table_copies:
        copy.start()
    for p in range(pieces):
        copy_in(p).start()
    for copy in table_copies:
        copy.wait()
    prepare(order, light, color, opacity, brick_at_ref, word_ref, light_rows_ref, first_ref, last_ref, later_ref)
    for p in range(pieces):
        copy_in(p).wait()
        for k in range(depth):
            for row in range(p * piece_rows, (p + 1) * piece_rows, SUB):
                lines = [field[k, row:row + SUB, c * LANES:(c + 1) * LANES] for c in range(chunks)]
                for c, value in enumerate(lines):
                    spread[pl.ds((row + 1) * block + k * chunks + c, SUB, stride=block), :] = value
    spread[(rows + 1) * block:, :] = spread[block:2 * block, :]
    spread[:block, :] = spread[rows * block:(rows + 1) * block, :]
    size = (tile_rows + 2) * block
    for place, t in enumerate(exchange_order(tiles)):
        start = t * tile_rows * block
        out_ref[place] = spread[start:start + size, :]


def prepare(order_ref, light_ref, color_ref, opacity_ref,
            brick_at_ref, word_ref, light_rows_ref, first_ref, last_ref, later_ref):
    bins = color_ref.shape[1] - 1
    _, halves, chunks, lanes = word_ref.shape
    shape = (chunks, lanes)

    def parts(values, unit):
        scaled = (values.astype(jnp.float32) * float(unit)).astype(jnp.int32)
        return scaled[:, :bins], scaled[:, 1:] - scaled[:, :bins]

    start, slope = parts(opacity_ref[...].reshape(1, bins + 1), OPACITY_UNIT)
    pieces = [start & 511, (start >> 9) + ((slope & 31) << 4), (slope >> 5) & 511]
    start, slope = parts(color_ref[...], COLOR_UNIT)
    upper = (slope << 20) + ((start - COLOR_LEAST) << 9)
    for c in range(3):
        word = upper[c:c + 1] + pieces[c]
        for h in range(halves):
            word_ref[c, h] = jnp.broadcast_to(word[:, h * lanes:(h + 1) * lanes], shape)
    for i in range(3):
        light_rows_ref[i] = jnp.full(shape, light_ref[i], jnp.float32) * math.sqrt(0.75)
    here, last = lax.axis_index("gz"), order_ref.shape[0] - 1
    for ref, place in [(first_ref, here == 0), (last_ref, here == last), (later_ref, here != 0)]:
        ref[...] = jnp.full(shape, place.astype(jnp.float32), jnp.float32)
    for place, b in enumerate(exchange_order(order_ref.shape[0])):
        brick_at_ref[order_ref[b]] = place


def table_lookup(word_ref):
    _, halves, _, lanes = word_ref.shape
    bins = halves * lanes

    def look_up(x):
        scaled = x * float(bins)
        index = jnp.minimum(scaled.astype(jnp.int32), bins - 1)
        fraction = scaled - index.astype(jnp.float32)
        low_bits = index & (lanes - 1)
        words = []
        for c in range(3):
            found = [
                jnp.take_along_axis(word_ref[c, h], low_bits, axis=1, mode="promise_in_bounds")
                for h in range(halves)
            ]
            word = found[0]
            for h in range(1, halves):
                word = jnp.where(index >= h * lanes, found[h], word)
            words.append(word)

        def blended(start, slope):
            return start.astype(jnp.float32) + fraction * slope.astype(jnp.float32)

        color = [blended(((w >> 9) & 2047) + COLOR_LEAST, w >> 20) for w in words]
        low, middle, high = words
        start = (low & 511) + ((middle & 15) << 9)
        slope = ((high << 23) >> 18) + ((middle >> 4) & 31)
        return color, blended(start, slope) * (1.0 / OPACITY_UNIT)

    return look_up


def column_differences(fields, carried_ref, first):
    chunks, lanes = fields[0].shape
    count = carried_ref.shape[0] // (chunks + 2)
    lane = lax.broadcasted_iota(jnp.int32, (chunks, lanes), 1)
    at_first, at_last = lane == 0, lane == lanes - 1
    after = [pltpu.roll(x, lanes - 1, 1) for x in fields]
    before = [pltpu.roll(x, 1, 1) for x in fields]
    for i, (right, left) in enumerate(zip(after, before), first):
        carried_ref[pl.ds(count + i, chunks, stride=count), :] = jnp.where(at_last, right, left)
    differences = []
    for i, (right, left) in enumerate(zip(after, before), first):
        further = carried_ref[pl.ds(2 * count + i, chunks, stride=count), :]
        back = carried_ref[pl.ds(i, chunks, stride=count), :]
        differences.append(jnp.where(at_last, further, right) - jnp.where(at_first, back, left))
    return differences


def depth_differences(field):
    last = len(field) - 1
    made = {}
    for k in range(last + 1):
        ends = (min(k + 1, last), max(k - 1, 0))
        if ends not in made:
            made[ends] = field[ends[0]] - field[ends[1]]
    return [made[(min(k + 1, last), max(k - 1, 0))] for k in range(last + 1)]


def shading_of(facing, squared_plus_one):
    return 0.25 + (facing * facing) * pltpu.reciprocal(squared_plus_one, approx=True)


def main_kernel(edge_rows, brick_at, light_ref, word_ref, tile_ref,
                part_ref, color_sum_ref, keep_ref, carried):
    bricks, padded_rows, depth, chunks, lanes = tile_ref.shape
    rows = padded_rows - 2
    inner_rows = [r for r in range(rows) if r not in edge_rows]
    shape = (chunks, lanes)
    look_up = table_lookup(word_ref)
    border = carried.shape[0] // (chunks + 2)
    carried[:border, :] = jnp.zeros((border, lanes), jnp.float32)
    carried[-border:, :] = jnp.zeros((border, lanes), jnp.float32)
    light = [light_ref[i] for i in range(3)]
    together = border // (rows * depth)

    def step(trip, carry):
        colors, keeps = list(carry[0]), list(carry[1])
        at = [brick_at[trip * together + u] for u in range(together)]
        fields = [[[tile_ref[b, r, k] for k in range(depth)] for r in range(padded_rows)] for b in at]
        kept = []
        for u, (b, field) in enumerate(zip(at, fields)):
            cells = [x for line in field[1:-1] for x in line]
            column = column_differences(cells, carried, u * len(cells))
            for r in range(rows):
                for k, dz in enumerate(depth_differences(field[r + 1])):
                    x = field[r + 1][k]
                    dx = column[r * depth + k]
                    color, opacity = look_up(x)
                    weight = keeps[r] * opacity
                    facing = dz * light[0] + dx * light[2]
                    squared = (dz * dz + 1.0) + dx * dx
                    if r in edge_rows:
                        values = [weight * color[c] for c in range(3)] + [facing, squared]
                        kept.append((b, edge_rows.index(r), k, values))
                    else:
                        i = inner_rows.index(r)
                        dy = field[r + 2][k] - field[r][k]
                        shaded = weight * shading_of(facing + dy * light[1], squared + dy * dy)
                        for c in range(3):
                            slot = c * len(inner_rows) + i
                            colors[slot] = colors[slot] + shaded * color[c]
                    keeps[r] = keeps[r] - weight
        for b, i, k, values in kept:
            for v, value in enumerate(values):
                part_ref[b, i, k, v] = value
        return tuple(colors), tuple(keeps)

    zero, one = jnp.zeros(shape, jnp.float32), jnp.ones(shape, jnp.float32)
    colors, keeps = lax.fori_loop(
        0, bricks // together, step, ((zero,) * (3 * len(inner_rows)), (one,) * rows))
    for i, value in enumerate(colors):
        color_sum_ref[i] = value
    for r, value in enumerate(keeps):
        keep_ref[r] = value


def finish_kernel(edge_rows, first_ref, last_ref, light_ref, tile_ref, other_ref, part_ref, color_sum_ref, keep_ref,
                  out_ref, staged):
    bricks, padded_rows, depth, chunks, lanes = tile_ref.shape
    rows = padded_rows - 2
    inner_rows = [r for r in range(rows) if r not in edge_rows]
    shape = (chunks, lanes)
    light_rows = light_ref[1]
    is_first, is_last = first_ref[...] == 1.0, last_ref[...] == 1.0

    together = 16 if bricks % 16 == 0 else 1

    def step(trip, colors):
        colors = list(colors)
        for u in range(together):
            b = trip * together + u
            for i, r in enumerate(edge_rows):
                for k in range(depth):
                    above, below = tile_ref[b, r, k], tile_ref[b, r + 2, k]
                    if r == 0:
                        above = jnp.where(is_first, other_ref[b, k], above)
                    if r == rows - 1:
                        below = jnp.where(is_last, other_ref[b, k], below)
                    dy = below - above
                    facing = part_ref[b, i, k, 3] + dy * light_rows
                    shading = shading_of(facing, part_ref[b, i, k, 4] + dy * dy)
                    for c in range(3):
                        slot = c * len(edge_rows) + i
                        colors[slot] = colors[slot] + shading * part_ref[b, i, k, c]
        return tuple(colors)

    zero = jnp.zeros(shape, jnp.float32)
    edge_colors = lax.fori_loop(0, bricks // together, step, (zero,) * (3 * len(edge_rows)))
    for r in range(rows):
        for c in range(3):
            if r in edge_rows:
                value = edge_colors[c * len(edge_rows) + edge_rows.index(r)]
            else:
                value = color_sum_ref[c * len(inner_rows) + inner_rows.index(r)]
            at = (c * rows + r) * chunks
            staged[at:at + chunks, :] = value * (1.0 / COLOR_UNIT)
        at = (3 * rows + r) * chunks
        staged[at:at + chunks, :] = 1.0 - keep_ref[r]
    for c in range(4):
        for q in range(chunks):
            source = pl.ds(c * rows * chunks + q, rows, stride=chunks) if rows > 1 else pl.ds(c * chunks + q, 1)
            out_ref[c, 0, :, q * LANES:(q + 1) * LANES] = staged[source, :]


def shards(scalar, bin_index, color_table, opacity_table, light_dir, view_order):
    depth, rows, cols = scalar.shape
    bricks, bands = lax.axis_size("gz"), lax.axis_size("gy")
    tile_rows = rows // bricks
    chunks = cols // LANES
    edge_rows = sorted({0, tile_rows - 1})
    inner_count = tile_rows - len(edge_rows)
    vmem = pl.BlockSpec(memory_space=pltpu.VMEM)
    smem = pl.BlockSpec(memory_space=pltpu.SMEM)
    params = pltpu.CompilerParams(vmem_limit_bytes=32 << 20)
    cells = bricks * depth * cols
    lines = (chunks, LANES)
    halves = (color_table.shape[1] - 1) // LANES
    together = 8 if bricks % 8 == 0 else 1
    pieces = 4 if rows % (4 * SUB) == 0 else 1
    hbm = pl.BlockSpec(memory_space=pltpu.HBM)
    given = [scalar, view_order, light_dir, color_table, opacity_table]
    sent, brick_at, words, light_rows, first, final, later = pl.pallas_call(
        functools.partial(pack_kernel, bricks),
        out_shape=[
            pltpu.VMEM((bricks, (tile_rows + 2) * depth * chunks, LANES), jnp.float32),
            pltpu.SMEM((bricks,), jnp.int32),
            jax.ShapeDtypeStruct((3, halves) + lines, jnp.int32),
            jax.ShapeDtypeStruct((3,) + lines, jnp.float32),
        ] + [jax.ShapeDtypeStruct(lines, jnp.float32)] * 3,
        in_specs=[hbm] * 5,
        out_specs=[vmem, smem] + [vmem] * 5,
        scratch_shapes=[
            pltpu.VMEM(scalar.shape, scalar.dtype),
            pltpu.VMEM(((rows + 2) * depth * chunks, LANES), scalar.dtype),
            pltpu.SMEM(view_order.shape, view_order.dtype),
            pltpu.SMEM(light_dir.shape, light_dir.dtype),
            pltpu.VMEM(color_table.shape, color_table.dtype),
            pltpu.VMEM(opacity_table.shape, opacity_table.dtype),
            pltpu.SemaphoreType.DMA((pieces,)),
            pltpu.SemaphoreType.DMA((4,)),
        ],
        compiler_params=params,
        name="pack_rows",
    )(*[pltpu.with_memory_space_constraint(x, pltpu.HBM) for x in given])
    arrived = lax.all_to_all(
        sent, "gz", split_axis=0, concat_axis=0, tiled=True, axis_index_groups=[exchange_order(bricks)])
    tiles = arrived.reshape(bricks, tile_rows + 2, depth, chunks, LANES)

    last = bricks - 1
    pairs = [(g, g + 1) for g in range(bands - 1)]
    pairs += [(last * bands + g + 1, last * bands + g) for g in range(bands - 1)]
    wrapped = tiles[:, 0] * first + tiles[:, -1] * later
    other = lax.ppermute(wrapped, ("gz", "gy"), pairs)
    parts, color_sums, keeps = pl.pallas_call(
        functools.partial(main_kernel, edge_rows),
        out_shape=[
            jax.ShapeDtypeStruct((bricks, len(edge_rows), depth, 5, chunks, LANES), jnp.float32),
            jax.ShapeDtypeStruct((max(3 * inner_count, 1), chunks, LANES), jnp.float32),
            jax.ShapeDtypeStruct((tile_rows, chunks, LANES), jnp.float32),
        ],
        in_specs=[smem] + [vmem] * 3,
        out_specs=[vmem, vmem, vmem],
        scratch_shapes=[pltpu.VMEM(((chunks + 2) * together * tile_rows * depth, LANES), jnp.float32)],
        compiler_params=params,
        cost_estimate=pl.CostEstimate(
            flops=100 * cells * tile_rows, bytes_accessed=24 * cells * tile_rows, transcendentals=0),
        name="main_rows",
    )(brick_at, light_rows, words, tiles)
    return pl.pallas_call(
        functools.partial(finish_kernel, edge_rows),
        out_shape=jax.ShapeDtypeStruct((4, 1, tile_rows, cols), jnp.float32),
        in_specs=[vmem] * 8,
        out_specs=vmem,
        scratch_shapes=[pltpu.VMEM((4 * tile_rows * chunks, LANES), jnp.float32)],
        compiler_params=params,
        cost_estimate=pl.CostEstimate(
            flops=10 * cells * tile_rows, bytes_accessed=24 * cells * tile_rows, transcendentals=0),
        name="edge_rows",
    )(first, final, light_rows, tiles, other, parts, color_sums, keeps)


def solution(mesh):
    in_specs = (P("gz", "gy", None), P("gz", "gy", None), P(), P(), P(), P())
    out_specs = P(None, "gy", "gz", None)
    return jax.shard_map(shards, mesh=mesh, in_specs=in_specs, out_specs=out_specs, check_vma=False)
```

```python
import functools
import math

import jax
import jax.numpy as jnp
from jax import lax
from jax.experimental import pallas as pl
from jax.experimental.pallas import tpu as pltpu
from jax.sharding import PartitionSpec as P

SUB, LANES = 8, 128
COLOR_UNIT, COLOR_LEAST, OPACITY_UNIT = 2 ** 11, 204, 2 ** 18


def exchange_order(tiles):
    parts = 4 if tiles % 4 == 0 else 1
    return [(parts - 1 - i % parts) * (tiles // parts) + i // parts for i in range(tiles)]


def pack_kernel(tiles, field_ref, order_ref, light_ref, color_ref, opacity_ref,
                out_ref, brick_at_ref, word_ref, light_rows_ref, first_ref, last_ref, later_ref,
                field, spread, order, light, color, opacity, sems, table_sems):
    depth, rows, cols = field_ref.shape
    chunks = cols // LANES
    block = depth * chunks
    tile_rows = rows // tiles
    pieces = sems.shape[0]
    piece_rows = rows // pieces

    def copy_in(p):
        part = pl.ds(p * piece_rows, piece_rows)
        return pltpu.make_async_copy(field_ref.at[:, part], field.at[:, part], sems.at[p])

    table_copies = [
        pltpu.make_async_copy(source, target, table_sems.at[i])
        for i, (source, target) in enumerate(
            [(color_ref, color), (opacity_ref, opacity), (order_ref, order), (light_ref, light)])
    ]
    for copy in table_copies:
        copy.start()
    for p in range(pieces):
        copy_in(p).start()
    for copy in table_copies:
        copy.wait()
    prepare(order, light, color, opacity, brick_at_ref, word_ref, light_rows_ref, first_ref, last_ref, later_ref)
    for p in range(pieces):
        copy_in(p).wait()
        for k in range(depth):
            for row in range(p * piece_rows, (p + 1) * piece_rows, SUB):
                lines = [field[k, row:row + SUB, c * LANES:(c + 1) * LANES] for c in range(chunks)]
                for c, value in enumerate(lines):
                    spread[pl.ds((row + 1) * block + k * chunks + c, SUB, stride=block), :] = value
    spread[(rows + 1) * block:, :] = spread[block:2 * block, :]
    spread[:block, :] = spread[rows * block:(rows + 1) * block, :]
    size = (tile_rows + 2) * block
    for place, t in enumerate(exchange_order(tiles)):
        start = t * tile_rows * block
        out_ref[place] = spread[start:start + size, :]


def prepare(order_ref, light_ref, color_ref, opacity_ref,
            brick_at_ref, word_ref, light_rows_ref, first_ref, last_ref, later_ref):
    bins = color_ref.shape[1] - 1
    _, halves, chunks, lanes = word_ref.shape
    shape = (chunks, lanes)

    def parts(values, unit):
        scaled = (values.astype(jnp.float32) * float(unit)).astype(jnp.int32)
        return scaled[:, :bins], scaled[:, 1:] - scaled[:, :bins]

    start, slope = parts(opacity_ref[...].reshape(1, bins + 1), OPACITY_UNIT)
    pieces = [start & 511, (start >> 9) + ((slope & 31) << 4), (slope >> 5) & 511]
    start, slope = parts(color_ref[...], COLOR_UNIT)
    upper = (slope << 20) + ((start - COLOR_LEAST) << 9)
    for c in range(3):
        word = upper[c:c + 1] + pieces[c]
        for h in range(halves):
            word_ref[c, h] = jnp.broadcast_to(word[:, h * lanes:(h + 1) * lanes], shape)
    for i in range(3):
        light_rows_ref[i] = jnp.full(shape, light_ref[i], jnp.float32) * math.sqrt(0.75)
    here, last = lax.axis_index("gz"), order_ref.shape[0] - 1
    for ref, place in [(first_ref, here == 0), (last_ref, here == last), (later_ref, here != 0)]:
        ref[...] = jnp.full(shape, place.astype(jnp.float32), jnp.float32)
    for place, b in enumerate(exchange_order(order_ref.shape[0])):
        brick_at_ref[order_ref[b]] = place


def table_lookup(word_ref):
    _, halves, _, lanes = word_ref.shape
    bins = halves * lanes

    def look_up(x):
        scaled = x * float(bins)
        index = jnp.minimum(scaled.astype(jnp.int32), bins - 1)
        fraction = scaled - index.astype(jnp.float32)
        low_bits = index & (lanes - 1)
        words = []
        for c in range(3):
            found = [
                jnp.take_along_axis(word_ref[c, h], low_bits, axis=1, mode="promise_in_bounds")
                for h in range(halves)
            ]
            word = found[0]
            for h in range(1, halves):
                word = jnp.where(index >= h * lanes, found[h], word)
            words.append(word)

        def blended(start, slope):
            return start.astype(jnp.float32) + fraction * slope.astype(jnp.float32)

        color = [blended(((w >> 9) & 2047) + COLOR_LEAST, w >> 20) for w in words]
        low, middle, high = words
        start = (low & 511) + ((middle & 15) << 9)
        slope = ((high << 23) >> 18) + ((middle >> 4) & 31)
        return color, blended(start, slope) * (1.0 / OPACITY_UNIT)

    return look_up


def column_differences(fields, carried_ref, first):
    chunks, lanes = fields[0].shape
    count = carried_ref.shape[0] // (chunks + 2)
    lane = lax.broadcasted_iota(jnp.int32, (chunks, lanes), 1)
    at_first, at_last = lane == 0, lane == lanes - 1
    after = [pltpu.roll(x, lanes - 1, 1) for x in fields]
    before = [pltpu.roll(x, 1, 1) for x in fields]
    for i, (right, left) in enumerate(zip(after, before), first):
        carried_ref[pl.ds(count + i, chunks, stride=count), :] = jnp.where(at_last, right, left)
    differences = []
    for i, (right, left) in enumerate(zip(after, before), first):
        further = carried_ref[pl.ds(2 * count + i, chunks, stride=count), :]
        back = carried_ref[pl.ds(i, chunks, stride=count), :]
        differences.append(jnp.where(at_last, further, right) - jnp.where(at_first, back, left))
    return differences


def depth_differences(field):
    last = len(field) - 1
    made = {}
    for k in range(last + 1):
        ends = (min(k + 1, last), max(k - 1, 0))
        if ends not in made:
            made[ends] = field[ends[0]] - field[ends[1]]
    return [made[(min(k + 1, last), max(k - 1, 0))] for k in range(last + 1)]


def shading_of(facing, squared_plus_one):
    return 0.25 + (facing * facing) * pltpu.reciprocal(squared_plus_one, approx=True)


def main_kernel(edge_rows, brick_at, light_ref, word_ref, tile_ref,
                part_ref, color_sum_ref, keep_ref, carried):
    bricks, padded_rows, depth, chunks, lanes = tile_ref.shape
    rows = padded_rows - 2
    inner_rows = [r for r in range(rows) if r not in edge_rows]
    shape = (chunks, lanes)
    look_up = table_lookup(word_ref)
    border = carried.shape[0] // (chunks + 2)
    carried[:border, :] = jnp.zeros((border, lanes), jnp.float32)
    carried[-border:, :] = jnp.zeros((border, lanes), jnp.float32)
    light = [light_ref[i] for i in range(3)]
    together = border // (rows * depth)

    def step(trip, carry):
        colors, keeps = list(carry[0]), list(carry[1])
        at = [brick_at[trip * together + u] for u in range(together)]
        fields = [[[tile_ref[b, r, k] for k in range(depth)] for r in range(padded_rows)] for b in at]
        kept = []
        for u, (b, field) in enumerate(zip(at, fields)):
            cells = [x for line in field[1:-1] for x in line]
            column = column_differences(cells, carried, u * len(cells))
            for r in range(rows):
                for k, dz in enumerate(depth_differences(field[r + 1])):
                    x = field[r + 1][k]
                    dx = column[r * depth + k]
                    color, opacity = look_up(x)
                    weight = keeps[r] * opacity
                    facing = dz * light[0] + dx * light[2]
                    squared = (dz * dz + 1.0) + dx * dx
                    if r in edge_rows:
                        values = [weight * color[c] for c in range(3)] + [facing, squared]
                        kept.append((b, edge_rows.index(r), k, values))
                    else:
                        i = inner_rows.index(r)
                        dy = field[r + 2][k] - field[r][k]
                        shaded = weight * shading_of(facing + dy * light[1], squared + dy * dy)
                        for c in range(3):
                            slot = c * len(inner_rows) + i
                            colors[slot] = colors[slot] + shaded * color[c]
                    keeps[r] = keeps[r] - weight
        for b, i, k, values in kept:
            for v, value in enumerate(values):
                part_ref[b, i, k, v] = value
        return tuple(colors), tuple(keeps)

    zero, one = jnp.zeros(shape, jnp.float32), jnp.ones(shape, jnp.float32)
    colors, keeps = lax.fori_loop(
        0, bricks // together, step, ((zero,) * (3 * len(inner_rows)), (one,) * rows))
    for i, value in enumerate(colors):
        color_sum_ref[i] = value
    for r, value in enumerate(keeps):
        keep_ref[r] = value


def finish_kernel(edge_rows, first_ref, last_ref, light_ref, tile_ref, other_ref, part_ref, color_sum_ref, keep_ref,
                  out_ref, staged):
    bricks, padded_rows, depth, chunks, lanes = tile_ref.shape
    rows = padded_rows - 2
    inner_rows = [r for r in range(rows) if r not in edge_rows]
    shape = (chunks, lanes)
    light_rows = light_ref[1]
    is_first, is_last = first_ref[...] == 1.0, last_ref[...] == 1.0

    together = 16 if bricks % 16 == 0 else 1

    def step(trip, colors):
        colors = list(colors)
        for u in range(together):
            b = trip * together + u
            for i, r in enumerate(edge_rows):
                for k in range(depth):
                    above, below = tile_ref[b, r, k], tile_ref[b, r + 2, k]
                    if r == 0:
                        above = jnp.where(is_first, other_ref[b, k], above)
                    if r == rows - 1:
                        below = jnp.where(is_last, other_ref[b, k], below)
                    dy = below - above
                    facing = part_ref[b, i, k, 3] + dy * light_rows
                    shading = shading_of(facing, part_ref[b, i, k, 4] + dy * dy)
                    for c in range(3):
                        slot = c * len(edge_rows) + i
                        colors[slot] = colors[slot] + shading * part_ref[b, i, k, c]
        return tuple(colors)

    zero = jnp.zeros(shape, jnp.float32)
    edge_colors = lax.fori_loop(0, bricks // together, step, (zero,) * (3 * len(edge_rows)))
    for r in range(rows):
        for c in range(3):
            if r in edge_rows:
                value = edge_colors[c * len(edge_rows) + edge_rows.index(r)]
            else:
                value = color_sum_ref[c * len(inner_rows) + inner_rows.index(r)]
            at = (c * rows + r) * chunks
            staged[at:at + chunks, :] = value * (1.0 / COLOR_UNIT)
        at = (3 * rows + r) * chunks
        staged[at:at + chunks, :] = 1.0 - keep_ref[r]
    for c in range(4):
        for q in range(chunks):
            source = pl.ds(c * rows * chunks + q, rows, stride=chunks) if rows > 1 else pl.ds(c * chunks + q, 1)
            out_ref[c, 0, :, q * LANES:(q + 1) * LANES] = staged[source, :]


def shards(scalar, bin_index, color_table, opacity_table, light_dir, view_order):
    depth, rows, cols = scalar.shape
    bricks, bands = lax.axis_size("gz"), lax.axis_size("gy")
    tile_rows = rows // bricks
    chunks = cols // LANES
    edge_rows = sorted({0, tile_rows - 1})
    inner_count = tile_rows - len(edge_rows)
    vmem = pl.BlockSpec(memory_space=pltpu.VMEM)
    smem = pl.BlockSpec(memory_space=pltpu.SMEM)
    params = pltpu.CompilerParams(vmem_limit_bytes=32 << 20)
    cells = bricks * depth * cols
    lines = (chunks, LANES)
    halves = (color_table.shape[1] - 1) // LANES
    together = 8 if bricks % 8 == 0 else 1
    pieces = 4 if rows % (4 * SUB) == 0 else 1
    hbm = pl.BlockSpec(memory_space=pltpu.HBM)
    given = [scalar, view_order, light_dir, color_table, opacity_table]
    sent, brick_at, words, light_rows, first, final, later = pl.pallas_call(
        functools.partial(pack_kernel, bricks),
        out_shape=[
            pltpu.VMEM((bricks, (tile_rows + 2) * depth * chunks, LANES), jnp.float32),
            pltpu.SMEM((bricks,), jnp.int32),
            jax.ShapeDtypeStruct((3, halves) + lines, jnp.int32),
            jax.ShapeDtypeStruct((3,) + lines, jnp.float32),
        ] + [jax.ShapeDtypeStruct(lines, jnp.float32)] * 3,
        in_specs=[hbm] * 5,
        out_specs=[vmem, smem] + [vmem] * 5,
        scratch_shapes=[
            pltpu.VMEM(scalar.shape, scalar.dtype),
            pltpu.VMEM(((rows + 2) * depth * chunks, LANES), scalar.dtype),
            pltpu.SMEM(view_order.shape, view_order.dtype),
            pltpu.SMEM(light_dir.shape, light_dir.dtype),
            pltpu.VMEM(color_table.shape, color_table.dtype),
            pltpu.VMEM(opacity_table.shape, opacity_table.dtype),
            pltpu.SemaphoreType.DMA((pieces,)),
            pltpu.SemaphoreType.DMA((4,)),
        ],
        compiler_params=params,
        name="pack_rows",
    )(*[pltpu.with_memory_space_constraint(x, pltpu.HBM) for x in given])
    arrived = lax.all_to_all(
        sent, "gz", split_axis=0, concat_axis=0, tiled=True, axis_index_groups=[exchange_order(bricks)])
    tiles = arrived.reshape(bricks, tile_rows + 2, depth, chunks, LANES)

    last = bricks - 1
    pairs = [(g, g + 1) for g in range(bands - 1)]
    pairs += [(last * bands + g + 1, last * bands + g) for g in range(bands - 1)]
    wrapped = tiles[:, 0] * first + tiles[:, -1] * later
    other = lax.ppermute(wrapped, ("gz", "gy"), pairs)
    parts, color_sums, keeps = pl.pallas_call(
        functools.partial(main_kernel, edge_rows),
        out_shape=[
            jax.ShapeDtypeStruct((bricks, len(edge_rows), depth, 5, chunks, LANES), jnp.float32),
            jax.ShapeDtypeStruct((max(3 * inner_count, 1), chunks, LANES), jnp.float32),
            jax.ShapeDtypeStruct((tile_rows, chunks, LANES), jnp.float32),
        ],
        in_specs=[smem] + [vmem] * 3,
        out_specs=[vmem, vmem, vmem],
        scratch_shapes=[pltpu.VMEM(((chunks + 2) * (together * tile_rows * depth + 1), LANES), jnp.float32)],
        compiler_params=params,
        cost_estimate=pl.CostEstimate(
            flops=100 * cells * tile_rows, bytes_accessed=24 * cells * tile_rows, transcendentals=0),
        name="main_rows",
    )(brick_at, light_rows, words, tiles)
    return pl.pallas_call(
        functools.partial(finish_kernel, edge_rows),
        out_shape=jax.ShapeDtypeStruct((4, 1, tile_rows, cols), jnp.float32),
        in_specs=[vmem] * 8,
        out_specs=vmem,
        scratch_shapes=[pltpu.VMEM((4 * tile_rows * chunks, LANES), jnp.float32)],
        compiler_params=params,
        cost_estimate=pl.CostEstimate(
            flops=10 * cells * tile_rows, bytes_accessed=24 * cells * tile_rows, transcendentals=0),
        name="edge_rows",
    )(first, final, light_rows, tiles, other, parts, color_sums, keeps)


def solution(mesh):
    in_specs = (P("gz", "gy", None), P("gz", "gy", None), P(), P(), P(), P())
    out_specs = P(None, "gy", "gz", None)
    return jax.shard_map(shards, mesh=mesh, in_specs=in_specs, out_specs=out_specs, check_vma=False)
```

```python
import functools
import math

import jax
import jax.numpy as jnp
from jax import lax
from jax.experimental import pallas as pl
from jax.experimental.pallas import tpu as pltpu
from jax.sharding import PartitionSpec as P

SUB, LANES = 8, 128
COLOR_UNIT, COLOR_LEAST, OPACITY_UNIT = 2 ** 11, 204, 2 ** 18


def exchange_order(tiles):
    parts = 4 if tiles % 4 == 0 else 1
    return [(parts - 1 - i % parts) * (tiles // parts) + i // parts for i in range(tiles)]


def pack_kernel(tiles, field_ref, order_ref, light_ref, color_ref, opacity_ref,
                out_ref, brick_at_ref, word_ref, light_rows_ref, first_ref, last_ref, later_ref,
                field, spread, order, light, color, opacity, sems, table_sems):
    depth, rows, cols = field_ref.shape
    chunks = cols // LANES
    block = depth * chunks
    tile_rows = rows // tiles
    pieces = sems.shape[0]
    order_of_tiles = exchange_order(tiles)
    piece_rows = rows // pieces

    def copy_in(p):
        part = pl.ds(p * piece_rows, piece_rows)
        return pltpu.make_async_copy(field_ref.at[:, part], field.at[:, part], sems.at[p])

    table_copies = [
        pltpu.make_async_copy(source, target, table_sems.at[i])
        for i, (source, target) in enumerate(
            [(color_ref, color), (opacity_ref, opacity), (order_ref, order), (light_ref, light)])
    ]
    for copy in table_copies:
        copy.start()
    for p in range(pieces):
        copy_in(p).start()
    size = (tile_rows + 2) * block
    placed = 0
    for p in range(pieces):
        copy_in(p).wait()
        rows_here = range(p * piece_rows, (p + 1) * piece_rows)
        for k in range(depth):
            for row in rows_here[::SUB]:
                lines = [field[k, row:row + SUB, c * LANES:(c + 1) * LANES] for c in range(chunks)]
                for c, value in enumerate(lines):
                    spread[pl.ds((row + 1) * block + k * chunks + c, SUB, stride=block), :] = value
        ready = [t for t in range(1, tiles) if (t + 1) * tile_rows in range(rows_here.stop)]
        if p == 0:
            spread[(rows + 1) * block:, :] = spread[block:2 * block, :]
        if p == pieces - 1:
            spread[:block, :] = spread[rows * block:(rows + 1) * block, :]
            ready = list(range(1, tiles)) + [0]
        for t in ready[placed:]:
            start = t * tile_rows * block
            out_ref[order_of_tiles.index(t)] = spread[start:start + size, :]
        placed = len(ready)
        if p == 0:
            for copy in table_copies:
                copy.wait()
            prepare(order, light, color, opacity, brick_at_ref, word_ref, light_rows_ref, first_ref, last_ref, later_ref)


def prepare(order_ref, light_ref, color_ref, opacity_ref,
            brick_at_ref, word_ref, light_rows_ref, first_ref, last_ref, later_ref):
    bins = color_ref.shape[1] - 1
    _, halves, chunks, lanes = word_ref.shape
    shape = (chunks, lanes)

    def parts(values, unit):
        scaled = (values.astype(jnp.float32) * float(unit)).astype(jnp.int32)
        return scaled[:, :bins], scaled[:, 1:] - scaled[:, :bins]

    start, slope = parts(opacity_ref[...].reshape(1, bins + 1), OPACITY_UNIT)
    pieces = [start & 511, (start >> 9) + ((slope & 31) << 4), (slope >> 5) & 511]
    start, slope = parts(color_ref[...], COLOR_UNIT)
    upper = (slope << 20) + ((start - COLOR_LEAST) << 9)
    for c in range(3):
        word = upper[c:c + 1] + pieces[c]
        for h in range(halves):
            word_ref[c, h] = jnp.broadcast_to(word[:, h * lanes:(h + 1) * lanes], shape)
    for i in range(3):
        light_rows_ref[i] = jnp.full(shape, light_ref[i], jnp.float32) * math.sqrt(0.75)
    here, last = lax.axis_index("gz"), order_ref.shape[0] - 1
    for ref, place in [(first_ref, here == 0), (last_ref, here == last), (later_ref, here != 0)]:
        ref[...] = jnp.full(shape, place.astype(jnp.float32), jnp.float32)
    for place, b in enumerate(exchange_order(order_ref.shape[0])):
        brick_at_ref[order_ref[b]] = place


def table_lookup(word_ref):
    _, halves, _, lanes = word_ref.shape
    bins = halves * lanes

    def look_up(x):
        scaled = x * float(bins)
        index = jnp.minimum(scaled.astype(jnp.int32), bins - 1)
        fraction = scaled - index.astype(jnp.float32)
        low_bits = index & (lanes - 1)
        words = []
        for c in range(3):
            found = [
                jnp.take_along_axis(word_ref[c, h], low_bits, axis=1, mode="promise_in_bounds")
                for h in range(halves)
            ]
            word = found[0]
            for h in range(1, halves):
                word = jnp.where(index >= h * lanes, found[h], word)
            words.append(word)

        def blended(start, slope):
            return start.astype(jnp.float32) + fraction * slope.astype(jnp.float32)

        color = [blended(((w >> 9) & 2047) + COLOR_LEAST, w >> 20) for w in words]
        low, middle, high = words
        start = (low & 511) + ((middle & 15) << 9)
        slope = ((high << 23) >> 18) + ((middle >> 4) & 31)
        return color, blended(start, slope) * (1.0 / OPACITY_UNIT)

    return look_up


def column_differences(fields, carried_ref, first):
    chunks, lanes = fields[0].shape
    count = carried_ref.shape[0] // (chunks + 2)
    lane = lax.broadcasted_iota(jnp.int32, (chunks, lanes), 1)
    at_first, at_last = lane == 0, lane == lanes - 1
    after = [pltpu.roll(x, lanes - 1, 1) for x in fields]
    before = [pltpu.roll(x, 1, 1) for x in fields]
    for i, (right, left) in enumerate(zip(after, before), first):
        carried_ref[pl.ds(count + i, chunks, stride=count), :] = jnp.where(at_last, right, left)
    differences = []
    for i, (right, left) in enumerate(zip(after, before), first):
        further = carried_ref[pl.ds(2 * count + i, chunks, stride=count), :]
        back = carried_ref[pl.ds(i, chunks, stride=count), :]
        differences.append(jnp.where(at_last, further, right) - jnp.where(at_first, back, left))
    return differences


def depth_differences(field):
    last = len(field) - 1
    made = {}
    for k in range(last + 1):
        ends = (min(k + 1, last), max(k - 1, 0))
        if ends not in made:
            made[ends] = field[ends[0]] - field[ends[1]]
    return [made[(min(k + 1, last), max(k - 1, 0))] for k in range(last + 1)]


def shading_of(facing, squared_plus_one):
    return 0.25 + (facing * facing) * pltpu.reciprocal(squared_plus_one, approx=True)


def main_kernel(edge_rows, brick_at, light_ref, word_ref, tile_ref,
                part_ref, color_sum_ref, keep_ref, carried):
    bricks, padded_rows, depth, chunks, lanes = tile_ref.shape
    rows = padded_rows - 2
    inner_rows = [r for r in range(rows) if r not in edge_rows]
    shape = (chunks, lanes)
    look_up = table_lookup(word_ref)
    border = carried.shape[0] // (chunks + 2)
    carried[:border, :] = jnp.zeros((border, lanes), jnp.float32)
    carried[-border:, :] = jnp.zeros((border, lanes), jnp.float32)
    light = [light_ref[i] for i in range(3)]
    together = border // (rows * depth)

    def step(trip, carry):
        colors, keeps = list(carry[0]), list(carry[1])
        at = [brick_at[trip * together + u] for u in range(together)]
        fields = [[[tile_ref[b, r, k] for k in range(depth)] for r in range(padded_rows)] for b in at]
        kept = []
        for u, (b, field) in enumerate(zip(at, fields)):
            cells = [x for line in field[1:-1] for x in line]
            column = column_differences(cells, carried, u * len(cells))
            for r in range(rows):
                for k, dz in enumerate(depth_differences(field[r + 1])):
                    x = field[r + 1][k]
                    dx = column[r * depth + k]
                    color, opacity = look_up(x)
                    weight = keeps[r] * opacity
                    facing = dz * light[0] + dx * light[2]
                    squared = (dz * dz + 1.0) + dx * dx
                    if r in edge_rows:
                        values = [weight * color[c] for c in range(3)] + [facing, squared]
                        kept.append((b, edge_rows.index(r), k, values))
                    else:
                        i = inner_rows.index(r)
                        dy = field[r + 2][k] - field[r][k]
                        shaded = weight * shading_of(facing + dy * light[1], squared + dy * dy)
                        for c in range(3):
                            slot = c * len(inner_rows) + i
                            colors[slot] = colors[slot] + shaded * color[c]
                    keeps[r] = keeps[r] - weight
        for b, i, k, values in kept:
            for v, value in enumerate(values):
                part_ref[b, i, k, v] = value
        return tuple(colors), tuple(keeps)

    zero, one = jnp.zeros(shape, jnp.float32), jnp.ones(shape, jnp.float32)
    colors, keeps = lax.fori_loop(
        0, bricks // together, step, ((zero,) * (3 * len(inner_rows)), (one,) * rows))
    for i, value in enumerate(colors):
        color_sum_ref[i] = value
    for r, value in enumerate(keeps):
        keep_ref[r] = value


def finish_kernel(edge_rows, first_ref, last_ref, light_ref, tile_ref, other_ref, part_ref, color_sum_ref, keep_ref,
                  out_ref, staged):
    bricks, padded_rows, depth, chunks, lanes = tile_ref.shape
    rows = padded_rows - 2
    inner_rows = [r for r in range(rows) if r not in edge_rows]
    shape = (chunks, lanes)
    light_rows = light_ref[1]
    is_first, is_last = first_ref[...] == 1.0, last_ref[...] == 1.0

    together = 16 if bricks % 16 == 0 else 1

    def step(trip, colors):
        colors = list(colors)
        for u in range(together):
            b = trip * together + u
            for i, r in enumerate(edge_rows):
                for k in range(depth):
                    above, below = tile_ref[b, r, k], tile_ref[b, r + 2, k]
                    if r == 0:
                        above = jnp.where(is_first, other_ref[b, k], above)
                    if r == rows - 1:
                        below = jnp.where(is_last, other_ref[b, k], below)
                    dy = below - above
                    facing = part_ref[b, i, k, 3] + dy * light_rows
                    shading = shading_of(facing, part_ref[b, i, k, 4] + dy * dy)
                    for c in range(3):
                        slot = c * len(edge_rows) + i
                        colors[slot] = colors[slot] + shading * part_ref[b, i, k, c]
        return tuple(colors)

    zero = jnp.zeros(shape, jnp.float32)
    edge_colors = lax.fori_loop(0, bricks // together, step, (zero,) * (3 * len(edge_rows)))
    for r in range(rows):
        for c in range(3):
            if r in edge_rows:
                value = edge_colors[c * len(edge_rows) + edge_rows.index(r)]
            else:
                value = color_sum_ref[c * len(inner_rows) + inner_rows.index(r)]
            at = (c * rows + r) * chunks
            staged[at:at + chunks, :] = value * (1.0 / COLOR_UNIT)
        at = (3 * rows + r) * chunks
        staged[at:at + chunks, :] = 1.0 - keep_ref[r]
    for c in range(4):
        for q in range(chunks):
            source = pl.ds(c * rows * chunks + q, rows, stride=chunks) if rows > 1 else pl.ds(c * chunks + q, 1)
            out_ref[c, 0, :, q * LANES:(q + 1) * LANES] = staged[source, :]


def shards(scalar, bin_index, color_table, opacity_table, light_dir, view_order):
    depth, rows, cols = scalar.shape
    bricks, bands = lax.axis_size("gz"), lax.axis_size("gy")
    tile_rows = rows // bricks
    chunks = cols // LANES
    edge_rows = sorted({0, tile_rows - 1})
    inner_count = tile_rows - len(edge_rows)
    vmem = pl.BlockSpec(memory_space=pltpu.VMEM)
    smem = pl.BlockSpec(memory_space=pltpu.SMEM)
    params = pltpu.CompilerParams(vmem_limit_bytes=32 << 20)
    cells = bricks * depth * cols
    lines = (chunks, LANES)
    halves = (color_table.shape[1] - 1) // LANES
    together = 8 if bricks % 8 == 0 else 1
    pieces = rows // SUB
    hbm = pl.BlockSpec(memory_space=pltpu.HBM)
    given = [scalar, view_order, light_dir, color_table, opacity_table]
    sent, brick_at, words, light_rows, first, final, later = pl.pallas_call(
        functools.partial(pack_kernel, bricks),
        out_shape=[
            pltpu.VMEM((bricks, (tile_rows + 2) * depth * chunks, LANES), jnp.float32),
            pltpu.SMEM((bricks,), jnp.int32),
            jax.ShapeDtypeStruct((3, halves) + lines, jnp.int32),
            jax.ShapeDtypeStruct((3,) + lines, jnp.float32),
        ] + [jax.ShapeDtypeStruct(lines, jnp.float32)] * 3,
        in_specs=[hbm] * 5,
        out_specs=[vmem, smem] + [vmem] * 5,
        scratch_shapes=[
            pltpu.VMEM(scalar.shape, scalar.dtype),
            pltpu.VMEM(((rows + 2) * depth * chunks, LANES), scalar.dtype),
            pltpu.SMEM(view_order.shape, view_order.dtype),
            pltpu.SMEM(light_dir.shape, light_dir.dtype),
            pltpu.VMEM(color_table.shape, color_table.dtype),
            pltpu.VMEM(opacity_table.shape, opacity_table.dtype),
            pltpu.SemaphoreType.DMA((pieces,)),
            pltpu.SemaphoreType.DMA((4,)),
        ],
        compiler_params=params,
        name="pack_rows",
    )(*[pltpu.with_memory_space_constraint(x, pltpu.HBM) for x in given])
    arrived = lax.all_to_all(
        sent, "gz", split_axis=0, concat_axis=0, tiled=True, axis_index_groups=[exchange_order(bricks)])
    tiles = arrived.reshape(bricks, tile_rows + 2, depth, chunks, LANES)

    last = bricks - 1
    pairs = [(g, g + 1) for g in range(bands - 1)]
    pairs += [(last * bands + g + 1, last * bands + g) for g in range(bands - 1)]
    wrapped = tiles[:, 0] * first + tiles[:, -1] * later
    other = lax.ppermute(wrapped, ("gz", "gy"), pairs)
    parts, color_sums, keeps = pl.pallas_call(
        functools.partial(main_kernel, edge_rows),
        out_shape=[
            jax.ShapeDtypeStruct((bricks, len(edge_rows), depth, 5, chunks, LANES), jnp.float32),
            jax.ShapeDtypeStruct((max(3 * inner_count, 1), chunks, LANES), jnp.float32),
            jax.ShapeDtypeStruct((tile_rows, chunks, LANES), jnp.float32),
        ],
        in_specs=[smem] + [vmem] * 3,
        out_specs=[vmem, vmem, vmem],
        scratch_shapes=[pltpu.VMEM(((chunks + 2) * (together * tile_rows * depth + 1), LANES), jnp.float32)],
        compiler_params=params,
        cost_estimate=pl.CostEstimate(
            flops=100 * cells * tile_rows, bytes_accessed=24 * cells * tile_rows, transcendentals=0),
        name="main_rows",
    )(brick_at, light_rows, words, tiles)
    return pl.pallas_call(
        functools.partial(finish_kernel, edge_rows),
        out_shape=jax.ShapeDtypeStruct((4, 1, tile_rows, cols), jnp.float32),
        in_specs=[vmem] * 8,
        out_specs=vmem,
        scratch_shapes=[pltpu.VMEM((4 * tile_rows * chunks, LANES), jnp.float32)],
        compiler_params=params,
        cost_estimate=pl.CostEstimate(
            flops=10 * cells * tile_rows, bytes_accessed=24 * cells * tile_rows, transcendentals=0),
        name="edge_rows",
    )(first, final, light_rows, tiles, other, parts, color_sums, keeps)


def solution(mesh):
    in_specs = (P("gz", "gy", None), P("gz", "gy", None), P(), P(), P(), P())
    out_specs = P(None, "gy", "gz", None)
    return jax.shard_map(shards, mesh=mesh, in_specs=in_specs, out_specs=out_specs, check_vma=False)
```

```python
import functools
import math

import jax
import jax.numpy as jnp
from jax import lax
from jax.experimental import pallas as pl
from jax.experimental.pallas import tpu as pltpu
from jax.sharding import PartitionSpec as P

SUB, LANES = 8, 128
COLOR_UNIT, COLOR_LEAST, OPACITY_UNIT = 2 ** 11, 204, 2 ** 18


def exchange_orders(tiles):
    parts = 4 if tiles % 4 == 0 else 1
    size = tiles // parts
    quarters = range(parts)[::-1]
    return ([p * size + i for i in range(size) for p in quarters],
            [p * size + i for p in quarters for i in range(size)])


def of_band(even, odd):
    return jnp.where(lax.rem(lax.axis_index("gy"), 2) == 0, even, odd)


def pack_kernel(tiles, field_ref, order_ref, light_ref, color_ref, opacity_ref,
                out_ref, brick_at_ref, word_ref, light_rows_ref, first_ref, last_ref, later_ref,
                field, spread, order, light, color, opacity, sems, table_sems):
    depth, rows, cols = field_ref.shape
    chunks = cols // LANES
    block = depth * chunks
    tile_rows = rows // tiles
    pieces = sems.shape[0]
    piece_rows = rows // pieces

    def copy_in(p):
        part = pl.ds(p * piece_rows, piece_rows)
        return pltpu.make_async_copy(field_ref.at[:, part], field.at[:, part], sems.at[p])

    table_copies = [
        pltpu.make_async_copy(source, target, table_sems.at[i])
        for i, (source, target) in enumerate(
            [(color_ref, color), (opacity_ref, opacity), (order_ref, order), (light_ref, light)])
    ]
    for copy in table_copies:
        copy.start()
    for p in range(pieces):
        copy_in(p).start()
    for copy in table_copies:
        copy.wait()
    prepare(order, light, color, opacity, brick_at_ref, word_ref, light_rows_ref, first_ref, last_ref, later_ref)
    for p in range(pieces):
        copy_in(p).wait()
        for k in range(depth):
            for row in range(p * piece_rows, (p + 1) * piece_rows, SUB):
                lines = [field[k, row:row + SUB, c * LANES:(c + 1) * LANES] for c in range(chunks)]
                for c, value in enumerate(lines):
                    spread[pl.ds((row + 1) * block + k * chunks + c, SUB, stride=block), :] = value
    spread[(rows + 1) * block:, :] = spread[block:2 * block, :]
    spread[:block, :] = spread[rows * block:(rows + 1) * block, :]
    size = (tile_rows + 2) * block
    for place, (even, odd) in enumerate(zip(*exchange_orders(tiles))):
        start = pl.multiple_of(of_band(even, odd) * (tile_rows * block), tile_rows * block)
        out_ref[place] = spread[pl.ds(start, size), :]


def prepare(order_ref, light_ref, color_ref, opacity_ref,
            brick_at_ref, word_ref, light_rows_ref, first_ref, last_ref, later_ref):
    bins = color_ref.shape[1] - 1
    _, halves, chunks, lanes = word_ref.shape
    shape = (chunks, lanes)

    def parts(values, unit):
        scaled = (values.astype(jnp.float32) * float(unit)).astype(jnp.int32)
        return scaled[:, :bins], scaled[:, 1:] - scaled[:, :bins]

    start, slope = parts(opacity_ref[...].reshape(1, bins + 1), OPACITY_UNIT)
    pieces = [start & 511, (start >> 9) + ((slope & 31) << 4), (slope >> 5) & 511]
    start, slope = parts(color_ref[...], COLOR_UNIT)
    upper = (slope << 20) + ((start - COLOR_LEAST) << 9)
    for c in range(3):
        word = upper[c:c + 1] + pieces[c]
        for h in range(halves):
            word_ref[c, h] = jnp.broadcast_to(word[:, h * lanes:(h + 1) * lanes], shape)
    for i in range(3):
        light_rows_ref[i] = jnp.full(shape, light_ref[i], jnp.float32) * math.sqrt(0.75)
    here, last = lax.axis_index("gz"), order_ref.shape[0] - 1
    for ref, place in [(first_ref, here == 0), (last_ref, here == last), (later_ref, here != 0)]:
        ref[...] = jnp.full(shape, place.astype(jnp.float32), jnp.float32)
    for place, (even, odd) in enumerate(zip(*exchange_orders(order_ref.shape[0]))):
        brick_at_ref[order_ref[of_band(even, odd)]] = place


def table_lookup(word_ref):
    _, halves, _, lanes = word_ref.shape
    bins = halves * lanes

    def look_up(x):
        scaled = x * float(bins)
        index = jnp.minimum(scaled.astype(jnp.int32), bins - 1)
        fraction = scaled - index.astype(jnp.float32)
        low_bits = index & (lanes - 1)
        words = []
        for c in range(3):
            found = [
                jnp.take_along_axis(word_ref[c, h], low_bits, axis=1, mode="promise_in_bounds")
                for h in range(halves)
            ]
            word = found[0]
            for h in range(1, halves):
                word = jnp.where(index >= h * lanes, found[h], word)
            words.append(word)

        def blended(start, slope):
            return start.astype(jnp.float32) + fraction * slope.astype(jnp.float32)

        color = [blended(((w >> 9) & 2047) + COLOR_LEAST, w >> 20) for w in words]
        low, middle, high = words
        start = (low & 511) + ((middle & 15) << 9)
        slope = ((high << 23) >> 18) + ((middle >> 4) & 31)
        return color, blended(start, slope) * (1.0 / OPACITY_UNIT)

    return look_up


def column_differences(fields, carried_ref, first):
    chunks, lanes = fields[0].shape
    count = carried_ref.shape[0] // (chunks + 2)
    lane = lax.broadcasted_iota(jnp.int32, (chunks, lanes), 1)
    at_first, at_last = lane == 0, lane == lanes - 1
    after = [pltpu.roll(x, lanes - 1, 1) for x in fields]
    before = [pltpu.roll(x, 1, 1) for x in fields]
    for i, (right, left) in enumerate(zip(after, before), first):
        carried_ref[pl.ds(count + i, chunks, stride=count), :] = jnp.where(at_last, right, left)
    differences = []
    for i, (right, left) in enumerate(zip(after, before), first):
        further = carried_ref[pl.ds(2 * count + i, chunks, stride=count), :]
        back = carried_ref[pl.ds(i, chunks, stride=count), :]
        differences.append(jnp.where(at_last, further, right) - jnp.where(at_first, back, left))
    return differences


def depth_differences(field):
    last = len(field) - 1
    made = {}
    for k in range(last + 1):
        ends = (min(k + 1, last), max(k - 1, 0))
        if ends not in made:
            made[ends] = field[ends[0]] - field[ends[1]]
    return [made[(min(k + 1, last), max(k - 1, 0))] for k in range(last + 1)]


def shading_of(facing, squared_plus_one):
    return 0.25 + (facing * facing) * pltpu.reciprocal(squared_plus_one, approx=True)


def main_kernel(edge_rows, brick_at, light_ref, word_ref, tile_ref,
                part_ref, color_sum_ref, keep_ref, carried):
    bricks, padded_rows, depth, chunks, lanes = tile_ref.shape
    rows = padded_rows - 2
    inner_rows = [r for r in range(rows) if r not in edge_rows]
    shape = (chunks, lanes)
    look_up = table_lookup(word_ref)
    border = carried.shape[0] // (chunks + 2)
    carried[:border, :] = jnp.zeros((border, lanes), jnp.float32)
    carried[-border:, :] = jnp.zeros((border, lanes), jnp.float32)
    light = [light_ref[i] for i in range(3)]
    together = border // (rows * depth)

    def step(trip, carry):
        colors, keeps = list(carry[0]), list(carry[1])
        at = [brick_at[trip * together + u] for u in range(together)]
        fields = [[[tile_ref[b, r, k] for k in range(depth)] for r in range(padded_rows)] for b in at]
        kept = []
        for u, (b, field) in enumerate(zip(at, fields)):
            cells = [x for line in field[1:-1] for x in line]
            column = column_differences(cells, carried, u * len(cells))
            for r in range(rows):
                for k, dz in enumerate(depth_differences(field[r + 1])):
                    x = field[r + 1][k]
                    dx = column[r * depth + k]
                    color, opacity = look_up(x)
                    weight = keeps[r] * opacity
                    facing = dz * light[0] + dx * light[2]
                    squared = (dz * dz + 1.0) + dx * dx
                    if r in edge_rows:
                        values = [weight * color[c] for c in range(3)] + [facing, squared]
                        kept.append((b, edge_rows.index(r), k, values))
                    else:
                        i = inner_rows.index(r)
                        dy = field[r + 2][k] - field[r][k]
                        shaded = weight * shading_of(facing + dy * light[1], squared + dy * dy)
                        for c in range(3):
                            slot = c * len(inner_rows) + i
                            colors[slot] = colors[slot] + shaded * color[c]
                    keeps[r] = keeps[r] - weight
        for b, i, k, values in kept:
            for v, value in enumerate(values):
                part_ref[b, i, k, v] = value
        return tuple(colors), tuple(keeps)

    zero, one = jnp.zeros(shape, jnp.float32), jnp.ones(shape, jnp.float32)
    colors, keeps = lax.fori_loop(
        0, bricks // together, step, ((zero,) * (3 * len(inner_rows)), (one,) * rows))
    for i, value in enumerate(colors):
        color_sum_ref[i] = value
    for r, value in enumerate(keeps):
        keep_ref[r] = value


def finish_kernel(edge_rows, first_ref, last_ref, light_ref, tile_ref, other_ref, part_ref, color_sum_ref, keep_ref,
                  out_ref, staged):
    bricks, padded_rows, depth, chunks, lanes = tile_ref.shape
    rows = padded_rows - 2
    inner_rows = [r for r in range(rows) if r not in edge_rows]
    shape = (chunks, lanes)
    light_rows = light_ref[1]
    is_first, is_last = first_ref[...] == 1.0, last_ref[...] == 1.0

    together = 16 if bricks % 16 == 0 else 1

    even, odd = exchange_orders(bricks)
    places = [of_band(odd.index(even[b]), even.index(odd[b])) for b in range(bricks)]

    def step(b_first, colors):
        colors = list(colors)
        for b in range(b_first, b_first + together):
            there = places[b]
            for i, r in enumerate(edge_rows):
                for k in range(depth):
                    above, below = tile_ref[b, r, k], tile_ref[b, r + 2, k]
                    if r == 0:
                        above = jnp.where(is_first, other_ref[there, k], above)
                    if r == rows - 1:
                        below = jnp.where(is_last, other_ref[there, k], below)
                    dy = below - above
                    facing = part_ref[b, i, k, 3] + dy * light_rows
                    shading = shading_of(facing, part_ref[b, i, k, 4] + dy * dy)
                    for c in range(3):
                        slot = c * len(edge_rows) + i
                        colors[slot] = colors[slot] + shading * part_ref[b, i, k, c]
        return tuple(colors)

    zero = jnp.zeros(shape, jnp.float32)
    edge_colors = (zero,) * (3 * len(edge_rows))
    for b in range(0, bricks, together):
        edge_colors = step(b, edge_colors)
    for r in range(rows):
        for c in range(3):
            if r in edge_rows:
                value = edge_colors[c * len(edge_rows) + edge_rows.index(r)]
            else:
                value = color_sum_ref[c * len(inner_rows) + inner_rows.index(r)]
            at = (c * rows + r) * chunks
            staged[at:at + chunks, :] = value * (1.0 / COLOR_UNIT)
        at = (3 * rows + r) * chunks
        staged[at:at + chunks, :] = 1.0 - keep_ref[r]
    for c in range(4):
        for q in range(chunks):
            source = pl.ds(c * rows * chunks + q, rows, stride=chunks) if rows > 1 else pl.ds(c * chunks + q, 1)
            out_ref[c, 0, :, q * LANES:(q + 1) * LANES] = staged[source, :]


def shards(scalar, bin_index, color_table, opacity_table, light_dir, view_order):
    depth, rows, cols = scalar.shape
    bricks, bands = lax.axis_size("gz"), lax.axis_size("gy")
    tile_rows = rows // bricks
    chunks = cols // LANES
    edge_rows = sorted({0, tile_rows - 1})
    inner_count = tile_rows - len(edge_rows)
    vmem = pl.BlockSpec(memory_space=pltpu.VMEM)
    smem = pl.BlockSpec(memory_space=pltpu.SMEM)
    params = pltpu.CompilerParams(vmem_limit_bytes=32 << 20)
    cells = bricks * depth * cols
    lines = (chunks, LANES)
    halves = (color_table.shape[1] - 1) // LANES
    together = 8 if bricks % 8 == 0 else 1
    pieces = 4 if rows % (4 * SUB) == 0 else 1
    hbm = pl.BlockSpec(memory_space=pltpu.HBM)
    given = [scalar, view_order, light_dir, color_table, opacity_table]
    sent, brick_at, words, light_rows, first, final, later = pl.pallas_call(
        functools.partial(pack_kernel, bricks),
        out_shape=[
            pltpu.VMEM((bricks, (tile_rows + 2) * depth * chunks, LANES), jnp.float32),
            pltpu.SMEM((bricks,), jnp.int32),
            jax.ShapeDtypeStruct((3, halves) + lines, jnp.int32),
            jax.ShapeDtypeStruct((3,) + lines, jnp.float32),
        ] + [jax.ShapeDtypeStruct(lines, jnp.float32)] * 3,
        in_specs=[hbm] * 5,
        out_specs=[vmem, smem] + [vmem] * 5,
        scratch_shapes=[
            pltpu.VMEM(scalar.shape, scalar.dtype),
            pltpu.VMEM(((rows + 2) * depth * chunks, LANES), scalar.dtype),
            pltpu.SMEM(view_order.shape, view_order.dtype),
            pltpu.SMEM(light_dir.shape, light_dir.dtype),
            pltpu.VMEM(color_table.shape, color_table.dtype),
            pltpu.VMEM(opacity_table.shape, opacity_table.dtype),
            pltpu.SemaphoreType.DMA((pieces,)),
            pltpu.SemaphoreType.DMA((4,)),
        ],
        compiler_params=params,
        name="pack_rows",
    )(*[pltpu.with_memory_space_constraint(x, pltpu.HBM) for x in given])
    orders = exchange_orders(bricks)
    groups = [[t * bands + g for t in orders[g % 2]] for g in range(bands)]
    arrived = lax.all_to_all(
        sent, ("gz", "gy"), split_axis=0, concat_axis=0, tiled=True, axis_index_groups=groups)
    tiles = arrived.reshape(bricks, tile_rows + 2, depth, chunks, LANES)

    last = bricks - 1
    pairs = [(g, g + 1) for g in range(bands - 1)]
    pairs += [(last * bands + g + 1, last * bands + g) for g in range(bands - 1)]
    wrapped = tiles[:, 0] * first + tiles[:, -1] * later
    other = lax.ppermute(wrapped, ("gz", "gy"), pairs)
    parts, color_sums, keeps = pl.pallas_call(
        functools.partial(main_kernel, edge_rows),
        out_shape=[
            jax.ShapeDtypeStruct((bricks, len(edge_rows), depth, 5, chunks, LANES), jnp.float32),
            jax.ShapeDtypeStruct((max(3 * inner_count, 1), chunks, LANES), jnp.float32),
            jax.ShapeDtypeStruct((tile_rows, chunks, LANES), jnp.float32),
        ],
        in_specs=[smem] + [vmem] * 3,
        out_specs=[vmem, vmem, vmem],
        scratch_shapes=[pltpu.VMEM(((chunks + 2) * (together * tile_rows * depth + 1), LANES), jnp.float32)],
        compiler_params=params,
        cost_estimate=pl.CostEstimate(
            flops=100 * cells * tile_rows, bytes_accessed=24 * cells * tile_rows, transcendentals=0),
        name="main_rows",
    )(brick_at, light_rows, words, tiles)
    return pl.pallas_call(
        functools.partial(finish_kernel, edge_rows),
        out_shape=jax.ShapeDtypeStruct((4, 1, tile_rows, cols), jnp.float32),
        in_specs=[vmem] * 8,
        out_specs=vmem,
        scratch_shapes=[pltpu.VMEM((4 * tile_rows * chunks, LANES), jnp.float32)],
        compiler_params=params,
        cost_estimate=pl.CostEstimate(
            flops=10 * cells * tile_rows, bytes_accessed=24 * cells * tile_rows, transcendentals=0),
        name="edge_rows",
    )(first, final, light_rows, tiles, other, parts, color_sums, keeps)


def solution(mesh):
    in_specs = (P("gz", "gy", None), P("gz", "gy", None), P(), P(), P(), P())
    out_specs = P(None, "gy", "gz", None)
    return jax.shard_map(shards, mesh=mesh, in_specs=in_specs, out_specs=out_specs, check_vma=False)
```

```python
import functools
import math

import jax
import jax.numpy as jnp
from jax import lax
from jax.experimental import pallas as pl
from jax.experimental.pallas import tpu as pltpu
from jax.sharding import PartitionSpec as P

SUB, LANES = 8, 128
ROW_STEP = 3
COLOR_UNIT, COLOR_LEAST, OPACITY_UNIT = 2 ** 11, 204, 2 ** 18


def exchange_order(tiles):
    parts = 4 if tiles % 4 == 0 else 1
    return [(parts - 1 - i % parts) * (tiles // parts) + i // parts for i in range(tiles)]


def pack_kernel(tiles, field_ref, order_ref, light_ref, color_ref, opacity_ref,
                out_ref, brick_at_ref, word_ref, light_rows_ref, first_ref, last_ref, later_ref,
                field, spread, order, light, color, opacity, sems, table_sems):
    depth, rows, cols = field_ref.shape
    chunks = cols // LANES
    pitch = rows * ROW_STEP + 1
    tile_rows = rows // tiles
    pieces = sems.shape[0]
    piece_rows = rows // pieces

    def copy_in(p):
        part = pl.ds(p * piece_rows, piece_rows)
        return pltpu.make_async_copy(field_ref.at[:, part], field.at[:, part], sems.at[p])

    table_copies = [
        pltpu.make_async_copy(source, target, table_sems.at[i])
        for i, (source, target) in enumerate(
            [(color_ref, color), (opacity_ref, opacity), (order_ref, order), (light_ref, light)])
    ]
    for copy in table_copies:
        copy.start()
    for p in range(pieces):
        copy_in(p).start()
    for copy in table_copies:
        copy.wait()
    prepare(order, light, color, opacity, brick_at_ref, word_ref, light_rows_ref, first_ref, last_ref, later_ref)
    for p in range(pieces):
        copy_in(p).wait()
        for k in range(depth):
            for row in range(p * piece_rows, (p + 1) * piece_rows, SUB):
                lines = [field[k, row:row + SUB, c * LANES:(c + 1) * LANES] for c in range(chunks)]
                for c, value in enumerate(lines):
                    spread[pl.ds((k * chunks + c) * pitch + row * ROW_STEP, SUB, stride=ROW_STEP), :] = value
    for place, t in enumerate(exchange_order(tiles)):
        for i in range(tile_rows + 2):
            row = (t * tile_rows + i - 1) % rows
            for k in range(depth):
                at = (i * depth + k) * chunks
                line = spread[pl.ds(k * chunks * pitch + row * ROW_STEP, chunks, stride=pitch), :]
                out_ref[place, at:at + chunks, :] = line


def prepare(order_ref, light_ref, color_ref, opacity_ref,
            brick_at_ref, word_ref, light_rows_ref, first_ref, last_ref, later_ref):
    bins = color_ref.shape[1] - 1
    _, halves, chunks, lanes = word_ref.shape
    shape = (chunks, lanes)

    def parts(values, unit):
        scaled = (values.astype(jnp.float32) * float(unit)).astype(jnp.int32)
        return scaled[:, :bins], scaled[:, 1:] - scaled[:, :bins]

    start, slope = parts(opacity_ref[...].reshape(1, bins + 1), OPACITY_UNIT)
    pieces = [start & 511, (start >> 9) + ((slope & 31) << 4), (slope >> 5) & 511]
    start, slope = parts(color_ref[...], COLOR_UNIT)
    upper = (slope << 20) + ((start - COLOR_LEAST) << 9)
    for c in range(3):
        word = upper[c:c + 1] + pieces[c]
        for h in range(halves):
            word_ref[c, h] = jnp.broadcast_to(word[:, h * lanes:(h + 1) * lanes], shape)
    for i in range(3):
        light_rows_ref[i] = jnp.full(shape, light_ref[i], jnp.float32) * math.sqrt(0.75)
    here, last = lax.axis_index("gz"), order_ref.shape[0] - 1
    for ref, place in [(first_ref, here == 0), (last_ref, here == last), (later_ref, here != 0)]:
        ref[...] = jnp.full(shape, place.astype(jnp.float32), jnp.float32)
    for place, b in enumerate(exchange_order(order_ref.shape[0])):
        brick_at_ref[order_ref[b]] = place


def table_lookup(word_ref):
    _, halves, _, lanes = word_ref.shape
    bins = halves * lanes

    def look_up(x):
        scaled = x * float(bins)
        index = jnp.minimum(scaled.astype(jnp.int32), bins - 1)
        fraction = scaled - index.astype(jnp.float32)
        low_bits = index & (lanes - 1)
        words = []
        for c in range(3):
            found = [
                jnp.take_along_axis(word_ref[c, h], low_bits, axis=1, mode="promise_in_bounds")
                for h in range(halves)
            ]
            word = found[0]
            for h in range(1, halves):
                word = jnp.where(index >= h * lanes, found[h], word)
            words.append(word)

        def blended(start, slope):
            return start.astype(jnp.float32) + fraction * slope.astype(jnp.float32)

        color = [blended(((w >> 9) & 2047) + COLOR_LEAST, w >> 20) for w in words]
        low, middle, high = words
        start = (low & 511) + ((middle & 15) << 9)
        slope = ((high << 23) >> 18) + ((middle >> 4) & 31)
        return color, blended(start, slope) * (1.0 / OPACITY_UNIT)

    return look_up


def column_differences(fields, carried_ref, first):
    chunks, lanes = fields[0].shape
    count = carried_ref.shape[0] // (chunks + 2)
    lane = lax.broadcasted_iota(jnp.int32, (chunks, lanes), 1)
    at_first, at_last = lane == 0, lane == lanes - 1
    after = [pltpu.roll(x, lanes - 1, 1) for x in fields]
    before = [pltpu.roll(x, 1, 1) for x in fields]
    for i, (right, left) in enumerate(zip(after, before), first):
        carried_ref[pl.ds(count + i, chunks, stride=count), :] = jnp.where(at_last, right, left)
    differences = []
    for i, (right, left) in enumerate(zip(after, before), first):
        further = carried_ref[pl.ds(2 * count + i, chunks, stride=count), :]
        back = carried_ref[pl.ds(i, chunks, stride=count), :]
        differences.append(jnp.where(at_last, further, right) - jnp.where(at_first, back, left))
    return differences


def depth_differences(field):
    last = len(field) - 1
    made = {}
    for k in range(last + 1):
        ends = (min(k + 1, last), max(k - 1, 0))
        if ends not in made:
            made[ends] = field[ends[0]] - field[ends[1]]
    return [made[(min(k + 1, last), max(k - 1, 0))] for k in range(last + 1)]


def shading_of(facing, squared_plus_one):
    return 0.25 + (facing * facing) * pltpu.reciprocal(squared_plus_one, approx=True)


def main_kernel(edge_rows, brick_at, light_ref, word_ref, tile_ref,
                part_ref, color_sum_ref, keep_ref, carried):
    bricks, padded_rows, depth, chunks, lanes = tile_ref.shape
    rows = padded_rows - 2
    inner_rows = [r for r in range(rows) if r not in edge_rows]
    shape = (chunks, lanes)
    look_up = table_lookup(word_ref)
    border = carried.shape[0] // (chunks + 2)
    carried[:border, :] = jnp.zeros((border, lanes), jnp.float32)
    carried[-border:, :] = jnp.zeros((border, lanes), jnp.float32)
    light = [light_ref[i] for i in range(3)]
    together = border // (rows * depth)

    def step(trip, carry):
        colors, keeps = list(carry[0]), list(carry[1])
        at = [brick_at[trip * together + u] for u in range(together)]
        fields = [[[tile_ref[b, r, k] for k in range(depth)] for r in range(padded_rows)] for b in at]
        kept = []
        for u, (b, field) in enumerate(zip(at, fields)):
            cells = [x for line in field[1:-1] for x in line]
            column = column_differences(cells, carried, u * len(cells))
            for r in range(rows):
                for k, dz in enumerate(depth_differences(field[r + 1])):
                    x = field[r + 1][k]
                    dx = column[r * depth + k]
                    color, opacity = look_up(x)
                    weight = keeps[r] * opacity
                    facing = dz * light[0] + dx * light[2]
                    squared = (dz * dz + 1.0) + dx * dx
                    if r in edge_rows:
                        values = [weight * color[c] for c in range(3)] + [facing, squared]
                        kept.append((b, edge_rows.index(r), k, values))
                    else:
                        i = inner_rows.index(r)
                        dy = field[r + 2][k] - field[r][k]
                        shaded = weight * shading_of(facing + dy * light[1], squared + dy * dy)
                        for c in range(3):
                            slot = c * len(inner_rows) + i
                            colors[slot] = colors[slot] + shaded * color[c]
                    keeps[r] = keeps[r] - weight
        for b, i, k, values in kept:
            for v, value in enumerate(values):
                part_ref[b, i, k, v] = value
        return tuple(colors), tuple(keeps)

    zero, one = jnp.zeros(shape, jnp.float32), jnp.ones(shape, jnp.float32)
    colors, keeps = lax.fori_loop(
        0, bricks // together, step, ((zero,) * (3 * len(inner_rows)), (one,) * rows))
    for i, value in enumerate(colors):
        color_sum_ref[i] = value
    for r, value in enumerate(keeps):
        keep_ref[r] = value


def finish_kernel(edge_rows, first_ref, last_ref, light_ref, tile_ref, other_ref, part_ref, color_sum_ref, keep_ref,
                  out_ref, staged):
    bricks, padded_rows, depth, chunks, lanes = tile_ref.shape
    rows = padded_rows - 2
    inner_rows = [r for r in range(rows) if r not in edge_rows]
    shape = (chunks, lanes)
    light_rows = light_ref[1]
    is_first, is_last = first_ref[...] == 1.0, last_ref[...] == 1.0

    together = 16 if bricks % 16 == 0 else 1

    def step(trip, colors):
        colors = list(colors)
        for u in range(together):
            b = trip * together + u
            for i, r in enumerate(edge_rows):
                for k in range(depth):
                    above, below = tile_ref[b, r, k], tile_ref[b, r + 2, k]
                    if r == 0:
                        above = jnp.where(is_first, other_ref[b, k], above)
                    if r == rows - 1:
                        below = jnp.where(is_last, other_ref[b, k], below)
                    dy = below - above
                    facing = part_ref[b, i, k, 3] + dy * light_rows
                    shading = shading_of(facing, part_ref[b, i, k, 4] + dy * dy)
                    for c in range(3):
                        slot = c * len(edge_rows) + i
                        colors[slot] = colors[slot] + shading * part_ref[b, i, k, c]
        return tuple(colors)

    zero = jnp.zeros(shape, jnp.float32)
    pitch = 4 * rows * ROW_STEP + 1
    edge_colors = lax.fori_loop(0, bricks // together, step, (zero,) * (3 * len(edge_rows)))
    for r in range(rows):
        for c in range(3):
            if r in edge_rows:
                value = edge_colors[c * len(edge_rows) + edge_rows.index(r)]
            else:
                value = color_sum_ref[c * len(inner_rows) + inner_rows.index(r)]
            staged[pl.ds((c * rows + r) * ROW_STEP, chunks, stride=pitch), :] = value * (1.0 / COLOR_UNIT)
        staged[pl.ds((3 * rows + r) * ROW_STEP, chunks, stride=pitch), :] = 1.0 - keep_ref[r]
    for c in range(4):
        for q in range(chunks):
            start = q * pitch + c * rows * ROW_STEP
            source = pl.ds(start, rows, stride=ROW_STEP) if rows > 1 else pl.ds(start, 1)
            out_ref[c, 0, :, q * LANES:(q + 1) * LANES] = staged[source, :]


def shards(scalar, bin_index, color_table, opacity_table, light_dir, view_order):
    depth, rows, cols = scalar.shape
    bricks, bands = lax.axis_size("gz"), lax.axis_size("gy")
    tile_rows = rows // bricks
    chunks = cols // LANES
    edge_rows = sorted({0, tile_rows - 1})
    inner_count = tile_rows - len(edge_rows)
    vmem = pl.BlockSpec(memory_space=pltpu.VMEM)
    smem = pl.BlockSpec(memory_space=pltpu.SMEM)
    params = pltpu.CompilerParams(vmem_limit_bytes=32 << 20)
    cells = bricks * depth * cols
    lines = (chunks, LANES)
    halves = (color_table.shape[1] - 1) // LANES
    together = 8 if bricks % 8 == 0 else 1
    pieces = 4 if rows % (4 * SUB) == 0 else 1
    hbm = pl.BlockSpec(memory_space=pltpu.HBM)
    given = [scalar, view_order, light_dir, color_table, opacity_table]
    sent, brick_at, words, light_rows, first, final, later = pl.pallas_call(
        functools.partial(pack_kernel, bricks),
        out_shape=[
            pltpu.VMEM((bricks, (tile_rows + 2) * depth * chunks, LANES), jnp.float32),
            pltpu.SMEM((bricks,), jnp.int32),
            jax.ShapeDtypeStruct((3, halves) + lines, jnp.int32),
            jax.ShapeDtypeStruct((3,) + lines, jnp.float32),
        ] + [jax.ShapeDtypeStruct(lines, jnp.float32)] * 3,
        in_specs=[hbm] * 5,
        out_specs=[vmem, smem] + [vmem] * 5,
        scratch_shapes=[
            pltpu.VMEM(scalar.shape, scalar.dtype),
            pltpu.VMEM((depth * chunks * (rows * ROW_STEP + 1), LANES), scalar.dtype),
            pltpu.SMEM(view_order.shape, view_order.dtype),
            pltpu.SMEM(light_dir.shape, light_dir.dtype),
            pltpu.VMEM(color_table.shape, color_table.dtype),
            pltpu.VMEM(opacity_table.shape, opacity_table.dtype),
            pltpu.SemaphoreType.DMA((pieces,)),
            pltpu.SemaphoreType.DMA((4,)),
        ],
        compiler_params=params,
        name="pack_rows",
    )(*[pltpu.with_memory_space_constraint(x, pltpu.HBM) for x in given])
    arrived = lax.all_to_all(
        sent, "gz", split_axis=0, concat_axis=0, tiled=True, axis_index_groups=[exchange_order(bricks)])
    tiles = arrived.reshape(bricks, tile_rows + 2, depth, chunks, LANES)

    last = bricks - 1
    pairs = [(g, g + 1) for g in range(bands - 1)]
    pairs += [(last * bands + g + 1, last * bands + g) for g in range(bands - 1)]
    wrapped = tiles[:, 0] * first + tiles[:, -1] * later
    other = lax.ppermute(wrapped, ("gz", "gy"), pairs)
    parts, color_sums, keeps = pl.pallas_call(
        functools.partial(main_kernel, edge_rows),
        out_shape=[
            jax.ShapeDtypeStruct((bricks, len(edge_rows), depth, 5, chunks, LANES), jnp.float32),
            jax.ShapeDtypeStruct((max(3 * inner_count, 1), chunks, LANES), jnp.float32),
            jax.ShapeDtypeStruct((tile_rows, chunks, LANES), jnp.float32),
        ],
        in_specs=[smem] + [vmem] * 3,
        out_specs=[vmem, vmem, vmem],
        scratch_shapes=[pltpu.VMEM(((chunks + 2) * (together * tile_rows * depth + 1), LANES), jnp.float32)],
        compiler_params=params,
        cost_estimate=pl.CostEstimate(
            flops=100 * cells * tile_rows, bytes_accessed=24 * cells * tile_rows, transcendentals=0),
        name="main_rows",
    )(brick_at, light_rows, words, tiles)
    return pl.pallas_call(
        functools.partial(finish_kernel, edge_rows),
        out_shape=jax.ShapeDtypeStruct((4, 1, tile_rows, cols), jnp.float32),
        in_specs=[vmem] * 8,
        out_specs=vmem,
        scratch_shapes=[pltpu.VMEM((chunks * (4 * tile_rows * ROW_STEP + 1), LANES), jnp.float32)],
        compiler_params=params,
        cost_estimate=pl.CostEstimate(
            flops=10 * cells * tile_rows, bytes_accessed=24 * cells * tile_rows, transcendentals=0),
        name="edge_rows",
    )(first, final, light_rows, tiles, other, parts, color_sums, keeps)


def solution(mesh):
    in_specs = (P("gz", "gy", None), P("gz", "gy", None), P(), P(), P(), P())
    out_specs = P(None, "gy", "gz", None)
    return jax.shard_map(shards, mesh=mesh, in_specs=in_specs, out_specs=out_specs, check_vma=False)
```

```python
import functools
import math

import jax
import jax.numpy as jnp
from jax import lax
from jax.experimental import pallas as pl
from jax.experimental.pallas import tpu as pltpu
from jax.sharding import PartitionSpec as P

SUB, LANES = 8, 128
ROW_STEP = 3
COLOR_UNIT, COLOR_LEAST, OPACITY_UNIT = 2 ** 11, 204, 2 ** 18


def exchange_order(tiles):
    parts = 4 if tiles % 4 == 0 else 1
    size = tiles // parts
    return [p * size + -i % size for i in range(size) for p in range(parts)[::-1]]


def pack_kernel(tiles, field_ref, order_ref, light_ref, color_ref, opacity_ref,
                out_ref, brick_at_ref, word_ref, light_rows_ref, first_ref, last_ref, later_ref,
                field, spread, order, light, color, opacity, sems, table_sems):
    depth, rows, cols = field_ref.shape
    chunks = cols // LANES
    pitch = rows * ROW_STEP + 1
    tile_rows = rows // tiles
    pieces = sems.shape[0]
    piece_rows = rows // pieces

    def copy_in(p):
        part = pl.ds(p * piece_rows, piece_rows)
        return pltpu.make_async_copy(field_ref.at[:, part], field.at[:, part], sems.at[p])

    table_copies = [
        pltpu.make_async_copy(source, target, table_sems.at[i])
        for i, (source, target) in enumerate(
            [(color_ref, color), (opacity_ref, opacity), (order_ref, order), (light_ref, light)])
    ]
    for copy in table_copies:
        copy.start()
    for p in range(pieces):
        copy_in(p).start()
    for copy in table_copies:
        copy.wait()
    prepare(order, light, color, opacity, brick_at_ref, word_ref, light_rows_ref, first_ref, last_ref, later_ref)
    for p in range(pieces):
        copy_in(p).wait()
        for k in range(depth):
            for row in range(p * piece_rows, (p + 1) * piece_rows, SUB):
                lines = [field[k, row:row + SUB, c * LANES:(c + 1) * LANES] for c in range(chunks)]
                for c, value in enumerate(lines):
                    spread[pl.ds((k * chunks + c) * pitch + row * ROW_STEP, SUB, stride=ROW_STEP), :] = value
    for place, t in enumerate(exchange_order(tiles)):
        for i in range(tile_rows + 2):
            row = (t * tile_rows + i - 1) % rows
            for k in range(depth):
                at = (i * depth + k) * chunks
                line = spread[pl.ds(k * chunks * pitch + row * ROW_STEP, chunks, stride=pitch), :]
                out_ref[place, at:at + chunks, :] = line


def prepare(order_ref, light_ref, color_ref, opacity_ref,
            brick_at_ref, word_ref, light_rows_ref, first_ref, last_ref, later_ref):
    bins = color_ref.shape[1] - 1
    _, halves, chunks, lanes = word_ref.shape
    shape = (chunks, lanes)

    def parts(values, unit):
        scaled = (values.astype(jnp.float32) * float(unit)).astype(jnp.int32)
        return scaled[:, :bins], scaled[:, 1:] - scaled[:, :bins]

    start, slope = parts(opacity_ref[...].reshape(1, bins + 1), OPACITY_UNIT)
    pieces = [start & 511, (start >> 9) + ((slope & 31) << 4), (slope >> 5) & 511]
    start, slope = parts(color_ref[...], COLOR_UNIT)
    upper = (slope << 20) + ((start - COLOR_LEAST) << 9)
    for c in range(3):
        word = upper[c:c + 1] + pieces[c]
        for h in range(halves):
            word_ref[c, h] = jnp.broadcast_to(word[:, h * lanes:(h + 1) * lanes], shape)
    for i in range(3):
        light_rows_ref[i] = jnp.full(shape, light_ref[i], jnp.float32) * math.sqrt(0.75)
    here, last = lax.axis_index("gz"), order_ref.shape[0] - 1
    for ref, place in [(first_ref, here == 0), (last_ref, here == last), (later_ref, here != 0)]:
        ref[...] = jnp.full(shape, place.astype(jnp.float32), jnp.float32)
    for place, b in enumerate(exchange_order(order_ref.shape[0])):
        brick_at_ref[order_ref[b]] = place


def table_lookup(word_ref):
    _, halves, _, lanes = word_ref.shape
    bins = halves * lanes

    def look_up(x):
        scaled = x * float(bins)
        index = jnp.minimum(scaled.astype(jnp.int32), bins - 1)
        fraction = scaled - index.astype(jnp.float32)
        low_bits = index & (lanes - 1)
        words = []
        for c in range(3):
            found = [
                jnp.take_along_axis(word_ref[c, h], low_bits, axis=1, mode="promise_in_bounds")
                for h in range(halves)
            ]
            word = found[0]
            for h in range(1, halves):
                word = jnp.where(index >= h * lanes, found[h], word)
            words.append(word)

        def blended(start, slope):
            return start.astype(jnp.float32) + fraction * slope.astype(jnp.float32)

        color = [blended(((w >> 9) & 2047) + COLOR_LEAST, w >> 20) for w in words]
        low, middle, high = words
        start = (low & 511) + ((middle & 15) << 9)
        slope = ((high << 23) >> 18) + ((middle >> 4) & 31)
        return color, blended(start, slope) * (1.0 / OPACITY_UNIT)

    return look_up


def column_differences(fields, carried_ref, first):
    chunks, lanes = fields[0].shape
    count = carried_ref.shape[0] // (chunks + 2)
    lane = lax.broadcasted_iota(jnp.int32, (chunks, lanes), 1)
    at_first, at_last = lane == 0, lane == lanes - 1
    after = [pltpu.roll(x, lanes - 1, 1) for x in fields]
    before = [pltpu.roll(x, 1, 1) for x in fields]
    for i, (right, left) in enumerate(zip(after, before), first):
        carried_ref[pl.ds(count + i, chunks, stride=count), :] = jnp.where(at_last, right, left)
    differences = []
    for i, (right, left) in enumerate(zip(after, before), first):
        further = carried_ref[pl.ds(2 * count + i, chunks, stride=count), :]
        back = carried_ref[pl.ds(i, chunks, stride=count), :]
        differences.append(jnp.where(at_last, further, right) - jnp.where(at_first, back, left))
    return differences


def depth_differences(field):
    last = len(field) - 1
    made = {}
    for k in range(last + 1):
        ends = (min(k + 1, last), max(k - 1, 0))
        if ends not in made:
            made[ends] = field[ends[0]] - field[ends[1]]
    return [made[(min(k + 1, last), max(k - 1, 0))] for k in range(last + 1)]


def shading_of(facing, squared_plus_one):
    return 0.25 + (facing * facing) * pltpu.reciprocal(squared_plus_one, approx=True)


def main_kernel(edge_rows, brick_at, light_ref, word_ref, tile_ref,
                part_ref, color_sum_ref, keep_ref, carried):
    bricks, padded_rows, depth, chunks, lanes = tile_ref.shape
    rows = padded_rows - 2
    inner_rows = [r for r in range(rows) if r not in edge_rows]
    shape = (chunks, lanes)
    look_up = table_lookup(word_ref)
    border = carried.shape[0] // (chunks + 2)
    carried[:border, :] = jnp.zeros((border, lanes), jnp.float32)
    carried[-border:, :] = jnp.zeros((border, lanes), jnp.float32)
    light = [light_ref[i] for i in range(3)]
    together = border // (rows * depth)

    def step(trip, carry):
        colors, keeps = list(carry[0]), list(carry[1])
        at = [brick_at[trip * together + u] for u in range(together)]
        fields = [[[tile_ref[b, r, k] for k in range(depth)] for r in range(padded_rows)] for b in at]
        kept = []
        for u, (b, field) in enumerate(zip(at, fields)):
            cells = [x for line in field[1:-1] for x in line]
            column = column_differences(cells, carried, u * len(cells))
            for r in range(rows):
                for k, dz in enumerate(depth_differences(field[r + 1])):
                    x = field[r + 1][k]
                    dx = column[r * depth + k]
                    color, opacity = look_up(x)
                    weight = keeps[r] * opacity
                    facing = dz * light[0] + dx * light[2]
                    squared = (dz * dz + 1.0) + dx * dx
                    if r in edge_rows:
                        values = [weight * color[c] for c in range(3)] + [facing, squared]
                        kept.append((b, edge_rows.index(r), k, values))
                    else:
                        i = inner_rows.index(r)
                        dy = field[r + 2][k] - field[r][k]
                        shaded = weight * shading_of(facing + dy * light[1], squared + dy * dy)
                        for c in range(3):
                            slot = c * len(inner_rows) + i
                            colors[slot] = colors[slot] + shaded * color[c]
                    keeps[r] = keeps[r] - weight
        for b, i, k, values in kept:
            for v, value in enumerate(values):
                part_ref[b, i, k, v] = value
        return tuple(colors), tuple(keeps)

    zero, one = jnp.zeros(shape, jnp.float32), jnp.ones(shape, jnp.float32)
    colors, keeps = lax.fori_loop(
        0, bricks // together, step, ((zero,) * (3 * len(inner_rows)), (one,) * rows))
    for i, value in enumerate(colors):
        color_sum_ref[i] = value
    for r, value in enumerate(keeps):
        keep_ref[r] = value


def finish_kernel(edge_rows, first_ref, last_ref, light_ref, tile_ref, other_ref, part_ref, color_sum_ref, keep_ref,
                  out_ref, staged):
    bricks, padded_rows, depth, chunks, lanes = tile_ref.shape
    rows = padded_rows - 2
    inner_rows = [r for r in range(rows) if r not in edge_rows]
    shape = (chunks, lanes)
    light_rows = light_ref[1]
    is_first, is_last = first_ref[...] == 1.0, last_ref[...] == 1.0

    together = 16 if bricks % 16 == 0 else 1

    def step(trip, colors):
        colors = list(colors)
        for u in range(together):
            b = trip * together + u
            for i, r in enumerate(edge_rows):
                for k in range(depth):
                    above, below = tile_ref[b, r, k], tile_ref[b, r + 2, k]
                    if r == 0:
                        above = jnp.where(is_first, other_ref[b, k], above)
                    if r == rows - 1:
                        below = jnp.where(is_last, other_ref[b, k], below)
                    dy = below - above
                    facing = part_ref[b, i, k, 3] + dy * light_rows
                    shading = shading_of(facing, part_ref[b, i, k, 4] + dy * dy)
                    for c in range(3):
                        slot = c * len(edge_rows) + i
                        colors[slot] = colors[slot] + shading * part_ref[b, i, k, c]
        return tuple(colors)

    zero = jnp.zeros(shape, jnp.float32)
    pitch = 4 * rows * ROW_STEP + 1
    edge_colors = lax.fori_loop(0, bricks // together, step, (zero,) * (3 * len(edge_rows)))
    for r in range(rows):
        for c in range(3):
            if r in edge_rows:
                value = edge_colors[c * len(edge_rows) + edge_rows.index(r)]
            else:
                value = color_sum_ref[c * len(inner_rows) + inner_rows.index(r)]
            staged[pl.ds((c * rows + r) * ROW_STEP, chunks, stride=pitch), :] = value * (1.0 / COLOR_UNIT)
        staged[pl.ds((3 * rows + r) * ROW_STEP, chunks, stride=pitch), :] = 1.0 - keep_ref[r]
    for c in range(4):
        for q in range(chunks):
            start = q * pitch + c * rows * ROW_STEP
            source = pl.ds(start, rows, stride=ROW_STEP) if rows > 1 else pl.ds(start, 1)
            out_ref[c, 0, :, q * LANES:(q + 1) * LANES] = staged[source, :]


def shards(scalar, bin_index, color_table, opacity_table, light_dir, view_order):
    depth, rows, cols = scalar.shape
    bricks, bands = lax.axis_size("gz"), lax.axis_size("gy")
    tile_rows = rows // bricks
    chunks = cols // LANES
    edge_rows = sorted({0, tile_rows - 1})
    inner_count = tile_rows - len(edge_rows)
    vmem = pl.BlockSpec(memory_space=pltpu.VMEM)
    smem = pl.BlockSpec(memory_space=pltpu.SMEM)
    params = pltpu.CompilerParams(vmem_limit_bytes=32 << 20)
    cells = bricks * depth * cols
    lines = (chunks, LANES)
    halves = (color_table.shape[1] - 1) // LANES
    together = 8 if bricks % 8 == 0 else 1
    pieces = 4 if rows % (4 * SUB) == 0 else 1
    hbm = pl.BlockSpec(memory_space=pltpu.HBM)
    given = [scalar, view_order, light_dir, color_table, opacity_table]
    sent, brick_at, words, light_rows, first, final, later = pl.pallas_call(
        functools.partial(pack_kernel, bricks),
        out_shape=[
            pltpu.VMEM((bricks, (tile_rows + 2) * depth * chunks, LANES), jnp.float32),
            pltpu.SMEM((bricks,), jnp.int32),
            jax.ShapeDtypeStruct((3, halves) + lines, jnp.int32),
            jax.ShapeDtypeStruct((3,) + lines, jnp.float32),
        ] + [jax.ShapeDtypeStruct(lines, jnp.float32)] * 3,
        in_specs=[hbm] * 5,
        out_specs=[vmem, smem] + [vmem] * 5,
        scratch_shapes=[
            pltpu.VMEM(scalar.shape, scalar.dtype),
            pltpu.VMEM((depth * chunks * (rows * ROW_STEP + 1), LANES), scalar.dtype),
            pltpu.SMEM(view_order.shape, view_order.dtype),
            pltpu.SMEM(light_dir.shape, light_dir.dtype),
            pltpu.VMEM(color_table.shape, color_table.dtype),
            pltpu.VMEM(opacity_table.shape, opacity_table.dtype),
            pltpu.SemaphoreType.DMA((pieces,)),
            pltpu.SemaphoreType.DMA((4,)),
        ],
        compiler_params=params,
        name="pack_rows",
    )(*[pltpu.with_memory_space_constraint(x, pltpu.HBM) for x in given])
    arrived = lax.all_to_all(
        sent, "gz", split_axis=0, concat_axis=0, tiled=True, axis_index_groups=[exchange_order(bricks)])
    tiles = arrived.reshape(bricks, tile_rows + 2, depth, chunks, LANES)

    last = bricks - 1
    pairs = [(g, g + 1) for g in range(bands - 1)]
    pairs += [(last * bands + g + 1, last * bands + g) for g in range(bands - 1)]
    wrapped = tiles[:, 0] * first + tiles[:, -1] * later
    other = lax.ppermute(wrapped, ("gz", "gy"), pairs)
    parts, color_sums, keeps = pl.pallas_call(
        functools.partial(main_kernel, edge_rows),
        out_shape=[
            jax.ShapeDtypeStruct((bricks, len(edge_rows), depth, 5, chunks, LANES), jnp.float32),
            jax.ShapeDtypeStruct((max(3 * inner_count, 1), chunks, LANES), jnp.float32),
            jax.ShapeDtypeStruct((tile_rows, chunks, LANES), jnp.float32),
        ],
        in_specs=[smem] + [vmem] * 3,
        out_specs=[vmem, vmem, vmem],
        scratch_shapes=[pltpu.VMEM(((chunks + 2) * (together * tile_rows * depth + 1), LANES), jnp.float32)],
        compiler_params=params,
        cost_estimate=pl.CostEstimate(
            flops=100 * cells * tile_rows, bytes_accessed=24 * cells * tile_rows, transcendentals=0),
        name="main_rows",
    )(brick_at, light_rows, words, tiles)
    return pl.pallas_call(
        functools.partial(finish_kernel, edge_rows),
        out_shape=jax.ShapeDtypeStruct((4, 1, tile_rows, cols), jnp.float32),
        in_specs=[vmem] * 8,
        out_specs=vmem,
        scratch_shapes=[pltpu.VMEM((chunks * (4 * tile_rows * ROW_STEP + 1), LANES), jnp.float32)],
        compiler_params=params,
        cost_estimate=pl.CostEstimate(
            flops=10 * cells * tile_rows, bytes_accessed=24 * cells * tile_rows, transcendentals=0),
        name="edge_rows",
    )(first, final, light_rows, tiles, other, parts, color_sums, keeps)


def solution(mesh):
    in_specs = (P("gz", "gy", None), P("gz", "gy", None), P(), P(), P(), P())
    out_specs = P(None, "gy", "gz", None)
    return jax.shard_map(shards, mesh=mesh, in_specs=in_specs, out_specs=out_specs, check_vma=False)
```

```python
import functools
import math

import jax
import jax.numpy as jnp
from jax import lax
from jax.experimental import pallas as pl
from jax.experimental.pallas import tpu as pltpu
from jax.sharding import PartitionSpec as P

SUB, LANES = 8, 128
ROW_STEP = 3
COLOR_UNIT, COLOR_LEAST, OPACITY_UNIT = 2 ** 11, 204, 2 ** 18


def exchange_order(tiles):
    parts = 4 if tiles % 4 == 0 else 1
    return [(parts - 1 - i % parts) * (tiles // parts) + i // parts for i in range(tiles)]


def pack_kernel(tiles, field_ref, order_ref, light_ref, color_ref, opacity_ref,
                out_ref, brick_at_ref, word_ref, light_rows_ref, first_ref, last_ref, later_ref,
                field, spread, order, light, color, opacity, sems, table_sems):
    depth, rows, cols = field_ref.shape
    chunks = cols // LANES
    pitch = rows * ROW_STEP + 1
    tile_rows = rows // tiles
    pieces = sems.shape[0]
    piece_rows = rows // pieces

    def copy_in(p):
        part = pl.ds(p * piece_rows, piece_rows)
        return pltpu.make_async_copy(field_ref.at[:, part], field.at[:, part], sems.at[p])

    table_copies = [
        pltpu.make_async_copy(source, target, table_sems.at[i])
        for i, (source, target) in enumerate(
            [(color_ref, color), (opacity_ref, opacity), (order_ref, order), (light_ref, light)])
    ]
    for copy in table_copies:
        copy.start()
    for p in range(pieces):
        copy_in(p).start()
    for copy in table_copies:
        copy.wait()
    prepare(order, light, color, opacity, brick_at_ref, word_ref, light_rows_ref, first_ref, last_ref, later_ref)
    for p in range(pieces):
        copy_in(p).wait()
        for k in range(depth):
            for row in range(p * piece_rows, (p + 1) * piece_rows, SUB):
                lines = [field[k, row:row + SUB, c * LANES:(c + 1) * LANES] for c in range(chunks)]
                for c, value in enumerate(lines):
                    spread[pl.ds((k * chunks + c) * pitch + row * ROW_STEP, SUB, stride=ROW_STEP), :] = value
    for place, t in enumerate(exchange_order(tiles)):
        for i in range(tile_rows + 2):
            row = (t * tile_rows + i - 1) % rows
            for k in range(depth):
                at = (i * depth + k) * chunks
                line = spread[pl.ds(k * chunks * pitch + row * ROW_STEP, chunks, stride=pitch), :]
                out_ref[place, at:at + chunks, :] = line


def prepare(order_ref, light_ref, color_ref, opacity_ref,
            brick_at_ref, word_ref, light_rows_ref, first_ref, last_ref, later_ref):
    bins = color_ref.shape[1] - 1
    _, halves, chunks, lanes = word_ref.shape
    shape = (chunks, lanes)

    def parts(values, unit):
        scaled = (values.astype(jnp.float32) * float(unit)).astype(jnp.int32)
        return scaled[:, :bins], scaled[:, 1:] - scaled[:, :bins]

    start, slope = parts(opacity_ref[...].reshape(1, bins + 1), OPACITY_UNIT)
    pieces = [start & 511, (start >> 9) + ((slope & 31) << 4), (slope >> 5) & 511]
    start, slope = parts(color_ref[...], COLOR_UNIT)
    upper = (slope << 20) + ((start - COLOR_LEAST) << 9)
    for c in range(3):
        word = upper[c:c + 1] + pieces[c]
        for h in range(halves):
            word_ref[c, h] = jnp.broadcast_to(word[:, h * lanes:(h + 1) * lanes], shape)
    for i in range(3):
        light_rows_ref[i] = jnp.full(shape, light_ref[i], jnp.float32) * math.sqrt(0.75)
    here, last = lax.axis_index("gz"), order_ref.shape[0] - 1
    for ref, place in [(first_ref, here == 0), (last_ref, here == last), (later_ref, here != 0)]:
        ref[...] = jnp.full(shape, place.astype(jnp.float32), jnp.float32)
    for place, b in enumerate(exchange_order(order_ref.shape[0])):
        brick_at_ref[order_ref[b]] = place


def table_lookup(word_ref):
    _, halves, _, lanes = word_ref.shape
    bins = halves * lanes

    def look_up(x):
        scaled = x * float(bins)
        index = jnp.minimum(scaled.astype(jnp.int32), bins - 1)
        fraction = scaled - index.astype(jnp.float32)
        low_bits = index & (lanes - 1)
        words = []
        for c in range(3):
            found = [
                jnp.take_along_axis(word_ref[c, h], low_bits, axis=1, mode="promise_in_bounds")
                for h in range(halves)
            ]
            word = found[0]
            for h in range(1, halves):
                word = jnp.where(index >= h * lanes, found[h], word)
            words.append(word)

        def blended(start, slope):
            return start.astype(jnp.float32) + fraction * slope.astype(jnp.float32)

        color = [blended(((w >> 9) & 2047) + COLOR_LEAST, w >> 20) for w in words]
        low, middle, high = words
        start = (low & 511) + ((middle & 15) << 9)
        slope = ((high << 23) >> 18) + ((middle >> 4) & 31)
        return color, blended(start, slope) * (1.0 / OPACITY_UNIT)

    return look_up


def column_differences(fields, carried_ref, first):
    chunks, lanes = fields[0].shape
    count = carried_ref.shape[0] // (chunks + 2)
    lane = lax.broadcasted_iota(jnp.int32, (chunks, lanes), 1)
    at_first, at_last = lane == 0, lane == lanes - 1
    after = [pltpu.roll(x, lanes - 1, 1) for x in fields]
    before = [pltpu.roll(x, 1, 1) for x in fields]
    for i, (right, left) in enumerate(zip(after, before), first):
        carried_ref[pl.ds(count + i, chunks, stride=count), :] = jnp.where(at_last, right, left)
    differences = []
    for i, (right, left) in enumerate(zip(after, before), first):
        further = carried_ref[pl.ds(2 * count + i, chunks, stride=count), :]
        back = carried_ref[pl.ds(i, chunks, stride=count), :]
        differences.append(jnp.where(at_last, further, right) - jnp.where(at_first, back, left))
    return differences


def depth_differences(field):
    last = len(field) - 1
    made = {}
    for k in range(last + 1):
        ends = (min(k + 1, last), max(k - 1, 0))
        if ends not in made:
            made[ends] = field[ends[0]] - field[ends[1]]
    return [made[(min(k + 1, last), max(k - 1, 0))] for k in range(last + 1)]


def shading_of(facing, squared_plus_one):
    return 0.25 + (facing * facing) * pltpu.reciprocal(squared_plus_one, approx=True)


def main_kernel(edge_rows, brick_at, light_ref, word_ref, tile_ref,
                part_ref, color_sum_ref, keep_ref, carried):
    bricks, padded_rows, depth, chunks, lanes = tile_ref.shape
    rows = padded_rows - 2
    inner_rows = [r for r in range(rows) if r not in edge_rows]
    shape = (chunks, lanes)
    look_up = table_lookup(word_ref)
    border = carried.shape[0] // (chunks + 2)
    carried[:border, :] = jnp.zeros((border, lanes), jnp.float32)
    carried[-border:, :] = jnp.zeros((border, lanes), jnp.float32)
    light = [light_ref[i] for i in range(3)]
    together = border // (rows * depth)

    def step(trip, carry):
        colors, keeps = list(carry[0]), list(carry[1])
        at = [brick_at[trip * together + u] for u in range(together)]
        fields = [[[tile_ref[b, r, k] for k in range(depth)] for r in range(padded_rows)] for b in at]
        kept = []
        for u, (b, field) in enumerate(zip(at, fields)):
            cells = [x for line in field[1:-1] for x in line]
            column = column_differences(cells, carried, u * len(cells))
            for r in range(rows):
                for k, dz in enumerate(depth_differences(field[r + 1])):
                    x = field[r + 1][k]
                    dx = column[r * depth + k]
                    color, opacity = look_up(x)
                    weight = keeps[r] * opacity
                    facing = dz * light[0] + dx * light[2]
                    squared = (dz * dz + 1.0) + dx * dx
                    if r in edge_rows:
                        values = [weight * color[c] for c in range(3)] + [facing, squared]
                        kept.append((b, edge_rows.index(r), k, values))
                    else:
                        i = inner_rows.index(r)
                        dy = field[r + 2][k] - field[r][k]
                        shaded = weight * shading_of(facing + dy * light[1], squared + dy * dy)
                        for c in range(3):
                            slot = c * len(inner_rows) + i
                            colors[slot] = colors[slot] + shaded * color[c]
                    keeps[r] = keeps[r] - weight
        for b, i, k, values in kept:
            for v, value in enumerate(values):
                part_ref[b, i, k, v] = value
        return tuple(colors), tuple(keeps)

    zero, one = jnp.zeros(shape, jnp.float32), jnp.ones(shape, jnp.float32)
    colors, keeps = lax.fori_loop(
        0, bricks // together, step, ((zero,) * (3 * len(inner_rows)), (one,) * rows))
    for i, value in enumerate(colors):
        color_sum_ref[i] = value
    for r, value in enumerate(keeps):
        keep_ref[r] = value


def finish_kernel(edge_rows, first_ref, last_ref, light_ref, tile_ref, other_ref, part_ref, color_sum_ref, keep_ref,
                  out_ref, staged):
    bricks, padded_rows, depth, chunks, lanes = tile_ref.shape
    rows = padded_rows - 2
    inner_rows = [r for r in range(rows) if r not in edge_rows]
    shape = (chunks, lanes)
    light_rows = light_ref[1]
    is_first, is_last = first_ref[...] == 1.0, last_ref[...] == 1.0

    together = 16 if bricks % 16 == 0 else 1

    def step(trip, colors):
        colors = list(colors)
        for u in range(together):
            b = trip * together + u
            for i, r in enumerate(edge_rows):
                for k in range(depth):
                    above, below = tile_ref[b, r, k], tile_ref[b, r + 2, k]
                    if r == 0:
                        above = jnp.where(is_first, other_ref[b, k], above)
                    if r == rows - 1:
                        below = jnp.where(is_last, other_ref[b, k], below)
                    dy = below - above
                    facing = part_ref[b, i, k, 3] + dy * light_rows
                    shading = shading_of(facing, part_ref[b, i, k, 4] + dy * dy)
                    for c in range(3):
                        slot = c * len(edge_rows) + i
                        colors[slot] = colors[slot] + shading * part_ref[b, i, k, c]
        return tuple(colors)

    zero = jnp.zeros(shape, jnp.float32)
    pitch = 4 * rows * ROW_STEP + 1
    edge_colors = lax.fori_loop(0, bricks // together, step, (zero,) * (3 * len(edge_rows)))
    for r in range(rows):
        for c in range(3):
            if r in edge_rows:
                value = edge_colors[c * len(edge_rows) + edge_rows.index(r)]
            else:
                value = color_sum_ref[c * len(inner_rows) + inner_rows.index(r)]
            staged[pl.ds((c * rows + r) * ROW_STEP, chunks, stride=pitch), :] = value * (1.0 / COLOR_UNIT)
        staged[pl.ds((3 * rows + r) * ROW_STEP, chunks, stride=pitch), :] = 1.0 - keep_ref[r]
    for c in range(4):
        for q in range(chunks):
            start = q * pitch + c * rows * ROW_STEP
            source = pl.ds(start, rows, stride=ROW_STEP) if rows > 1 else pl.ds(start, 1)
            out_ref[c, 0, :, q * LANES:(q + 1) * LANES] = staged[source, :]


def shards(scalar, bin_index, color_table, opacity_table, light_dir, view_order):
    depth, rows, cols = scalar.shape
    bricks, bands = lax.axis_size("gz"), lax.axis_size("gy")
    tile_rows = rows // bricks
    chunks = cols // LANES
    edge_rows = sorted({0, tile_rows - 1})
    inner_count = tile_rows - len(edge_rows)
    vmem = pl.BlockSpec(memory_space=pltpu.VMEM)
    smem = pl.BlockSpec(memory_space=pltpu.SMEM)
    params = pltpu.CompilerParams(vmem_limit_bytes=32 << 20)
    cells = bricks * depth * cols
    lines = (chunks, LANES)
    halves = (color_table.shape[1] - 1) // LANES
    together = 16 if bricks % 16 == 0 else 1
    pieces = 4 if rows % (4 * SUB) == 0 else 1
    hbm = pl.BlockSpec(memory_space=pltpu.HBM)
    given = [scalar, view_order, light_dir, color_table, opacity_table]
    sent, brick_at, words, light_rows, first, final, later = pl.pallas_call(
        functools.partial(pack_kernel, bricks),
        out_shape=[
            pltpu.VMEM((bricks, (tile_rows + 2) * depth * chunks, LANES), jnp.float32),
            pltpu.SMEM((bricks,), jnp.int32),
            jax.ShapeDtypeStruct((3, halves) + lines, jnp.int32),
            jax.ShapeDtypeStruct((3,) + lines, jnp.float32),
        ] + [jax.ShapeDtypeStruct(lines, jnp.float32)] * 3,
        in_specs=[hbm] * 5,
        out_specs=[vmem, smem] + [vmem] * 5,
        scratch_shapes=[
            pltpu.VMEM(scalar.shape, scalar.dtype),
            pltpu.VMEM((depth * chunks * (rows * ROW_STEP + 1), LANES), scalar.dtype),
            pltpu.SMEM(view_order.shape, view_order.dtype),
            pltpu.SMEM(light_dir.shape, light_dir.dtype),
            pltpu.VMEM(color_table.shape, color_table.dtype),
            pltpu.VMEM(opacity_table.shape, opacity_table.dtype),
            pltpu.SemaphoreType.DMA((pieces,)),
            pltpu.SemaphoreType.DMA((4,)),
        ],
        compiler_params=params,
        name="pack_rows",
    )(*[pltpu.with_memory_space_constraint(x, pltpu.HBM) for x in given])
    arrived = lax.all_to_all(
        sent, "gz", split_axis=0, concat_axis=0, tiled=True, axis_index_groups=[exchange_order(bricks)])
    tiles = arrived.reshape(bricks, tile_rows + 2, depth, chunks, LANES)

    last = bricks - 1
    pairs = [(g, g + 1) for g in range(bands - 1)]
    pairs += [(last * bands + g + 1, last * bands + g) for g in range(bands - 1)]
    wrapped = tiles[:, 0] * first + tiles[:, -1] * later
    other = lax.ppermute(wrapped, ("gz", "gy"), pairs)
    parts, color_sums, keeps = pl.pallas_call(
        functools.partial(main_kernel, edge_rows),
        out_shape=[
            jax.ShapeDtypeStruct((bricks, len(edge_rows), depth, 5, chunks, LANES), jnp.float32),
            jax.ShapeDtypeStruct((max(3 * inner_count, 1), chunks, LANES), jnp.float32),
            jax.ShapeDtypeStruct((tile_rows, chunks, LANES), jnp.float32),
        ],
        in_specs=[smem] + [vmem] * 3,
        out_specs=[vmem, vmem, vmem],
        scratch_shapes=[pltpu.VMEM(((chunks + 2) * (together * tile_rows * depth + 1), LANES), jnp.float32)],
        compiler_params=params,
        cost_estimate=pl.CostEstimate(
            flops=100 * cells * tile_rows, bytes_accessed=24 * cells * tile_rows, transcendentals=0),
        name="main_rows",
    )(brick_at, light_rows, words, tiles)
    return pl.pallas_call(
        functools.partial(finish_kernel, edge_rows),
        out_shape=jax.ShapeDtypeStruct((4, 1, tile_rows, cols), jnp.float32),
        in_specs=[vmem] * 8,
        out_specs=vmem,
        scratch_shapes=[pltpu.VMEM((chunks * (4 * tile_rows * ROW_STEP + 1), LANES), jnp.float32)],
        compiler_params=params,
        cost_estimate=pl.CostEstimate(
            flops=10 * cells * tile_rows, bytes_accessed=24 * cells * tile_rows, transcendentals=0),
        name="edge_rows",
    )(first, final, light_rows, tiles, other, parts, color_sums, keeps)


def solution(mesh):
    in_specs = (P("gz", "gy", None), P("gz", "gy", None), P(), P(), P(), P())
    out_specs = P(None, "gy", "gz", None)
    return jax.shard_map(shards, mesh=mesh, in_specs=in_specs, out_specs=out_specs, check_vma=False)
```

```python
import functools
import math

import jax
import jax.numpy as jnp
from jax import lax
from jax.experimental import pallas as pl
from jax.experimental.pallas import tpu as pltpu
from jax.sharding import PartitionSpec as P

SUB, LANES = 8, 128
ROW_STEP = 3
COLOR_UNIT, COLOR_LEAST, OPACITY_UNIT = 2 ** 11, 204, 2 ** 18


def exchange_order(tiles):
    parts = 4 if tiles % 4 == 0 else 1
    size = tiles // parts
    chips = sorted(range(size), key=lambda i: i % 2)
    return [p * size + i for i in chips for p in range(parts)[::-1]]


def pack_kernel(tiles, field_ref, order_ref, light_ref, color_ref, opacity_ref,
                out_ref, brick_at_ref, word_ref, light_rows_ref, first_ref, last_ref, later_ref,
                field, spread, order, light, color, opacity, sems, table_sems):
    depth, rows, cols = field_ref.shape
    chunks = cols // LANES
    pitch = rows * ROW_STEP + 1
    tile_rows = rows // tiles
    pieces = sems.shape[0]
    piece_rows = rows // pieces

    def copy_in(p):
        part = pl.ds(p * piece_rows, piece_rows)
        return pltpu.make_async_copy(field_ref.at[:, part], field.at[:, part], sems.at[p])

    table_copies = [
        pltpu.make_async_copy(source, target, table_sems.at[i])
        for i, (source, target) in enumerate(
            [(color_ref, color), (opacity_ref, opacity), (order_ref, order), (light_ref, light)])
    ]
    for copy in table_copies:
        copy.start()
    for p in range(pieces):
        copy_in(p).start()
    for copy in table_copies:
        copy.wait()
    prepare(order, light, color, opacity, brick_at_ref, word_ref, light_rows_ref, first_ref, last_ref, later_ref)
    for p in range(pieces):
        copy_in(p).wait()
        for k in range(depth):
            for row in range(p * piece_rows, (p + 1) * piece_rows, SUB):
                lines = [field[k, row:row + SUB, c * LANES:(c + 1) * LANES] for c in range(chunks)]
                for c, value in enumerate(lines):
                    spread[pl.ds((k * chunks + c) * pitch + row * ROW_STEP, SUB, stride=ROW_STEP), :] = value
    for place, t in enumerate(exchange_order(tiles)):
        for i in range(tile_rows + 2):
            row = (t * tile_rows + i - 1) % rows
            for k in range(depth):
                at = (i * depth + k) * chunks
                line = spread[pl.ds(k * chunks * pitch + row * ROW_STEP, chunks, stride=pitch), :]
                out_ref[place, at:at + chunks, :] = line


def prepare(order_ref, light_ref, color_ref, opacity_ref,
            brick_at_ref, word_ref, light_rows_ref, first_ref, last_ref, later_ref):
    bins = color_ref.shape[1] - 1
    _, halves, chunks, lanes = word_ref.shape
    shape = (chunks, lanes)

    def parts(values, unit):
        scaled = (values.astype(jnp.float32) * float(unit)).astype(jnp.int32)
        return scaled[:, :bins], scaled[:, 1:] - scaled[:, :bins]

    start, slope = parts(opacity_ref[...].reshape(1, bins + 1), OPACITY_UNIT)
    pieces = [start & 511, (start >> 9) + ((slope & 31) << 4), (slope >> 5) & 511]
    start, slope = parts(color_ref[...], COLOR_UNIT)
    upper = (slope << 20) + ((start - COLOR_LEAST) << 9)
    for c in range(3):
        word = upper[c:c + 1] + pieces[c]
        for h in range(halves):
            word_ref[c, h] = jnp.broadcast_to(word[:, h * lanes:(h + 1) * lanes], shape)
    for i in range(3):
        light_rows_ref[i] = jnp.full(shape, light_ref[i], jnp.float32) * math.sqrt(0.75)
    here, last = lax.axis_index("gz"), order_ref.shape[0] - 1
    for ref, place in [(first_ref, here == 0), (last_ref, here == last), (later_ref, here != 0)]:
        ref[...] = jnp.full(shape, place.astype(jnp.float32), jnp.float32)
    for place, b in enumerate(exchange_order(order_ref.shape[0])):
        brick_at_ref[order_ref[b]] = place


def table_lookup(word_ref):
    _, halves, _, lanes = word_ref.shape
    bins = halves * lanes

    def look_up(x):
        scaled = x * float(bins)
        index = jnp.minimum(scaled.astype(jnp.int32), bins - 1)
        fraction = scaled - index.astype(jnp.float32)
        low_bits = index & (lanes - 1)
        words = []
        for c in range(3):
            found = [
                jnp.take_along_axis(word_ref[c, h], low_bits, axis=1, mode="promise_in_bounds")
                for h in range(halves)
            ]
            word = found[0]
            for h in range(1, halves):
                word = jnp.where(index >= h * lanes, found[h], word)
            words.append(word)

        def blended(start, slope):
            return start.astype(jnp.float32) + fraction * slope.astype(jnp.float32)

        color = [blended(((w >> 9) & 2047) + COLOR_LEAST, w >> 20) for w in words]
        low, middle, high = words
        start = (low & 511) + ((middle & 15) << 9)
        slope = ((high << 23) >> 18) + ((middle >> 4) & 31)
        return color, blended(start, slope) * (1.0 / OPACITY_UNIT)

    return look_up


def column_differences(fields, carried_ref, first):
    chunks, lanes = fields[0].shape
    count = carried_ref.shape[0] // (chunks + 2)
    lane = lax.broadcasted_iota(jnp.int32, (chunks, lanes), 1)
    at_first, at_last = lane == 0, lane == lanes - 1
    after = [pltpu.roll(x, lanes - 1, 1) for x in fields]
    before = [pltpu.roll(x, 1, 1) for x in fields]
    for i, (right, left) in enumerate(zip(after, before), first):
        carried_ref[pl.ds(count + i, chunks, stride=count), :] = jnp.where(at_last, right, left)
    differences = []
    for i, (right, left) in enumerate(zip(after, before), first):
        further = carried_ref[pl.ds(2 * count + i, chunks, stride=count), :]
        back = carried_ref[pl.ds(i, chunks, stride=count), :]
        differences.append(jnp.where(at_last, further, right) - jnp.where(at_first, back, left))
    return differences


def depth_differences(field):
    last = len(field) - 1
    made = {}
    for k in range(last + 1):
        ends = (min(k + 1, last), max(k - 1, 0))
        if ends not in made:
            made[ends] = field[ends[0]] - field[ends[1]]
    return [made[(min(k + 1, last), max(k - 1, 0))] for k in range(last + 1)]


def shading_of(facing, squared_plus_one):
    return 0.25 + (facing * facing) * pltpu.reciprocal(squared_plus_one, approx=True)


def main_kernel(edge_rows, brick_at, light_ref, word_ref, tile_ref,
                part_ref, color_sum_ref, keep_ref, carried):
    bricks, padded_rows, depth, chunks, lanes = tile_ref.shape
    rows = padded_rows - 2
    inner_rows = [r for r in range(rows) if r not in edge_rows]
    shape = (chunks, lanes)
    look_up = table_lookup(word_ref)
    border = carried.shape[0] // (chunks + 2)
    carried[:border, :] = jnp.zeros((border, lanes), jnp.float32)
    carried[-border:, :] = jnp.zeros((border, lanes), jnp.float32)
    light = [light_ref[i] for i in range(3)]
    together = border // (rows * depth)

    def step(trip, carry):
        colors, keeps = list(carry[0]), list(carry[1])
        at = [brick_at[trip * together + u] for u in range(together)]
        fields = [[[tile_ref[b, r, k] for k in range(depth)] for r in range(padded_rows)] for b in at]
        kept = []
        for u, (b, field) in enumerate(zip(at, fields)):
            cells = [x for line in field[1:-1] for x in line]
            column = column_differences(cells, carried, u * len(cells))
            for r in range(rows):
                for k, dz in enumerate(depth_differences(field[r + 1])):
                    x = field[r + 1][k]
                    dx = column[r * depth + k]
                    color, opacity = look_up(x)
                    weight = keeps[r] * opacity
                    facing = dz * light[0] + dx * light[2]
                    squared = (dz * dz + 1.0) + dx * dx
                    if r in edge_rows:
                        values = [weight * color[c] for c in range(3)] + [facing, squared]
                        kept.append((b, edge_rows.index(r), k, values))
                    else:
                        i = inner_rows.index(r)
                        dy = field[r + 2][k] - field[r][k]
                        shaded = weight * shading_of(facing + dy * light[1], squared + dy * dy)
                        for c in range(3):
                            slot = c * len(inner_rows) + i
                            colors[slot] = colors[slot] + shaded * color[c]
                    keeps[r] = keeps[r] - weight
        for b, i, k, values in kept:
            for v, value in enumerate(values):
                part_ref[b, i, k, v] = value
        return tuple(colors), tuple(keeps)

    zero, one = jnp.zeros(shape, jnp.float32), jnp.ones(shape, jnp.float32)
    colors, keeps = lax.fori_loop(
        0, bricks // together, step, ((zero,) * (3 * len(inner_rows)), (one,) * rows))
    for i, value in enumerate(colors):
        color_sum_ref[i] = value
    for r, value in enumerate(keeps):
        keep_ref[r] = value


def finish_kernel(edge_rows, first_ref, last_ref, light_ref, tile_ref, other_ref, part_ref, color_sum_ref, keep_ref,
                  out_ref, staged):
    bricks, padded_rows, depth, chunks, lanes = tile_ref.shape
    rows = padded_rows - 2
    inner_rows = [r for r in range(rows) if r not in edge_rows]
    shape = (chunks, lanes)
    light_rows = light_ref[1]
    is_first, is_last = first_ref[...] == 1.0, last_ref[...] == 1.0

    together = 16 if bricks % 16 == 0 else 1

    def step(trip, colors):
        colors = list(colors)
        for u in range(together):
            b = trip * together + u
            for i, r in enumerate(edge_rows):
                for k in range(depth):
                    above, below = tile_ref[b, r, k], tile_ref[b, r + 2, k]
                    if r == 0:
                        above = jnp.where(is_first, other_ref[b, k], above)
                    if r == rows - 1:
                        below = jnp.where(is_last, other_ref[b, k], below)
                    dy = below - above
                    facing = part_ref[b, i, k, 3] + dy * light_rows
                    shading = shading_of(facing, part_ref[b, i, k, 4] + dy * dy)
                    for c in range(3):
                        slot = c * len(edge_rows) + i
                        colors[slot] = colors[slot] + shading * part_ref[b, i, k, c]
        return tuple(colors)

    zero = jnp.zeros(shape, jnp.float32)
    pitch = 4 * rows * ROW_STEP + 1
    edge_colors = lax.fori_loop(0, bricks // together, step, (zero,) * (3 * len(edge_rows)))
    for r in range(rows):
        for c in range(3):
            if r in edge_rows:
                value = edge_colors[c * len(edge_rows) + edge_rows.index(r)]
            else:
                value = color_sum_ref[c * len(inner_rows) + inner_rows.index(r)]
            staged[pl.ds((c * rows + r) * ROW_STEP, chunks, stride=pitch), :] = value * (1.0 / COLOR_UNIT)
        staged[pl.ds((3 * rows + r) * ROW_STEP, chunks, stride=pitch), :] = 1.0 - keep_ref[r]
    for c in range(4):
        for q in range(chunks):
            start = q * pitch + c * rows * ROW_STEP
            source = pl.ds(start, rows, stride=ROW_STEP) if rows > 1 else pl.ds(start, 1)
            out_ref[c, 0, :, q * LANES:(q + 1) * LANES] = staged[source, :]


def shards(scalar, bin_index, color_table, opacity_table, light_dir, view_order):
    depth, rows, cols = scalar.shape
    bricks, bands = lax.axis_size("gz"), lax.axis_size("gy")
    tile_rows = rows // bricks
    chunks = cols // LANES
    edge_rows = sorted({0, tile_rows - 1})
    inner_count = tile_rows - len(edge_rows)
    vmem = pl.BlockSpec(memory_space=pltpu.VMEM)
    smem = pl.BlockSpec(memory_space=pltpu.SMEM)
    params = pltpu.CompilerParams(vmem_limit_bytes=32 << 20)
    cells = bricks * depth * cols
    lines = (chunks, LANES)
    halves = (color_table.shape[1] - 1) // LANES
    together = 16 if bricks % 16 == 0 else 1
    pieces = 4 if rows % (4 * SUB) == 0 else 1
    hbm = pl.BlockSpec(memory_space=pltpu.HBM)
    given = [scalar, view_order, light_dir, color_table, opacity_table]
    sent, brick_at, words, light_rows, first, final, later = pl.pallas_call(
        functools.partial(pack_kernel, bricks),
        out_shape=[
            pltpu.VMEM((bricks, (tile_rows + 2) * depth * chunks, LANES), jnp.float32),
            pltpu.SMEM((bricks,), jnp.int32),
            jax.ShapeDtypeStruct((3, halves) + lines, jnp.int32),
            jax.ShapeDtypeStruct((3,) + lines, jnp.float32),
        ] + [jax.ShapeDtypeStruct(lines, jnp.float32)] * 3,
        in_specs=[hbm] * 5,
        out_specs=[vmem, smem] + [vmem] * 5,
        scratch_shapes=[
            pltpu.VMEM(scalar.shape, scalar.dtype),
            pltpu.VMEM((depth * chunks * (rows * ROW_STEP + 1), LANES), scalar.dtype),
            pltpu.SMEM(view_order.shape, view_order.dtype),
            pltpu.SMEM(light_dir.shape, light_dir.dtype),
            pltpu.VMEM(color_table.shape, color_table.dtype),
            pltpu.VMEM(opacity_table.shape, opacity_table.dtype),
            pltpu.SemaphoreType.DMA((pieces,)),
            pltpu.SemaphoreType.DMA((4,)),
        ],
        compiler_params=params,
        name="pack_rows",
    )(*[pltpu.with_memory_space_constraint(x, pltpu.HBM) for x in given])
    arrived = lax.all_to_all(
        sent, "gz", split_axis=0, concat_axis=0, tiled=True, axis_index_groups=[exchange_order(bricks)])
    tiles = arrived.reshape(bricks, tile_rows + 2, depth, chunks, LANES)

    last = bricks - 1
    pairs = [(g, g + 1) for g in range(bands - 1)]
    pairs += [(last * bands + g + 1, last * bands + g) for g in range(bands - 1)]
    wrapped = tiles[:, 0] * first + tiles[:, -1] * later
    other = lax.ppermute(wrapped, ("gz", "gy"), pairs)
    parts, color_sums, keeps = pl.pallas_call(
        functools.partial(main_kernel, edge_rows),
        out_shape=[
            jax.ShapeDtypeStruct((bricks, len(edge_rows), depth, 5, chunks, LANES), jnp.float32),
            jax.ShapeDtypeStruct((max(3 * inner_count, 1), chunks, LANES), jnp.float32),
            jax.ShapeDtypeStruct((tile_rows, chunks, LANES), jnp.float32),
        ],
        in_specs=[smem] + [vmem] * 3,
        out_specs=[vmem, vmem, vmem],
        scratch_shapes=[pltpu.VMEM(((chunks + 2) * (together * tile_rows * depth + 1), LANES), jnp.float32)],
        compiler_params=params,
        cost_estimate=pl.CostEstimate(
            flops=100 * cells * tile_rows, bytes_accessed=24 * cells * tile_rows, transcendentals=0),
        name="main_rows",
    )(brick_at, light_rows, words, tiles)
    return pl.pallas_call(
        functools.partial(finish_kernel, edge_rows),
        out_shape=jax.ShapeDtypeStruct((4, 1, tile_rows, cols), jnp.float32),
        in_specs=[vmem] * 8,
        out_specs=vmem,
        scratch_shapes=[pltpu.VMEM((chunks * (4 * tile_rows * ROW_STEP + 1), LANES), jnp.float32)],
        compiler_params=params,
        cost_estimate=pl.CostEstimate(
            flops=10 * cells * tile_rows, bytes_accessed=24 * cells * tile_rows, transcendentals=0),
        name="edge_rows",
    )(first, final, light_rows, tiles, other, parts, color_sums, keeps)


def solution(mesh):
    in_specs = (P("gz", "gy", None), P("gz", "gy", None), P(), P(), P(), P())
    out_specs = P(None, "gy", "gz", None)
    return jax.shard_map(shards, mesh=mesh, in_specs=in_specs, out_specs=out_specs, check_vma=False)
```

```python
import functools
import math

import jax
import jax.numpy as jnp
from jax import lax
from jax.experimental import pallas as pl
from jax.experimental.pallas import tpu as pltpu
from jax.sharding import PartitionSpec as P

SUB, LANES = 8, 128
ROW_STEP = 3
COLOR_UNIT, COLOR_LEAST, OPACITY_UNIT = 2 ** 11, 204, 2 ** 18


def exchange_orders(tiles):
    parts = 4 if tiles % 4 == 0 else 1
    size = tiles // parts
    return [
        [p * size + i for i in chips for p in range(parts)[::-1]]
        for chips in (sorted(range(size), key=lambda i: i % 2), range(size))
    ]


def of_band(even, odd):
    return jnp.where(lax.rem(lax.axis_index("gy"), 2) == 0, even, odd)


def pack_kernel(tiles, field_ref, order_ref, light_ref, color_ref, opacity_ref,
                out_ref, brick_at_ref, word_ref, light_rows_ref, first_ref, last_ref, later_ref,
                field, spread, order, light, color, opacity, sems, table_sems):
    depth, rows, cols = field_ref.shape
    chunks = cols // LANES
    pitch = rows * ROW_STEP + 1
    tile_rows = rows // tiles
    pieces = sems.shape[0]
    piece_rows = rows // pieces

    def copy_in(p):
        part = pl.ds(p * piece_rows, piece_rows)
        return pltpu.make_async_copy(field_ref.at[:, part], field.at[:, part], sems.at[p])

    table_copies = [
        pltpu.make_async_copy(source, target, table_sems.at[i])
        for i, (source, target) in enumerate(
            [(color_ref, color), (opacity_ref, opacity), (order_ref, order), (light_ref, light)])
    ]
    for copy in table_copies:
        copy.start()
    for p in range(pieces):
        copy_in(p).start()
    for copy in table_copies:
        copy.wait()
    prepare(order, light, color, opacity, brick_at_ref, word_ref, light_rows_ref, first_ref, last_ref, later_ref)
    for p in range(pieces):
        copy_in(p).wait()
        for k in range(depth):
            for row in range(p * piece_rows, (p + 1) * piece_rows, SUB):
                lines = [field[k, row:row + SUB, c * LANES:(c + 1) * LANES] for c in range(chunks)]
                for c, value in enumerate(lines):
                    spread[pl.ds((k * chunks + c) * pitch + row * ROW_STEP, SUB, stride=ROW_STEP), :] = value
    even, odd = exchange_orders(tiles)
    for t in range(tiles):
        place = of_band(even.index(t), odd.index(t))
        for i in range(tile_rows + 2):
            row = (t * tile_rows + i - 1) % rows
            for k in range(depth):
                at = (i * depth + k) * chunks
                line = spread[pl.ds(k * chunks * pitch + row * ROW_STEP, chunks, stride=pitch), :]
                out_ref[place, at:at + chunks, :] = line


def prepare(order_ref, light_ref, color_ref, opacity_ref,
            brick_at_ref, word_ref, light_rows_ref, first_ref, last_ref, later_ref):
    bins = color_ref.shape[1] - 1
    _, halves, chunks, lanes = word_ref.shape
    shape = (chunks, lanes)

    def parts(values, unit):
        scaled = (values.astype(jnp.float32) * float(unit)).astype(jnp.int32)
        return scaled[:, :bins], scaled[:, 1:] - scaled[:, :bins]

    start, slope = parts(opacity_ref[...].reshape(1, bins + 1), OPACITY_UNIT)
    pieces = [start & 511, (start >> 9) + ((slope & 31) << 4), (slope >> 5) & 511]
    start, slope = parts(color_ref[...], COLOR_UNIT)
    upper = (slope << 20) + ((start - COLOR_LEAST) << 9)
    for c in range(3):
        word = upper[c:c + 1] + pieces[c]
        for h in range(halves):
            word_ref[c, h] = jnp.broadcast_to(word[:, h * lanes:(h + 1) * lanes], shape)
    for i in range(3):
        light_rows_ref[i] = jnp.full(shape, light_ref[i], jnp.float32) * math.sqrt(0.75)
    here, last = lax.axis_index("gz"), order_ref.shape[0] - 1
    for ref, place in [(first_ref, here == 0), (last_ref, here == last), (later_ref, here != 0)]:
        ref[...] = jnp.full(shape, place.astype(jnp.float32), jnp.float32)
    even, odd = exchange_orders(order_ref.shape[0])
    for b in range(order_ref.shape[0]):
        brick_at_ref[order_ref[b]] = of_band(even.index(b), odd.index(b))


def table_lookup(word_ref):
    _, halves, _, lanes = word_ref.shape
    bins = halves * lanes

    def look_up(x):
        scaled = x * float(bins)
        index = jnp.minimum(scaled.astype(jnp.int32), bins - 1)
        fraction = scaled - index.astype(jnp.float32)
        low_bits = index & (lanes - 1)
        words = []
        for c in range(3):
            found = [
                jnp.take_along_axis(word_ref[c, h], low_bits, axis=1, mode="promise_in_bounds")
                for h in range(halves)
            ]
            word = found[0]
            for h in range(1, halves):
                word = jnp.where(index >= h * lanes, found[h], word)
            words.append(word)

        def blended(start, slope):
            return start.astype(jnp.float32) + fraction * slope.astype(jnp.float32)

        color = [blended(((w >> 9) & 2047) + COLOR_LEAST, w >> 20) for w in words]
        low, middle, high = words
        start = (low & 511) + ((middle & 15) << 9)
        slope = ((high << 23) >> 18) + ((middle >> 4) & 31)
        return color, blended(start, slope) * (1.0 / OPACITY_UNIT)

    return look_up


def column_differences(fields, carried_ref, first):
    chunks, lanes = fields[0].shape
    count = carried_ref.shape[0] // (chunks + 2)
    lane = lax.broadcasted_iota(jnp.int32, (chunks, lanes), 1)
    at_first, at_last = lane == 0, lane == lanes - 1
    after = [pltpu.roll(x, lanes - 1, 1) for x in fields]
    before = [pltpu.roll(x, 1, 1) for x in fields]
    for i, (right, left) in enumerate(zip(after, before), first):
        carried_ref[pl.ds(count + i, chunks, stride=count), :] = jnp.where(at_last, right, left)
    differences = []
    for i, (right, left) in enumerate(zip(after, before), first):
        further = carried_ref[pl.ds(2 * count + i, chunks, stride=count), :]
        back = carried_ref[pl.ds(i, chunks, stride=count), :]
        differences.append(jnp.where(at_last, further, right) - jnp.where(at_first, back, left))
    return differences


def depth_differences(field):
    last = len(field) - 1
    made = {}
    for k in range(last + 1):
        ends = (min(k + 1, last), max(k - 1, 0))
        if ends not in made:
            made[ends] = field[ends[0]] - field[ends[1]]
    return [made[(min(k + 1, last), max(k - 1, 0))] for k in range(last + 1)]


def shading_of(facing, squared_plus_one):
    return 0.25 + (facing * facing) * pltpu.reciprocal(squared_plus_one, approx=True)


def main_kernel(edge_rows, brick_at, light_ref, word_ref, tile_ref,
                part_ref, color_sum_ref, keep_ref, carried):
    bricks, padded_rows, depth, chunks, lanes = tile_ref.shape
    rows = padded_rows - 2
    inner_rows = [r for r in range(rows) if r not in edge_rows]
    shape = (chunks, lanes)
    look_up = table_lookup(word_ref)
    border = carried.shape[0] // (chunks + 2)
    carried[:border, :] = jnp.zeros((border, lanes), jnp.float32)
    carried[-border:, :] = jnp.zeros((border, lanes), jnp.float32)
    light = [light_ref[i] for i in range(3)]
    together = border // (rows * depth)

    def step(trip, carry):
        colors, keeps = list(carry[0]), list(carry[1])
        at = [brick_at[trip * together + u] for u in range(together)]
        fields = [[[tile_ref[b, r, k] for k in range(depth)] for r in range(padded_rows)] for b in at]
        kept = []
        for u, (b, field) in enumerate(zip(at, fields)):
            cells = [x for line in field[1:-1] for x in line]
            column = column_differences(cells, carried, u * len(cells))
            for r in range(rows):
                for k, dz in enumerate(depth_differences(field[r + 1])):
                    x = field[r + 1][k]
                    dx = column[r * depth + k]
                    color, opacity = look_up(x)
                    weight = keeps[r] * opacity
                    facing = dz * light[0] + dx * light[2]
                    squared = (dz * dz + 1.0) + dx * dx
                    if r in edge_rows:
                        values = [weight * color[c] for c in range(3)] + [facing, squared]
                        kept.append((b, edge_rows.index(r), k, values))
                    else:
                        i = inner_rows.index(r)
                        dy = field[r + 2][k] - field[r][k]
                        shaded = weight * shading_of(facing + dy * light[1], squared + dy * dy)
                        for c in range(3):
                            slot = c * len(inner_rows) + i
                            colors[slot] = colors[slot] + shaded * color[c]
                    keeps[r] = keeps[r] - weight
        for b, i, k, values in kept:
            for v, value in enumerate(values):
                part_ref[b, i, k, v] = value
        return tuple(colors), tuple(keeps)

    zero, one = jnp.zeros(shape, jnp.float32), jnp.ones(shape, jnp.float32)
    colors, keeps = lax.fori_loop(
        0, bricks // together, step, ((zero,) * (3 * len(inner_rows)), (one,) * rows))
    for i, value in enumerate(colors):
        color_sum_ref[i] = value
    for r, value in enumerate(keeps):
        keep_ref[r] = value


def finish_kernel(edge_rows, first_ref, last_ref, light_ref, tile_ref, other_ref, part_ref, color_sum_ref, keep_ref,
                  out_ref, staged):
    bricks, padded_rows, depth, chunks, lanes = tile_ref.shape
    rows = padded_rows - 2
    inner_rows = [r for r in range(rows) if r not in edge_rows]
    shape = (chunks, lanes)
    light_rows = light_ref[1]
    is_first, is_last = first_ref[...] == 1.0, last_ref[...] == 1.0

    even, odd = exchange_orders(bricks)
    places = [of_band(odd.index(even[b]), even.index(odd[b])) for b in range(bricks)]

    def step(colors):
        colors = list(colors)
        for b, there in enumerate(places):
            for i, r in enumerate(edge_rows):
                for k in range(depth):
                    above, below = tile_ref[b, r, k], tile_ref[b, r + 2, k]
                    if r == 0:
                        above = jnp.where(is_first, other_ref[there, k], above)
                    if r == rows - 1:
                        below = jnp.where(is_last, other_ref[there, k], below)
                    dy = below - above
                    facing = part_ref[b, i, k, 3] + dy * light_rows
                    shading = shading_of(facing, part_ref[b, i, k, 4] + dy * dy)
                    for c in range(3):
                        slot = c * len(edge_rows) + i
                        colors[slot] = colors[slot] + shading * part_ref[b, i, k, c]
        return tuple(colors)

    zero = jnp.zeros(shape, jnp.float32)
    pitch = 4 * rows * ROW_STEP + 1
    edge_colors = step((zero,) * (3 * len(edge_rows)))
    for r in range(rows):
        for c in range(3):
            if r in edge_rows:
                value = edge_colors[c * len(edge_rows) + edge_rows.index(r)]
            else:
                value = color_sum_ref[c * len(inner_rows) + inner_rows.index(r)]
            staged[pl.ds((c * rows + r) * ROW_STEP, chunks, stride=pitch), :] = value * (1.0 / COLOR_UNIT)
        staged[pl.ds((3 * rows + r) * ROW_STEP, chunks, stride=pitch), :] = 1.0 - keep_ref[r]
    for c in range(4):
        for q in range(chunks):
            start = q * pitch + c * rows * ROW_STEP
            source = pl.ds(start, rows, stride=ROW_STEP) if rows > 1 else pl.ds(start, 1)
            out_ref[c, 0, :, q * LANES:(q + 1) * LANES] = staged[source, :]


def shards(scalar, bin_index, color_table, opacity_table, light_dir, view_order):
    depth, rows, cols = scalar.shape
    bricks, bands = lax.axis_size("gz"), lax.axis_size("gy")
    tile_rows = rows // bricks
    chunks = cols // LANES
    edge_rows = sorted({0, tile_rows - 1})
    inner_count = tile_rows - len(edge_rows)
    vmem = pl.BlockSpec(memory_space=pltpu.VMEM)
    smem = pl.BlockSpec(memory_space=pltpu.SMEM)
    params = pltpu.CompilerParams(vmem_limit_bytes=32 << 20)
    cells = bricks * depth * cols
    lines = (chunks, LANES)
    halves = (color_table.shape[1] - 1) // LANES
    together = 16 if bricks % 16 == 0 else 1
    pieces = 4 if rows % (4 * SUB) == 0 else 1
    hbm = pl.BlockSpec(memory_space=pltpu.HBM)
    given = [scalar, view_order, light_dir, color_table, opacity_table]
    sent, brick_at, words, light_rows, first, final, later = pl.pallas_call(
        functools.partial(pack_kernel, bricks),
        out_shape=[
            pltpu.VMEM((bricks, (tile_rows + 2) * depth * chunks, LANES), jnp.float32),
            pltpu.SMEM((bricks,), jnp.int32),
            jax.ShapeDtypeStruct((3, halves) + lines, jnp.int32),
            jax.ShapeDtypeStruct((3,) + lines, jnp.float32),
        ] + [jax.ShapeDtypeStruct(lines, jnp.float32)] * 3,
        in_specs=[hbm] * 5,
        out_specs=[vmem, smem] + [vmem] * 5,
        scratch_shapes=[
            pltpu.VMEM(scalar.shape, scalar.dtype),
            pltpu.VMEM((depth * chunks * (rows * ROW_STEP + 1), LANES), scalar.dtype),
            pltpu.SMEM(view_order.shape, view_order.dtype),
            pltpu.SMEM(light_dir.shape, light_dir.dtype),
            pltpu.VMEM(color_table.shape, color_table.dtype),
            pltpu.VMEM(opacity_table.shape, opacity_table.dtype),
            pltpu.SemaphoreType.DMA((pieces,)),
            pltpu.SemaphoreType.DMA((4,)),
        ],
        compiler_params=params,
        name="pack_rows",
    )(*[pltpu.with_memory_space_constraint(x, pltpu.HBM) for x in given])
    orders = exchange_orders(bricks)
    groups = [[t * bands + g for t in orders[g % 2]] for g in range(bands)]
    arrived = lax.all_to_all(
        sent, ("gz", "gy"), split_axis=0, concat_axis=0, tiled=True, axis_index_groups=groups)
    tiles = arrived.reshape(bricks, tile_rows + 2, depth, chunks, LANES)

    last = bricks - 1
    pairs = [(g, g + 1) for g in range(bands - 1)]
    pairs += [(last * bands + g + 1, last * bands + g) for g in range(bands - 1)]
    wrapped = tiles[:, 0] * first + tiles[:, -1] * later
    other = lax.ppermute(wrapped, ("gz", "gy"), pairs)
    parts, color_sums, keeps = pl.pallas_call(
        functools.partial(main_kernel, edge_rows),
        out_shape=[
            jax.ShapeDtypeStruct((bricks, len(edge_rows), depth, 5, chunks, LANES), jnp.float32),
            jax.ShapeDtypeStruct((max(3 * inner_count, 1), chunks, LANES), jnp.float32),
            jax.ShapeDtypeStruct((tile_rows, chunks, LANES), jnp.float32),
        ],
        in_specs=[smem] + [vmem] * 3,
        out_specs=[vmem, vmem, vmem],
        scratch_shapes=[pltpu.VMEM(((chunks + 2) * (together * tile_rows * depth + 1), LANES), jnp.float32)],
        compiler_params=params,
        cost_estimate=pl.CostEstimate(
            flops=100 * cells * tile_rows, bytes_accessed=24 * cells * tile_rows, transcendentals=0),
        name="main_rows",
    )(brick_at, light_rows, words, tiles)
    return pl.pallas_call(
        functools.partial(finish_kernel, edge_rows),
        out_shape=jax.ShapeDtypeStruct((4, 1, tile_rows, cols), jnp.float32),
        in_specs=[vmem] * 8,
        out_specs=vmem,
        scratch_shapes=[pltpu.VMEM((chunks * (4 * tile_rows * ROW_STEP + 1), LANES), jnp.float32)],
        compiler_params=params,
        cost_estimate=pl.CostEstimate(
            flops=10 * cells * tile_rows, bytes_accessed=24 * cells * tile_rows, transcendentals=0),
        name="edge_rows",
    )(first, final, light_rows, tiles, other, parts, color_sums, keeps)


def solution(mesh):
    in_specs = (P("gz", "gy", None), P("gz", "gy", None), P(), P(), P(), P())
    out_specs = P(None, "gy", "gz", None)
    return jax.shard_map(shards, mesh=mesh, in_specs=in_specs, out_specs=out_specs, check_vma=False)
```

```python
import functools
import math

import jax
import jax.numpy as jnp
from jax import lax
from jax.experimental import pallas as pl
from jax.experimental.pallas import tpu as pltpu
from jax.sharding import PartitionSpec as P

SUB, LANES = 8, 128
ROW_STEP = 3
COLOR_UNIT, COLOR_LEAST, OPACITY_UNIT = 2 ** 11, 204, 2 ** 18


def exchange_order(tiles):
    parts = 4 if tiles % 4 == 0 else 1
    size = tiles // parts
    chips = sorted(range(size), key=lambda i: i % 2)
    return [p * size + i for i in chips for p in range(parts)[::-1]]


def pack_kernel(tiles, field_ref, order_ref, light_ref, color_ref, opacity_ref,
                out_ref, brick_at_ref, word_ref, light_rows_ref, first_ref, last_ref, later_ref,
                field, spread, order, light, color, opacity, sems, table_sems):
    depth, rows, cols = field_ref.shape
    chunks = cols // LANES
    pitch = rows * ROW_STEP + 1
    tile_rows = rows // tiles
    pieces = sems.shape[0]
    piece_rows = rows // pieces

    def copy_in(p):
        part = pl.ds(p * piece_rows, piece_rows)
        return pltpu.make_async_copy(field_ref.at[:, part], field.at[:, part], sems.at[p])

    table_copies = [
        pltpu.make_async_copy(source, target, table_sems.at[i])
        for i, (source, target) in enumerate(
            [(color_ref, color), (opacity_ref, opacity), (order_ref, order), (light_ref, light)])
    ]
    for p in range(pieces):
        copy_in(p).start()
    for copy in table_copies:
        copy.start()
    for p in range(pieces):
        copy_in(p).wait()
        for k in range(depth):
            for row in range(p * piece_rows, (p + 1) * piece_rows, SUB):
                lines = [field[k, row:row + SUB, c * LANES:(c + 1) * LANES] for c in range(chunks)]
                for c, value in enumerate(lines):
                    spread[pl.ds((k * chunks + c) * pitch + row * ROW_STEP, SUB, stride=ROW_STEP), :] = value
        if p == 0:
            for copy in table_copies:
                copy.wait()
            prepare(order, light, color, opacity, brick_at_ref, word_ref, light_rows_ref, first_ref, last_ref, later_ref)
    for place, t in enumerate(exchange_order(tiles)):
        for i in range(tile_rows + 2):
            row = (t * tile_rows + i - 1) % rows
            for k in range(depth):
                at = (i * depth + k) * chunks
                line = spread[pl.ds(k * chunks * pitch + row * ROW_STEP, chunks, stride=pitch), :]
                out_ref[place, at:at + chunks, :] = line


def prepare(order_ref, light_ref, color_ref, opacity_ref,
            brick_at_ref, word_ref, light_rows_ref, first_ref, last_ref, later_ref):
    bins = color_ref.shape[1] - 1
    _, halves, chunks, lanes = word_ref.shape
    shape = (chunks, lanes)

    def parts(values, unit):
        scaled = (values.astype(jnp.float32) * float(unit)).astype(jnp.int32)
        return scaled[:, :bins], scaled[:, 1:] - scaled[:, :bins]

    start, slope = parts(opacity_ref[...].reshape(1, bins + 1), OPACITY_UNIT)
    pieces = [start & 511, (start >> 9) + ((slope & 31) << 4), (slope >> 5) & 511]
    start, slope = parts(color_ref[...], COLOR_UNIT)
    upper = (slope << 20) + ((start - COLOR_LEAST) << 9)
    for c in range(3):
        word = upper[c:c + 1] + pieces[c]
        for h in range(halves):
            word_ref[c, h] = jnp.broadcast_to(word[:, h * lanes:(h + 1) * lanes], shape)
    for i in range(3):
        light_rows_ref[i] = jnp.full(shape, light_ref[i], jnp.float32) * math.sqrt(0.75)
    here, last = lax.axis_index("gz"), order_ref.shape[0] - 1
    for ref, place in [(first_ref, here == 0), (last_ref, here == last), (later_ref, here != 0)]:
        ref[...] = jnp.full(shape, place.astype(jnp.float32), jnp.float32)
    for place, b in enumerate(exchange_order(order_ref.shape[0])):
        brick_at_ref[order_ref[b]] = place


def table_lookup(word_ref):
    _, halves, _, lanes = word_ref.shape
    bins = halves * lanes

    def look_up(x):
        scaled = x * float(bins)
        index = jnp.minimum(scaled.astype(jnp.int32), bins - 1)
        fraction = scaled - index.astype(jnp.float32)
        low_bits = index & (lanes - 1)
        words = []
        for c in range(3):
            found = [
                jnp.take_along_axis(word_ref[c, h], low_bits, axis=1, mode="promise_in_bounds")
                for h in range(halves)
            ]
            word = found[0]
            for h in range(1, halves):
                word = jnp.where(index >= h * lanes, found[h], word)
            words.append(word)

        def blended(start, slope):
            return start.astype(jnp.float32) + fraction * slope.astype(jnp.float32)

        color = [blended(((w >> 9) & 2047) + COLOR_LEAST, w >> 20) for w in words]
        low, middle, high = words
        start = (low & 511) + ((middle & 15) << 9)
        slope = ((high << 23) >> 18) + ((middle >> 4) & 31)
        return color, blended(start, slope) * (1.0 / OPACITY_UNIT)

    return look_up


def column_differences(fields, carried_ref, first):
    chunks, lanes = fields[0].shape
    count = carried_ref.shape[0] // (chunks + 2)
    lane = lax.broadcasted_iota(jnp.int32, (chunks, lanes), 1)
    at_first, at_last = lane == 0, lane == lanes - 1
    after = [pltpu.roll(x, lanes - 1, 1) for x in fields]
    before = [pltpu.roll(x, 1, 1) for x in fields]
    for i, (right, left) in enumerate(zip(after, before), first):
        carried_ref[pl.ds(count + i, chunks, stride=count), :] = jnp.where(at_last, right, left)
    differences = []
    for i, (right, left) in enumerate(zip(after, before), first):
        further = carried_ref[pl.ds(2 * count + i, chunks, stride=count), :]
        back = carried_ref[pl.ds(i, chunks, stride=count), :]
        differences.append(jnp.where(at_last, further, right) - jnp.where(at_first, back, left))
    return differences


def depth_differences(field):
    last = len(field) - 1
    made = {}
    for k in range(last + 1):
        ends = (min(k + 1, last), max(k - 1, 0))
        if ends not in made:
            made[ends] = field[ends[0]] - field[ends[1]]
    return [made[(min(k + 1, last), max(k - 1, 0))] for k in range(last + 1)]


def shading_of(facing, squared_plus_one):
    return 0.25 + (facing * facing) * pltpu.reciprocal(squared_plus_one, approx=True)


def main_kernel(edge_rows, brick_at, light_ref, word_ref, tile_ref,
                part_ref, color_sum_ref, keep_ref, carried):
    bricks, padded_rows, depth, chunks, lanes = tile_ref.shape
    rows = padded_rows - 2
    inner_rows = [r for r in range(rows) if r not in edge_rows]
    shape = (chunks, lanes)
    look_up = table_lookup(word_ref)
    border = carried.shape[0] // (chunks + 2)
    carried[:border, :] = jnp.zeros((border, lanes), jnp.float32)
    carried[-border:, :] = jnp.zeros((border, lanes), jnp.float32)
    light = [light_ref[i] for i in range(3)]
    together = border // (rows * depth)

    def step(trip, carry):
        colors, keeps = list(carry[0]), list(carry[1])
        at = [brick_at[trip * together + u] for u in range(together)]
        fields = [[[tile_ref[b, r, k] for k in range(depth)] for r in range(padded_rows)] for b in at]
        kept = []
        for u, (b, field) in enumerate(zip(at, fields)):
            cells = [x for line in field[1:-1] for x in line]
            column = column_differences(cells, carried, u * len(cells))
            for r in range(rows):
                for k, dz in enumerate(depth_differences(field[r + 1])):
                    x = field[r + 1][k]
                    dx = column[r * depth + k]
                    color, opacity = look_up(x)
                    weight = keeps[r] * opacity
                    facing = dz * light[0] + dx * light[2]
                    squared = (dz * dz + 1.0) + dx * dx
                    if r in edge_rows:
                        values = [weight * color[c] for c in range(3)] + [facing, squared]
                        kept.append((b, edge_rows.index(r), k, values))
                    else:
                        i = inner_rows.index(r)
                        dy = field[r + 2][k] - field[r][k]
                        shaded = weight * shading_of(facing + dy * light[1], squared + dy * dy)
                        for c in range(3):
                            slot = c * len(inner_rows) + i
                            colors[slot] = colors[slot] + shaded * color[c]
                    keeps[r] = keeps[r] - weight
        for b, i, k, values in kept:
            for v, value in enumerate(values):
                part_ref[b, i, k, v] = value
        return tuple(colors), tuple(keeps)

    zero, one = jnp.zeros(shape, jnp.float32), jnp.ones(shape, jnp.float32)
    colors, keeps = lax.fori_loop(
        0, bricks // together, step, ((zero,) * (3 * len(inner_rows)), (one,) * rows))
    for i, value in enumerate(colors):
        color_sum_ref[i] = value
    for r, value in enumerate(keeps):
        keep_ref[r] = value


def finish_kernel(edge_rows, first_ref, last_ref, light_ref, tile_ref, other_ref, part_ref, color_sum_ref, keep_ref,
                  out_ref, staged):
    bricks, padded_rows, depth, chunks, lanes = tile_ref.shape
    rows = padded_rows - 2
    inner_rows = [r for r in range(rows) if r not in edge_rows]
    shape = (chunks, lanes)
    light_rows = light_ref[1]
    is_first, is_last = first_ref[...] == 1.0, last_ref[...] == 1.0

    together = 16 if bricks % 16 == 0 else 1

    def step(trip, colors):
        colors = list(colors)
        for u in range(together):
            b = trip * together + u
            for i, r in enumerate(edge_rows):
                for k in range(depth):
                    above, below = tile_ref[b, r, k], tile_ref[b, r + 2, k]
                    if r == 0:
                        above = jnp.where(is_first, other_ref[b, k], above)
                    if r == rows - 1:
                        below = jnp.where(is_last, other_ref[b, k], below)
                    dy = below - above
                    facing = part_ref[b, i, k, 3] + dy * light_rows
                    shading = shading_of(facing, part_ref[b, i, k, 4] + dy * dy)
                    for c in range(3):
                        slot = c * len(edge_rows) + i
                        colors[slot] = colors[slot] + shading * part_ref[b, i, k, c]
        return tuple(colors)

    zero = jnp.zeros(shape, jnp.float32)
    pitch = 4 * rows * ROW_STEP + 1
    edge_colors = lax.fori_loop(0, bricks // together, step, (zero,) * (3 * len(edge_rows)))
    for r in range(rows):
        for c in range(3):
            if r in edge_rows:
                value = edge_colors[c * len(edge_rows) + edge_rows.index(r)]
            else:
                value = color_sum_ref[c * len(inner_rows) + inner_rows.index(r)]
            staged[pl.ds((c * rows + r) * ROW_STEP, chunks, stride=pitch), :] = value * (1.0 / COLOR_UNIT)
        staged[pl.ds((3 * rows + r) * ROW_STEP, chunks, stride=pitch), :] = 1.0 - keep_ref[r]
    for c in range(4):
        for q in range(chunks):
            start = q * pitch + c * rows * ROW_STEP
            source = pl.ds(start, rows, stride=ROW_STEP) if rows > 1 else pl.ds(start, 1)
            out_ref[c, 0, :, q * LANES:(q + 1) * LANES] = staged[source, :]


def shards(scalar, bin_index, color_table, opacity_table, light_dir, view_order):
    depth, rows, cols = scalar.shape
    bricks, bands = lax.axis_size("gz"), lax.axis_size("gy")
    tile_rows = rows // bricks
    chunks = cols // LANES
    edge_rows = sorted({0, tile_rows - 1})
    inner_count = tile_rows - len(edge_rows)
    vmem = pl.BlockSpec(memory_space=pltpu.VMEM)
    smem = pl.BlockSpec(memory_space=pltpu.SMEM)
    params = pltpu.CompilerParams(vmem_limit_bytes=32 << 20)
    cells = bricks * depth * cols
    lines = (chunks, LANES)
    halves = (color_table.shape[1] - 1) // LANES
    together = 16 if bricks % 16 == 0 else 1
    pieces = 4 if rows % (4 * SUB) == 0 else 1
    hbm = pl.BlockSpec(memory_space=pltpu.HBM)
    given = [scalar, view_order, light_dir, color_table, opacity_table]
    sent, brick_at, words, light_rows, first, final, later = pl.pallas_call(
        functools.partial(pack_kernel, bricks),
        out_shape=[
            pltpu.VMEM((bricks, (tile_rows + 2) * depth * chunks, LANES), jnp.float32),
            pltpu.SMEM((bricks,), jnp.int32),
            jax.ShapeDtypeStruct((3, halves) + lines, jnp.int32),
            jax.ShapeDtypeStruct((3,) + lines, jnp.float32),
        ] + [jax.ShapeDtypeStruct(lines, jnp.float32)] * 3,
        in_specs=[hbm] * 5,
        out_specs=[vmem, smem] + [vmem] * 5,
        scratch_shapes=[
            pltpu.VMEM(scalar.shape, scalar.dtype),
            pltpu.VMEM((depth * chunks * (rows * ROW_STEP + 1), LANES), scalar.dtype),
            pltpu.SMEM(view_order.shape, view_order.dtype),
            pltpu.SMEM(light_dir.shape, light_dir.dtype),
            pltpu.VMEM(color_table.shape, color_table.dtype),
            pltpu.VMEM(opacity_table.shape, opacity_table.dtype),
            pltpu.SemaphoreType.DMA((pieces,)),
            pltpu.SemaphoreType.DMA((4,)),
        ],
        compiler_params=params,
        name="pack_rows",
    )(*[pltpu.with_memory_space_constraint(x, pltpu.HBM) for x in given])
    arrived = lax.all_to_all(
        sent, "gz", split_axis=0, concat_axis=0, tiled=True, axis_index_groups=[exchange_order(bricks)])
    tiles = arrived.reshape(bricks, tile_rows + 2, depth, chunks, LANES)

    last = bricks - 1
    pairs = [(g, g + 1) for g in range(bands - 1)]
    pairs += [(last * bands + g + 1, last * bands + g) for g in range(bands - 1)]
    wrapped = tiles[:, 0] * first + tiles[:, -1] * later
    other = lax.ppermute(wrapped, ("gz", "gy"), pairs)
    parts, color_sums, keeps = pl.pallas_call(
        functools.partial(main_kernel, edge_rows),
        out_shape=[
            jax.ShapeDtypeStruct((bricks, len(edge_rows), depth, 5, chunks, LANES), jnp.float32),
            jax.ShapeDtypeStruct((max(3 * inner_count, 1), chunks, LANES), jnp.float32),
            jax.ShapeDtypeStruct((tile_rows, chunks, LANES), jnp.float32),
        ],
        in_specs=[smem] + [vmem] * 3,
        out_specs=[vmem, vmem, vmem],
        scratch_shapes=[pltpu.VMEM(((chunks + 2) * (together * tile_rows * depth + 1), LANES), jnp.float32)],
        compiler_params=params,
        cost_estimate=pl.CostEstimate(
            flops=100 * cells * tile_rows, bytes_accessed=24 * cells * tile_rows, transcendentals=0),
        name="main_rows",
    )(brick_at, light_rows, words, tiles)
    return pl.pallas_call(
        functools.partial(finish_kernel, edge_rows),
        out_shape=jax.ShapeDtypeStruct((4, 1, tile_rows, cols), jnp.float32),
        in_specs=[vmem] * 8,
        out_specs=vmem,
        scratch_shapes=[pltpu.VMEM((chunks * (4 * tile_rows * ROW_STEP + 1), LANES), jnp.float32)],
        compiler_params=params,
        cost_estimate=pl.CostEstimate(
            flops=10 * cells * tile_rows, bytes_accessed=24 * cells * tile_rows, transcendentals=0),
        name="edge_rows",
    )(first, final, light_rows, tiles, other, parts, color_sums, keeps)


def solution(mesh):
    in_specs = (P("gz", "gy", None), P("gz", "gy", None), P(), P(), P(), P())
    out_specs = P(None, "gy", "gz", None)
    return jax.shard_map(shards, mesh=mesh, in_specs=in_specs, out_specs=out_specs, check_vma=False)
```

```python
import functools
import math

import jax
import jax.numpy as jnp
from jax import lax
from jax.experimental import pallas as pl
from jax.experimental.pallas import tpu as pltpu
from jax.sharding import PartitionSpec as P

SUB, LANES = 8, 128
ROW_STEP = 3
COLOR_UNIT, COLOR_LEAST, OPACITY_UNIT = 2 ** 11, 204, 2 ** 18


def exchange_order(tiles):
    parts = 4 if tiles % 4 == 0 else 1
    size = tiles // parts
    chips = sorted(range(size), key=lambda i: i % 2)
    return [p * size + i for i in chips for p in range(parts)[::-1]]


def pack_kernel(tiles, bands, field_ref, order_ref, light_ref, color_ref, opacity_ref,
                out_ref, brick_at_ref, word_ref, light_rows_ref, first_ref, last_ref, later_ref, inside_ref,
                field, spread, order, light, color, opacity, sems, table_sems):
    depth, rows, cols = field_ref.shape
    chunks = cols // LANES
    pitch = rows * ROW_STEP + 1
    tile_rows = rows // tiles
    pieces = sems.shape[0]
    piece_rows = rows // pieces

    def copy_in(p):
        part = pl.ds(p * piece_rows, piece_rows)
        return pltpu.make_async_copy(field_ref.at[:, part], field.at[:, part], sems.at[p])

    table_copies = [
        pltpu.make_async_copy(source, target, table_sems.at[i])
        for i, (source, target) in enumerate(
            [(color_ref, color), (opacity_ref, opacity), (order_ref, order), (light_ref, light)])
    ]
    for copy in table_copies:
        copy.start()
    for p in range(pieces):
        copy_in(p).start()
    for copy in table_copies:
        copy.wait()
    prepare(bands, order, light, color, opacity, brick_at_ref, word_ref, light_rows_ref,
            first_ref, last_ref, later_ref, inside_ref)
    for p in range(pieces):
        copy_in(p).wait()
        for k in range(depth):
            for row in range(p * piece_rows, (p + 1) * piece_rows, SUB):
                lines = [field[k, row:row + SUB, c * LANES:(c + 1) * LANES] for c in range(chunks)]
                for c, value in enumerate(lines):
                    spread[pl.ds((k * chunks + c) * pitch + row * ROW_STEP, SUB, stride=ROW_STEP), :] = value
    for place, t in enumerate(exchange_order(tiles)):
        for i in range(tile_rows + 2):
            row = (t * tile_rows + i - 1) % rows
            for k in range(depth):
                at = (i * depth + k) * chunks
                line = spread[pl.ds(k * chunks * pitch + row * ROW_STEP, chunks, stride=pitch), :]
                out_ref[place, at:at + chunks, :] = line


def prepare(bands, order_ref, light_ref, color_ref, opacity_ref,
            brick_at_ref, word_ref, light_rows_ref, first_ref, last_ref, later_ref, inside_ref):
    bins = color_ref.shape[1] - 1
    _, halves, chunks, lanes = word_ref.shape
    shape = (chunks, lanes)

    def parts(values, unit):
        scaled = (values.astype(jnp.float32) * float(unit)).astype(jnp.int32)
        return scaled[:, :bins], scaled[:, 1:] - scaled[:, :bins]

    start, slope = parts(opacity_ref[...].reshape(1, bins + 1), OPACITY_UNIT)
    pieces = [start & 511, (start >> 9) + ((slope & 31) << 4), (slope >> 5) & 511]
    start, slope = parts(color_ref[...], COLOR_UNIT)
    upper = (slope << 20) + ((start - COLOR_LEAST) << 9)
    for c in range(3):
        word = upper[c:c + 1] + pieces[c]
        for h in range(halves):
            word_ref[c, h] = jnp.broadcast_to(word[:, h * lanes:(h + 1) * lanes], shape)
    for i in range(3):
        light_rows_ref[i] = jnp.full(shape, light_ref[i], jnp.float32) * math.sqrt(0.75)
    here, last = lax.axis_index("gz"), order_ref.shape[0] - 1
    band = lax.axis_index("gy")
    inside = jnp.where(here == 0, band > 0, band < bands - 1)
    for ref, place in [
        (first_ref, here == 0), (last_ref, here == last), (later_ref, here != 0), (inside_ref, inside)]:
        ref[...] = jnp.full(shape, place.astype(jnp.float32), jnp.float32)
    for place, b in enumerate(exchange_order(order_ref.shape[0])):
        brick_at_ref[order_ref[b]] = place


def table_lookup(word_ref):
    _, halves, _, lanes = word_ref.shape
    bins = halves * lanes

    def look_up(x):
        scaled = x * float(bins)
        index = jnp.minimum(scaled.astype(jnp.int32), bins - 1)
        fraction = scaled - index.astype(jnp.float32)
        low_bits = index & (lanes - 1)
        words = []
        for c in range(3):
            found = [
                jnp.take_along_axis(word_ref[c, h], low_bits, axis=1, mode="promise_in_bounds")
                for h in range(halves)
            ]
            word = found[0]
            for h in range(1, halves):
                word = jnp.where(index >= h * lanes, found[h], word)
            words.append(word)

        def blended(start, slope):
            return start.astype(jnp.float32) + fraction * slope.astype(jnp.float32)

        color = [blended(((w >> 9) & 2047) + COLOR_LEAST, w >> 20) for w in words]
        low, middle, high = words
        start = (low & 511) + ((middle & 15) << 9)
        slope = ((high << 23) >> 18) + ((middle >> 4) & 31)
        return color, blended(start, slope) * (1.0 / OPACITY_UNIT)

    return look_up


def column_differences(fields, carried_ref, first):
    chunks, lanes = fields[0].shape
    count = carried_ref.shape[0] // (chunks + 2)
    lane = lax.broadcasted_iota(jnp.int32, (chunks, lanes), 1)
    at_first, at_last = lane == 0, lane == lanes - 1
    after = [pltpu.roll(x, lanes - 1, 1) for x in fields]
    before = [pltpu.roll(x, 1, 1) for x in fields]
    for i, (right, left) in enumerate(zip(after, before), first):
        carried_ref[pl.ds(count + i, chunks, stride=count), :] = jnp.where(at_last, right, left)
    differences = []
    for i, (right, left) in enumerate(zip(after, before), first):
        further = carried_ref[pl.ds(2 * count + i, chunks, stride=count), :]
        back = carried_ref[pl.ds(i, chunks, stride=count), :]
        differences.append(jnp.where(at_last, further, right) - jnp.where(at_first, back, left))
    return differences


def depth_differences(field):
    last = len(field) - 1
    made = {}
    for k in range(last + 1):
        ends = (min(k + 1, last), max(k - 1, 0))
        if ends not in made:
            made[ends] = field[ends[0]] - field[ends[1]]
    return [made[(min(k + 1, last), max(k - 1, 0))] for k in range(last + 1)]


def shading_of(facing, squared_plus_one):
    return 0.25 + (facing * facing) * pltpu.reciprocal(squared_plus_one, approx=True)


def main_kernel(edge_rows, brick_at, light_ref, word_ref, tile_ref,
                part_ref, color_sum_ref, keep_ref, carried):
    bricks, padded_rows, depth, chunks, lanes = tile_ref.shape
    rows = padded_rows - 2
    inner_rows = [r for r in range(rows) if r not in edge_rows]
    shape = (chunks, lanes)
    look_up = table_lookup(word_ref)
    border = carried.shape[0] // (chunks + 2)
    carried[:border, :] = jnp.zeros((border, lanes), jnp.float32)
    carried[-border:, :] = jnp.zeros((border, lanes), jnp.float32)
    light = [light_ref[i] for i in range(3)]
    together = border // (rows * depth)

    def step(trip, carry):
        colors, keeps = list(carry[0]), list(carry[1])
        at = [brick_at[trip * together + u] for u in range(together)]
        fields = [[[tile_ref[b, r, k] for k in range(depth)] for r in range(padded_rows)] for b in at]
        kept = []
        for u, (b, field) in enumerate(zip(at, fields)):
            cells = [x for line in field[1:-1] for x in line]
            column = column_differences(cells, carried, u * len(cells))
            for r in range(rows):
                for k, dz in enumerate(depth_differences(field[r + 1])):
                    x = field[r + 1][k]
                    dx = column[r * depth + k]
                    color, opacity = look_up(x)
                    weight = keeps[r] * opacity
                    facing = dz * light[0] + dx * light[2]
                    squared = (dz * dz + 1.0) + dx * dx
                    if r in edge_rows:
                        values = [weight * color[c] for c in range(3)] + [facing, squared]
                        kept.append((b, edge_rows.index(r), k, values))
                    else:
                        i = inner_rows.index(r)
                        dy = field[r + 2][k] - field[r][k]
                        shaded = weight * shading_of(facing + dy * light[1], squared + dy * dy)
                        for c in range(3):
                            slot = c * len(inner_rows) + i
                            colors[slot] = colors[slot] + shaded * color[c]
                    keeps[r] = keeps[r] - weight
        for b, i, k, values in kept:
            for v, value in enumerate(values):
                part_ref[b, i, k, v] = value
        return tuple(colors), tuple(keeps)

    zero, one = jnp.zeros(shape, jnp.float32), jnp.ones(shape, jnp.float32)
    colors, keeps = lax.fori_loop(
        0, bricks // together, step, ((zero,) * (3 * len(inner_rows)), (one,) * rows))
    for i, value in enumerate(colors):
        color_sum_ref[i] = value
    for r, value in enumerate(keeps):
        keep_ref[r] = value


def finish_kernel(edge_rows, first_ref, last_ref, inside_ref, light_ref, tile_ref, other_ref, part_ref, color_sum_ref, keep_ref,
                  out_ref, staged):
    bricks, padded_rows, depth, chunks, lanes = tile_ref.shape
    rows = padded_rows - 2
    inner_rows = [r for r in range(rows) if r not in edge_rows]
    shape = (chunks, lanes)
    light_rows = light_ref[1]
    is_first, is_last = first_ref[...] == 1.0, last_ref[...] == 1.0
    inside = inside_ref[...]

    together = 16 if bricks % 16 == 0 else 1

    def step(trip, colors):
        colors = list(colors)
        for u in range(together):
            b = trip * together + u
            for i, r in enumerate(edge_rows):
                for k in range(depth):
                    above, below = tile_ref[b, r, k], tile_ref[b, r + 2, k]
                    if r == 0:
                        above = jnp.where(is_first, other_ref[b, k] * inside, above)
                    if r == rows - 1:
                        below = jnp.where(is_last, other_ref[b, k] * inside, below)
                    dy = below - above
                    facing = part_ref[b, i, k, 3] + dy * light_rows
                    shading = shading_of(facing, part_ref[b, i, k, 4] + dy * dy)
                    for c in range(3):
                        slot = c * len(edge_rows) + i
                        colors[slot] = colors[slot] + shading * part_ref[b, i, k, c]
        return tuple(colors)

    zero = jnp.zeros(shape, jnp.float32)
    pitch = 4 * rows * ROW_STEP + 1
    edge_colors = lax.fori_loop(0, bricks // together, step, (zero,) * (3 * len(edge_rows)))
    for r in range(rows):
        for c in range(3):
            if r in edge_rows:
                value = edge_colors[c * len(edge_rows) + edge_rows.index(r)]
            else:
                value = color_sum_ref[c * len(inner_rows) + inner_rows.index(r)]
            staged[pl.ds((c * rows + r) * ROW_STEP, chunks, stride=pitch), :] = value * (1.0 / COLOR_UNIT)
        staged[pl.ds((3 * rows + r) * ROW_STEP, chunks, stride=pitch), :] = 1.0 - keep_ref[r]
    for c in range(4):
        for q in range(chunks):
            start = q * pitch + c * rows * ROW_STEP
            source = pl.ds(start, rows, stride=ROW_STEP) if rows > 1 else pl.ds(start, 1)
            out_ref[c, 0, :, q * LANES:(q + 1) * LANES] = staged[source, :]


def shards(scalar, bin_index, color_table, opacity_table, light_dir, view_order):
    depth, rows, cols = scalar.shape
    bricks, bands = lax.axis_size("gz"), lax.axis_size("gy")
    tile_rows = rows // bricks
    chunks = cols // LANES
    edge_rows = sorted({0, tile_rows - 1})
    inner_count = tile_rows - len(edge_rows)
    vmem = pl.BlockSpec(memory_space=pltpu.VMEM)
    smem = pl.BlockSpec(memory_space=pltpu.SMEM)
    params = pltpu.CompilerParams(vmem_limit_bytes=32 << 20)
    cells = bricks * depth * cols
    lines = (chunks, LANES)
    halves = (color_table.shape[1] - 1) // LANES
    together = 16 if bricks % 16 == 0 else 1
    pieces = 4 if rows % (4 * SUB) == 0 else 1
    hbm = pl.BlockSpec(memory_space=pltpu.HBM)
    given = [scalar, view_order, light_dir, color_table, opacity_table]
    sent, brick_at, words, light_rows, first, final, later, inside = pl.pallas_call(
        functools.partial(pack_kernel, bricks, bands),
        out_shape=[
            pltpu.VMEM((bricks, (tile_rows + 2) * depth * chunks, LANES), jnp.float32),
            pltpu.SMEM((bricks,), jnp.int32),
            jax.ShapeDtypeStruct((3, halves) + lines, jnp.int32),
            jax.ShapeDtypeStruct((3,) + lines, jnp.float32),
        ] + [jax.ShapeDtypeStruct(lines, jnp.float32)] * 4,
        in_specs=[hbm] * 5,
        out_specs=[vmem, smem] + [vmem] * 6,
        scratch_shapes=[
            pltpu.VMEM(scalar.shape, scalar.dtype),
            pltpu.VMEM((depth * chunks * (rows * ROW_STEP + 1), LANES), scalar.dtype),
            pltpu.SMEM(view_order.shape, view_order.dtype),
            pltpu.SMEM(light_dir.shape, light_dir.dtype),
            pltpu.VMEM(color_table.shape, color_table.dtype),
            pltpu.VMEM(opacity_table.shape, opacity_table.dtype),
            pltpu.SemaphoreType.DMA((pieces,)),
            pltpu.SemaphoreType.DMA((4,)),
        ],
        compiler_params=params,
        name="pack_rows",
    )(*[pltpu.with_memory_space_constraint(x, pltpu.HBM) for x in given])
    arrived = lax.all_to_all(
        sent, "gz", split_axis=0, concat_axis=0, tiled=True, axis_index_groups=[exchange_order(bricks)])
    tiles = arrived.reshape(bricks, tile_rows + 2, depth, chunks, LANES)

    last = bricks - 1
    pairs = [(g, g + 1) for g in range(bands - 1)]
    pairs += [(last * bands + g + 1, last * bands + g) for g in range(bands - 1)]
    if bands == 2:
        pairs += [(j, i) for i, j in pairs]
    wrapped = tiles[:, 0] * first + tiles[:, -1] * later
    other = lax.ppermute(wrapped, ("gz", "gy"), pairs)
    parts, color_sums, keeps = pl.pallas_call(
        functools.partial(main_kernel, edge_rows),
        out_shape=[
            jax.ShapeDtypeStruct((bricks, len(edge_rows), depth, 5, chunks, LANES), jnp.float32),
            jax.ShapeDtypeStruct((max(3 * inner_count, 1), chunks, LANES), jnp.float32),
            jax.ShapeDtypeStruct((tile_rows, chunks, LANES), jnp.float32),
        ],
        in_specs=[smem] + [vmem] * 3,
        out_specs=[vmem, vmem, vmem],
        scratch_shapes=[pltpu.VMEM(((chunks + 2) * (together * tile_rows * depth + 1), LANES), jnp.float32)],
        compiler_params=params,
        cost_estimate=pl.CostEstimate(
            flops=100 * cells * tile_rows, bytes_accessed=24 * cells * tile_rows, transcendentals=0),
        name="main_rows",
    )(brick_at, light_rows, words, tiles)
    return pl.pallas_call(
        functools.partial(finish_kernel, edge_rows),
        out_shape=jax.ShapeDtypeStruct((4, 1, tile_rows, cols), jnp.float32),
        in_specs=[vmem] * 9,
        out_specs=vmem,
        scratch_shapes=[pltpu.VMEM((chunks * (4 * tile_rows * ROW_STEP + 1), LANES), jnp.float32)],
        compiler_params=params,
        cost_estimate=pl.CostEstimate(
            flops=10 * cells * tile_rows, bytes_accessed=24 * cells * tile_rows, transcendentals=0),
        name="edge_rows",
    )(first, final, inside, light_rows, tiles, other, parts, color_sums, keeps)


def solution(mesh):
    in_specs = (P("gz", "gy", None), P("gz", "gy", None), P(), P(), P(), P())
    out_specs = P(None, "gy", "gz", None)
    return jax.shard_map(shards, mesh=mesh, in_specs=in_specs, out_specs=out_specs, check_vma=False)
```

```python
import functools
import math

import jax
import jax.numpy as jnp
from jax import lax
from jax.experimental import pallas as pl
from jax.experimental.pallas import tpu as pltpu
from jax.sharding import PartitionSpec as P

SUB, LANES = 8, 128
ROW_STEP = 3
COLOR_UNIT, COLOR_LEAST, OPACITY_UNIT = 2 ** 11, 204, 2 ** 18


def exchange_order(tiles):
    parts = 4 if tiles % 4 == 0 else 1
    size = tiles // parts
    chips = sorted(range(size), key=lambda i: i % 2)
    return [p * size + i for i in chips for p in range(parts)[::-1]]


def pack_kernel(tiles, field_ref, order_ref, light_ref, color_ref, opacity_ref,
                out_ref, brick_at_ref, word_ref, light_rows_ref, first_ref, last_ref, later_ref,
                field, spread, order, light, color, opacity, sems, table_sems):
    depth, rows, cols = field_ref.shape
    chunks = cols // LANES
    pitch = rows * ROW_STEP + 1
    tile_rows = rows // tiles
    pieces = sems.shape[0]
    piece_rows = rows // pieces

    def copy_in(p):
        part = pl.ds(p * piece_rows, piece_rows)
        return pltpu.make_async_copy(field_ref.at[:, part], field.at[:, part], sems.at[p])

    table_copies = [
        pltpu.make_async_copy(source, target, table_sems.at[i])
        for i, (source, target) in enumerate(
            [(color_ref, color), (opacity_ref, opacity), (order_ref, order), (light_ref, light)])
    ]
    for copy in table_copies:
        copy.start()
    for p in range(pieces):
        copy_in(p).start()
    for copy in table_copies:
        copy.wait()
    prepare(order, light, color, opacity, brick_at_ref, word_ref, light_rows_ref, first_ref, last_ref, later_ref)
    for p in range(pieces):
        copy_in(p).wait()
        for k in range(depth):
            for row in range(p * piece_rows, (p + 1) * piece_rows, SUB):
                lines = [field[k, row:row + SUB, c * LANES:(c + 1) * LANES] for c in range(chunks)]
                for c, value in enumerate(lines):
                    spread[pl.ds((k * chunks + c) * pitch + row * ROW_STEP, SUB, stride=ROW_STEP), :] = value
    for place, t in enumerate(exchange_order(tiles)):
        for i in range(tile_rows + 2):
            row = (t * tile_rows + i - 1) % rows
            for k in range(depth):
                at = (i * depth + k) * chunks
                line = spread[pl.ds(k * chunks * pitch + row * ROW_STEP, chunks, stride=pitch), :]
                out_ref[place, at:at + chunks, :] = line


def prepare(order_ref, light_ref, color_ref, opacity_ref,
            brick_at_ref, word_ref, light_rows_ref, first_ref, last_ref, later_ref):
    bins = color_ref.shape[1] - 1
    _, halves, chunks, lanes = word_ref.shape
    shape = (chunks, lanes)

    def parts(values, unit):
        scaled = (values.astype(jnp.float32) * float(unit)).astype(jnp.int32)
        return scaled[:, :bins], scaled[:, 1:] - scaled[:, :bins]

    start, slope = parts(opacity_ref[...].reshape(1, bins + 1), OPACITY_UNIT)
    pieces = [start & 511, (start >> 9) + ((slope & 31) << 4), (slope >> 5) & 511]
    start, slope = parts(color_ref[...], COLOR_UNIT)
    upper = (slope << 20) + ((start - COLOR_LEAST) << 9)
    for c in range(3):
        word = upper[c:c + 1] + pieces[c]
        for h in range(halves):
            word_ref[c, h] = jnp.broadcast_to(word[:, h * lanes:(h + 1) * lanes], shape)
    for i in range(3):
        light_rows_ref[i] = jnp.full(shape, light_ref[i], jnp.float32) * math.sqrt(0.75)
    here, last = lax.axis_index("gz"), order_ref.shape[0] - 1
    for ref, place in [(first_ref, here == 0), (last_ref, here == last), (later_ref, here != 0)]:
        ref[...] = jnp.full(shape, place.astype(jnp.float32), jnp.float32)
    for place, b in enumerate(exchange_order(order_ref.shape[0])):
        brick_at_ref[order_ref[b]] = place


def table_lookup(word_ref):
    _, halves, _, lanes = word_ref.shape
    bins = halves * lanes

    def look_up(x):
        scaled = x * float(bins)
        index = jnp.minimum(scaled.astype(jnp.int32), bins - 1)
        fraction = scaled - index.astype(jnp.float32)
        low_bits = index & (lanes - 1)
        words = []
        for c in range(3):
            found = [
                jnp.take_along_axis(word_ref[c, h], low_bits, axis=1, mode="promise_in_bounds")
                for h in range(halves)
            ]
            word = found[0]
            for h in range(1, halves):
                word = jnp.where(index >= h * lanes, found[h], word)
            words.append(word)

        def blended(start, slope):
            return start.astype(jnp.float32) + fraction * slope.astype(jnp.float32)

        color = [blended(((w >> 9) & 2047) + COLOR_LEAST, w >> 20) for w in words]
        low, middle, high = words
        start = (low & 511) + ((middle & 15) << 9)
        slope = ((high << 23) >> 18) + ((middle >> 4) & 31)
        return color, blended(start, slope) * (1.0 / OPACITY_UNIT)

    return look_up


def column_differences(fields, carried_ref, first):
    chunks, lanes = fields[0].shape
    count = carried_ref.shape[0] // (chunks + 2)
    lane = lax.broadcasted_iota(jnp.int32, (chunks, lanes), 1)
    at_first, at_last = lane == 0, lane == lanes - 1
    after = [pltpu.roll(x, lanes - 1, 1) for x in fields]
    before = [pltpu.roll(x, 1, 1) for x in fields]
    for i, (right, left) in enumerate(zip(after, before), first):
        carried_ref[pl.ds(count + i, chunks, stride=count), :] = jnp.where(at_last, right, left)
    differences = []
    for i, (right, left) in enumerate(zip(after, before), first):
        further = carried_ref[pl.ds(2 * count + i, chunks, stride=count), :]
        back = carried_ref[pl.ds(i, chunks, stride=count), :]
        differences.append(jnp.where(at_last, further, right) - jnp.where(at_first, back, left))
    return differences


def depth_differences(field):
    last = len(field) - 1
    made = {}
    for k in range(last + 1):
        ends = (min(k + 1, last), max(k - 1, 0))
        if ends not in made:
            made[ends] = field[ends[0]] - field[ends[1]]
    return [made[(min(k + 1, last), max(k - 1, 0))] for k in range(last + 1)]


def shading_of(facing, squared_plus_one):
    return 0.25 + (facing * facing) * pltpu.reciprocal(squared_plus_one, approx=True)


def main_kernel(edge_rows, brick_at, light_ref, word_ref, tile_ref,
                part_ref, color_sum_ref, keep_ref, carried):
    bricks, padded_rows, depth, chunks, lanes = tile_ref.shape
    rows = padded_rows - 2
    inner_rows = [r for r in range(rows) if r not in edge_rows]
    shape = (chunks, lanes)
    look_up = table_lookup(word_ref)
    border = carried.shape[0] // (chunks + 2)
    carried[:border, :] = jnp.zeros((border, lanes), jnp.float32)
    carried[-border:, :] = jnp.zeros((border, lanes), jnp.float32)
    light = [light_ref[i] for i in range(3)]
    together = border // (rows * depth)

    def step(trip, carry):
        colors, keeps = list(carry[0]), list(carry[1])
        at = [brick_at[trip * together + u] for u in range(together)]

        def loaded(b):
            return [[tile_ref[b, r, k] for k in range(depth)] for r in range(padded_rows)]

        following = loaded(at[0])
        for u, b in enumerate(at):
            field, kept = following, []
            following = loaded(at[u + 1]) if u + 1 < together else None
            cells = [x for line in field[1:-1] for x in line]
            column = column_differences(cells, carried, u * len(cells))
            for r in range(rows):
                for k, dz in enumerate(depth_differences(field[r + 1])):
                    x = field[r + 1][k]
                    dx = column[r * depth + k]
                    color, opacity = look_up(x)
                    weight = keeps[r] * opacity
                    facing = dz * light[0] + dx * light[2]
                    squared = (dz * dz + 1.0) + dx * dx
                    if r in edge_rows:
                        values = [weight * color[c] for c in range(3)] + [facing, squared]
                        kept.append((edge_rows.index(r), k, values))
                    else:
                        i = inner_rows.index(r)
                        dy = field[r + 2][k] - field[r][k]
                        shaded = weight * shading_of(facing + dy * light[1], squared + dy * dy)
                        for c in range(3):
                            slot = c * len(inner_rows) + i
                            colors[slot] = colors[slot] + shaded * color[c]
                    keeps[r] = keeps[r] - weight
            for i, k, values in kept:
                for v, value in enumerate(values):
                    part_ref[b, i, k, v] = value
        return tuple(colors), tuple(keeps)

    zero, one = jnp.zeros(shape, jnp.float32), jnp.ones(shape, jnp.float32)
    colors, keeps = lax.fori_loop(
        0, bricks // together, step, ((zero,) * (3 * len(inner_rows)), (one,) * rows))
    for i, value in enumerate(colors):
        color_sum_ref[i] = value
    for r, value in enumerate(keeps):
        keep_ref[r] = value


def finish_kernel(edge_rows, first_ref, last_ref, light_ref, tile_ref, other_ref, part_ref, color_sum_ref, keep_ref,
                  out_ref, staged):
    bricks, padded_rows, depth, chunks, lanes = tile_ref.shape
    rows = padded_rows - 2
    inner_rows = [r for r in range(rows) if r not in edge_rows]
    shape = (chunks, lanes)
    light_rows = light_ref[1]
    is_first, is_last = first_ref[...] == 1.0, last_ref[...] == 1.0

    together = 16 if bricks % 16 == 0 else 1

    def step(trip, colors):
        colors = list(colors)
        for u in range(together):
            b = trip * together + u
            for i, r in enumerate(edge_rows):
                for k in range(depth):
                    above, below = tile_ref[b, r, k], tile_ref[b, r + 2, k]
                    if r == 0:
                        above = jnp.where(is_first, other_ref[b, k], above)
                    if r == rows - 1:
                        below = jnp.where(is_last, other_ref[b, k], below)
                    dy = below - above
                    facing = part_ref[b, i, k, 3] + dy * light_rows
                    shading = shading_of(facing, part_ref[b, i, k, 4] + dy * dy)
                    for c in range(3):
                        slot = c * len(edge_rows) + i
                        colors[slot] = colors[slot] + shading * part_ref[b, i, k, c]
        return tuple(colors)

    zero = jnp.zeros(shape, jnp.float32)
    pitch = 4 * rows * ROW_STEP + 1
    edge_colors = lax.fori_loop(0, bricks // together, step, (zero,) * (3 * len(edge_rows)))
    for r in range(rows):
        for c in range(3):
            if r in edge_rows:
                value = edge_colors[c * len(edge_rows) + edge_rows.index(r)]
            else:
                value = color_sum_ref[c * len(inner_rows) + inner_rows.index(r)]
            staged[pl.ds((c * rows + r) * ROW_STEP, chunks, stride=pitch), :] = value * (1.0 / COLOR_UNIT)
        staged[pl.ds((3 * rows + r) * ROW_STEP, chunks, stride=pitch), :] = 1.0 - keep_ref[r]
    for c in range(4):
        for q in range(chunks):
            start = q * pitch + c * rows * ROW_STEP
            source = pl.ds(start, rows, stride=ROW_STEP) if rows > 1 else pl.ds(start, 1)
            out_ref[c, 0, :, q * LANES:(q + 1) * LANES] = staged[source, :]


def shards(scalar, bin_index, color_table, opacity_table, light_dir, view_order):
    depth, rows, cols = scalar.shape
    bricks, bands = lax.axis_size("gz"), lax.axis_size("gy")
    tile_rows = rows // bricks
    chunks = cols // LANES
    edge_rows = sorted({0, tile_rows - 1})
    inner_count = tile_rows - len(edge_rows)
    vmem = pl.BlockSpec(memory_space=pltpu.VMEM)
    smem = pl.BlockSpec(memory_space=pltpu.SMEM)
    params = pltpu.CompilerParams(vmem_limit_bytes=32 << 20)
    cells = bricks * depth * cols
    lines = (chunks, LANES)
    halves = (color_table.shape[1] - 1) // LANES
    together = 16 if bricks % 16 == 0 else 1
    pieces = 4 if rows % (4 * SUB) == 0 else 1
    hbm = pl.BlockSpec(memory_space=pltpu.HBM)
    given = [scalar, view_order, light_dir, color_table, opacity_table]
    sent, brick_at, words, light_rows, first, final, later = pl.pallas_call(
        functools.partial(pack_kernel, bricks),
        out_shape=[
            pltpu.VMEM((bricks, (tile_rows + 2) * depth * chunks, LANES), jnp.float32),
            pltpu.SMEM((bricks,), jnp.int32),
            jax.ShapeDtypeStruct((3, halves) + lines, jnp.int32),
            jax.ShapeDtypeStruct((3,) + lines, jnp.float32),
        ] + [jax.ShapeDtypeStruct(lines, jnp.float32)] * 3,
        in_specs=[hbm] * 5,
        out_specs=[vmem, smem] + [vmem] * 5,
        scratch_shapes=[
            pltpu.VMEM(scalar.shape, scalar.dtype),
            pltpu.VMEM((depth * chunks * (rows * ROW_STEP + 1), LANES), scalar.dtype),
            pltpu.SMEM(view_order.shape, view_order.dtype),
            pltpu.SMEM(light_dir.shape, light_dir.dtype),
            pltpu.VMEM(color_table.shape, color_table.dtype),
            pltpu.VMEM(opacity_table.shape, opacity_table.dtype),
            pltpu.SemaphoreType.DMA((pieces,)),
            pltpu.SemaphoreType.DMA((4,)),
        ],
        compiler_params=params,
        name="pack_rows",
    )(*[pltpu.with_memory_space_constraint(x, pltpu.HBM) for x in given])
    arrived = lax.all_to_all(
        sent, "gz", split_axis=0, concat_axis=0, tiled=True, axis_index_groups=[exchange_order(bricks)])
    tiles = arrived.reshape(bricks, tile_rows + 2, depth, chunks, LANES)

    last = bricks - 1
    pairs = [(g, g + 1) for g in range(bands - 1)]
    pairs += [(last * bands + g + 1, last * bands + g) for g in range(bands - 1)]
    wrapped = tiles[:, 0] * first + tiles[:, -1] * later
    other = lax.ppermute(wrapped, ("gz", "gy"), pairs)
    parts, color_sums, keeps = pl.pallas_call(
        functools.partial(main_kernel, edge_rows),
        out_shape=[
            jax.ShapeDtypeStruct((bricks, len(edge_rows), depth, 5, chunks, LANES), jnp.float32),
            jax.ShapeDtypeStruct((max(3 * inner_count, 1), chunks, LANES), jnp.float32),
            jax.ShapeDtypeStruct((tile_rows, chunks, LANES), jnp.float32),
        ],
        in_specs=[smem] + [vmem] * 3,
        out_specs=[vmem, vmem, vmem],
        scratch_shapes=[pltpu.VMEM(((chunks + 2) * (together * tile_rows * depth + 1), LANES), jnp.float32)],
        compiler_params=params,
        cost_estimate=pl.CostEstimate(
            flops=100 * cells * tile_rows, bytes_accessed=24 * cells * tile_rows, transcendentals=0),
        name="main_rows",
    )(brick_at, light_rows, words, tiles)
    return pl.pallas_call(
        functools.partial(finish_kernel, edge_rows),
        out_shape=jax.ShapeDtypeStruct((4, 1, tile_rows, cols), jnp.float32),
        in_specs=[vmem] * 8,
        out_specs=vmem,
        scratch_shapes=[pltpu.VMEM((chunks * (4 * tile_rows * ROW_STEP + 1), LANES), jnp.float32)],
        compiler_params=params,
        cost_estimate=pl.CostEstimate(
            flops=10 * cells * tile_rows, bytes_accessed=24 * cells * tile_rows, transcendentals=0),
        name="edge_rows",
    )(first, final, light_rows, tiles, other, parts, color_sums, keeps)


def solution(mesh):
    in_specs = (P("gz", "gy", None), P("gz", "gy", None), P(), P(), P(), P())
    out_specs = P(None, "gy", "gz", None)
    return jax.shard_map(shards, mesh=mesh, in_specs=in_specs, out_specs=out_specs, check_vma=False)
```

```python
import functools
import math

import jax
import jax.numpy as jnp
from jax import lax
from jax.experimental import pallas as pl
from jax.experimental.pallas import tpu as pltpu
from jax.sharding import PartitionSpec as P

SUB, LANES = 8, 128
ROW_STEP = 3
COLOR_UNIT, COLOR_LEAST, OPACITY_UNIT = 2 ** 11, 204, 2 ** 18


def exchange_order(tiles):
    parts = 4 if tiles % 4 == 0 else 1
    size = tiles // parts
    chips = sorted(range(size), key=lambda i: i % 2)
    return [p * size + i for i in chips for p in range(parts)[::-1]]


def pack_kernel(tiles, field_ref, order_ref, light_ref, color_ref, opacity_ref,
                out_ref, brick_at_ref, word_ref, light_rows_ref, first_ref, last_ref, later_ref,
                field, spread, order, light, color, opacity, sems, table_sems):
    depth, rows, cols = field_ref.shape
    chunks = cols // LANES
    pitch = rows * ROW_STEP + 1
    tile_rows = rows // tiles
    pieces = sems.shape[0]
    piece_rows = rows // pieces

    def copy_in(p):
        part = pl.ds(p * piece_rows, piece_rows)
        return pltpu.make_async_copy(field_ref.at[:, part], field.at[:, part], sems.at[p])

    table_copies = [
        pltpu.make_async_copy(source, target, table_sems.at[i])
        for i, (source, target) in enumerate(
            [(color_ref, color), (opacity_ref, opacity), (order_ref, order), (light_ref, light)])
    ]
    for copy in table_copies:
        copy.start()
    for p in range(pieces):
        copy_in(p).start()
    for p in range(pieces):
        if p == pieces - 1:
            for copy in table_copies:
                copy.wait()
            prepare(order, light, color, opacity, brick_at_ref, word_ref, light_rows_ref, first_ref, last_ref, later_ref)
        copy_in(p).wait()
        for k in range(depth):
            for row in range(p * piece_rows, (p + 1) * piece_rows, SUB):
                lines = [field[k, row:row + SUB, c * LANES:(c + 1) * LANES] for c in range(chunks)]
                for c, value in enumerate(lines):
                    spread[pl.ds((k * chunks + c) * pitch + row * ROW_STEP, SUB, stride=ROW_STEP), :] = value
    for place, t in enumerate(exchange_order(tiles)):
        for i in range(tile_rows + 2):
            row = (t * tile_rows + i - 1) % rows
            for k in range(depth):
                at = (i * depth + k) * chunks
                line = spread[pl.ds(k * chunks * pitch + row * ROW_STEP, chunks, stride=pitch), :]
                out_ref[place, at:at + chunks, :] = line


def prepare(order_ref, light_ref, color_ref, opacity_ref,
            brick_at_ref, word_ref, light_rows_ref, first_ref, last_ref, later_ref):
    bins = color_ref.shape[1] - 1
    _, halves, chunks, lanes = word_ref.shape
    shape = (chunks, lanes)

    def parts(values, unit):
        scaled = (values.astype(jnp.float32) * float(unit)).astype(jnp.int32)
        return scaled[:, :bins], scaled[:, 1:] - scaled[:, :bins]

    start, slope = parts(opacity_ref[...].reshape(1, bins + 1), OPACITY_UNIT)
    pieces = [start & 511, (start >> 9) + ((slope & 31) << 4), (slope >> 5) & 511]
    start, slope = parts(color_ref[...], COLOR_UNIT)
    upper = (slope << 20) + ((start - COLOR_LEAST) << 9)
    for c in range(3):
        word = upper[c:c + 1] + pieces[c]
        for h in range(halves):
            word_ref[c, h] = jnp.broadcast_to(word[:, h * lanes:(h + 1) * lanes], shape)
    for i in range(3):
        light_rows_ref[i] = jnp.full(shape, light_ref[i], jnp.float32) * math.sqrt(0.75)
    here, last = lax.axis_index("gz"), order_ref.shape[0] - 1
    for ref, place in [(first_ref, here == 0), (last_ref, here == last), (later_ref, here != 0)]:
        ref[...] = jnp.full(shape, place.astype(jnp.float32), jnp.float32)
    for place, b in enumerate(exchange_order(order_ref.shape[0])):
        brick_at_ref[order_ref[b]] = place


def table_lookup(word_ref):
    _, halves, _, lanes = word_ref.shape
    bins = halves * lanes

    def look_up(x):
        scaled = x * float(bins)
        index = jnp.minimum(scaled.astype(jnp.int32), bins - 1)
        fraction = scaled - index.astype(jnp.float32)
        low_bits = index & (lanes - 1)
        words = []
        for c in range(3):
            found = [
                jnp.take_along_axis(word_ref[c, h], low_bits, axis=1, mode="promise_in_bounds")
                for h in range(halves)
            ]
            word = found[0]
            for h in range(1, halves):
                word = jnp.where(index >= h * lanes, found[h], word)
            words.append(word)

        def blended(start, slope):
            return start.astype(jnp.float32) + fraction * slope.astype(jnp.float32)

        color = [blended(((w >> 9) & 2047) + COLOR_LEAST, w >> 20) for w in words]
        low, middle, high = words
        start = (low & 511) + ((middle & 15) << 9)
        slope = ((high << 23) >> 18) + ((middle >> 4) & 31)
        return color, blended(start, slope) * (1.0 / OPACITY_UNIT)

    return look_up


def column_differences(fields, carried_ref, first):
    chunks, lanes = fields[0].shape
    count = carried_ref.shape[0] // (chunks + 2)
    lane = lax.broadcasted_iota(jnp.int32, (chunks, lanes), 1)
    at_first, at_last = lane == 0, lane == lanes - 1
    after = [pltpu.roll(x, lanes - 1, 1) for x in fields]
    before = [pltpu.roll(x, 1, 1) for x in fields]
    for i, (right, left) in enumerate(zip(after, before), first):
        carried_ref[pl.ds(count + i, chunks, stride=count), :] = jnp.where(at_last, right, left)
    differences = []
    for i, (right, left) in enumerate(zip(after, before), first):
        further = carried_ref[pl.ds(2 * count + i, chunks, stride=count), :]
        back = carried_ref[pl.ds(i, chunks, stride=count), :]
        differences.append(jnp.where(at_last, further, right) - jnp.where(at_first, back, left))
    return differences


def depth_differences(field):
    last = len(field) - 1
    made = {}
    for k in range(last + 1):
        ends = (min(k + 1, last), max(k - 1, 0))
        if ends not in made:
            made[ends] = field[ends[0]] - field[ends[1]]
    return [made[(min(k + 1, last), max(k - 1, 0))] for k in range(last + 1)]


def shading_of(facing, squared_plus_one):
    return 0.25 + (facing * facing) * pltpu.reciprocal(squared_plus_one, approx=True)


def main_kernel(edge_rows, brick_at, light_ref, word_ref, tile_ref,
                part_ref, color_sum_ref, keep_ref, carried):
    bricks, padded_rows, depth, chunks, lanes = tile_ref.shape
    rows = padded_rows - 2
    inner_rows = [r for r in range(rows) if r not in edge_rows]
    shape = (chunks, lanes)
    look_up = table_lookup(word_ref)
    border = carried.shape[0] // (chunks + 2)
    carried[:border, :] = jnp.zeros((border, lanes), jnp.float32)
    carried[-border:, :] = jnp.zeros((border, lanes), jnp.float32)
    light = [light_ref[i] for i in range(3)]
    together = border // (rows * depth)

    def step(trip, carry):
        colors, keeps = list(carry[0]), list(carry[1])
        at = [brick_at[trip * together + u] for u in range(together)]
        fields = [[[tile_ref[b, r, k] for k in range(depth)] for r in range(padded_rows)] for b in at]
        kept = []
        for u, (b, field) in enumerate(zip(at, fields)):
            cells = [x for line in field[1:-1] for x in line]
            column = column_differences(cells, carried, u * len(cells))
            for r in range(rows):
                for k, dz in enumerate(depth_differences(field[r + 1])):
                    x = field[r + 1][k]
                    dx = column[r * depth + k]
                    color, opacity = look_up(x)
                    weight = keeps[r] * opacity
                    facing = dz * light[0] + dx * light[2]
                    squared = (dz * dz + 1.0) + dx * dx
                    if r in edge_rows:
                        values = [weight * color[c] for c in range(3)] + [facing, squared]
                        kept.append((b, edge_rows.index(r), k, values))
                    else:
                        i = inner_rows.index(r)
                        dy = field[r + 2][k] - field[r][k]
                        shaded = weight * shading_of(facing + dy * light[1], squared + dy * dy)
                        for c in range(3):
                            slot = c * len(inner_rows) + i
                            colors[slot] = colors[slot] + shaded * color[c]
                    keeps[r] = keeps[r] - weight
        for b, i, k, values in kept:
            for v, value in enumerate(values):
                part_ref[b, i, k, v] = value
        return tuple(colors), tuple(keeps)

    zero, one = jnp.zeros(shape, jnp.float32), jnp.ones(shape, jnp.float32)
    colors, keeps = lax.fori_loop(
        0, bricks // together, step, ((zero,) * (3 * len(inner_rows)), (one,) * rows))
    for i, value in enumerate(colors):
        color_sum_ref[i] = value
    for r, value in enumerate(keeps):
        keep_ref[r] = value


def finish_kernel(edge_rows, first_ref, last_ref, light_ref, tile_ref, other_ref, part_ref, color_sum_ref, keep_ref,
                  out_ref, staged):
    bricks, padded_rows, depth, chunks, lanes = tile_ref.shape
    rows = padded_rows - 2
    inner_rows = [r for r in range(rows) if r not in edge_rows]
    shape = (chunks, lanes)
    light_rows = light_ref[1]
    is_first, is_last = first_ref[...] == 1.0, last_ref[...] == 1.0

    together = 16 if bricks % 16 == 0 else 1

    def step(trip, colors):
        colors = list(colors)
        for u in range(together):
            b = trip * together + u
            for i, r in enumerate(edge_rows):
                for k in range(depth):
                    above, below = tile_ref[b, r, k], tile_ref[b, r + 2, k]
                    if r == 0:
                        above = jnp.where(is_first, other_ref[b, k], above)
                    if r == rows - 1:
                        below = jnp.where(is_last, other_ref[b, k], below)
                    dy = below - above
                    facing = part_ref[b, i, k, 3] + dy * light_rows
                    shading = shading_of(facing, part_ref[b, i, k, 4] + dy * dy)
                    for c in range(3):
                        slot = c * len(edge_rows) + i
                        colors[slot] = colors[slot] + shading * part_ref[b, i, k, c]
        return tuple(colors)

    zero = jnp.zeros(shape, jnp.float32)
    pitch = 4 * rows * ROW_STEP + 1
    edge_colors = lax.fori_loop(0, bricks // together, step, (zero,) * (3 * len(edge_rows)))
    for r in range(rows):
        for c in range(3):
            if r in edge_rows:
                value = edge_colors[c * len(edge_rows) + edge_rows.index(r)]
            else:
                value = color_sum_ref[c * len(inner_rows) + inner_rows.index(r)]
            staged[pl.ds((c * rows + r) * ROW_STEP, chunks, stride=pitch), :] = value * (1.0 / COLOR_UNIT)
        staged[pl.ds((3 * rows + r) * ROW_STEP, chunks, stride=pitch), :] = 1.0 - keep_ref[r]
    for c in range(4):
        for q in range(chunks):
            start = q * pitch + c * rows * ROW_STEP
            source = pl.ds(start, rows, stride=ROW_STEP) if rows > 1 else pl.ds(start, 1)
            out_ref[c, 0, :, q * LANES:(q + 1) * LANES] = staged[source, :]


def shards(scalar, bin_index, color_table, opacity_table, light_dir, view_order):
    depth, rows, cols = scalar.shape
    bricks, bands = lax.axis_size("gz"), lax.axis_size("gy")
    tile_rows = rows // bricks
    chunks = cols // LANES
    edge_rows = sorted({0, tile_rows - 1})
    inner_count = tile_rows - len(edge_rows)
    vmem = pl.BlockSpec(memory_space=pltpu.VMEM)
    smem = pl.BlockSpec(memory_space=pltpu.SMEM)
    params = pltpu.CompilerParams(vmem_limit_bytes=32 << 20)
    cells = bricks * depth * cols
    lines = (chunks, LANES)
    halves = (color_table.shape[1] - 1) // LANES
    together = 16 if bricks % 16 == 0 else 1
    pieces = 4 if rows % (4 * SUB) == 0 else 1
    hbm = pl.BlockSpec(memory_space=pltpu.HBM)
    given = [scalar, view_order, light_dir, color_table, opacity_table]
    sent, brick_at, words, light_rows, first, final, later = pl.pallas_call(
        functools.partial(pack_kernel, bricks),
        out_shape=[
            pltpu.VMEM((bricks, (tile_rows + 2) * depth * chunks, LANES), jnp.float32),
            pltpu.SMEM((bricks,), jnp.int32),
            jax.ShapeDtypeStruct((3, halves) + lines, jnp.int32),
            jax.ShapeDtypeStruct((3,) + lines, jnp.float32),
        ] + [jax.ShapeDtypeStruct(lines, jnp.float32)] * 3,
        in_specs=[hbm] * 5,
        out_specs=[vmem, smem] + [vmem] * 5,
        scratch_shapes=[
            pltpu.VMEM(scalar.shape, scalar.dtype),
            pltpu.VMEM((depth * chunks * (rows * ROW_STEP + 1), LANES), scalar.dtype),
            pltpu.SMEM(view_order.shape, view_order.dtype),
            pltpu.SMEM(light_dir.shape, light_dir.dtype),
            pltpu.VMEM(color_table.shape, color_table.dtype),
            pltpu.VMEM(opacity_table.shape, opacity_table.dtype),
            pltpu.SemaphoreType.DMA((pieces,)),
            pltpu.SemaphoreType.DMA((4,)),
        ],
        compiler_params=params,
        name="pack_rows",
    )(*[pltpu.with_memory_space_constraint(x, pltpu.HBM) for x in given])
    arrived = lax.all_to_all(
        sent, "gz", split_axis=0, concat_axis=0, tiled=True, axis_index_groups=[exchange_order(bricks)])
    tiles = arrived.reshape(bricks, tile_rows + 2, depth, chunks, LANES)

    last = bricks - 1
    pairs = [(g, g + 1) for g in range(bands - 1)]
    pairs += [(last * bands + g + 1, last * bands + g) for g in range(bands - 1)]
    wrapped = tiles[:, 0] * first + tiles[:, -1] * later
    other = lax.ppermute(wrapped, ("gz", "gy"), pairs)
    parts, color_sums, keeps = pl.pallas_call(
        functools.partial(main_kernel, edge_rows),
        out_shape=[
            jax.ShapeDtypeStruct((bricks, len(edge_rows), depth, 5, chunks, LANES), jnp.float32),
            jax.ShapeDtypeStruct((max(3 * inner_count, 1), chunks, LANES), jnp.float32),
            jax.ShapeDtypeStruct((tile_rows, chunks, LANES), jnp.float32),
        ],
        in_specs=[smem] + [vmem] * 3,
        out_specs=[vmem, vmem, vmem],
        scratch_shapes=[pltpu.VMEM(((chunks + 2) * (together * tile_rows * depth + 1), LANES), jnp.float32)],
        compiler_params=params,
        cost_estimate=pl.CostEstimate(
            flops=100 * cells * tile_rows, bytes_accessed=24 * cells * tile_rows, transcendentals=0),
        name="main_rows",
    )(brick_at, light_rows, words, tiles)
    return pl.pallas_call(
        functools.partial(finish_kernel, edge_rows),
        out_shape=jax.ShapeDtypeStruct((4, 1, tile_rows, cols), jnp.float32),
        in_specs=[vmem] * 8,
        out_specs=vmem,
        scratch_shapes=[pltpu.VMEM((chunks * (4 * tile_rows * ROW_STEP + 1), LANES), jnp.float32)],
        compiler_params=params,
        cost_estimate=pl.CostEstimate(
            flops=10 * cells * tile_rows, bytes_accessed=24 * cells * tile_rows, transcendentals=0),
        name="edge_rows",
    )(first, final, light_rows, tiles, other, parts, color_sums, keeps)


def solution(mesh):
    in_specs = (P("gz", "gy", None), P("gz", "gy", None), P(), P(), P(), P())
    out_specs = P(None, "gy", "gz", None)
    return jax.shard_map(shards, mesh=mesh, in_specs=in_specs, out_specs=out_specs, check_vma=False)
```

```python
import functools
import math

import jax
import jax.numpy as jnp
from jax import lax
from jax.experimental import pallas as pl
from jax.experimental.pallas import tpu as pltpu
from jax.sharding import PartitionSpec as P

SUB, LANES = 8, 128
ROW_STEP = 3
COLOR_UNIT, COLOR_LEAST, OPACITY_UNIT = 2 ** 11, 204, 2 ** 18


def exchange_order(tiles):
    parts = 4 if tiles % 4 == 0 else 1
    size = tiles // parts
    chips = sorted(range(size), key=lambda i: i % 2)
    return [p * size + i for i in chips for p in range(parts)[::-1]]


def pack_kernel(tiles, field_ref, order_ref, light_ref, color_ref, opacity_ref,
                out_ref, brick_at_ref, word_ref, light_rows_ref, first_ref, last_ref, later_ref,
                field, spread, order, light, color, opacity, sems, table_sems):
    depth, rows, cols = field_ref.shape
    chunks = cols // LANES
    pitch = rows * ROW_STEP + 1
    tile_rows = rows // tiles
    pieces = sems.shape[0]
    piece_rows = rows // pieces

    def copy_in(p):
        part = pl.ds(p * piece_rows, piece_rows)
        return pltpu.make_async_copy(field_ref.at[:, part], field.at[:, part], sems.at[p])

    table_copies = [
        pltpu.make_async_copy(source, target, table_sems.at[i])
        for i, (source, target) in enumerate(
            [(color_ref, color), (opacity_ref, opacity), (order_ref, order), (light_ref, light)])
    ]
    for copy in table_copies:
        copy.start()
    for p in range(pieces):
        copy_in(p).start()
    for copy in table_copies:
        copy.wait()
    prepare(order, light, color, opacity, brick_at_ref, word_ref, light_rows_ref, first_ref, last_ref, later_ref)
    for p in range(pieces):
        copy_in(p).wait()
        for k in range(depth):
            for row in range(p * piece_rows, (p + 1) * piece_rows, SUB):
                lines = [field[k, row:row + SUB, c * LANES:(c + 1) * LANES] for c in range(chunks)]
                for c, value in enumerate(lines):
                    spread[pl.ds((k * chunks + c) * pitch + row * ROW_STEP, SUB, stride=ROW_STEP), :] = value
    for place, t in enumerate(exchange_order(tiles)):
        for i in range(tile_rows + 2):
            row = (t * tile_rows + i - 1) % rows
            for k in range(depth):
                at = (i * depth + k) * chunks
                line = spread[pl.ds(k * chunks * pitch + row * ROW_STEP, chunks, stride=pitch), :]
                out_ref[place, at:at + chunks, :] = line


def prepare(order_ref, light_ref, color_ref, opacity_ref,
            brick_at_ref, word_ref, light_rows_ref, first_ref, last_ref, later_ref):
    bins = color_ref.shape[1] - 1
    _, halves, chunks, lanes = word_ref.shape
    shape = (chunks, lanes)

    def parts(values, unit):
        scaled = (values.astype(jnp.float32) * float(unit)).astype(jnp.int32)
        return scaled[:, :bins], scaled[:, 1:] - scaled[:, :bins]

    start, slope = parts(opacity_ref[...].reshape(1, bins + 1), OPACITY_UNIT)
    pieces = [start & 511, (start >> 9) + ((slope & 31) << 4), (slope >> 5) & 511]
    start, slope = parts(color_ref[...], COLOR_UNIT)
    upper = (slope << 20) + ((start - COLOR_LEAST) << 9)
    for c in range(3):
        word = upper[c:c + 1] + pieces[c]
        for h in range(halves):
            word_ref[c, h] = jnp.broadcast_to(word[:, h * lanes:(h + 1) * lanes], shape)
    for i in range(3):
        light_rows_ref[i] = jnp.full(shape, light_ref[i], jnp.float32) * math.sqrt(0.75)
    here, last = lax.axis_index("gz"), order_ref.shape[0] - 1
    for ref, place in [(first_ref, here == 0), (last_ref, here == last), (later_ref, here != 0)]:
        ref[...] = jnp.full(shape, place.astype(jnp.float32), jnp.float32)
    for place, b in enumerate(exchange_order(order_ref.shape[0])):
        brick_at_ref[order_ref[b]] = place


def table_lookup(word_ref):
    _, halves, _, lanes = word_ref.shape
    bins = halves * lanes

    def look_up(x):
        scaled = x * float(bins)
        index = jnp.minimum(scaled.astype(jnp.int32), bins - 1)
        fraction = scaled - index.astype(jnp.float32)
        low_bits = index & (lanes - 1)
        words = []
        for c in range(3):
            found = [
                jnp.take_along_axis(word_ref[c, h], low_bits, axis=1, mode="promise_in_bounds")
                for h in range(halves)
            ]
            word = found[0]
            for h in range(1, halves):
                word = jnp.where(index >= h * lanes, found[h], word)
            words.append(word)

        def blended(start, slope):
            return start.astype(jnp.float32) + fraction * slope.astype(jnp.float32)

        color = [blended(((w >> 9) & 2047) + COLOR_LEAST, w >> 20) for w in words]
        low, middle, high = words
        start = (low & 511) + ((middle & 15) << 9)
        slope = ((high << 23) >> 18) + ((middle >> 4) & 31)
        return color, blended(start, slope) * (1.0 / OPACITY_UNIT)

    return look_up


def column_differences(fields, carried_ref, first):
    chunks, lanes = fields[0].shape
    count = carried_ref.shape[0] // (chunks + 2)
    lane = lax.broadcasted_iota(jnp.int32, (chunks, lanes), 1)
    at_first, at_last = lane == 0, lane == lanes - 1
    after = [pltpu.roll(x, lanes - 1, 1) for x in fields]
    before = [pltpu.roll(x, 1, 1) for x in fields]
    for i, (right, left) in enumerate(zip(after, before), first):
        carried_ref[pl.ds(count + i, chunks, stride=count), :] = jnp.where(at_last, right, left)
    differences = []
    for i, (right, left) in enumerate(zip(after, before), first):
        further = carried_ref[pl.ds(2 * count + i, chunks, stride=count), :]
        back = carried_ref[pl.ds(i, chunks, stride=count), :]
        differences.append(jnp.where(at_last, further, right) - jnp.where(at_first, back, left))
    return differences


def depth_differences(field):
    last = len(field) - 1
    made = {}
    for k in range(last + 1):
        ends = (min(k + 1, last), max(k - 1, 0))
        if ends not in made:
            made[ends] = field[ends[0]] - field[ends[1]]
    return [made[(min(k + 1, last), max(k - 1, 0))] for k in range(last + 1)]


def shading_of(facing, squared_plus_one):
    return 0.25 + (facing * facing) * pltpu.reciprocal(squared_plus_one, approx=True)


def main_kernel(edge_rows, brick_at, light_ref, word_ref, tile_ref,
                part_ref, color_sum_ref, keep_ref, carried):
    bricks, padded_rows, depth, chunks, lanes = tile_ref.shape
    rows = padded_rows - 2
    inner_rows = [r for r in range(rows) if r not in edge_rows]
    shape = (chunks, lanes)
    look_up = table_lookup(word_ref)
    border = carried.shape[0] // (chunks + 2)
    carried[:border, :] = jnp.zeros((border, lanes), jnp.float32)
    carried[-border:, :] = jnp.zeros((border, lanes), jnp.float32)
    light = [light_ref[i] for i in range(3)]
    together = border // (rows * depth)

    def step(trip, carry):
        colors, keeps = list(carry[0]), list(carry[1])
        at = [brick_at[trip * together + u] for u in range(together)]
        fields = [[[tile_ref[b, r, k] for k in range(depth)] for r in range(padded_rows)] for b in at]
        kept = []
        for u, (b, field) in enumerate(zip(at, fields)):
            cells = [x for line in field[1:-1] for x in line]
            column = column_differences(cells, carried, u * len(cells))
            for r in range(rows):
                for k, dz in enumerate(depth_differences(field[r + 1])):
                    x = field[r + 1][k]
                    dx = column[r * depth + k]
                    color, opacity = look_up(x)
                    weight = keeps[r] * opacity
                    facing = dz * light[0] + dx * light[2]
                    squared = (dz * dz + 1.0) + dx * dx
                    if r in edge_rows:
                        values = [weight * color[c] for c in range(3)] + [facing, squared]
                        kept.append((b, edge_rows.index(r), k, values))
                    else:
                        i = inner_rows.index(r)
                        dy = field[r + 2][k] - field[r][k]
                        shaded = weight * shading_of(facing + dy * light[1], squared + dy * dy)
                        for c in range(3):
                            slot = c * len(inner_rows) + i
                            colors[slot] = colors[slot] + shaded * color[c]
                    keeps[r] = keeps[r] - weight
        for b, i, k, values in kept:
            for v, value in enumerate(values):
                part_ref[b, i, k, v] = value
        return tuple(colors), tuple(keeps)

    zero, one = jnp.zeros(shape, jnp.float32), jnp.ones(shape, jnp.float32)
    colors, keeps = lax.fori_loop(
        0, bricks // together, step, ((zero,) * (3 * len(inner_rows)), (one,) * rows))
    for i, value in enumerate(colors):
        color_sum_ref[i] = value
    for r, value in enumerate(keeps):
        keep_ref[r] = value


def finish_kernel(edge_rows, first_ref, last_ref, light_ref, tile_ref, other_ref, part_ref, color_sum_ref, keep_ref,
                  out_ref, staged):
    bricks, padded_rows, depth, chunks, lanes = tile_ref.shape
    rows = padded_rows - 2
    inner_rows = [r for r in range(rows) if r not in edge_rows]
    shape = (chunks, lanes)
    light_rows = light_ref[1]
    is_first, is_last = first_ref[...] == 1.0, last_ref[...] == 1.0

    together = 16 if bricks % 16 == 0 else 1

    def step(trip, colors):
        colors = list(colors)
        for u in range(together):
            b = trip * together + u
            for i, r in enumerate(edge_rows):
                for k in range(depth):
                    above, below = tile_ref[b, r, k], tile_ref[b, r + 2, k]
                    if r == 0:
                        above = jnp.where(is_first, other_ref[b, k], above)
                    if r == rows - 1:
                        below = jnp.where(is_last, other_ref[b, k], below)
                    dy = below - above
                    facing = part_ref[b, i, k, 3] + dy * light_rows
                    shading = shading_of(facing, part_ref[b, i, k, 4] + dy * dy)
                    for c in range(3):
                        slot = c * len(edge_rows) + i
                        colors[slot] = colors[slot] + shading * part_ref[b, i, k, c]
        return tuple(colors)

    zero = jnp.zeros(shape, jnp.float32)
    pitch = 4 * rows * ROW_STEP + 1
    edge_colors = lax.fori_loop(0, bricks // together, step, (zero,) * (3 * len(edge_rows)))
    for r in range(rows):
        for c in range(3):
            if r in edge_rows:
                value = edge_colors[c * len(edge_rows) + edge_rows.index(r)]
            else:
                value = color_sum_ref[c * len(inner_rows) + inner_rows.index(r)]
            staged[pl.ds((c * rows + r) * ROW_STEP, chunks, stride=pitch), :] = value * (1.0 / COLOR_UNIT)
        staged[pl.ds((3 * rows + r) * ROW_STEP, chunks, stride=pitch), :] = 1.0 - keep_ref[r]
    for c in range(4):
        for q in range(chunks):
            start = q * pitch + c * rows * ROW_STEP
            source = pl.ds(start, rows, stride=ROW_STEP) if rows > 1 else pl.ds(start, 1)
            out_ref[c, 0, :, q * LANES:(q + 1) * LANES] = staged[source, :]


def shards(scalar, bin_index, color_table, opacity_table, light_dir, view_order):
    depth, rows, cols = scalar.shape
    bricks, bands = lax.axis_size("gz"), lax.axis_size("gy")
    tile_rows = rows // bricks
    chunks = cols // LANES
    edge_rows = sorted({0, tile_rows - 1})
    inner_count = tile_rows - len(edge_rows)
    vmem = pl.BlockSpec(memory_space=pltpu.VMEM)
    smem = pl.BlockSpec(memory_space=pltpu.SMEM)
    params = pltpu.CompilerParams(vmem_limit_bytes=32 << 20)
    cells = bricks * depth * cols
    lines = (chunks, LANES)
    halves = (color_table.shape[1] - 1) // LANES
    together = 16 if bricks % 16 == 0 else 1
    pieces = 2 if rows % (2 * SUB) == 0 else 1
    hbm = pl.BlockSpec(memory_space=pltpu.HBM)
    given = [scalar, view_order, light_dir, color_table, opacity_table]
    sent, brick_at, words, light_rows, first, final, later = pl.pallas_call(
        functools.partial(pack_kernel, bricks),
        out_shape=[
            pltpu.VMEM((bricks, (tile_rows + 2) * depth * chunks, LANES), jnp.float32),
            pltpu.SMEM((bricks,), jnp.int32),
            jax.ShapeDtypeStruct((3, halves) + lines, jnp.int32),
            jax.ShapeDtypeStruct((3,) + lines, jnp.float32),
        ] + [jax.ShapeDtypeStruct(lines, jnp.float32)] * 3,
        in_specs=[hbm] * 5,
        out_specs=[vmem, smem] + [vmem] * 5,
        scratch_shapes=[
            pltpu.VMEM(scalar.shape, scalar.dtype),
            pltpu.VMEM((depth * chunks * (rows * ROW_STEP + 1), LANES), scalar.dtype),
            pltpu.SMEM(view_order.shape, view_order.dtype),
            pltpu.SMEM(light_dir.shape, light_dir.dtype),
            pltpu.VMEM(color_table.shape, color_table.dtype),
            pltpu.VMEM(opacity_table.shape, opacity_table.dtype),
            pltpu.SemaphoreType.DMA((pieces,)),
            pltpu.SemaphoreType.DMA((4,)),
        ],
        compiler_params=params,
        name="pack_rows",
    )(*[pltpu.with_memory_space_constraint(x, pltpu.HBM) for x in given])
    arrived = lax.all_to_all(
        sent, "gz", split_axis=0, concat_axis=0, tiled=True, axis_index_groups=[exchange_order(bricks)])
    tiles = arrived.reshape(bricks, tile_rows + 2, depth, chunks, LANES)

    last = bricks - 1
    pairs = [(g, g + 1) for g in range(bands - 1)]
    pairs += [(last * bands + g + 1, last * bands + g) for g in range(bands - 1)]
    wrapped = tiles[:, 0] * first + tiles[:, -1] * later
    other = lax.ppermute(wrapped, ("gz", "gy"), pairs)
    parts, color_sums, keeps = pl.pallas_call(
        functools.partial(main_kernel, edge_rows),
        out_shape=[
            jax.ShapeDtypeStruct((bricks, len(edge_rows), depth, 5, chunks, LANES), jnp.float32),
            jax.ShapeDtypeStruct((max(3 * inner_count, 1), chunks, LANES), jnp.float32),
            jax.ShapeDtypeStruct((tile_rows, chunks, LANES), jnp.float32),
        ],
        in_specs=[smem] + [vmem] * 3,
        out_specs=[vmem, vmem, vmem],
        scratch_shapes=[pltpu.VMEM(((chunks + 2) * (together * tile_rows * depth + 1), LANES), jnp.float32)],
        compiler_params=params,
        cost_estimate=pl.CostEstimate(
            flops=100 * cells * tile_rows, bytes_accessed=24 * cells * tile_rows, transcendentals=0),
        name="main_rows",
    )(brick_at, light_rows, words, tiles)
    return pl.pallas_call(
        functools.partial(finish_kernel, edge_rows),
        out_shape=jax.ShapeDtypeStruct((4, 1, tile_rows, cols), jnp.float32),
        in_specs=[vmem] * 8,
        out_specs=vmem,
        scratch_shapes=[pltpu.VMEM((chunks * (4 * tile_rows * ROW_STEP + 1), LANES), jnp.float32)],
        compiler_params=params,
        cost_estimate=pl.CostEstimate(
            flops=10 * cells * tile_rows, bytes_accessed=24 * cells * tile_rows, transcendentals=0),
        name="edge_rows",
    )(first, final, light_rows, tiles, other, parts, color_sums, keeps)


def solution(mesh):
    in_specs = (P("gz", "gy", None), P("gz", "gy", None), P(), P(), P(), P())
    out_specs = P(None, "gy", "gz", None)
    return jax.shard_map(shards, mesh=mesh, in_specs=in_specs, out_specs=out_specs, check_vma=False)
```
